32 devices in a mesh: section: 4 (over x, core), dp: 8 (over z, y).
Axes of the slice: x: 2, y: 2, z: 4, core: 2. Of those that a mesh axis runs over, the one named last changes fastest.
Arguments:
- section_ins: bfloat16 [4, 8192, 768], P('section', 'dp'), may hold values from -6 to 6
- segments: int32 [16, 512], P('dp'), may hold values from 0 to 3, never falling along the last dimension, each value on 1 to 256 neighbouring positions
- buckets: int32 [2, 1023], replicated, may hold values from 0 to 31
- section_mats: bfloat16 [4, 3, 768, 3072], P('section'), may hold values from -3 to 3
- gains: float32 [7, 768], replicated, may hold values from 0.1 to 1.9
- tables: float32 [2, 32, 12], replicated, may hold values from -4 to 4
Outputs:
- section_outs: float32 [4, 8192, 768], P('section', 'dp')
- mats_grad: float32 [4, 3, 768, 3072], P('section', None, 'dp')
- gains_grad: float32 [7, 768], replicated
- tables_grad: float32 [2, 32, 12], replicated
The draws below stay inside these ranges and needn't reach their ends.
All inputs are finite; a program needn't handle non-finite values.
Results may differ from the reference program's by a relative error of at most 0.025.
Values may be sent and summed in bfloat16 or wider, within the bound.
No kernel may reach another device: no remote copies, remote signals or barrier semaphores. Data moves between devices by JAX's collectives and lax.ppermute only.
A program may use at most 384 MiB of HBM per device.

```python
import math
from functools import partial
import jax
import jax.numpy as jnp
import numpy as np
from jax import lax

D = 768
H = 12
HD = 64
FF = 3072
NB = 32
LEN = 512
ROWS = 16
TOKENS = 8192
N_SECTION = 4


def draw_section_mats(key, part):
    shape = (4, 3, D, FF)
    noise = jax.random.truncated_normal(key, -4.0, 4.0, shape, jnp.float32)
    section_ids = lax.broadcasted_iota(jnp.int32, shape, 0)
    slot_ids = lax.broadcasted_iota(jnp.int32, shape, 1)
    column_group = lax.broadcasted_iota(jnp.int32, shape, 3) // D
    base = float(D) ** (-0.5)
    attention_scale = jnp.where(column_group < 2, 0.45 * base, jnp.where(column_group == 2, base, 4.0 * base))
    attention_slot = (slot_ids == 0) & (section_ids != 1)
    output_slot = (section_ids == 1) & (slot_ids == 1) | (section_ids == 3) & (slot_ids == 2)
    scale = jnp.where(attention_slot, attention_scale, jnp.where(output_slot, 1.4 * float(FF) ** (-0.5), base))
    return (noise * scale).astype(jnp.bfloat16)


def with_ends(values, rng, low, largest):
    shape = values.shape
    index_at = [jax.random.randint(jax.random.fold_in(rng, axis), (), 0, shape[axis]) for axis in range(len(shape))]
    values = values.at[tuple(index_at)].set(low)
    longest = shape.index(max(shape))
    index_at[longest] = (index_at[longest] + 1) % shape[longest]
    return values.at[tuple(index_at)].set(largest)


def block_levels(stream_key, dims, pieces, least, largest):
    def one(position, shards_of):
        steps = jax.random.uniform(jax.random.fold_in(jax.random.fold_in(stream_key, 6), position), (shards_of,), jnp.float32, least / len(pieces), largest / len(pieces))
        return jnp.repeat(jnp.exp(steps), dims[position] // shards_of).reshape((-1,) + (1,) * (len(dims) - position - 1))

    factor_of = one(*pieces[0])
    for cut in pieces[1:]:
        factor_of = factor_of * one(*cut)
    return factor_of


def length_profile(number_of, total, bound, lean):
    weights = [(1 << 20) // math.isqrt(standing ** lean) + 1 for standing in range(2, number_of + 1)]
    rest, given = total - bound - (number_of - 1), [1] * (number_of - 1)
    while rest > 0:
        movable = [i for i in range(number_of - 1) if given[i] < bound]
        whole, left = sum([weights[i] for i in movable]), rest
        for i in movable:
            extra = min(bound - given[i], max(1, left * weights[i] // whole), rest)
            given[i] = given[i] + extra
            rest = rest - extra
    return np.array([bound] + given)


def uneven_parts(rng, number_of, total, limit, lean):
    if number_of == 2:
        one = jax.random.randint(rng, (), max(1, total - limit), min(limit, total - 1) + 1)
        return jnp.stack([one, total - one])
    tallies = jnp.asarray(length_profile(number_of, total, limit, lean), jnp.int32)
    couples = (number_of - 1) // 2
    source_of, receiver = tallies[1:1 + 2 * couples:2], tallies[2:2 + 2 * couples:2]
    room = jnp.minimum(source_of - 1, limit - receiver)
    shifted = jax.random.randint(jax.random.fold_in(rng, 1), (couples,), 0, 1 << 20) % (room + 1)
    tallies = tallies.at[1:1 + 2 * couples:2].set(source_of - shifted).at[2:2 + 2 * couples:2].set(receiver + shifted)
    return tallies[jax.random.permutation(jax.random.fold_in(rng, 2), number_of)]


def bell_draw(stream_key, extent, scale, most, shards=(), held_as=jnp.bfloat16):
    level = block_levels(stream_key, extent, shards, -0.22, 0.18) if shards else 1.0
    drawn = jax.random.normal(stream_key, extent, jnp.float32) * scale * level
    return jnp.minimum(jnp.maximum(drawn, -most), most).astype(held_as)


def setup_inputs(seed: int = 0) -> dict:
    seeds = jax.random.split(jax.random.key(seed), 7)
    section_ins = bell_draw(seeds[0], (N_SECTION, TOKENS, D), 1.0, 6.0, ((0, 4), (1, 8)))
    segments = jax.vmap(lambda own: jnp.searchsorted(jnp.cumsum(uneven_parts(own, 4, LEN, LEN // 2, 0)), jnp.arange(LEN), side="right"))(jax.random.split(seeds[1], ROWS)).reshape((ROWS, LEN)).astype(jnp.int32)
    buckets = with_ends(jax.random.randint(seeds[2], (2, 2 * LEN - 1), 0, NB), jax.random.fold_in(seeds[2], 1), 0, NB - 1).astype(jnp.int32)
    section_mats = draw_section_mats(jax.random.fold_in(seeds[6], 71), 0)
    gains = jnp.clip(1.0 + 0.18 * jax.random.normal(seeds[4], (7, D), jnp.float32), 0.1, 1.9)
    tables = bell_draw(seeds[5], (2, NB, H), 1.0, 4.0, (), jnp.float32)
    return dict(section_ins=section_ins, segments=segments, buckets=buckets, section_mats=section_mats, gains=gains, tables=tables)


@jax.custom_vjp
def low(v):
    return lax.optimization_barrier(v.astype(jnp.bfloat16)).astype(jnp.float32)

@jax.custom_vjp
def low_back(v):
    return v

def low_keep(v):
    return (low(v), None)

def low_pass(kept, grad):
    return (grad,)

def back_keep(v):
    return (v, None)

def back_low(kept, grad):
    return (low(grad),)
low.defvjp(low_keep, low_pass)
low_back.defvjp(back_keep, back_low)
epsilon = 1e-06
negative_fill = -1000000000.0
highest = lax.Precision.HIGHEST

def norm(stream, gain):
    return stream * lax.rsqrt(lax.optimization_barrier(jnp.mean(stream * stream, axis=-1, keepdims=True)) + epsilon) * gain

def position_bias(table, bucket_row):
    offsets = jnp.arange(LEN, dtype=jnp.int32)[None, :] - jnp.arange(LEN, dtype=jnp.int32)[:, None] + LEN - 1
    return jnp.transpose(table[bucket_row[offsets]], (2, 0, 1))

def attend(bias, causal, query, keys, values, segs):
    query_heads = query.reshape(LEN, H, HD)
    key_heads = keys.reshape(LEN, H, HD)
    value_heads = values.reshape(LEN, H, HD)
    scores = low_back(jnp.einsum('ihd,jhd->hij', query_heads, key_heads, precision=highest) + bias)
    allowed = segs[:, None] == segs[None, :]
    if causal:
        allowed = allowed & (jnp.arange(LEN)[None, :] <= jnp.arange(LEN)[:, None])
    scores = jnp.where(allowed[None], scores, negative_fill)
    top = lax.optimization_barrier(jnp.max(scores, axis=-1, keepdims=True))
    exponent = jnp.exp(scores - top)
    weights = low(exponent / lax.optimization_barrier(jnp.sum(exponent, axis=-1, keepdims=True)))
    mixed = jnp.einsum('hij,jhd->ihd', weights, value_heads, precision=highest)
    return mixed.reshape(LEN, D)

def attention(query, keys, values, segments, bias, causal):
    rows = segments.shape[0]
    row_attend = jax.checkpoint(partial(attend, bias, causal))
    mixed = lax.map(lambda items: row_attend(*items), (query.reshape(rows, LEN, D), keys.reshape(rows, LEN, D), values.reshape(rows, LEN, D), segments))
    return mixed.reshape(rows * LEN, D)

def self_block(stream, gain, weight, table, bucket_row, segments, causal):
    normed = low(norm(stream, gain))
    projected = low(low_back(jnp.dot(normed, weight[:, :3 * D], precision=highest)))
    mixed = attention(projected[:, :D], projected[:, D:2 * D], projected[:, 2 * D:], segments, position_bias(table, bucket_row), causal)
    mixed = low(low_back(mixed))
    return stream + low_back(jnp.dot(mixed, weight[:, 3 * D:], precision=highest))

def cross_block(stream, memory, gain, weight, segments):
    normed = low(norm(stream, gain))
    query = low(low_back(jnp.dot(normed, weight[:, :D], precision=highest)))
    keyval = low(low_back(jnp.dot(memory, weight[:, D:3 * D], precision=highest)))
    mixed = low(low_back(attention(query, keyval[:, :D], keyval[:, D:], segments, 0.0, False)))
    return stream + low_back(jnp.dot(mixed, weight[:, 3 * D:], precision=highest))

def ffn_block(stream, gain, weight_in, weight_out):
    normed = low(norm(stream, gain))
    upward = low_back(jnp.dot(normed, weight_in, precision=highest))
    hidden = low(jax.nn.gelu(upward, approximate=True))
    return stream + low_back(jnp.dot(hidden, weight_out.T, precision=highest))

def forward(enc_in, dec_in, mats, gains, tables, segments, buckets):
    first = low(low_back(self_block(enc_in, gains[0], mats[0, 0], tables[0], buckets[0], segments, False)))
    enc_out = norm(ffn_block(first, gains[1], mats[1, 0], mats[1, 1]), gains[2])
    decoded = low(low_back(self_block(dec_in, gains[3], mats[2, 0], tables[1], buckets[1], segments, True)))
    memory = low(low_back(enc_out))
    crossed = cross_block(decoded, memory, gains[4], mats[3, 0], segments)
    dec_out = norm(ffn_block(crossed, gains[5], mats[3, 1], mats[3, 2]), gains[6])
    return (enc_out, dec_out)

def reference(section_ins, segments, buckets, section_mats, gains, tables):
    inputs = section_ins.astype(jnp.float32)
    mats = section_mats.astype(jnp.float32)

    def wrapped(enc_in, dec_in, mat_values, gain_values, table_values):
        return forward(enc_in, dec_in, mat_values, gain_values, table_values, segments, buckets)
    (enc_out, dec_out), pull = jax.vjp(wrapped, inputs[0], inputs[2], mats, gains, tables)
    grad_enc, grad_dec, grad_mats, grad_gains, grad_tables = pull((inputs[1], inputs[3]))
    section_outs = jnp.stack([grad_enc, enc_out, grad_dec, dec_out])
    return (section_outs, grad_mats, grad_gains, grad_tables)
```

```python
from functools import partial

import jax
import jax.numpy as jnp
from jax import lax
from jax.experimental import pallas as pl
from jax.experimental.pallas import tpu as pltpu
from jax.sharding import PartitionSpec as P

H = 12
HD = 64
PAIRS = H // 2
EPS = 1e-06
GELU = 0.7978845608028654
CUBIC = 0.044715
MASKED = -1e38
F32 = jnp.float32
BF16 = jnp.bfloat16
ROW_STEP = 128
VMEM_LIMIT = 60 * 1024 * 1024


def mm(a, b):
    return jnp.dot(a, b, preferred_element_type=F32)


def mm_nt(a, b):
    return lax.dot_general(a, b, (((1,), (1,)), ((), ())), preferred_element_type=F32)


def inverse_rms(x):
    return lax.rsqrt(jnp.mean(x * x, axis=-1, keepdims=True) + EPS)


def row_chunks(length):
    return [pl.ds(start, ROW_STEP) for start in range(0, length, ROW_STEP)]


def rms_back(x, gain, dy):
    r = inverse_rms(x)
    inner = jnp.mean(dy * gain * x, axis=-1, keepdims=True)
    dx = r * gain * dy - x * (r * r * r) * inner
    return dx, jnp.sum(dy * x * r, axis=0, keepdims=True)


def copy_all(sems, first, *pairs):
    started = []
    for offset, (source, target) in enumerate(pairs):
        one = pltpu.make_async_copy(source, target, sems.at[first + offset])
        one.start()
        started.append(one)
    return started


def wait_all(started):
    for one in started:
        one.wait()


def head_lanes(second):
    lane = lax.broadcasted_iota(jnp.int32, (1, 2 * HD), 1)
    return (lane >= HD) if second else (lane < HD)


def fill_mask(mask_v, seg_row, transposed, slack):
    length = seg_row.shape[1]
    down = jnp.broadcast_to(seg_row, (128, length)).T
    for c in range(length // 128):
        along = seg_row[:, c * 128 : (c + 1) * 128]
        r = lax.broadcasted_iota(jnp.int32, (length, 128), 0)
        q = lax.broadcasted_iota(jnp.int32, (length, 128), 1) + c * 128
        key, query = (r, q) if transposed else (q, r)
        ok = (down == along) & (key <= query + slack)
        mask_v[:, c * 128 : (c + 1) * 128] = jnp.where(ok, 0.0, MASKED)


def fill_toeplitz(toe_v, vec_v, table, bucket_row):
    count = bucket_row.shape[1]
    ids = lax.broadcasted_iota(jnp.int32, (table.shape[1], count), 0)
    onehot = (ids == bucket_row).astype(F32)
    vec = jnp.dot(table, onehot, precision=lax.Precision.HIGHEST, preferred_element_type=F32)
    vec_v[:, :count] = vec

    @pl.loop(0, H)
    def _(h):
        wide = jnp.broadcast_to(vec_v[pl.ds(h, 1), :], (128, vec_v.shape[1]))
        rolled = pltpu.roll(wide, vec_v.shape[1] - 127, 1, stride=1, stride_axis=0)
        toe_v[h] = rolled[:, : toe_v.shape[2]]


def attend(q_v, k_v, v_v, q0, k0, v0, mask_v, toe_v, s_v, p_v, mix_v, lse_v):
    length = mix_v.shape[0]

    @pl.loop(0, PAIRS)
    def _(hp):
        at = lambda base: pl.ds(pl.multiple_of(base + hp * 128, 128), 128)
        q2, k2, v2 = q_v[:, at(q0)], k_v[:, at(k0)], v_v[:, at(v0)]
        low = head_lanes(False)
        outs, tops = [], []
        for a in range(2):
            mine = head_lanes(a == 1)
            s_v[a] = mm_nt(jnp.where(mine, q2, jnp.zeros_like(q2)), k2)
            top = []
            for c in range(length // 128):
                rows = pl.ds(c * 128, 128)
                s = s_v[a, rows, :] + mask_v[rows, :]
                if toe_v is not None:
                    left = toe_v.shape[2] - length - c * 128
                    s = s + toe_v[2 * hp + a, :, left : left + length]
                m = jnp.max(s, axis=-1, keepdims=True)
                p_v[a, rows, :] = jnp.exp(s - m).astype(BF16)
                top.append(m)
            tops.append(jnp.concatenate(top, axis=0))
            outs.append(mm(p_v[a], jnp.where(mine, v2, jnp.ones_like(v2))))
        total = pltpu.roll(jnp.where(low, outs[1], outs[0]), HD, 1)
        mix_v[:, at(0)] = (jnp.where(low, outs[0], outs[1]) / total).astype(BF16)
        stat = (jnp.where(low, tops[0], tops[1]) + jnp.log(total)).T
        lse_v[pl.ds(2 * hp, 1), :] = stat[0:1, :]
        lse_v[pl.ds(2 * hp + 1, 1), :] = stat[HD : HD + 1, :]


def attend_back(q_v, k_v, v_v, dm_v, mix_v, q0, k0, v0, mask_v, toe_v, lse_v, dp_v, s_v, p_v, ds_v, out_v, o0, acc_v):
    length = mix_v.shape[0]

    @pl.loop(0, PAIRS)
    def _(hp):
        at = lambda base: pl.ds(pl.multiple_of(base + hp * 128, 128), 128)
        q2, k2, v2, dm2 = q_v[:, at(q0)], k_v[:, at(k0)], v_v[:, at(v0)], dm_v[:, at(0)]
        low = head_lanes(False)
        prod = (dm2.astype(F32) * mix_v[:, at(0)].astype(F32)).T
        k2t = k2.T
        dvs, dks, dqs = [], [], []
        for a in range(2):
            mine = head_lanes(a == 1)
            s_v[a] = mm_nt(jnp.where(mine, k2, jnp.zeros_like(k2)), q2)
            dp_v[a] = mm_nt(jnp.where(mine, v2, jnp.zeros_like(v2)), dm2)
            delta = jnp.sum(prod[a * HD : (a + 1) * HD, :], axis=0, keepdims=True)
            lse = lse_v[pl.ds(2 * hp + a, 1), :]
            for c in range(length // 128):
                rows = pl.ds(c * 128, 128)
                s = s_v[a, rows, :] + mask_v[rows, :]
                if toe_v is not None:
                    left = toe_v.shape[2] - length - c * 128
                    s = s + toe_v[2 * hp + a, :, left : left + length]
                p = jnp.exp(s - lse)
                p_v[a, rows, :] = p.astype(BF16)
                ds = p * (dp_v[a, rows, :] - delta)
                ds_v[a, rows, :] = ds.astype(BF16)
                if acc_v is not None:
                    acc_v[2 * hp + a, :, left : left + length] += ds
            dvs.append(mm(p_v[a], dm2))
            dks.append(mm(ds_v[a], q2))
            dqs.append(mm(k2t[a * HD : (a + 1) * HD, :], ds_v[a]))
        out_v[:, at(o0)] = jnp.concatenate(dqs, axis=0).T.astype(BF16)
        out_v[:, at(o0 + PAIRS * 128)] = jnp.where(low, dks[0], dks[1]).astype(BF16)
        out_v[:, at(o0 + 2 * PAIRS * 128)] = jnp.where(low, dvs[0], dvs[1]).astype(BF16)


def fold_diagonals(acc_v, diag_v, fold_v):
    extent = acc_v.shape[2]

    @pl.loop(0, H)
    def _(h):
        fold_v[:, :extent] = acc_v[h]
        fold_v[:, extent:] = jnp.zeros((128, fold_v.shape[1] - extent), F32)
        wide = fold_v.shape[1]
        half = 64
        value = fold_v[...]
        while half >= 1:
            upper, lower = value[:half], value[half:]
            value = pltpu.roll(upper, half, 1) + lower
            half //= 2
        diag_v[pl.ds(h, 1), :] = value


def gelu_parts(u):
    square = u * u
    bend = u * (GELU + (GELU * CUBIC) * square)
    half = 0.5 + 0.5 * jnp.tanh(bend)
    hidden = u * half
    slope = half + 2.0 * hidden * (1.0 - half) * (GELU + (3.0 * GELU * CUBIC) * square)
    return hidden, slope


def ffn_up(n_v, win_v, h_v, slope_v):
    tile = 512

    @pl.loop(0, win_v.shape[1] // tile)
    def _(t):
        cols = pl.ds(pl.multiple_of(t * tile, tile), tile)
        hidden, slope = gelu_parts(mm(n_v[...], win_v[:, cols]))
        h_v[:, cols] = hidden.astype(BF16)
        slope_v[:, cols] = slope.astype(BF16)


def rows_out(a_v, w_v, w0, out_v, add):
    tile = 256
    depth = a_v.shape[1]

    @pl.loop(0, w_v.shape[0] // tile)
    def _(t):
        cols = pl.ds(pl.multiple_of(t * tile, tile), tile)
        part = mm_nt(a_v[...], w_v[cols, w0 : w0 + depth])
        if add:
            out_v[:, cols] = out_v[:, cols] + part
        else:
            out_v[:, cols] = part.astype(out_v.dtype)


def ffn_down(d_v, wout_v, slope_v, du_v):
    tile = 512

    @pl.loop(0, wout_v.shape[1] // tile)
    def _(t):
        cols = pl.ds(pl.multiple_of(t * tile, tile), tile)
        grad = mm(d_v[...], wout_v[:, cols])
        du_v[:, cols] = (grad * slope_v[:, cols].astype(F32)).astype(BF16)


def project(a_v, w_v, w0, out_v, o0, width):
    tile = 384

    @pl.loop(0, width // tile)
    def _(t):
        source = pl.ds(pl.multiple_of(w0 + t * tile, 128), tile)
        target = pl.ds(pl.multiple_of(o0 + t * tile, 128), tile)
        out_v[:, target] = mm(a_v[...], w_v[:, source]).astype(out_v.dtype)


def flops_of(matmuls, size):
    return pl.CostEstimate(flops=matmuls * 2 * 512 * 768 * 3072, bytes_accessed=size, transcendentals=0)


def call(kernel, outs, scratch, ins, in_vmem, cost):
    spec = lambda small: pl.BlockSpec(memory_space=pltpu.VMEM if small else pl.ANY)
    return pl.pallas_call(
        kernel,
        out_shape=outs,
        in_specs=[spec(small) for small in in_vmem],
        out_specs=[spec(False) for _ in outs],
        scratch_shapes=scratch,
        compiler_params=pltpu.CompilerParams(vmem_limit_bytes=VMEM_LIMIT),
        cost_estimate=cost,
    )(*ins)


def shape(dims, kind):
    return jax.ShapeDtypeStruct(dims, kind)


def self_forward(row, ins, mats, gains, segs, tables, buckets):
    length, width = segs.shape[1], ins.shape[1]
    dist = 2 * length

    def kernel(x_h, w_h, gain_r, seg_r, table_r, bucket_r, e_h, n_h, qkv_h, mix_h, lse_h,
               x_v, w_v, n_v, qkv_v, mix_v, lse_v, e_v, mask_v, toe_v, vec_v, s_v, p_v, sems):
        section = lax.axis_index("section")

        @pl.when(section % 2 == 0)
        def _():
            side = section // 2
            loads = copy_all(
                sems, 0,
                (x_h.at[pl.ds(row * length, length)], x_v),
                *[(w_h.at[0, :, pl.ds(c * width, width)], w_v.at[:, pl.ds(c * width, width)]) for c in range(4)],
            )
            fill_mask(mask_v, seg_r[row : row + 1, :], False, jnp.where(section == 2, 0, 2 * length))
            fill_toeplitz(toe_v, vec_v, table_r[side], bucket_r[pl.ds(side, 1), :])
            gain = gain_r[pl.ds(3 * side, 1), :]
            loads[0].wait()
            for rows in row_chunks(length):
                x = x_v[rows, :].astype(F32)
                n_v[rows, :] = (x * inverse_rms(x) * gain).astype(BF16)
            stores = copy_all(sems, 5, (n_v, n_h))
            wait_all(loads[1:4])
            project(n_v, w_v, 0, qkv_v, 0, 3 * width)
            stores += copy_all(sems, 6, (qkv_v, qkv_h))
            attend(qkv_v, qkv_v, qkv_v, 0, width, 2 * width, mask_v, toe_v, s_v, p_v, mix_v, lse_v)
            stores += copy_all(sems, 7, (mix_v, mix_h), (lse_v, lse_h))
            loads[4].wait()

            @pl.loop(0, width // 256)
            def _(t):
                cols = pl.ds(pl.multiple_of(t * 256, 256), 256)
                part = mm(mix_v[...], w_v[:, pl.ds(pl.multiple_of(3 * width + t * 256, 256), 256)])
                e_v[:, cols] = (x_v[:, cols].astype(F32) + part).astype(BF16)

            stores += copy_all(sems, 9, (e_v, e_h))
            wait_all(stores)

    return call(
        kernel,
        [
            shape((length, width), BF16),
            shape((length, width), BF16),
            shape((length, 3 * width), BF16),
            shape((length, width), BF16),
            shape((16, length), F32),
        ],
        [
            pltpu.VMEM((length, width), BF16),
            pltpu.VMEM((width, 4 * width), BF16),
            pltpu.VMEM((length, width), BF16),
            pltpu.VMEM((length, 3 * width), BF16),
            pltpu.VMEM((length, width), BF16),
            pltpu.VMEM((16, length), F32),
            pltpu.VMEM((length, width), BF16),
            pltpu.VMEM((length, length), F32),
            pltpu.VMEM((H, 128, 2 * length - 128), F32),
            pltpu.VMEM((16, dist), F32),
            pltpu.VMEM((2, length, length), F32),
            pltpu.VMEM((2, length, length), BF16),
            pltpu.SemaphoreType.DMA((10,)),
        ],
        [ins, mats, gains, segs, tables, buckets],
        [False, False, True, True, True, True],
        flops_of(3, 12 << 20),
    )


def self_backward(first, ins, mats, gains, segs, tables, flipped, g_enc, g_dec, kept):
    length, width = segs.shape[1], ins.shape[1]
    dist = 2 * length

    def kernel(x_h, w_h, gain_r, seg_r, table_r, bucket_r, ge_h, gd_h, n0_h, qkv0_h, mix0_h, lse0_h,
               n1_h, qkv1_h, mix1_h, lse1_h, gx_h, dgain_h, diag_h, a_h, b_h,
               x_v, w_v, qkv_v, mix_v, lse_v, d_v, dm_v, dqkv_v, dn_v, gx_v, dgain_v, diag_v,
               mask_v, toe_v, acc_v, vec_v, fold_v, s_v, dp_v, p_v, ds_v, sems):
        section = lax.axis_index("section")

        def run(side, row, g_h, n_h, qkv_h, mix_h, lse_h):
            loads = copy_all(
                sems, 0,
                (g_h, d_v),
                (w_h.at[0, :, pl.ds(3 * width, width)], w_v.at[:, pl.ds(3 * width, width)]),
                (mix_h, mix_v),
                (lse_h, lse_v),
                (qkv_h, qkv_v),
                (w_h.at[0, :, pl.ds(0, 3 * width)], w_v.at[:, pl.ds(0, 3 * width)]),
                (x_h.at[pl.ds(row * length, length)], x_v),
            )
            through = copy_all(
                sems, 7,
                (n_h, a_h.at[:, pl.ds(0, width)]),
                (mix_h, a_h.at[:, pl.ds(width, width)]),
                (g_h, b_h.at[:, pl.ds(3 * width, width)]),
            )
            fill_mask(mask_v, seg_r[row : row + 1, :], True, 0 if side else 2 * length)
            fill_toeplitz(toe_v, vec_v, table_r[side], bucket_r[side : side + 1, :])
            acc_v[...] = jnp.zeros_like(acc_v)
            gain = gain_r[3 * side : 3 * side + 1, :]
            wait_all(loads[:2])
            rows_out(d_v, w_v, 3 * width, dm_v, False)
            wait_all(loads[2:5])
            attend_back(qkv_v, qkv_v, qkv_v, dm_v, mix_v, 0, width, 2 * width, mask_v, toe_v, lse_v,
                        dp_v, s_v, p_v, ds_v, dqkv_v, 0, acc_v)
            stores = copy_all(sems, 10, (dqkv_v, b_h.at[:, pl.ds(0, 3 * width)]))
            wait_all(loads[5:])
            rows_out(dqkv_v, w_v, 0, dn_v, False)
            total = jnp.zeros((1, width), F32)
            for rows in row_chunks(length):
                dx, dgain = rms_back(x_v[rows, :].astype(F32), gain, dn_v[rows, :])
                gx_v[rows, :] = d_v[rows, :].astype(F32) + dx
                total = total + dgain
            dgain_v[...] = total
            stores += copy_all(sems, 11, (gx_v, gx_h), (dgain_v, dgain_h))
            fold_diagonals(acc_v, diag_v, fold_v)
            stores += copy_all(sems, 13, (diag_v, diag_h))
            wait_all(through)
            wait_all(stores)

        @pl.when(section == 0)
        def _():
            kept_refs = (n0_h, qkv0_h, mix0_h, lse0_h) if first else (n1_h, qkv1_h, mix1_h, lse1_h)
            run(0, 0 if first else 1, ge_h, *kept_refs)

        @pl.when(section == 2)
        def _():
            kept_refs = (n1_h, qkv1_h, mix1_h, lse1_h) if first else (n0_h, qkv0_h, mix0_h, lse0_h)
            run(1, 1 if first else 0, gd_h, *kept_refs)

    kept0, kept1 = kept
    return call(
        kernel,
        [
            shape((length, width), F32),
            shape((1, width), F32),
            shape((16, dist), F32),
            shape((length, 2 * width), BF16),
            shape((length, 4 * width), BF16),
        ],
        [
            pltpu.VMEM((length, width), BF16),
            pltpu.VMEM((width, 4 * width), BF16),
            pltpu.VMEM((length, 3 * width), BF16),
            pltpu.VMEM((length, width), BF16),
            pltpu.VMEM((16, length), F32),
            pltpu.VMEM((length, width), BF16),
            pltpu.VMEM((length, width), BF16),
            pltpu.VMEM((length, 3 * width), BF16),
            pltpu.VMEM((length, width), F32),
            pltpu.VMEM((length, width), F32),
            pltpu.VMEM((1, width), F32),
            pltpu.VMEM((16, dist), F32),
            pltpu.VMEM((length, length), F32),
            pltpu.VMEM((H, 128, dist - 128), F32),
            pltpu.VMEM((H, 128, dist - 128), F32),
            pltpu.VMEM((16, dist), F32),
            pltpu.VMEM((128, dist), F32),
            pltpu.VMEM((2, length, length), F32),
            pltpu.VMEM((2, length, length), F32),
            pltpu.VMEM((2, length, length), BF16),
            pltpu.VMEM((2, length, length), BF16),
            pltpu.SemaphoreType.DMA((14,)),
        ],
        [ins, mats, gains, segs, tables, flipped, g_enc, g_dec, *kept0, *kept1],
        [False, False, True, True, True, True] + [False] * 10,
        flops_of(6, 16 << 20),
    )


def encoder_forward(e1, mats, gains):
    length, width = e1.shape
    hidden = mats.shape[2]

    def kernel(e_h, w_h, gain_r, out_h, send_h, mid_h, n_h, h_h, slope_h,
               e_v, win_v, wout_v, n_v, h_v, slope_v, mid_v, out_v, send_v, sems):
        @pl.when(lax.axis_index("section") == 1)
        def _():
            loads = copy_all(sems, 0, (e_h, e_v), (w_h.at[0], win_v), (w_h.at[1], wout_v))
            loads[0].wait()
            for rows in row_chunks(length):
                x = e_v[rows, :].astype(F32)
                mid_v[rows, :] = x
                n_v[rows, :] = (x * inverse_rms(x) * gain_r[1:2, :]).astype(BF16)
            stores = copy_all(sems, 3, (n_v, n_h))
            loads[1].wait()
            ffn_up(n_v, win_v, h_v, slope_v)
            stores += copy_all(sems, 4, (h_v, h_h), (slope_v, slope_h))
            loads[2].wait()
            rows_out(h_v, wout_v, 0, mid_v, True)
            for rows in row_chunks(length):
                x = mid_v[rows, :]
                y = x * inverse_rms(x) * gain_r[2:3, :]
                out_v[rows, :] = y
                send_v[rows, :] = y.astype(BF16)
            stores += copy_all(sems, 6, (send_v, send_h), (out_v, out_h), (mid_v, mid_h))
            wait_all(stores)

    return call(
        kernel,
        [
            shape((length, width), F32),
            shape((length, width), BF16),
            shape((length, width), F32),
            shape((length, width), BF16),
            shape((length, hidden), BF16),
            shape((length, hidden), BF16),
        ],
        [
            pltpu.VMEM((length, width), BF16),
            pltpu.VMEM((width, hidden), BF16),
            pltpu.VMEM((width, hidden), BF16),
            pltpu.VMEM((length, width), BF16),
            pltpu.VMEM((length, hidden), BF16),
            pltpu.VMEM((length, hidden), BF16),
            pltpu.VMEM((length, width), F32),
            pltpu.VMEM((length, width), F32),
            pltpu.VMEM((length, width), BF16),
            pltpu.SemaphoreType.DMA((9,)),
        ],
        [e1, mats, gains],
        [False, False, True],
        flops_of(2, 20 << 20),
    )


def encoder_backward(row, ins, extra, e1, mid, slope, mats, gains):
    length, width = e1.shape
    hidden = mats.shape[2]

    def kernel(cot_h, extra_h, e_h, mid_h, slope_h, w_h, gain_r, g_h, d_h, du_h, dgain_h,
               cot_v, extra_v, e_v, mid_v, slope_v, win_v, wout_v, d_v, du_v, dn_v, gm_v, g_v, dgain_v, sems):
        @pl.when(lax.axis_index("section") == 1)
        def _():
            loads = copy_all(
                sems, 0,
                (cot_h.at[pl.ds(row * length, length)], cot_v), (extra_h, extra_v), (mid_h, mid_v),
                (w_h.at[1], wout_v), (slope_h, slope_v), (w_h.at[0], win_v), (e_h, e_v),
            )
            wait_all(loads[:3])
            total = jnp.zeros((1, width), F32)
            for rows in row_chunks(length):
                dy = cot_v[rows, :].astype(F32) + extra_v[rows, :].astype(F32)
                dx, dgain = rms_back(mid_v[rows, :], gain_r[2:3, :], dy)
                gm_v[rows, :] = dx
                d_v[rows, :] = dx.astype(BF16)
                total = total + dgain
            dgain_v[1:2, :] = total
            stores = copy_all(sems, 7, (d_v, d_h))
            wait_all(loads[3:5])
            ffn_down(d_v, wout_v, slope_v, du_v)
            stores += copy_all(sems, 8, (du_v, du_h))
            wait_all(loads[5:])
            rows_out(du_v, win_v, 0, dn_v, False)
            total = jnp.zeros((1, width), F32)
            for rows in row_chunks(length):
                dx, dgain = rms_back(e_v[rows, :].astype(F32), gain_r[1:2, :], dn_v[rows, :])
                g_v[rows, :] = (gm_v[rows, :] + dx).astype(BF16)
                total = total + dgain
            dgain_v[0:1, :] = total
            stores += copy_all(sems, 9, (g_v, g_h), (dgain_v, dgain_h))
            wait_all(stores)

    return call(
        kernel,
        [
            shape((length, width), BF16),
            shape((length, width), BF16),
            shape((length, hidden), BF16),
            shape((2, width), F32),
        ],
        [
            pltpu.VMEM((length, width), BF16),
            pltpu.VMEM((length, width), BF16),
            pltpu.VMEM((length, width), BF16),
            pltpu.VMEM((length, width), F32),
            pltpu.VMEM((length, hidden), BF16),
            pltpu.VMEM((width, hidden), BF16),
            pltpu.VMEM((width, hidden), BF16),
            pltpu.VMEM((length, width), BF16),
            pltpu.VMEM((length, hidden), BF16),
            pltpu.VMEM((length, width), F32),
            pltpu.VMEM((length, width), F32),
            pltpu.VMEM((length, width), BF16),
            pltpu.VMEM((2, width), F32),
            pltpu.SemaphoreType.DMA((11,)),
        ],
        [ins, extra, e1, mid, slope, mats, gains],
        [False] * 6 + [True],
        flops_of(2, 20 << 20),
    )


def decoder_forward(d_own, d_got, m_three, m_two, ins, cot_got, mats, got_mats, gains, segs):
    length, width = d_own.shape
    hidden = mats.shape[2]
    wa, wb, wc = got_mats

    def kernel(d2_h, d3_h, m3_h, m2_h, c3_h, c2_h, w_h, wa_h, wb_h, wc_h, gain_r, seg_r,
               out_h, gc_h, q_h, mix_h, lse_h, n4_h, ka_h, kb_h, sa_h, sb_h, dgain_h,
               d_v, m_v, c_v, wca_v, win_v, wout_v, n_v, q_v, mix_v, lse_v, mask_v, s_v, p_v, h_v, slope_v,
               x_v, y_v, dn_v, n5_v, do_v, dgain_v, sems):
        section = lax.axis_index("section")

        def run(row, d_h, m_h, c_h, matrices, na_h, nb_h, oa_h, ob_h):
            loads = copy_all(
                sems, 0,
                (d_h, d_v), (m_h, m_v), (matrices[0], wca_v), (matrices[1], win_v), (matrices[2], wout_v), (c_h, c_v),
            )
            fill_mask(mask_v, seg_r[row : row + 1, :], False, 2 * length)
            loads[0].wait()
            for rows in row_chunks(length):
                x = d_v[rows, :].astype(F32)
                x_v[rows, :] = x
                n_v[rows, :] = (x * inverse_rms(x) * gain_r[4:5, :]).astype(BF16)
            stores = copy_all(sems, 6, (n_v, n4_h))
            wait_all(loads[1:3])
            project(n_v, wca_v, 0, q_v, 0, width)
            project(m_v, wca_v, width, q_v, width, 2 * width)
            stores += copy_all(sems, 7, (q_v, q_h))
            attend(q_v, q_v, q_v, 0, width, 2 * width, mask_v, None, s_v, p_v, mix_v, lse_v)
            stores += copy_all(sems, 8, (mix_v, mix_h), (lse_v, lse_h))

            @pl.loop(0, width // 256)
            def _(t):
                cols = pl.ds(pl.multiple_of(t * 256, 256), 256)
                part = mm(mix_v[...], wca_v[:, pl.ds(pl.multiple_of(3 * width + t * 256, 256), 256)])
                x_v[:, cols] = x_v[:, cols] + part

            for rows in row_chunks(length):
                x = x_v[rows, :]
                y_v[rows, :] = x
                n5_v[rows, :] = (x * inverse_rms(x) * gain_r[5:6, :]).astype(BF16)
            stores += copy_all(sems, 10, (n5_v, na_h))
            loads[3].wait()
            ffn_up(n5_v, win_v, h_v, slope_v)
            stores += copy_all(sems, 11, (h_v, ob_h))
            loads[4].wait()
            rows_out(h_v, wout_v, 0, y_v, True)
            loads[5].wait()
            total = jnp.zeros((1, width), F32)
            for rows in row_chunks(length):
                y = y_v[rows, :]
                dn_v[rows, :] = y * inverse_rms(y) * gain_r[6:7, :]
                dy, dgain = rms_back(y, gain_r[6:7, :], c_v[rows, :].astype(F32))
                total = total + dgain
                do_v[rows, :] = dy.astype(BF16)
                y_v[rows, :] = dy
            dgain_v[1:2, :] = total
            last = copy_all(sems, 12, (dn_v, out_h))
            stores += copy_all(sems, 13, (do_v, oa_h))
            ffn_down(do_v, wout_v, slope_v, slope_v)
            stores += copy_all(sems, 14, (slope_v, nb_h))
            wait_all(last)
            rows_out(slope_v, win_v, 0, dn_v, False)
            total = jnp.zeros((1, width), F32)
            for rows in row_chunks(length):
                dx, dgain = rms_back(x_v[rows, :], gain_r[5:6, :], dn_v[rows, :])
                y_v[rows, :] = y_v[rows, :] + dx
                total = total + dgain
            dgain_v[0:1, :] = total
            stores += copy_all(sems, 15, (y_v, gc_h), (dgain_v, dgain_h))
            wait_all(stores)

        @pl.when(section == 3)
        def _():
            run(0, d3_h, m3_h, c3_h.at[pl.ds(0, length)], (w_h.at[0], w_h.at[1], w_h.at[2]), ka_h, kb_h, sa_h, sb_h)

        @pl.when(section == 2)
        def _():
            run(1, d2_h, m2_h, c2_h, (wa_h, wb_h, wc_h), sa_h, sb_h, ka_h, kb_h)

    return call(
        kernel,
        [
            shape((length, width), F32),
            shape((length, width), F32),
            shape((length, 3 * width), BF16),
            shape((length, width), BF16),
            shape((16, length), F32),
            shape((length, width), BF16),
            shape((length, width), BF16),
            shape((length, hidden), BF16),
            shape((length, width), BF16),
            shape((length, hidden), BF16),
            shape((2, width), F32),
        ],
        [
            pltpu.VMEM((length, width), BF16),
            pltpu.VMEM((length, width), BF16),
            pltpu.VMEM((length, width), BF16),
            pltpu.VMEM((width, 4 * width), BF16),
            pltpu.VMEM((width, hidden), BF16),
            pltpu.VMEM((width, hidden), BF16),
            pltpu.VMEM((length, width), BF16),
            pltpu.VMEM((length, 3 * width), BF16),
            pltpu.VMEM((length, width), BF16),
            pltpu.VMEM((16, length), F32),
            pltpu.VMEM((length, length), F32),
            pltpu.VMEM((2, length, length), F32),
            pltpu.VMEM((2, length, length), BF16),
            pltpu.VMEM((length, hidden), BF16),
            pltpu.VMEM((length, hidden), BF16),
            pltpu.VMEM((length, width), F32),
            pltpu.VMEM((length, width), F32),
            pltpu.VMEM((length, width), F32),
            pltpu.VMEM((length, width), BF16),
            pltpu.VMEM((length, width), BF16),
            pltpu.VMEM((2, width), F32),
            pltpu.SemaphoreType.DMA((17,)),
        ],
        [d_own, d_got, m_three, m_two, ins, cot_got, mats, wa, wb, wc, gains, segs],
        [False] * 10 + [True, True],
        flops_of(7, 30 << 20),
    )


def decoder_backward(d_own, d_got, m_three, m_two, kept, mats, got_mats, gains, segs):
    length, width = d_own.shape
    gc, q, mix, lse, n4 = kept

    def kernel(d2_h, d3_h, m3_h, m2_h, gc_h, q_h, mix_h, lse_h, n4_h, w_h, wa_h, gain_r, seg_r,
               gm_h, gd_h, ka_h, kb_h, sa_h, sb_h, dgain_h,
               d_v, gc_v, q_v, mix_v, lse_v, w_v, do_v, dm_v, dq_v, dn_v, gm_v, gd_v, dgain_v,
               mask_v, s_v, dp_v, p_v, ds_v, sems):
        section = lax.axis_index("section")

        def run(row, d_h, m_h, matrix, fa_h, fb_h, la_h, lb_h):
            left, right = pl.ds(0, width), pl.ds(width, width)
            loads = copy_all(
                sems, 0,
                (gc_h, gc_v), (matrix, w_v), (mix_h, mix_v), (lse_h, lse_v), (q_h, q_v), (d_h, d_v),
            )
            through = copy_all(
                sems, 6,
                (n4_h, fa_h.at[:, left]), (m_h, fa_h.at[:, right]), (m_h, la_h.at[:, left]), (mix_h, la_h.at[:, right]),
            )
            fill_mask(mask_v, seg_r[row : row + 1, :], True, 2 * length)
            loads[0].wait()
            for rows in row_chunks(length):
                do_v[rows, :] = gc_v[rows, :].astype(BF16)
            stores = copy_all(sems, 10, (do_v, lb_h.at[:, right]))
            loads[1].wait()
            rows_out(do_v, w_v, 3 * width, dm_v, False)
            wait_all(loads[2:5])
            attend_back(q_v, q_v, q_v, dm_v, mix_v, 0, width, 2 * width, mask_v, None, lse_v,
                        dp_v, s_v, p_v, ds_v, dq_v, 0, None)
            stores += copy_all(
                sems, 11,
                (dq_v.at[:, pl.ds(0, 2 * width)], fb_h), (dq_v.at[:, pl.ds(2 * width, width)], lb_h.at[:, left]),
            )
            rows_out(dq_v.at[:, width:], w_v, width, gm_v, False)
            stores += copy_all(sems, 13, (gm_v, gm_h))
            rows_out(dq_v.at[:, :width], w_v, 0, dn_v, False)
            loads[5].wait()
            total = jnp.zeros((1, width), F32)
            for rows in row_chunks(length):
                dx, dgain = rms_back(d_v[rows, :].astype(F32), gain_r[4:5, :], dn_v[rows, :])
                gd_v[rows, :] = (gc_v[rows, :] + dx).astype(BF16)
                total = total + dgain
            dgain_v[...] = total
            stores += copy_all(sems, 14, (gd_v, gd_h), (dgain_v, dgain_h))
            wait_all(through)
            wait_all(stores)

        @pl.when(section == 3)
        def _():
            run(0, d3_h, m3_h, w_h.at[0], ka_h, kb_h, sa_h, sb_h)

        @pl.when(section == 2)
        def _():
            run(1, d2_h, m2_h, wa_h, sa_h, sb_h, ka_h, kb_h)

    return call(
        kernel,
        [
            shape((length, width), BF16),
            shape((length, width), BF16),
            shape((length, 2 * width), BF16),
            shape((length, 2 * width), BF16),
            shape((length, 2 * width), BF16),
            shape((length, 2 * width), BF16),
            shape((1, width), F32),
        ],
        [
            pltpu.VMEM((length, width), BF16),
            pltpu.VMEM((length, width), F32),
            pltpu.VMEM((length, 3 * width), BF16),
            pltpu.VMEM((length, width), BF16),
            pltpu.VMEM((16, length), F32),
            pltpu.VMEM((width, 4 * width), BF16),
            pltpu.VMEM((length, width), BF16),
            pltpu.VMEM((length, width), BF16),
            pltpu.VMEM((length, 3 * width), BF16),
            pltpu.VMEM((length, width), F32),
            pltpu.VMEM((length, width), BF16),
            pltpu.VMEM((length, width), BF16),
            pltpu.VMEM((1, width), F32),
            pltpu.VMEM((length, length), F32),
            pltpu.VMEM((2, length, length), F32),
            pltpu.VMEM((2, length, length), F32),
            pltpu.VMEM((2, length, length), BF16),
            pltpu.VMEM((2, length, length), BF16),
            pltpu.SemaphoreType.DMA((16,)),
        ],
        [d_own, d_got, m_three, m_two, gc, q, mix, lse, n4, mats, got_mats[0], gains, segs],
        [False] * 11 + [True, True],
        flops_of(5, 16 << 20),
    )


def weight_grad(sections, groups, ndp):
    length, width = groups[0][0][0][0].shape[0], 768
    columns = sum(group[2] for group in groups)
    pieces = len(groups[0][0])
    bits = ndp.bit_length() - 1
    block = width // ndp
    refs, flat = [], []
    for a_list, b_list, _ in groups:
        for array, _ in a_list + b_list:
            if not any(array is other for other in flat):
                flat.append(array)
    place = lambda array: [index for index, other in enumerate(flat) if other is array][0]
    plan = [
        ([(place(a), a0) for a, a0 in a_list], [(place(b), b0) for b, b0 in b_list], count)
        for a_list, b_list, count in groups
    ]
    tile = 384 if columns % 384 == 0 else 256
    copies = 2 * pieces * len(groups)

    def kernel(*args):
        sources = args[: len(flat)]
        keep_h, send_h, a_v, at_v, b_v, out_v, sems = args[len(flat) :]
        me = lax.axis_index("dp")
        section = lax.axis_index("section")
        active = section == sections[0]
        for other in sections[1:]:
            active = active | (section == other)

        @pl.when(active)
        def _():
            loads, start = [], 0
            for g, (a_list, b_list, count) in enumerate(plan):
                group_loads = []
                for k in range(pieces):
                    rows = pl.ds(k * length, length)
                    (ai, a0), (bi, b0) = a_list[k], b_list[k]
                    group_loads += copy_all(
                        sems, 2 * (g * pieces + k),
                        (sources[ai].at[:, pl.ds(a0, width)], a_v.at[g, rows]),
                        (sources[bi].at[:, pl.ds(b0, count)], b_v.at[rows, pl.ds(start, count)]),
                    )
                loads.append(group_loads)
                start += count
            spots = []
            for b in range(ndp):
                code = jnp.bitwise_xor(me, b)
                spot = 0
                for k in range(bits):
                    spot = spot + ((code >> k) & 1) * (1 << (bits - 1 - k))
                spots.append(spot)
            start = 0
            for g, (_, _, count) in enumerate(plan):
                wait_all(loads[g])
                at_v[...] = a_v[g].T

                @pl.loop(0, count // tile)
                def _(t):
                    cols = pl.ds(pl.multiple_of(start + t * tile, 128), tile)
                    part = mm(at_v[...], b_v[:, cols])
                    for b in range(ndp):
                        out_v[spots[b], :, cols] = part[b * block : (b + 1) * block, :].astype(BF16)

                start += count
            wait_all(
                copy_all(
                    sems, copies,
                    (out_v.at[pl.ds(0, ndp // 2)], keep_h), (out_v.at[pl.ds(ndp // 2, ndp // 2)], send_h),
                )
            )

    return call(
        kernel,
        [shape((ndp // 2, block, columns), BF16)] * 2,
        [
            pltpu.VMEM((len(groups), pieces * length, width), BF16),
            pltpu.VMEM((width, pieces * length), BF16),
            pltpu.VMEM((pieces * length, columns), BF16),
            pltpu.VMEM((ndp, block, columns), BF16),
            pltpu.SemaphoreType.DMA((copies + 2,)),
        ],
        flat,
        [False] * len(flat),
        flops_of(2 * columns // 3072 or 1, 14 << 20),
    )


def along_dp(value, bit, sections, ndp):
    pairs = [(s * ndp + d, s * ndp + (d ^ bit)) for s in sections for d in range(ndp)]
    return lax.ppermute(value, ("section", "dp"), pairs)


def sum_shards(halves, sections, ndp):
    keep, send = halves
    bit = 1
    while True:
        got = along_dp(send, bit, sections, ndp)
        total = keep.astype(F32) + got.astype(F32)
        half = keep.shape[0] // 2
        if half == 0:
            return total[0]
        keep, send = total[:half].astype(BF16), total[half:].astype(BF16)
        bit *= 2


def per_device(section_ins, segments, buckets, section_mats, gains, tables):
    section = lax.axis_index("section")
    ndp = lax.axis_size("dp")
    ins = section_ins[0]
    mats = section_mats[0]
    rows, length = segments.shape
    width = ins.shape[1]
    segs = segments.astype(F32)
    flat_tables = jnp.pad(jnp.swapaxes(tables, 1, 2), ((0, 0), (0, 16 - H), (0, 0)))
    flipped = buckets[:, ::-1]
    move = lambda value, pairs: lax.ppermute(value, "section", pairs)

    got_mats = tuple(move(mats[slot], [(3, 2)]) for slot in range(3))
    cot_got = move(ins[length:], [(3, 2)])

    fwd0 = self_forward(0, ins, mats, gains, segs, flat_tables, buckets)
    first0 = move(fwd0[0], [(0, 1), (2, 3)])
    fwd1 = self_forward(1, ins, mats, gains, segs, flat_tables, buckets)
    first1 = move(fwd1[0], [(0, 1)])
    enc0 = encoder_forward(first0, mats, gains)
    m_three = move(enc0[1], [(1, 3)])
    enc1 = encoder_forward(first1, mats, gains)
    m_two = move(enc1[1], [(1, 2)])

    dec = decoder_forward(fwd1[0], first0, m_three, m_two, ins, cot_got, mats, got_mats, gains, segs)
    out_dec, gc, q, mix, lse, n4, keep_a, keep_b, send_a, send_b, dgain_d = dec
    got_a, got_b = move(send_a, [(2, 3), (3, 2)]), move(send_b, [(2, 3), (3, 2)])
    out_got = move(out_dec, [(2, 3)])
    back = decoder_backward(fwd1[0], first0, m_three, m_two, (gc, q, mix, lse, n4), mats, got_mats, gains, segs)
    g_mem, g_dec, ca_keep_a, ca_keep_b, ca_send_a, ca_send_b, dgain_c = back
    extra0 = move(g_mem, [(3, 1)])
    extra1 = move(g_mem, [(2, 1)])
    g_dec_got = move(g_dec, [(3, 2)])
    ca_got_a, ca_got_b = move(ca_send_a, [(2, 3), (3, 2)]), move(ca_send_b, [(2, 3), (3, 2)])

    halves = weight_grad((2, 3), [([(keep_a, 0), (got_a, 0)], [(keep_b, 0), (got_b, 0)], 4 * width)], ndp)
    shard_ffn = sum_shards(halves, (2, 3), ndp)

    bwd0 = encoder_backward(0, ins, extra0, first0, enc0[2], enc0[5], mats, gains)
    g0 = move(bwd0[0], [(1, 0)])
    halves = weight_grad(
        (2, 3),
        [
            ([(ca_keep_a, c), (ca_got_a, c)], [(ca_keep_b, c), (ca_got_b, c)], width)
            for c in (0, width)
        ],
        ndp,
    )
    shard_ca = sum_shards(halves, (2, 3), ndp)

    kept = (fwd0[1:], fwd1[1:])
    self_a = self_backward(True, ins, mats, gains, segs, flat_tables, flipped, g0, g_dec, kept)
    bwd1 = encoder_backward(1, ins, extra1, first1, enc1[2], enc1[5], mats, gains)
    g1 = move(bwd1[0], [(1, 0)])
    halves = weight_grad((1,), [([(enc0[3], 0), (enc1[3], 0)], [(bwd0[2], 0), (bwd1[2], 0)], 4 * width)], ndp)
    shard_in = sum_shards(halves, (1,), ndp)
    halves = weight_grad((1,), [([(bwd0[1], 0), (bwd1[1], 0)], [(enc0[4], 0), (enc1[4], 0)], 4 * width)], ndp)
    shard_out = sum_shards(halves, (1,), ndp)
    self_b = self_backward(False, ins, mats, gains, segs, flat_tables, flipped, g1, g_dec_got, kept)
    halves = weight_grad(
        (0, 2),
        [
            ([(self_a[3], 0), (self_b[3], 0)], [(self_a[4], 0), (self_b[4], 0)], 3 * width),
            ([(self_a[3], width), (self_b[3], width)], [(self_a[4], 3 * width), (self_b[4], 3 * width)], width),
        ],
        ndp,
    )
    shard_self = sum_shards(halves, (0, 2), ndp)

    def only(flag, value):
        return jnp.where(flag, value, jnp.zeros_like(value))

    on_self = section % 2 == 0
    self_gain = only(on_self, self_a[1] + self_b[1])
    enc_gain = only(section == 1, bwd0[3] + bwd1[3])
    cross_gain = only(section >= 2, dgain_c)
    ffn_gain = only(section >= 2, dgain_d)
    part_gain = jnp.concatenate(
        [
            only(section == 0, self_gain),
            enc_gain,
            only(section == 2, self_gain),
            cross_gain,
            ffn_gain,
        ],
        axis=0,
    )
    diag = only(on_self, self_a[2] + self_b[2])[:H]
    side = section // 2
    own_buckets = flipped[side]
    onehot = (own_buckets[:, None] == jnp.arange(tables.shape[1], dtype=jnp.int32)[None, :]).astype(F32)
    table_part = jnp.dot(diag[:, : own_buckets.shape[0]], onehot, precision=lax.Precision.HIGHEST).T
    sides = jnp.arange(tables.shape[0], dtype=jnp.int32)[:, None, None]
    part_table = jnp.where(sides == side, table_part[None], 0.0)
    small = jnp.concatenate([part_gain.reshape(-1, 128), part_table.reshape(-1, 128)], axis=0)
    everyone = lax.axis_size("section") * ndp
    bit = 1
    while bit < everyone:
        small = small + lax.ppermute(small, ("section", "dp"), [(d, d ^ bit) for d in range(everyone)])
        bit *= 2
    cut = gains.size // 128
    gains_grad = small[:cut].reshape(gains.shape)
    tables_grad = small[cut:].reshape(tables.shape)

    three = move(jnp.concatenate([shard_ffn, shard_ca], axis=1).astype(BF16), [(2, 3)]).astype(F32)
    ffn_got, ca_got = three[:, : 4 * width], three[:, 4 * width :]
    zero = jnp.zeros_like(shard_self)
    full_ca = jnp.concatenate([shard_ca, ca_got], axis=1)
    pick = lambda own, enc, dec: jnp.where(on_self, own, jnp.where(section == 1, enc, dec))
    mats_grad = jnp.stack(
        [pick(shard_self, shard_in, full_ca), pick(zero, shard_out, shard_ffn), pick(zero, zero, ffn_got)]
    )
    row0 = jnp.where(section == 0, self_a[0], jnp.where(section == 1, enc0[0], jnp.where(section == 2, self_b[0], out_dec)))
    row1 = jnp.where(section == 0, self_b[0], jnp.where(section == 1, enc1[0], jnp.where(section == 2, self_a[0], out_got)))
    return jnp.concatenate([row0, row1], axis=0)[None], mats_grad[None], gains_grad, tables_grad


def solution(mesh):
    placed = (
        P("section", "dp", None),
        P("dp", None),
        P(),
        P("section", None, None, None),
        P(),
        P(),
    )
    return jax.shard_map(
        per_device,
        mesh=mesh,
        in_specs=placed,
        out_specs=(P("section", "dp", None), P("section", None, "dp", None), P(), P()),
        check_vma=False,
    )
```

```python
from functools import partial

import jax
import jax.numpy as jnp
from jax import lax
from jax.experimental import pallas as pl
from jax.experimental.pallas import tpu as pltpu
from jax.sharding import PartitionSpec as P

H = 12
HD = 64
PAIRS = H // 2
EPS = 1e-06
GELU = 0.7978845608028654
CUBIC = 0.044715
MASKED = -1e38
F32 = jnp.float32
BF16 = jnp.bfloat16
ROW_STEP = 128
VMEM_LIMIT = 60 * 1024 * 1024


def mm(a, b):
    return jnp.dot(a, b, preferred_element_type=F32)


def mm_nt(a, b):
    return lax.dot_general(a, b, (((1,), (1,)), ((), ())), preferred_element_type=F32)


def inverse_rms(x):
    return lax.rsqrt(jnp.mean(x * x, axis=-1, keepdims=True) + EPS)


def row_chunks(length):
    return [pl.ds(start, ROW_STEP) for start in range(0, length, ROW_STEP)]


def rms_back(x, gain, dy):
    r = inverse_rms(x)
    inner = jnp.mean(dy * gain * x, axis=-1, keepdims=True)
    dx = r * gain * dy - x * (r * r * r) * inner
    return dx, jnp.sum(dy * x * r, axis=0, keepdims=True)


def copy_all(sems, first, *pairs):
    started = []
    for offset, (source, target) in enumerate(pairs):
        one = pltpu.make_async_copy(source, target, sems.at[first + offset])
        one.start()
        started.append(one)
    return started


def wait_all(started):
    for one in started:
        one.wait()


def head_lanes(second):
    lane = lax.broadcasted_iota(jnp.int32, (1, 2 * HD), 1)
    return (lane >= HD) if second else (lane < HD)


def fill_mask(mask_v, seg_row, transposed, slack):
    length = seg_row.shape[1]
    down = jnp.broadcast_to(seg_row, (128, length)).T
    for c in range(length // 128):
        along = seg_row[:, c * 128 : (c + 1) * 128]
        r = lax.broadcasted_iota(jnp.int32, (length, 128), 0)
        q = lax.broadcasted_iota(jnp.int32, (length, 128), 1) + c * 128
        key, query = (r, q) if transposed else (q, r)
        ok = (down == along) & (key <= query + slack)
        mask_v[:, c * 128 : (c + 1) * 128] = jnp.where(ok, 0.0, MASKED)


def fill_toeplitz(toe_v, vec_v, table, bucket_row):
    count = bucket_row.shape[1]
    ids = lax.broadcasted_iota(jnp.int32, (table.shape[1], count), 0)
    onehot = (ids == bucket_row).astype(F32)
    vec = jnp.dot(table, onehot, precision=lax.Precision.HIGHEST, preferred_element_type=F32)
    vec_v[:, :count] = vec

    @pl.loop(0, H)
    def _(h):
        wide = jnp.broadcast_to(vec_v[pl.ds(h, 1), :], (128, vec_v.shape[1]))
        rolled = pltpu.roll(wide, vec_v.shape[1] - 127, 1, stride=1, stride_axis=0)
        toe_v[h] = rolled[:, : toe_v.shape[2]]


def attend(q_v, k_v, v_v, q0, k0, v0, mask_v, toe_v, s_v, p_v, mix_v, lse_v):
    length = mix_v.shape[0]

    @pl.loop(0, PAIRS)
    def _(hp):
        at = lambda base: pl.ds(pl.multiple_of(base + hp * 128, 128), 128)
        q2, k2, v2 = q_v[:, at(q0)], k_v[:, at(k0)], v_v[:, at(v0)]
        low = head_lanes(False)
        outs, tops = [], []
        for a in range(2):
            mine = head_lanes(a == 1)
            s_v[a] = mm_nt(jnp.where(mine, q2, jnp.zeros_like(q2)), k2)
            top = []
            for c in range(length // 128):
                rows = pl.ds(c * 128, 128)
                s = s_v[a, rows, :] + mask_v[rows, :]
                if toe_v is not None:
                    left = toe_v.shape[2] - length - c * 128
                    s = s + toe_v[2 * hp + a, :, left : left + length]
                m = jnp.max(s, axis=-1, keepdims=True)
                p_v[a, rows, :] = jnp.exp(s - m).astype(BF16)
                top.append(m)
            tops.append(jnp.concatenate(top, axis=0))
            outs.append(mm(p_v[a], jnp.where(mine, v2, jnp.ones_like(v2))))
        total = pltpu.roll(jnp.where(low, outs[1], outs[0]), HD, 1)
        mix_v[:, at(0)] = (jnp.where(low, outs[0], outs[1]) / total).astype(BF16)
        stat = (jnp.where(low, tops[0], tops[1]) + jnp.log(total)).T
        lse_v[pl.ds(2 * hp, 1), :] = stat[0:1, :]
        lse_v[pl.ds(2 * hp + 1, 1), :] = stat[HD : HD + 1, :]


def attend_back(q_v, k_v, v_v, dm_v, mix_v, q0, k0, v0, mask_v, toe_v, lse_v, dp_v, s_v, p_v, ds_v, out_v, o0, acc_v):
    length = mix_v.shape[0]

    @pl.loop(0, PAIRS)
    def _(hp):
        at = lambda base: pl.ds(pl.multiple_of(base + hp * 128, 128), 128)
        q2, k2, v2, dm2 = q_v[:, at(q0)], k_v[:, at(k0)], v_v[:, at(v0)], dm_v[:, at(0)]
        low = head_lanes(False)
        prod = (dm2.astype(F32) * mix_v[:, at(0)].astype(F32)).T
        k2t = k2.T
        dvs, dks, dqs = [], [], []
        for a in range(2):
            mine = head_lanes(a == 1)
            s_v[a] = mm_nt(jnp.where(mine, k2, jnp.zeros_like(k2)), q2)
            dp_v[a] = mm_nt(jnp.where(mine, v2, jnp.zeros_like(v2)), dm2)
            delta = jnp.sum(prod[a * HD : (a + 1) * HD, :], axis=0, keepdims=True)
            lse = lse_v[pl.ds(2 * hp + a, 1), :]
            for c in range(length // 128):
                rows = pl.ds(c * 128, 128)
                s = s_v[a, rows, :] + mask_v[rows, :]
                if toe_v is not None:
                    left = toe_v.shape[2] - length - c * 128
                    s = s + toe_v[2 * hp + a, :, left : left + length]
                p = jnp.exp(s - lse)
                p_v[a, rows, :] = p.astype(BF16)
                ds = p * (dp_v[a, rows, :] - delta)
                ds_v[a, rows, :] = ds.astype(BF16)
                if acc_v is not None:
                    acc_v[2 * hp + a, :, left : left + length] += ds
            dvs.append(mm(p_v[a], dm2))
            dks.append(mm(ds_v[a], q2))
            dqs.append(mm(k2t[a * HD : (a + 1) * HD, :], ds_v[a]))
        out_v[:, at(o0)] = jnp.concatenate(dqs, axis=0).T.astype(BF16)
        out_v[:, at(o0 + PAIRS * 128)] = jnp.where(low, dks[0], dks[1]).astype(BF16)
        out_v[:, at(o0 + 2 * PAIRS * 128)] = jnp.where(low, dvs[0], dvs[1]).astype(BF16)


def fold_diagonals(acc_v, diag_v, fold_v):
    extent = acc_v.shape[2]

    @pl.loop(0, H)
    def _(h):
        fold_v[:, :extent] = acc_v[h]
        fold_v[:, extent:] = jnp.zeros((128, fold_v.shape[1] - extent), F32)
        wide = fold_v.shape[1]
        half = 64
        value = fold_v[...]
        while half >= 1:
            upper, lower = value[:half], value[half:]
            value = pltpu.roll(upper, half, 1) + lower
            half //= 2
        diag_v[pl.ds(h, 1), :] = value


def gelu_parts(u):
    square = u * u
    bend = u * (GELU + (GELU * CUBIC) * square)
    half = 0.5 + 0.5 * jnp.tanh(bend)
    hidden = u * half
    slope = half + 2.0 * hidden * (1.0 - half) * (GELU + (3.0 * GELU * CUBIC) * square)
    return hidden, slope


def ffn_up(n_v, win_v, h_v, slope_v):
    tile = 512

    @pl.loop(0, win_v.shape[1] // tile)
    def _(t):
        cols = pl.ds(pl.multiple_of(t * tile, tile), tile)
        hidden, slope = gelu_parts(mm(n_v[...], win_v[:, cols]))
        h_v[:, cols] = hidden.astype(BF16)
        slope_v[:, cols] = slope.astype(BF16)


def rows_out(a_v, w_v, w0, out_v, add):
    tile = 256
    depth = a_v.shape[1]

    @pl.loop(0, w_v.shape[0] // tile)
    def _(t):
        cols = pl.ds(pl.multiple_of(t * tile, tile), tile)
        part = mm_nt(a_v[...], w_v[cols, w0 : w0 + depth])
        if add:
            out_v[:, cols] = out_v[:, cols] + part
        else:
            out_v[:, cols] = part.astype(out_v.dtype)


def ffn_down(d_v, wout_v, slope_v, du_v):
    tile = 512

    @pl.loop(0, wout_v.shape[1] // tile)
    def _(t):
        cols = pl.ds(pl.multiple_of(t * tile, tile), tile)
        grad = mm(d_v[...], wout_v[:, cols])
        du_v[:, cols] = (grad * slope_v[:, cols].astype(F32)).astype(BF16)


def project(a_v, w_v, w0, out_v, o0, width):
    tile = 384

    @pl.loop(0, width // tile)
    def _(t):
        source = pl.ds(pl.multiple_of(w0 + t * tile, 128), tile)
        target = pl.ds(pl.multiple_of(o0 + t * tile, 128), tile)
        out_v[:, target] = mm(a_v[...], w_v[:, source]).astype(out_v.dtype)


def flops_of(matmuls, size):
    return pl.CostEstimate(flops=matmuls * 1000, bytes_accessed=size // 1000, transcendentals=0)


def shape(dims, kind):
    return jax.ShapeDtypeStruct(dims, kind)


def like(array):
    return shape(array.shape, array.dtype)


def call(kernel, ins, small, outs, scratch, cost, passed=(), after=()):
    space = lambda count, where: [pl.BlockSpec(memory_space=where)] * count
    lead = len(ins) + len(small)

    def body(*refs):
        start = lead + len(passed) + len(after)
        kernel(*refs[:lead], *refs[start:])

    return pl.pallas_call(
        body,
        out_shape=[like(array) for array in passed] + list(outs),
        in_specs=space(len(ins), pl.ANY) + space(len(small), pltpu.VMEM) + space(len(passed) + len(after), pl.ANY),
        out_specs=space(len(passed) + len(outs), pl.ANY),
        scratch_shapes=scratch,
        input_output_aliases={lead + index: index for index in range(len(passed))},
        compiler_params=pltpu.CompilerParams(vmem_limit_bytes=VMEM_LIMIT),
        cost_estimate=cost,
    )(*ins, *small, *passed, *after)


def through_vmem(cores, ins, outs, plan, after=()):
    parts = 4

    def kernel(*refs):
        sources, targets = refs[: len(ins)], refs[len(ins) : len(ins) + len(outs)]
        held, sems = refs[len(ins) + len(outs) : -1], refs[-1]
        core = lax.axis_index("section") % 2
        active = core >= min(cores)

        @pl.when(active)
        def _():
            loads, stores = [], []
            for n, (source, target, v) in enumerate(zip(plan(core, *sources), targets, held)):
                step = v.shape[-2] // parts
                for c in range(parts):
                    rows = (*[slice(None)] * (len(v.shape) - 2), pl.ds(c * step, step))
                    loads.append((copy_all(sems, 2 * (n * parts + c), (source.at[rows], v.at[rows]))[0], v, target, rows))
            for number, (load, v, target, rows) in enumerate(loads):
                load.wait()
                stores += copy_all(sems, 2 * number + 1, (v.at[rows], target.at[rows]))
            wait_all(stores)

    return call(
        kernel,
        ins,
        [],
        outs,
        [pltpu.VMEM(out.shape, out.dtype) for out in outs] + [pltpu.SemaphoreType.DMA((2 * parts * len(outs),))],
        flops_of(1, 6 << 20),
        after=after,
    )


def first_parts(ins, mats):
    length = ins.shape[0] // 2
    row = lambda core: pl.ds(pl.multiple_of((1 - core) * length, length), length)
    return through_vmem(
        (0, 1),
        [ins, mats],
        [shape((length, ins.shape[1]), BF16), shape((1,) + mats.shape[1:], BF16)],
        lambda core, x_h, w_h: (x_h.at[row(core)], w_h.at[pl.ds(0, 1)]),
    )


def later_parts(mats, after):
    outs = [shape((2,) + mats.shape[1:], BF16)]
    return through_vmem((1,), [mats], outs, lambda core, w_h: (w_h.at[pl.ds(1, 2)],), after)[0]


def self_forward(core, x, w, gains, segs, tables, buckets, passed):
    length, width = segs.shape[1], x.shape[1]
    dist = 2 * length
    outs = [
        shape((length, width), BF16),
        shape((length, width), BF16),
        shape((length, 3 * width), BF16),
        shape((length, width), BF16),
        shape((16, length), F32),
    ]

    def kernel(x_h, w_h, gain_r, seg_r, table_r, bucket_r, e_h, n_h, qkv_h, mix_h, lse_h,
               x_v, w_v, n_v, qkv_v, mix_v, lse_v, e_v, mask_v, toe_v, vec_v, s_v, p_v, sems):
        section = lax.axis_index("section")

        @pl.when(section % 2 == core)
        def _():
            side = section // 2
            loads = copy_all(
                sems, 0,
                (x_h.at[pl.ds(0, length)], x_v),
                *[(w_h.at[0, :, pl.ds(c * width, width)], w_v.at[:, pl.ds(c * width, width)]) for c in range(4)],
            )
            fill_toeplitz(toe_v, vec_v, table_r[side], bucket_r[pl.ds(side, 1), :])
            fill_mask(mask_v, seg_r[core : core + 1, :], False, jnp.where(side == 1, 0, 2 * length))
            gain = gain_r[pl.ds(3 * side, 1), :]
            loads[0].wait()
            for rows in row_chunks(length):
                x = x_v[rows, :].astype(F32)
                n_v[rows, :] = (x * inverse_rms(x) * gain).astype(BF16)
            stores = copy_all(sems, 5, (n_v, n_h))
            wait_all(loads[1:4])
            project(n_v, w_v, 0, qkv_v, 0, 3 * width)
            stores += copy_all(sems, 6, (qkv_v, qkv_h))
            attend(qkv_v, qkv_v, qkv_v, 0, width, 2 * width, mask_v, toe_v, s_v, p_v, mix_v, lse_v)
            stores += copy_all(sems, 7, (mix_v, mix_h), (lse_v, lse_h))
            loads[4].wait()

            @pl.loop(0, width // 256)
            def _(t):
                cols = pl.ds(pl.multiple_of(t * 256, 256), 256)
                part = mm(mix_v[...], w_v[:, pl.ds(pl.multiple_of(3 * width + t * 256, 256), 256)])
                e_v[:, cols] = (x_v[:, cols].astype(F32) + part).astype(BF16)

            stores += copy_all(sems, 9, (e_v, e_h))
            wait_all(stores)

    return call(
        kernel,
        [x, w],
        [gains, segs, tables, buckets],
        [] if passed else outs,
        [
            pltpu.VMEM((length, width), BF16),
            pltpu.VMEM((width, 4 * width), BF16),
            pltpu.VMEM((length, width), BF16),
            pltpu.VMEM((length, 3 * width), BF16),
            pltpu.VMEM((length, width), BF16),
            pltpu.VMEM((16, length), F32),
            pltpu.VMEM((length, width), BF16),
            pltpu.VMEM((length, length), F32),
            pltpu.VMEM((H, 128, dist - 128), F32),
            pltpu.VMEM((16, dist), F32),
            pltpu.VMEM((2, length, length), F32),
            pltpu.VMEM((2, length, length), BF16),
            pltpu.SemaphoreType.DMA((10,)),
        ],
        flops_of(3, 12 << 20),
        passed,
    )


def transposed_bias(tables, flipped, length, after):
    dist = 2 * length

    def kernel(table_r, bucket_r, toe_h, toe_v, vec_v, sems):
        side = lax.axis_index("section") // 2
        fill_toeplitz(toe_v, vec_v, table_r[side], bucket_r[pl.ds(side, 1), :])
        wait_all(copy_all(sems, 0, (toe_v, toe_h)))

    return call(
        kernel,
        [],
        [tables, flipped],
        [shape((H, 128, dist - 128), F32)],
        [pltpu.VMEM((H, 128, dist - 128), F32), pltpu.VMEM((16, dist), F32), pltpu.SemaphoreType.DMA((1,))],
        flops_of(1, 6 << 20),
        after=after,
    )[0]


def folded_diagonals(acc, after):
    dist = acc.shape[2] + 128

    def kernel(acc_h, diag_h, acc_v, diag_v, fold_v, sems):
        wait_all(copy_all(sems, 0, (acc_h, acc_v)))
        fold_diagonals(acc_v, diag_v, fold_v)
        wait_all(copy_all(sems, 1, (diag_v, diag_h)))

    return call(
        kernel,
        [acc],
        [],
        [shape((16, dist), F32)],
        [
            pltpu.VMEM(acc.shape, F32),
            pltpu.VMEM((16, dist), F32),
            pltpu.VMEM((128, dist), F32),
            pltpu.SemaphoreType.DMA((2,)),
        ],
        flops_of(1, 6 << 20),
        after=after,
    )[0]


def self_backward(ins, x_got, mats, w_got, gains, segs, toe, g, kept, after):
    length, width = segs.shape[1], ins.shape[1]
    dist = 2 * length

    def kernel(x0_h, x1_h, w0_h, w1_h, toe_h, g_h, n_h, qkv_h, mix_h, lse_h, gain_r, seg_r,
               gx_h, dgain_h, acc_h, ka_h, kb_h, sa_h, sb_h,
               x_v, w_v, n_v, qkv_v, mix_v, lse_v, d_v, dm_v, dqkv_v, dn_v, gx_v, dgain_v,
               mask_v, toe_v, acc_v, s_v, dp_v, p_v, ds_v, sems):
        section = lax.axis_index("section")
        side = section // 2

        def run(core, x_h, w_h, fa_h, fb_h, la_h, lb_h):
            left, right = pl.ds(0, width), pl.ds(width, width)
            loads = copy_all(
                sems, 0,
                (g_h, d_v),
                (w_h.at[0, :, pl.ds(3 * width, width)], w_v.at[:, pl.ds(3 * width, width)]),
                (mix_h, mix_v),
                (lse_h, lse_v),
                (qkv_h, qkv_v),
                (toe_h, toe_v),
                (w_h.at[0, :, pl.ds(0, 3 * width)], w_v.at[:, pl.ds(0, 3 * width)]),
                (x_h.at[pl.ds(0, length)], x_v),
                (n_h, n_v),
            )
            fill_mask(mask_v, seg_r[core : core + 1, :], True, jnp.where(side == 1, 0, 2 * length))
            acc_v[...] = jnp.zeros_like(acc_v)
            gain = gain_r[pl.ds(3 * side, 1), :]
            wait_all(loads[:2])
            rows_out(d_v, w_v, 3 * width, dm_v, False)
            wait_all(loads[2:6])
            attend_back(qkv_v, qkv_v, qkv_v, dm_v, mix_v, 0, width, 2 * width, mask_v, toe_v, lse_v,
                        dp_v, s_v, p_v, ds_v, dqkv_v, 0, acc_v)
            loads[8].wait()
            stores = copy_all(
                sems, 9,
                (dqkv_v.at[:, pl.ds(0, 2 * width)], fb_h), (dqkv_v.at[:, pl.ds(2 * width, width)], lb_h.at[:, left]),
                (d_v, lb_h.at[:, right]), (n_v, fa_h.at[:, left]), (n_v, fa_h.at[:, right]),
                (n_v, la_h.at[:, left]), (mix_v, la_h.at[:, right]), (acc_v, acc_h),
            )
            wait_all(loads[6:8])
            rows_out(dqkv_v, w_v, 0, dn_v, False)
            total = jnp.zeros((1, width), F32)
            for rows in row_chunks(length):
                dx, dgain = rms_back(x_v[rows, :].astype(F32), gain, dn_v[rows, :])
                gx_v[rows, :] = d_v[rows, :].astype(F32) + dx
                total = total + dgain
            dgain_v[...] = total
            stores += copy_all(sems, 17, (gx_v, gx_h), (dgain_v, dgain_h))
            wait_all(stores)

        @pl.when(section % 2 == 0)
        def _():
            run(0, x0_h, w0_h, ka_h, kb_h, sa_h, sb_h)

        @pl.when(section % 2 == 1)
        def _():
            run(1, x1_h, w1_h, sa_h, sb_h, ka_h, kb_h)

    pair = shape((length, 2 * width), BF16)
    return call(
        kernel,
        [ins, x_got, mats, w_got, toe, g, *kept],
        [gains, segs],
        [shape((length, width), F32), shape((1, width), F32), like(toe), pair, pair, pair, pair],
        [
            pltpu.VMEM((length, width), BF16),
            pltpu.VMEM((width, 4 * width), BF16),
            pltpu.VMEM((length, width), BF16),
            pltpu.VMEM((length, 3 * width), BF16),
            pltpu.VMEM((length, width), BF16),
            pltpu.VMEM((16, length), F32),
            pltpu.VMEM((length, width), BF16),
            pltpu.VMEM((length, width), BF16),
            pltpu.VMEM((length, 3 * width), BF16),
            pltpu.VMEM((length, width), F32),
            pltpu.VMEM((length, width), F32),
            pltpu.VMEM((1, width), F32),
            pltpu.VMEM((length, length), F32),
            pltpu.VMEM((H, 128, dist - 128), F32),
            pltpu.VMEM((H, 128, dist - 128), F32),
            pltpu.VMEM((2, length, length), F32),
            pltpu.VMEM((2, length, length), F32),
            pltpu.VMEM((2, length, length), BF16),
            pltpu.VMEM((2, length, length), BF16),
            pltpu.SemaphoreType.DMA((19,)),
        ],
        flops_of(6, 16 << 20),
        after=after,
    )


def encoder_forward(e1, mats, got_mats, gains):
    length, width = e1.shape
    hidden = mats.shape[2]

    def kernel(e_h, w1_h, w00_h, w01_h, gain_r, ka_h, kb_h, sa_h, sb_h, out_h, send_h, mid_h, slope_h,
               e_v, win_v, wout_v, n_v, h_v, slope_v, mid_v, out_v, send_v, sems):
        section = lax.axis_index("section")

        def run(in_h, out_w_h, na_h, hb_h):
            loads = copy_all(sems, 0, (e_h, e_v), (in_h, win_v), (out_w_h, wout_v))
            loads[0].wait()
            for rows in row_chunks(length):
                x = e_v[rows, :].astype(F32)
                mid_v[rows, :] = x
                n_v[rows, :] = (x * inverse_rms(x) * gain_r[1:2, :]).astype(BF16)
            stores = copy_all(sems, 3, (n_v, na_h))
            loads[1].wait()
            ffn_up(n_v, win_v, h_v, slope_v)
            stores += copy_all(sems, 4, (h_v, hb_h), (slope_v, slope_h))
            loads[2].wait()
            rows_out(h_v, wout_v, 0, mid_v, True)
            for rows in row_chunks(length):
                x = mid_v[rows, :]
                y = x * inverse_rms(x) * gain_r[2:3, :]
                out_v[rows, :] = y
                send_v[rows, :] = y.astype(BF16)
            stores += copy_all(sems, 6, (send_v, send_h), (out_v, out_h), (mid_v, mid_h))
            wait_all(stores)

        @pl.when(section == 0)
        def _():
            run(w00_h.at[0], w01_h.at[0], sa_h, kb_h)

        @pl.when(section == 1)
        def _():
            run(w1_h.at[0], w1_h.at[1], ka_h, sb_h)

    narrow, wide = shape((length, width), BF16), shape((length, hidden), BF16)
    return call(
        kernel,
        [e1, mats, *got_mats],
        [gains],
        [narrow, wide, narrow, wide, shape((length, width), F32), narrow, shape((length, width), F32), wide],
        [
            pltpu.VMEM((length, width), BF16),
            pltpu.VMEM((width, hidden), BF16),
            pltpu.VMEM((width, hidden), BF16),
            pltpu.VMEM((length, width), BF16),
            pltpu.VMEM((length, hidden), BF16),
            pltpu.VMEM((length, hidden), BF16),
            pltpu.VMEM((length, width), F32),
            pltpu.VMEM((length, width), F32),
            pltpu.VMEM((length, width), BF16),
            pltpu.SemaphoreType.DMA((9,)),
        ],
        flops_of(2, 20 << 20),
    )


def encoder_backward(ins, cot_got, extra, e1, mid, slope, mats, got_mats, gains, passed):
    length, width = e1.shape
    hidden = mats.shape[2]

    def kernel(c1_h, c0_h, extra_h, e_h, mid_h, slope_h, w1_h, w00_h, w01_h, gain_r, ka_h, kb_h, sa_h, sb_h, g_h, dgain_h,
               cot_v, extra_v, e_v, mid_v, slope_v, win_v, wout_v, d_v, du_v, dn_v, gm_v, g_v, dgain_v, sems):
        section = lax.axis_index("section")

        def run(cot_h, in_h, out_h, da_h, ub_h):
            loads = copy_all(
                sems, 0,
                (cot_h, cot_v), (extra_h, extra_v), (mid_h, mid_v),
                (out_h, wout_v), (slope_h, slope_v), (in_h, win_v), (e_h, e_v),
            )
            wait_all(loads[:3])
            total = jnp.zeros((1, width), F32)
            for rows in row_chunks(length):
                dy = cot_v[rows, :].astype(F32) + extra_v[rows, :].astype(F32)
                dx, dgain = rms_back(mid_v[rows, :], gain_r[2:3, :], dy)
                gm_v[rows, :] = dx
                d_v[rows, :] = dx.astype(BF16)
                total = total + dgain
            dgain_v[1:2, :] = total
            stores = copy_all(sems, 7, (d_v, da_h))
            wait_all(loads[3:5])
            ffn_down(d_v, wout_v, slope_v, du_v)
            stores += copy_all(sems, 8, (du_v, ub_h))
            wait_all(loads[5:])
            rows_out(du_v, win_v, 0, dn_v, False)
            total = jnp.zeros((1, width), F32)
            for rows in row_chunks(length):
                dx, dgain = rms_back(e_v[rows, :].astype(F32), gain_r[1:2, :], dn_v[rows, :])
                g_v[rows, :] = (gm_v[rows, :] + dx).astype(BF16)
                total = total + dgain
            dgain_v[0:1, :] = total
            stores += copy_all(sems, 9, (g_v, g_h), (dgain_v, dgain_h))
            wait_all(stores)

        @pl.when(section == 0)
        def _():
            run(c0_h, w00_h.at[0], w01_h.at[0], ka_h, sb_h)

        @pl.when(section == 1)
        def _():
            run(c1_h.at[pl.ds(length, length)], w1_h.at[0], w1_h.at[1], sa_h, kb_h)

    return call(
        kernel,
        [ins, cot_got, extra, e1, mid, slope, mats, *got_mats],
        [gains],
        [shape((2, width), F32)],
        [
            pltpu.VMEM((length, width), BF16),
            pltpu.VMEM((length, width), BF16),
            pltpu.VMEM((length, width), BF16),
            pltpu.VMEM((length, width), F32),
            pltpu.VMEM((length, hidden), BF16),
            pltpu.VMEM((width, hidden), BF16),
            pltpu.VMEM((width, hidden), BF16),
            pltpu.VMEM((length, width), BF16),
            pltpu.VMEM((length, hidden), BF16),
            pltpu.VMEM((length, width), F32),
            pltpu.VMEM((length, width), F32),
            pltpu.VMEM((length, width), BF16),
            pltpu.VMEM((2, width), F32),
            pltpu.SemaphoreType.DMA((11,)),
        ],
        flops_of(2, 20 << 20),
        passed,
    )


def decoder(d1, memory, ins, cot_got, mats, got_mats, gains, segs, passed, after):
    length, width = d1.shape
    hidden = mats.shape[2]

    def kernel(d_h, m_h, c1_h, c0_h, w1_h, w00_h, w01_h, gain_r, seg_r,
               ka_h, kb_h, sa_h, sb_h, out_h, gm_h, gd_h, xa_h, xb_h, ya_h, yb_h, dgain_h,
               d_v, m_v, c_v, wca_v, win_v, wout_v, n_v, q_v, mix_v, lse_v, mask_v, s_v, p_v, h_v, slope_v,
               x_v, y_v, dn_v, n5_v, do_v, dgain_v, dp_v, ds_v, dq_v, dm_v, do4_v, gm_v, gd_v, out_v, sems):
        section = lax.axis_index("section")

        def run(core, c_h, ws_h, na_h, ub_h, oa_h, hb_h, fa_h, fb_h, la_h, lb_h):
            left, right = pl.ds(0, width), pl.ds(width, width)
            loads = copy_all(
                sems, 0,
                (d_h, d_v), (m_h, m_v), (ws_h[0], wca_v), (ws_h[1], win_v), (ws_h[2], wout_v), (c_h, c_v),
            )
            fill_mask(mask_v, seg_r[core : core + 1, :], False, 2 * length)
            loads[0].wait()
            for rows in row_chunks(length):
                x = d_v[rows, :].astype(F32)
                x_v[rows, :] = x
                n_v[rows, :] = (x * inverse_rms(x) * gain_r[4:5, :]).astype(BF16)
            wait_all(loads[1:3])
            stores = copy_all(
                sems, 6, (n_v, fa_h.at[:, left]), (m_v, fa_h.at[:, right]), (m_v, la_h.at[:, left])
            )
            project(n_v, wca_v, 0, q_v, 0, width)
            project(m_v, wca_v, width, q_v, width, 2 * width)
            attend(q_v, q_v, q_v, 0, width, 2 * width, mask_v, None, s_v, p_v, mix_v, lse_v)
            stores += copy_all(sems, 9, (mix_v, la_h.at[:, right]))

            @pl.loop(0, width // 256)
            def _(t):
                cols = pl.ds(pl.multiple_of(t * 256, 256), 256)
                part = mm(mix_v[...], wca_v[:, pl.ds(pl.multiple_of(3 * width + t * 256, 256), 256)])
                x_v[:, cols] = x_v[:, cols] + part

            for rows in row_chunks(length):
                x = x_v[rows, :]
                y_v[rows, :] = x
                n5_v[rows, :] = (x * inverse_rms(x) * gain_r[5:6, :]).astype(BF16)
            stores += copy_all(sems, 10, (n5_v, na_h))
            loads[3].wait()
            ffn_up(n5_v, win_v, h_v, slope_v)
            stores += copy_all(sems, 11, (h_v, hb_h))
            loads[4].wait()
            rows_out(h_v, wout_v, 0, y_v, True)
            loads[5].wait()
            total = jnp.zeros((1, width), F32)
            for rows in row_chunks(length):
                y = y_v[rows, :]
                out_v[rows, :] = y * inverse_rms(y) * gain_r[6:7, :]
                dy, dgain = rms_back(y, gain_r[6:7, :], c_v[rows, :].astype(F32))
                total = total + dgain
                do_v[rows, :] = dy.astype(BF16)
                y_v[rows, :] = dy
            dgain_v[2:3, :] = total
            stores += copy_all(sems, 12, (out_v, out_h), (do_v, oa_h))
            ffn_down(do_v, wout_v, slope_v, slope_v)
            stores += copy_all(sems, 14, (slope_v, ub_h))
            rows_out(slope_v, win_v, 0, dn_v, False)
            total = jnp.zeros((1, width), F32)
            for rows in row_chunks(length):
                dx, dgain = rms_back(x_v[rows, :], gain_r[5:6, :], dn_v[rows, :])
                dx = y_v[rows, :] + dx
                y_v[rows, :] = dx
                do4_v[rows, :] = dx.astype(BF16)
                total = total + dgain
            dgain_v[1:2, :] = total
            stores += copy_all(sems, 15, (do4_v, lb_h.at[:, right]))
            rows_out(do4_v, wca_v, 3 * width, dm_v, False)
            attend_back(q_v, q_v, q_v, dm_v, mix_v, 0, width, 2 * width, mask_v, None, lse_v,
                        dp_v, s_v, p_v, ds_v, dq_v, 0, None)
            stores += copy_all(
                sems, 16,
                (dq_v.at[:, pl.ds(0, 2 * width)], fb_h), (dq_v.at[:, pl.ds(2 * width, width)], lb_h.at[:, left]),
            )
            rows_out(dq_v.at[:, width:], wca_v, width, gm_v, False)
            stores += copy_all(sems, 18, (gm_v, gm_h))
            rows_out(dq_v.at[:, :width], wca_v, 0, dn_v, False)
            total = jnp.zeros((1, width), F32)
            for rows in row_chunks(length):
                dx, dgain = rms_back(d_v[rows, :].astype(F32), gain_r[4:5, :], dn_v[rows, :])
                gd_v[rows, :] = (y_v[rows, :] + dx).astype(BF16)
                total = total + dgain
            dgain_v[0:1, :] = total
            stores += copy_all(sems, 19, (gd_v, gd_h), (dgain_v, dgain_h))
            wait_all(stores)

        @pl.when(section == 3)
        def _():
            run(1, c1_h.at[pl.ds(length, length)], [w1_h.at[slot] for slot in range(3)], ka_h, kb_h, sa_h, sb_h, xa_h, xb_h, ya_h, yb_h)

        @pl.when(section == 2)
        def _():
            run(0, c0_h, [w00_h.at[0], w01_h.at[0], w01_h.at[1]], sa_h, sb_h, ka_h, kb_h, ya_h, yb_h, xa_h, xb_h)

    pair = shape((length, 2 * width), BF16)
    narrow = shape((length, width), BF16)
    return call(
        kernel,
        [d1, memory, ins, cot_got, mats, *got_mats],
        [gains, segs],
        [shape((length, width), F32), narrow, narrow, pair, pair, pair, pair, shape((3, width), F32)],
        [
            pltpu.VMEM((length, width), BF16),
            pltpu.VMEM((length, width), BF16),
            pltpu.VMEM((length, width), BF16),
            pltpu.VMEM((width, 4 * width), BF16),
            pltpu.VMEM((width, hidden), BF16),
            pltpu.VMEM((width, hidden), BF16),
            pltpu.VMEM((length, width), BF16),
            pltpu.VMEM((length, 3 * width), BF16),
            pltpu.VMEM((length, width), BF16),
            pltpu.VMEM((16, length), F32),
            pltpu.VMEM((length, length), F32),
            pltpu.VMEM((2, length, length), F32),
            pltpu.VMEM((2, length, length), BF16),
            pltpu.VMEM((length, hidden), BF16),
            pltpu.VMEM((length, hidden), BF16),
            pltpu.VMEM((length, width), F32),
            pltpu.VMEM((length, width), F32),
            pltpu.VMEM((length, width), F32),
            pltpu.VMEM((length, width), BF16),
            pltpu.VMEM((length, width), BF16),
            pltpu.VMEM((3, width), F32),
            pltpu.VMEM((2, length, length), F32),
            pltpu.VMEM((2, length, length), BF16),
            pltpu.VMEM((length, 3 * width), BF16),
            pltpu.VMEM((length, width), BF16),
            pltpu.VMEM((length, width), BF16),
            pltpu.VMEM((length, width), BF16),
            pltpu.VMEM((length, width), BF16),
            pltpu.VMEM((length, width), F32),
            pltpu.SemaphoreType.DMA((21,)),
        ],
        flops_of(12, 30 << 20),
        passed,
        after,
    )


def weight_grad(sections, groups, chunks, ndp, after=()):
    length, width = groups[0][0][0][0].shape[0], 768
    columns = sum(group[2] for group in groups)
    pieces = len(groups[0][0])
    bits = ndp.bit_length() - 1
    block = width // ndp
    flat = []
    for a_list, b_list, _ in groups:
        for array, _ in a_list + b_list:
            if not any(array is other for other in flat):
                flat.append(array)
    place = lambda array: [index for index, other in enumerate(flat) if other is array][0]
    plan = [
        ([(place(a), a0) for a, a0 in a_list], [(place(b), b0) for b, b0 in b_list], count)
        for a_list, b_list, count in groups
    ]
    tile = 768
    copies = 2 * pieces * len(groups)

    def kernel(*args):
        sources = args[: len(flat)]
        outs = args[len(flat) : len(flat) + 2 * len(chunks)]
        a_v, at_v, b_v, out_v, sems = args[len(flat) + 2 * len(chunks) :]
        me = lax.axis_index("dp")
        section = lax.axis_index("section")
        active = section >= sections[0]

        @pl.when(active)
        def _():
            loads, start = [], 0
            for g, (a_list, b_list, count) in enumerate(plan):
                group_loads = []
                for k in range(pieces):
                    rows = pl.ds(k * length, length)
                    (ai, a0), (bi, b0) = a_list[k], b_list[k]
                    group_loads += copy_all(
                        sems, 2 * (g * pieces + k),
                        (sources[ai].at[:, pl.ds(a0, width)], a_v.at[g, rows]),
                        (sources[bi].at[:, pl.ds(b0, count)], b_v.at[rows, pl.ds(start, count)]),
                    )
                loads.append(group_loads)
                start += count
            stores, group, group_end, start = [], -1, 0, 0
            for number, (count, order) in enumerate(chunks):
                spots = []
                for b in range(ndp):
                    code = jnp.bitwise_xor(me, b)
                    spot = 0
                    for k in range(bits):
                        spot = spot + ((code >> order[k]) & 1) * (1 << (bits - 1 - k))
                    spots.append(spot)
                done, end = start, start + count
                while done < end:
                    if done == group_end:
                        group += 1
                        wait_all(loads[group])
                        at_v[...] = a_v[group].T
                        group_end += plan[group][2]
                    upto = min(end, group_end)

                    @pl.loop(0, (upto - done) // tile)
                    def _(t):
                        cols = pl.ds(pl.multiple_of(done + t * tile, 128), tile)
                        part = mm(at_v[...], b_v[:, cols])
                        for b in range(ndp):
                            out_v[spots[b], :, cols] = part[b * block : (b + 1) * block, :].astype(BF16)

                    done = upto
                for half in range(2):
                    source = out_v.at[pl.ds(half * (ndp // 2), ndp // 2), :, pl.ds(start, count)]
                    stores += copy_all(sems, copies + 2 * number + half, (source, outs[2 * number + half]))
                start = end
            wait_all(stores)

    made = call(
        kernel,
        flat,
        [],
        [shape((ndp // 2, block, count), BF16) for count, _ in chunks for _ in range(2)],
        [
            pltpu.VMEM((len(groups), pieces * length, width), BF16),
            pltpu.VMEM((width, pieces * length), BF16),
            pltpu.VMEM((pieces * length, columns), BF16),
            pltpu.VMEM((ndp, block, columns), BF16),
            pltpu.SemaphoreType.DMA((copies + 2 * len(chunks),)),
        ],
        flops_of(2, 14 << 20),
        after=after,
    )
    return [(made[2 * number], made[2 * number + 1]) for number in range(len(chunks))]


def along_dp(value, bit, sections, ndp):
    pairs = [(s * ndp + d, s * ndp + (d ^ bit)) for s in sections for d in range(ndp)]
    return lax.ppermute(value, ("section", "dp"), pairs)


def first_step(halves, sections, order, ndp):
    keep, send = halves
    got = along_dp(send, 1 << order[0], sections, ndp)
    total = keep.astype(F32) + got.astype(F32)
    half = keep.shape[0] // 2
    return total[:half].astype(BF16), total[half:].astype(BF16)


def other_steps(halves, sections, order, ndp):
    keep, send = halves
    for bit in order[1:]:
        got = along_dp(send, 1 << bit, sections, ndp)
        total = keep.astype(F32) + got.astype(F32)
        half = keep.shape[0] // 2
        if half == 0:
            return total[0]
        keep, send = total[:half].astype(BF16), total[half:].astype(BF16)


def per_device(section_ins, segments, buckets, section_mats, gains, tables):
    section = lax.axis_index("section")
    core = section % 2
    side = section // 2
    ndp = lax.axis_size("dp")
    ins = section_ins[0]
    mats = section_mats[0]
    length = segments.shape[1]
    width = ins.shape[1]
    segs = segments.astype(F32)
    flat_tables = jnp.pad(jnp.swapaxes(tables, 1, 2), ((0, 0), (0, 16 - H), (0, 0)))
    flipped = buckets[:, ::-1]
    everywhere = (0, 1, 2, 3)
    move = lambda value, pairs: lax.ppermute(value, "section", pairs)
    swap = lambda value: move(value, [(0, 1), (1, 0), (2, 3), (3, 2)])

    other_row, own_first = first_parts(ins, mats)
    got_first = swap(own_first)
    in_got = swap(other_row)
    got_later = move(later_parts(mats, [own_first]), [(1, 0), (3, 2)])
    got_mats = (got_first, got_later)
    self_got = got_first

    kept = self_forward(0, ins, mats, gains, segs, flat_tables, buckets, ())
    kept = self_forward(1, in_got, self_got, gains, segs, flat_tables, buckets, kept)
    e1, kept = kept[0], kept[1:]
    enc = encoder_forward(e1, mats, got_mats, gains)
    factors, (enc_out, enc_send, mid, slope) = enc[:4], enc[4:]
    memory = move(enc_send, [(0, 2), (1, 3)])
    toe = transposed_bias(flat_tables, flipped, length, [enc_send])
    dec = decoder(e1, memory, ins, in_got, mats, got_mats, gains, segs, factors, [toe])
    factors, (dec_out, g_mem, g_self), cross, dgain_d = dec[:4], dec[4:7], dec[7:11], dec[11]
    extra = move(g_mem, [(2, 0), (3, 1)])
    back = encoder_backward(ins, in_got, extra, e1, mid, slope, mats, got_mats, gains, [*factors, g_self])
    (keep_a, keep_b, send_a, send_b), g_self, dgain_e = back[:4], back[4], back[5]

    got_a, got_b = swap(send_a), swap(send_b)
    plain = tuple(range(ndp.bit_length() - 1))
    turned = (1, 0) + plain[2:]
    orders = (plain, turned)
    made_ffn = weight_grad(
        everywhere,
        [([(keep_a, 0), (got_a, 0)], [(keep_b, 0), (got_b, 0)], 4 * width)],
        [(2 * width, order) for order in orders],
        ndp,
    )
    part_ffn = [first_step(halves, everywhere, order, ndp) for halves, order in zip(made_ffn, orders)]

    got_a, got_b = [move(value, [(2, 3), (3, 2)]) for value in cross[2:]]
    halves = weight_grad(
        (2, 3),
        [([(cross[0], c), (got_a, c)], [(cross[1], c), (got_b, c)], width) for c in (0, width)],
        [(2 * width, plain)],
        ndp,
        [made_ffn[0][0]],
    )[0]
    part_cross = first_step(halves, (2, 3), plain, ndp)

    own = self_backward(ins, in_got, mats, self_got, gains, segs, toe, g_self, kept, [halves[0]])
    gx, dgain_s, acc = own[:3]
    keep_a, keep_b, send_a, send_b = own[3:]
    got_a, got_b = swap(send_a), swap(send_b)
    diag = folded_diagonals(acc, ())
    halves = weight_grad(
        everywhere,
        [([(keep_a, c), (got_a, c)], [(keep_b, c), (got_b, c)], width) for c in (0, width)],
        [(2 * width, plain)],
        ndp,
        [part[1] for part in part_ffn] + [part_cross[1], diag],
    )[0]
    halves, diag, dgain_s, dgain_d, dgain_e, gx = lax.optimization_barrier(
        (halves, diag, dgain_s, dgain_d, dgain_e, gx)
    )
    shard_ffn = jnp.concatenate(
        [other_steps(part, everywhere, order, ndp) for part, order in zip(part_ffn, orders)], axis=1
    )
    shard_cross = other_steps(part_cross, (2, 3), plain, ndp)
    shard_self = other_steps(first_step(halves, everywhere, plain, ndp), everywhere, plain, ndp)

    def only(flag, value):
        return jnp.where(flag, value, jnp.zeros_like(value))

    part_gain = jnp.concatenate(
        [only(side == 0, dgain_s), only(side == 0, dgain_e), only(side == 1, dgain_s), only(side == 1, dgain_d)], axis=0
    )
    own_buckets = flipped[side]
    onehot = (own_buckets[:, None] == jnp.arange(tables.shape[1], dtype=jnp.int32)[None, :]).astype(F32)
    table_part = jnp.dot(diag[:H, : own_buckets.shape[0]], onehot, precision=lax.Precision.HIGHEST).T
    sides = jnp.arange(tables.shape[0], dtype=jnp.int32)[:, None, None]
    part_table = jnp.where(sides == side, table_part[None], 0.0)
    small = jnp.concatenate([part_gain.reshape(-1, 128), part_table.reshape(-1, 128)], axis=0)
    everyone = lax.axis_size("section") * ndp
    bit = 1
    while bit < everyone:
        small = small + lax.ppermute(small, ("section", "dp"), [(d, d ^ bit) for d in range(everyone)])
        bit *= 2
    cut = gains.size // 128
    gains_grad = small[:cut].reshape(gains.shape)
    tables_grad = small[cut:].reshape(tables.shape)

    out_got = swap(jnp.where(core == 1, gx, jnp.where(side == 0, enc_out, dec_out)))
    ffn_got = swap(shard_ffn.astype(BF16)).astype(F32)
    cross_got = move(shard_cross.astype(BF16), [(2, 3)]).astype(F32)
    half_got = move(shard_self.astype(BF16), [(1, 0), (3, 2)]).astype(F32)
    zero = jnp.zeros_like(shard_ffn)
    full_self = jnp.concatenate([shard_self, half_got], axis=1)
    full_cross = jnp.concatenate([shard_cross, cross_got], axis=1)
    pick = lambda own, enc, dec: jnp.where(core == 0, own, jnp.where(side == 0, enc, dec))
    mats_grad = jnp.stack(
        [pick(full_self, shard_ffn, full_cross), pick(zero, ffn_got, shard_ffn), pick(zero, zero, ffn_got)]
    )
    mine = jnp.where(core == 0, gx, jnp.where(side == 0, enc_out, dec_out))
    rows = [jnp.where(core == 0, mine, out_got), jnp.where(core == 0, out_got, mine)]
    return jnp.concatenate(rows, axis=0)[None], mats_grad[None], gains_grad, tables_grad


def solution(mesh):
    placed = (
        P("section", "dp", None),
        P("dp", None),
        P(),
        P("section", None, None, None),
        P(),
        P(),
    )
    return jax.shard_map(
        per_device,
        mesh=mesh,
        in_specs=placed,
        out_specs=(P("section", "dp", None), P("section", None, "dp", None), P(), P()),
        check_vma=False,
    )
```

```python
from functools import partial

import jax
import jax.numpy as jnp
from jax import lax
from jax.experimental import pallas as pl
from jax.experimental.pallas import tpu as pltpu
from jax.sharding import PartitionSpec as P

H = 12
HD = 64
PAIRS = H // 2
EPS = 1e-06
GELU = 0.7978845608028654
CUBIC = 0.044715
MASKED = -1e38
F32 = jnp.float32
BF16 = jnp.bfloat16
ROW_STEP = 128
VMEM_LIMIT = 60 * 1024 * 1024


def mm(a, b):
    return jnp.dot(a, b, preferred_element_type=F32)


def mm_nt(a, b):
    return lax.dot_general(a, b, (((1,), (1,)), ((), ())), preferred_element_type=F32)


def inverse_rms(x):
    return lax.rsqrt(jnp.mean(x * x, axis=-1, keepdims=True) + EPS)


def row_chunks(length):
    return [pl.ds(start, ROW_STEP) for start in range(0, length, ROW_STEP)]


def rms_back(x, gain, dy):
    r = inverse_rms(x)
    inner = jnp.mean(dy * gain * x, axis=-1, keepdims=True)
    dx = r * gain * dy - x * (r * r * r) * inner
    return dx, jnp.sum(dy * x * r, axis=0, keepdims=True)


def copy_all(sems, first, *pairs):
    started = []
    for offset, (source, target) in enumerate(pairs):
        one = pltpu.make_async_copy(source, target, sems.at[first + offset])
        one.start()
        started.append(one)
    return started


class Either:
    def __init__(self, sem, flag, yes, no):
        self.done = pltpu.make_async_copy(*yes, sem)

        @pl.when(flag)
        def _():
            pltpu.make_async_copy(*yes, sem).start()

        @pl.when(jnp.logical_not(flag))
        def _():
            pltpu.make_async_copy(*no, sem).start()

    def wait(self):
        self.done.wait()


def either_all(sems, first, flag, *choices):
    return [Either(sems.at[first + offset], flag, *choice) for offset, choice in enumerate(choices)]


def wait_all(started):
    for one in started:
        one.wait()


def head_lanes(second):
    lane = lax.broadcasted_iota(jnp.int32, (1, 2 * HD), 1)
    return (lane >= HD) if second else (lane < HD)


def fill_mask(mask_v, seg_row, transposed, slack):
    length = seg_row.shape[1]
    down = jnp.broadcast_to(seg_row, (128, length)).T
    for c in range(length // 128):
        along = seg_row[:, c * 128 : (c + 1) * 128]
        r = lax.broadcasted_iota(jnp.int32, (length, 128), 0)
        q = lax.broadcasted_iota(jnp.int32, (length, 128), 1) + c * 128
        key, query = (r, q) if transposed else (q, r)
        ok = (down == along) & (key <= query + slack)
        mask_v[:, c * 128 : (c + 1) * 128] = jnp.where(ok, 0.0, MASKED)


def fill_toeplitz(toe_v, vec_v, table, bucket_row):
    count = bucket_row.shape[1]
    ids = lax.broadcasted_iota(jnp.int32, (table.shape[1], count), 0)
    onehot = (ids == bucket_row).astype(F32)
    vec = jnp.dot(table, onehot, precision=lax.Precision.HIGHEST, preferred_element_type=F32)
    vec_v[:, :count] = vec

    @pl.loop(0, H)
    def _(h):
        wide = jnp.broadcast_to(vec_v[pl.ds(h, 1), :], (128, vec_v.shape[1]))
        rolled = pltpu.roll(wide, vec_v.shape[1] - 127, 1, stride=1, stride_axis=0)
        toe_v[h] = rolled[:, : toe_v.shape[2]]


def attend(q_v, k_v, v_v, q0, k0, v0, mask_v, toe_v, s_v, p_v, mix_v, lse_v):
    length = mix_v.shape[0]

    @pl.loop(0, PAIRS)
    def _(hp):
        at = lambda base: pl.ds(pl.multiple_of(base + hp * 128, 128), 128)
        q2, k2, v2 = q_v[:, at(q0)], k_v[:, at(k0)], v_v[:, at(v0)]
        low = head_lanes(False)
        outs, tops = [], []
        for a in range(2):
            mine = head_lanes(a == 1)
            s_v[a] = mm_nt(jnp.where(mine, q2, jnp.zeros_like(q2)), k2)
            top = []
            for c in range(length // 128):
                rows = pl.ds(c * 128, 128)
                s = s_v[a, rows, :] + mask_v[rows, :]
                if toe_v is not None:
                    left = toe_v.shape[2] - length - c * 128
                    s = s + toe_v[2 * hp + a, :, left : left + length]
                m = jnp.max(s, axis=-1, keepdims=True)
                p_v[a, rows, :] = jnp.exp(s - m).astype(BF16)
                top.append(m)
            tops.append(jnp.concatenate(top, axis=0))
            outs.append(mm(p_v[a], jnp.where(mine, v2, jnp.ones_like(v2))))
        total = pltpu.roll(jnp.where(low, outs[1], outs[0]), HD, 1)
        mix_v[:, at(0)] = (jnp.where(low, outs[0], outs[1]) / total).astype(BF16)
        stat = (jnp.where(low, tops[0], tops[1]) + jnp.log(total)).T
        lse_v[pl.ds(2 * hp, 1), :] = stat[0:1, :]
        lse_v[pl.ds(2 * hp + 1, 1), :] = stat[HD : HD + 1, :]


def attend_back(q_v, k_v, v_v, dm_v, mix_v, q0, k0, v0, mask_v, toe_v, lse_v, dp_v, s_v, p_v, ds_v, out_v, o0, acc_v):
    length = mix_v.shape[0]

    @pl.loop(0, PAIRS)
    def _(hp):
        at = lambda base: pl.ds(pl.multiple_of(base + hp * 128, 128), 128)
        q2, k2, v2, dm2 = q_v[:, at(q0)], k_v[:, at(k0)], v_v[:, at(v0)], dm_v[:, at(0)]
        low = head_lanes(False)
        prod = (dm2.astype(F32) * mix_v[:, at(0)].astype(F32)).T
        k2t = k2.T
        dvs, dks, dqs = [], [], []
        for a in range(2):
            mine = head_lanes(a == 1)
            s_v[a] = mm_nt(jnp.where(mine, k2, jnp.zeros_like(k2)), q2)
            dp_v[a] = mm_nt(jnp.where(mine, v2, jnp.zeros_like(v2)), dm2)
            delta = jnp.sum(prod[a * HD : (a + 1) * HD, :], axis=0, keepdims=True)
            lse = lse_v[pl.ds(2 * hp + a, 1), :]
            for c in range(length // 128):
                rows = pl.ds(c * 128, 128)
                s = s_v[a, rows, :] + mask_v[rows, :]
                if toe_v is not None:
                    left = toe_v.shape[2] - length - c * 128
                    s = s + toe_v[2 * hp + a, :, left : left + length]
                p = jnp.exp(s - lse)
                p_v[a, rows, :] = p.astype(BF16)
                ds = p * (dp_v[a, rows, :] - delta)
                ds_v[a, rows, :] = ds.astype(BF16)
                if acc_v is not None:
                    acc_v[2 * hp + a, :, left : left + length] += ds
            dvs.append(mm(p_v[a], dm2))
            dks.append(mm(ds_v[a], q2))
            dqs.append(mm(k2t[a * HD : (a + 1) * HD, :], ds_v[a]))
        out_v[:, at(o0)] = jnp.concatenate(dqs, axis=0).T.astype(BF16)
        out_v[:, at(o0 + PAIRS * 128)] = jnp.where(low, dks[0], dks[1]).astype(BF16)
        out_v[:, at(o0 + 2 * PAIRS * 128)] = jnp.where(low, dvs[0], dvs[1]).astype(BF16)


def fold_diagonals(acc_v, diag_v):

    @pl.loop(0, H, unroll=3)
    def _(h):
        value = jnp.concatenate([acc_v[h], jnp.zeros((128, 128), F32)], axis=1)
        half = 64
        while half >= 1:
            value = pltpu.roll(value[:half], half, 1) + value[half:]
            half //= 2
        diag_v[pl.ds(h, 1), :] = value


def gelu_parts(u):
    square = u * u
    bend = u * (GELU + (GELU * CUBIC) * square)
    half = 0.5 + 0.5 * jnp.tanh(bend)
    hidden = u * half
    slope = half + 2.0 * hidden * (1.0 - half) * (GELU + (3.0 * GELU * CUBIC) * square)
    return hidden, slope


def ffn_up(n_v, win_v, h_v, slope_v):
    tile = 512

    @pl.loop(0, win_v.shape[1] // tile)
    def _(t):
        cols = pl.ds(pl.multiple_of(t * tile, tile), tile)
        hidden, slope = gelu_parts(mm(n_v[...], win_v[:, cols]))
        h_v[:, cols] = hidden.astype(BF16)
        slope_v[:, cols] = slope.astype(BF16)


def rows_out(a_v, w_v, w0, out_v, add):
    tile = 256
    depth = a_v.shape[1]

    @pl.loop(0, w_v.shape[0] // tile)
    def _(t):
        cols = pl.ds(pl.multiple_of(t * tile, tile), tile)
        part = mm_nt(a_v[...], w_v[cols, w0 : w0 + depth])
        if add:
            out_v[:, cols] = out_v[:, cols] + part
        else:
            out_v[:, cols] = part.astype(out_v.dtype)


def ffn_down(d_v, wout_v, slope_v, du_v):
    tile = 512

    @pl.loop(0, wout_v.shape[1] // tile)
    def _(t):
        cols = pl.ds(pl.multiple_of(t * tile, tile), tile)
        grad = mm(d_v[...], wout_v[:, cols])
        du_v[:, cols] = (grad * slope_v[:, cols].astype(F32)).astype(BF16)


def project(a_v, w_v, w0, out_v, o0, width):
    tile = 384

    @pl.loop(0, width // tile)
    def _(t):
        source = pl.ds(pl.multiple_of(w0 + t * tile, 128), tile)
        target = pl.ds(pl.multiple_of(o0 + t * tile, 128), tile)
        out_v[:, target] = mm(a_v[...], w_v[:, source]).astype(out_v.dtype)


def flops_of(matmuls, size):
    return pl.CostEstimate(flops=matmuls * 1000, bytes_accessed=size // 1000, transcendentals=0)


LONG = pl.CostEstimate(flops=8_000_000_000, bytes_accessed=8 << 20, transcendentals=0)


def shape(dims, kind):
    return jax.ShapeDtypeStruct(dims, kind)


def like(array):
    return shape(array.shape, array.dtype)


def job(kernel, ins, small, outs, scratch, passed=(), result=lambda made: made):
    return dict(kernel=kernel, ins=ins, small=small, outs=outs, scratch=scratch, passed=passed, result=result)


def run(jobs, after=(), cost=None):
    every = lambda key: [array for one in jobs for array in one[key]]
    ins, small, passed, outs, scratch = map(every, ("ins", "small", "passed", "outs", "scratch"))
    space = lambda count, where: [pl.BlockSpec(memory_space=where)] * count

    def body(*refs):
        refs = list(refs)
        take = lambda count: [refs.pop(0) for _ in range(count)]
        held = {"ins": take(len(ins)), "small": take(len(small))}
        take(len(passed) + len(after))
        held["passed"], held["outs"], held["scratch"] = take(len(passed)), take(len(outs)), refs
        for one in jobs:
            own = []
            for key in ("ins", "small", "passed", "outs", "scratch"):
                own += [held[key].pop(0) for _ in one[key]]
            one["kernel"](*own)

    lead = len(ins) + len(small)
    made = pl.pallas_call(
        body,
        out_shape=[like(array) for array in passed] + list(outs),
        in_specs=space(len(ins), pl.ANY) + space(len(small), pltpu.VMEM) + space(len(passed) + len(after), pl.ANY),
        out_specs=space(len(passed) + len(outs), pl.ANY),
        scratch_shapes=scratch,
        input_output_aliases={lead + index: index for index in range(len(passed))},
        compiler_params=pltpu.CompilerParams(vmem_limit_bytes=VMEM_LIMIT),
        cost_estimate=cost or flops_of(1, 1 << 20),
    )(*ins, *small, *passed, *after)
    changed, fresh, results = list(made[: len(passed)]), list(made[len(passed) :]), []
    for one in jobs:
        mine = [changed.pop(0) for _ in one["passed"]] + [fresh.pop(0) for _ in one["outs"]]
        results.append(one["result"](mine))
    return results


def call(kernel, ins, small, outs, scratch, cost, passed=(), after=()):
    return run([job(kernel, ins, small, outs, scratch, passed)], after, cost)[0]


def self_forward(row, x, w, gains, segs, tables, buckets):
    length, width = segs.shape[1], x.shape[1]
    dist = 2 * length
    outs = [
        shape((length, width), BF16),
        shape((length, width), BF16),
        shape((length, 3 * width), BF16),
        shape((length, width), BF16),
        shape((16, length), F32),
    ]

    def kernel(x_h, w_h, gain_r, seg_r, table_r, bucket_r, e_h, n_h, qkv_h, mix_h, lse_h,
               x_v, w_v, n_v, qkv_v, mix_v, lse_v, e_v, mask_v, toe_v, vec_v, s_v, p_v, sems):
        section = lax.axis_index("section")

        @pl.when(section % 2 == 0)
        def _():
            side = section // 2
            loads = copy_all(
                sems, 0,
                (x_h.at[pl.ds(row * length, length)], x_v),
                *[(w_h.at[0, :, pl.ds(c * width, width)], w_v.at[:, pl.ds(c * width, width)]) for c in range(4)],
            )
            fill_toeplitz(toe_v, vec_v, table_r[side], bucket_r[pl.ds(side, 1), :])
            fill_mask(mask_v, seg_r[row : row + 1, :], False, jnp.where(side == 1, 0, 2 * length))
            gain = gain_r[pl.ds(3 * side, 1), :]
            loads[0].wait()
            for rows in row_chunks(length):
                x = x_v[rows, :].astype(F32)
                n_v[rows, :] = (x * inverse_rms(x) * gain).astype(BF16)
            stores = copy_all(sems, 5, (n_v, n_h))
            wait_all(loads[1:4])
            project(n_v, w_v, 0, qkv_v, 0, 3 * width)
            stores += copy_all(sems, 6, (qkv_v, qkv_h))
            attend(qkv_v, qkv_v, qkv_v, 0, width, 2 * width, mask_v, toe_v, s_v, p_v, mix_v, lse_v)
            stores += copy_all(sems, 7, (mix_v, mix_h), (lse_v, lse_h))
            loads[4].wait()

            @pl.loop(0, width // 256)
            def _(t):
                cols = pl.ds(pl.multiple_of(t * 256, 256), 256)
                part = mm(mix_v[...], w_v[:, pl.ds(pl.multiple_of(3 * width + t * 256, 256), 256)])
                e_v[:, cols] = (x_v[:, cols].astype(F32) + part).astype(BF16)

            stores += copy_all(sems, 9, (e_v, e_h))
            wait_all(stores)

    return call(
        kernel,
        [x, w],
        [gains, segs, tables, buckets],
        outs,
        [
            pltpu.VMEM((length, width), BF16),
            pltpu.VMEM((width, 4 * width), BF16),
            pltpu.VMEM((length, width), BF16),
            pltpu.VMEM((length, 3 * width), BF16),
            pltpu.VMEM((length, width), BF16),
            pltpu.VMEM((16, length), F32),
            pltpu.VMEM((length, width), BF16),
            pltpu.VMEM((length, length), F32),
            pltpu.VMEM((H, 128, dist - 128), F32),
            pltpu.VMEM((16, dist), F32),
            pltpu.VMEM((2, length, length), F32),
            pltpu.VMEM((2, length, length), BF16),
            pltpu.SemaphoreType.DMA((10,)),
        ],
        flops_of(3, 12 << 20),
    )


def transposed_bias(tables, flipped, length, after):
    dist = 2 * length

    def kernel(table_r, bucket_r, toe_h, toe_v, vec_v, sems):
        section = lax.axis_index("section")

        @pl.when(section % 2 == 0)
        def _():
            side = section // 2
            fill_toeplitz(toe_v, vec_v, table_r[side], bucket_r[pl.ds(side, 1), :])
            wait_all(copy_all(sems, 0, (toe_v, toe_h)))

    return call(
        kernel,
        [],
        [tables, flipped],
        [shape((H, 128, dist - 128), F32)],
        [pltpu.VMEM((H, 128, dist - 128), F32), pltpu.VMEM((16, dist), F32), pltpu.SemaphoreType.DMA((1,))],
        flops_of(1, 6 << 20),
        after=after,
    )[0]


def marker(after):
    def kernel(out_h):
        pass

    return call(kernel, [], [], [shape((8, 128), F32)], [], flops_of(1, 1 << 20), after=after)[0]


def packed_small(acc, flipped, dgains_s, dgains_e, dgain_d):
    dist, width = acc.shape[2] + 128, dgain_d.shape[1]

    def kernel(acc_h, bucket_r, ds0_r, ds1_r, de0_r, de1_r, dd_r, out_h, acc_v, diag_v, out_v, sems):
        section = lax.axis_index("section")
        side = section // 2
        out_v[...] = jnp.zeros_like(out_v)

        @pl.when(section % 2 == 0)
        def _():
            loads = copy_all(sems, 0, (acc_h, acc_v))
            diag_v[...] = jnp.zeros_like(diag_v)
            wait_all(loads)
            fold_diagonals(acc_v, diag_v)
            ids = lax.broadcasted_iota(jnp.int32, (32, dist), 0)
            onehot = (ids == bucket_r[pl.ds(side, 1), :]).astype(F32)
            part = lax.dot_general(
                diag_v[...], onehot, (((1,), (1,)), ((), ())),
                precision=lax.Precision.HIGHEST, preferred_element_type=F32,
            )
            for own in range(2):
                @pl.when(side == own)
                def _():
                    out_v[3 * own : 3 * own + 1, :] = ds0_r[...] + ds1_r[...]
                    out_v[8:16, 256 * own : 256 * own + 32] = part[:8]
                    out_v[8:16, 256 * own + 128 : 256 * own + 160] = part[8:]

        @pl.when(section == 1)
        def _():
            out_v[1:3, :] = de0_r[...] + de1_r[...]

        @pl.when(side == 1)
        def _():
            out_v[4:7, :] = dd_r[...]

        wait_all(copy_all(sems, 1, (out_v, out_h)))

    return job(
        kernel,
        [acc],
        [flipped, *dgains_s, *dgains_e, dgain_d],
        [shape((16, width), F32)],
        [
            pltpu.VMEM(acc.shape, F32),
            pltpu.VMEM((16, dist), F32),
            pltpu.VMEM((16, width), F32),
            pltpu.SemaphoreType.DMA((2,)),
        ],
        result=lambda made: made[0],
    )


def self_backward(row, sections, ins, mats, gains, segs, toe, g_enc, g_dec, kept, passed, after):
    length, width = segs.shape[1], ins.shape[1]
    dist = 2 * length

    def kernel(x_h, w_h, toe_h, ge_h, gd_h, qkv_h, mix_h, lse_h, gain_r, seg_r, out_h, acc_h, dgain_h, b_h,
               x_v, w_v, qkv_v, mix_v, lse_v, d_v, dm_v, dqkv_v, dn_v, gx_v, dgain_v,
               mask_v, toe_v, acc_v, s_v, dp_v, p_v, ds_v, sems):
        section = lax.axis_index("section")
        side = section // 2

        active = section == sections[0]
        for one in sections[1:]:
            active = active | (section == one)

        @pl.when(active)
        def _():
            loads = either_all(sems, 0, side == 0, ((ge_h, d_v), (gd_h, d_v)))
            loads += copy_all(
                sems, 1,
                (w_h.at[0, :, pl.ds(3 * width, width)], w_v.at[:, pl.ds(3 * width, width)]),
                (mix_h, mix_v),
                (lse_h, lse_v),
                (qkv_h, qkv_v),
                (toe_h, toe_v),
                (w_h.at[0, :, pl.ds(0, 3 * width)], w_v.at[:, pl.ds(0, 3 * width)]),
                (x_h.at[pl.ds(row * length, length)], x_v),
            )
            sums = copy_all(sems, 8, (acc_h, acc_v)) if row else []
            fill_mask(mask_v, seg_r[row : row + 1, :], True, jnp.where(side == 1, 0, 2 * length))
            if not row:
                acc_v[...] = jnp.zeros_like(acc_v)
            gain = gain_r[pl.ds(3 * side, 1), :]
            wait_all(loads[:2])
            stores = copy_all(sems, 9, (d_v, b_h.at[:, pl.ds(3 * width, width)]))
            rows_out(d_v, w_v, 3 * width, dm_v, False)
            wait_all(loads[2:6] + sums)
            attend_back(qkv_v, qkv_v, qkv_v, dm_v, mix_v, 0, width, 2 * width, mask_v, toe_v, lse_v,
                        dp_v, s_v, p_v, ds_v, dqkv_v, 0, acc_v)
            stores += copy_all(sems, 10, (dqkv_v, b_h.at[:, pl.ds(0, 3 * width)]), (acc_v, acc_h))
            wait_all(loads[6:])
            rows_out(dqkv_v, w_v, 0, dn_v, False)
            total = jnp.zeros((1, width), F32)
            for rows in row_chunks(length):
                dx, dgain = rms_back(x_v[rows, :].astype(F32), gain, dn_v[rows, :])
                gx_v[rows, :] = d_v[rows, :].astype(F32) + dx
                total = total + dgain
            dgain_v[...] = total
            stores += copy_all(sems, 12, (gx_v, out_h.at[pl.ds(row * length, length)]), (dgain_v, dgain_h))
            wait_all(stores)

    n, qkv, mix, lse = kept
    return call(
        kernel,
        [ins, mats, toe, g_enc, g_dec, qkv, mix, lse],
        [gains, segs],
        [like(toe), shape((1, width), F32), shape((length, 4 * width), BF16)][len(passed) - 1 :],
        [
            pltpu.VMEM((length, width), BF16),
            pltpu.VMEM((width, 4 * width), BF16),
            pltpu.VMEM((length, 3 * width), BF16),
            pltpu.VMEM((length, width), BF16),
            pltpu.VMEM((16, length), F32),
            pltpu.VMEM((length, width), BF16),
            pltpu.VMEM((length, width), BF16),
            pltpu.VMEM((length, 3 * width), BF16),
            pltpu.VMEM((length, width), F32),
            pltpu.VMEM((length, width), F32),
            pltpu.VMEM((1, width), F32),
            pltpu.VMEM((length, length), F32),
            pltpu.VMEM((H, 128, dist - 128), F32),
            pltpu.VMEM((H, 128, dist - 128), F32),
            pltpu.VMEM((2, length, length), F32),
            pltpu.VMEM((2, length, length), F32),
            pltpu.VMEM((2, length, length), BF16),
            pltpu.VMEM((2, length, length), BF16),
            pltpu.SemaphoreType.DMA((14,)),
        ],
        flops_of(6, 16 << 20),
        passed,
        after,
    )


def encoder_forward(row, e1, mats, gains, out_rows):
    length, width = e1.shape
    hidden = mats.shape[2]
    narrow, wide = shape((length, width), BF16), shape((length, hidden), BF16)
    rows_shape = shape((2 * length, width), F32)
    kept = [narrow, shape((length, width), F32), narrow, wide, wide]

    def kernel(e_h, w_h, gain_r, out_h, send_h, mid_h, n_h, h_h, slope_h,
               e_v, win_v, wout_v, n_v, h_v, slope_v, mid_v, out_v, send_v, sems):
        @pl.when(lax.axis_index("section") == 1)
        def _():
            loads = copy_all(sems, 0, (e_h, e_v), (w_h.at[0], win_v), (w_h.at[1], wout_v))
            loads[0].wait()
            for rows in row_chunks(length):
                x = e_v[rows, :].astype(F32)
                mid_v[rows, :] = x
                n_v[rows, :] = (x * inverse_rms(x) * gain_r[1:2, :]).astype(BF16)
            stores = copy_all(sems, 3, (n_v, n_h))
            loads[1].wait()
            ffn_up(n_v, win_v, h_v, slope_v)
            stores += copy_all(sems, 4, (h_v, h_h), (slope_v, slope_h))
            loads[2].wait()
            rows_out(h_v, wout_v, 0, mid_v, True)
            for rows in row_chunks(length):
                x = mid_v[rows, :]
                y = x * inverse_rms(x) * gain_r[2:3, :]
                out_v[rows, :] = y
                send_v[rows, :] = y.astype(BF16)
            stores += copy_all(
                sems, 6, (send_v, send_h), (out_v, out_h.at[pl.ds(row * length, length)]), (mid_v, mid_h)
            )
            wait_all(stores)

    return call(
        kernel,
        [e1, mats],
        [gains],
        kept if row else [rows_shape] + kept,
        [
            pltpu.VMEM((length, width), BF16),
            pltpu.VMEM((width, hidden), BF16),
            pltpu.VMEM((width, hidden), BF16),
            pltpu.VMEM((length, width), BF16),
            pltpu.VMEM((length, hidden), BF16),
            pltpu.VMEM((length, hidden), BF16),
            pltpu.VMEM((length, width), F32),
            pltpu.VMEM((length, width), F32),
            pltpu.VMEM((length, width), BF16),
            pltpu.SemaphoreType.DMA((9,)),
        ],
        flops_of(2, 20 << 20),
        [out_rows] if row else [],
    )


def encoder_backward(row, ins, extra, e1, mid, slope, mats, gains, after):
    length, width = extra.shape
    hidden = mats.shape[2]

    def kernel(cot_h, extra_h, e_h, mid_h, slope_h, w_h, gain_r, g_h, d_h, du_h, dgain_h,
               cot_v, extra_v, e_v, mid_v, slope_v, win_v, wout_v, d_v, du_v, dn_v, gm_v, g_v, dgain_v, sems):
        @pl.when(lax.axis_index("section") == 1)
        def _():
            loads = copy_all(
                sems, 0,
                (cot_h.at[pl.ds(row * length, length)], cot_v), (extra_h, extra_v), (mid_h, mid_v),
                (w_h.at[1], wout_v), (slope_h, slope_v), (w_h.at[0], win_v), (e_h, e_v),
            )
            wait_all(loads[:3])
            total = jnp.zeros((1, width), F32)
            for rows in row_chunks(length):
                dy = cot_v[rows, :].astype(F32) + extra_v[rows, :].astype(F32)
                dx, dgain = rms_back(mid_v[rows, :], gain_r[2:3, :], dy)
                gm_v[rows, :] = dx
                d_v[rows, :] = dx.astype(BF16)
                total = total + dgain
            dgain_v[1:2, :] = total
            stores = copy_all(sems, 7, (d_v, d_h))
            wait_all(loads[3:5])
            ffn_down(d_v, wout_v, slope_v, du_v)
            stores += copy_all(sems, 8, (du_v, du_h))
            wait_all(loads[5:])
            rows_out(du_v, win_v, 0, dn_v, False)
            total = jnp.zeros((1, width), F32)
            for rows in row_chunks(length):
                dx, dgain = rms_back(e_v[rows, :].astype(F32), gain_r[1:2, :], dn_v[rows, :])
                g_v[rows, :] = (gm_v[rows, :] + dx).astype(BF16)
                total = total + dgain
            dgain_v[0:1, :] = total
            stores += copy_all(sems, 9, (g_v, g_h), (dgain_v, dgain_h))
            wait_all(stores)

    return call(
        kernel,
        [ins, extra, e1, mid, slope, mats],
        [gains],
        [
            shape((length, width), BF16),
            shape((length, width), BF16),
            shape((length, hidden), BF16),
            shape((2, width), F32),
        ],
        [
            pltpu.VMEM((length, width), BF16),
            pltpu.VMEM((length, width), BF16),
            pltpu.VMEM((length, width), BF16),
            pltpu.VMEM((length, width), F32),
            pltpu.VMEM((length, hidden), BF16),
            pltpu.VMEM((width, hidden), BF16),
            pltpu.VMEM((width, hidden), BF16),
            pltpu.VMEM((length, width), BF16),
            pltpu.VMEM((length, hidden), BF16),
            pltpu.VMEM((length, width), F32),
            pltpu.VMEM((length, width), F32),
            pltpu.VMEM((length, width), BF16),
            pltpu.VMEM((2, width), F32),
            pltpu.SemaphoreType.DMA((11,)),
        ],
        flops_of(2, 20 << 20),
        after=after,
    )


def decoder(d_own, d_got, m_two, m_three, ins, cot_got, mats, got_mats, gains, segs, passed, after):
    length, width = d_own.shape
    hidden = mats.shape[2]

    def kernel(d2_h, d3_h, m2_h, m3_h, c1_h, c0_h, w1_h, w0_h, gain_r, seg_r,
               out_h, fa_h, fb_h, other_h, gm_h, gd_h, dgain_h,
               d_v, m_v, c_v, wca_v, win_v, wout_v, n_v, q_v, mix_v, lse_v, mask_v, s_v, p_v, h_v, slope_v,
               x_v, y_v, dn_v, n5_v, do_v, dgain_v, dp_v, ds_v, dq_v, dm_v, do4_v, gm_v, gd_v, out_v, sems):
        section = lax.axis_index("section")

        @pl.when(section >= 2)
        def _():
            own = section == 3
            second = pl.ds(length, length)

            def put(first, *choices):
                return either_all(sems, first, own, *choices)

            loads = put(
                0,
                ((d3_h, d_v), (d2_h, d_v)),
                ((m3_h, m_v), (m2_h, m_v)),
                *[((w1_h.at[k], v), (w0_h.at[k], v)) for k, v in enumerate((wca_v, win_v, wout_v))],
                ((c1_h.at[second], c_v), (c0_h, c_v)),
            )
            fill_mask(mask_v, seg_r[pl.ds(section - 2, 1), :], False, 2 * length)
            loads[0].wait()
            for rows in row_chunks(length):
                x = d_v[rows, :].astype(F32)
                x_v[rows, :] = x
                n_v[rows, :] = (x * inverse_rms(x) * gain_r[4:5, :]).astype(BF16)
            wait_all(loads[1:3])
            late = lambda n, count=1: fb_h.at[:, pl.ds(n * width, count * width)]
            stores = copy_all(sems, 6, (n_v, late(5)), (m_v, late(6)))
            project(n_v, wca_v, 0, q_v, 0, width)
            project(m_v, wca_v, width, q_v, width, 2 * width)
            attend(q_v, q_v, q_v, 0, width, 2 * width, mask_v, None, s_v, p_v, mix_v, lse_v)
            stores += copy_all(sems, 9, (mix_v, late(7)))

            @pl.loop(0, width // 256)
            def _(t):
                cols = pl.ds(pl.multiple_of(t * 256, 256), 256)
                part = mm(mix_v[...], wca_v[:, pl.ds(pl.multiple_of(3 * width + t * 256, 256), 256)])
                x_v[:, cols] = x_v[:, cols] + part

            for rows in row_chunks(length):
                x = x_v[rows, :]
                y_v[rows, :] = x
                n5_v[rows, :] = (x * inverse_rms(x) * gain_r[5:6, :]).astype(BF16)
            stores += copy_all(sems, 10, (n5_v, fa_h.at[:, pl.ds(0, width)]))
            loads[3].wait()
            ffn_up(n5_v, win_v, h_v, slope_v)
            stores += copy_all(sems, 11, (h_v, late(1, 4)))
            loads[4].wait()
            rows_out(h_v, wout_v, 0, y_v, True)
            loads[5].wait()
            total = jnp.zeros((1, width), F32)
            for rows in row_chunks(length):
                y = y_v[rows, :]
                out_v[rows, :] = y * inverse_rms(y) * gain_r[6:7, :]
                dy, dgain = rms_back(y, gain_r[6:7, :], c_v[rows, :].astype(F32))
                total = total + dgain
                do_v[rows, :] = dy.astype(BF16)
                y_v[rows, :] = dy
            dgain_v[2:3, :] = total
            stores += put(12, ((out_v, out_h.at[second]), (out_v, other_h)))
            stores += copy_all(sems, 13, (do_v, late(0)))
            ffn_down(do_v, wout_v, slope_v, slope_v)
            stores += copy_all(sems, 14, (slope_v, fa_h.at[:, pl.ds(width, 4 * width)]))
            rows_out(slope_v, win_v, 0, dn_v, False)
            total = jnp.zeros((1, width), F32)
            for rows in row_chunks(length):
                dx, dgain = rms_back(x_v[rows, :], gain_r[5:6, :], dn_v[rows, :])
                dx = y_v[rows, :] + dx
                y_v[rows, :] = dx
                do4_v[rows, :] = dx.astype(BF16)
                total = total + dgain
            dgain_v[1:2, :] = total
            stores += copy_all(sems, 15, (do4_v, late(11)))
            rows_out(do4_v, wca_v, 3 * width, dm_v, False)
            attend_back(q_v, q_v, q_v, dm_v, mix_v, 0, width, 2 * width, mask_v, None, lse_v,
                        dp_v, s_v, p_v, ds_v, dq_v, 0, None)
            stores += copy_all(sems, 16, (dq_v, late(8, 3)))
            rows_out(dq_v.at[:, width:], wca_v, width, gm_v, False)
            stores += copy_all(sems, 18, (gm_v, gm_h))
            rows_out(dq_v.at[:, :width], wca_v, 0, dn_v, False)
            total = jnp.zeros((1, width), F32)
            for rows in row_chunks(length):
                dx, dgain = rms_back(d_v[rows, :].astype(F32), gain_r[4:5, :], dn_v[rows, :])
                gd_v[rows, :] = (y_v[rows, :] + dx).astype(BF16)
                total = total + dgain
            dgain_v[0:1, :] = total
            stores += copy_all(sems, 19, (gd_v, gd_h), (dgain_v, dgain_h))
            wait_all(stores)

    narrow = shape((length, width), BF16)
    return call(
        kernel,
        [d_own, d_got, m_two, m_three, ins, cot_got, mats, got_mats],
        [gains, segs],
        [
            shape((length, 5 * width), BF16),
            shape((length, 12 * width), BF16),
            shape((length, width), F32),
            *(narrow, narrow),
            shape((3, width), F32),
        ],
        [
            pltpu.VMEM((length, width), BF16),
            pltpu.VMEM((length, width), BF16),
            pltpu.VMEM((length, width), BF16),
            pltpu.VMEM((width, 4 * width), BF16),
            pltpu.VMEM((width, hidden), BF16),
            pltpu.VMEM((width, hidden), BF16),
            pltpu.VMEM((length, width), BF16),
            pltpu.VMEM((length, 3 * width), BF16),
            pltpu.VMEM((length, width), BF16),
            pltpu.VMEM((16, length), F32),
            pltpu.VMEM((length, length), F32),
            pltpu.VMEM((2, length, length), F32),
            pltpu.VMEM((2, length, length), BF16),
            pltpu.VMEM((length, hidden), BF16),
            pltpu.VMEM((length, hidden), BF16),
            pltpu.VMEM((length, width), F32),
            pltpu.VMEM((length, width), F32),
            pltpu.VMEM((length, width), F32),
            pltpu.VMEM((length, width), BF16),
            pltpu.VMEM((length, width), BF16),
            pltpu.VMEM((3, width), F32),
            pltpu.VMEM((2, length, length), F32),
            pltpu.VMEM((2, length, length), BF16),
            pltpu.VMEM((length, 3 * width), BF16),
            pltpu.VMEM((length, width), BF16),
            pltpu.VMEM((length, width), BF16),
            pltpu.VMEM((length, width), BF16),
            pltpu.VMEM((length, width), BF16),
            pltpu.VMEM((length, width), F32),
            pltpu.SemaphoreType.DMA((21,)),
        ],
        flops_of(12, 30 << 20),
        passed,
        after,
    )


def weight_grad(sections, groups, chunks, ndp, decoder=None):
    length, width = groups[0][0][0][0].shape[0], 768
    columns = sum(group[2] for group in groups)
    pieces = len(groups[0][0])
    bits = ndp.bit_length() - 1
    block = width // ndp
    flat = []
    for a_list, b_list, _ in groups + (decoder or []):
        for array, _ in a_list + b_list:
            if not any(array is other for other in flat):
                flat.append(array)
    place = lambda array: [index for index, other in enumerate(flat) if other is array][0]
    plan_of = lambda groups: [
        ([(place(a), a0) for a, a0 in a_list], [(place(b), b0) for b, b0 in b_list], count)
        for a_list, b_list, count in groups
    ]
    plan, other_plan = plan_of(groups), plan_of(decoder or groups)
    tile = 768
    copies = 2 * pieces * len(groups)

    def kernel(*args):
        sources = args[: len(flat)]
        outs = args[len(flat) : len(flat) + 2 * len(chunks)]
        a_v, at_v, b_v, out_v, sems = args[len(flat) + 2 * len(chunks) :]
        me = lax.axis_index("dp")
        section = lax.axis_index("section")
        active = section == sections[0]
        for one in sections[1:]:
            active = active | (section == one)

        @pl.when(active)
        def _():
            loads, start = [], 0
            for g, (a_list, b_list, count) in enumerate(plan):
                group_loads = []
                for k in range(pieces):
                    rows = pl.ds(k * length, length)
                    choices = []
                    for a_of, b_of, _ in (other_plan[g], plan[g]):
                        (ai, a0), (bi, b0) = a_of[k], b_of[k]
                        choices.append((
                            (sources[ai].at[:, pl.ds(a0, width)], a_v.at[g, rows]),
                            (sources[bi].at[:, pl.ds(b0, count)], b_v.at[rows, pl.ds(start, count)]),
                        ))
                    first = 2 * (g * pieces + k)
                    if decoder:
                        group_loads += either_all(sems, first, section >= 2, *zip(*choices))
                    else:
                        group_loads += copy_all(sems, first, *choices[0])
                loads.append(group_loads)
                start += count
            stores, group, group_end, start = [], -1, 0, 0
            for number, (count, order) in enumerate(chunks):
                spots = []
                for b in range(ndp):
                    code = jnp.bitwise_xor(me, b)
                    spot = 0
                    for k in range(bits):
                        spot = spot + ((code >> order[k]) & 1) * (1 << (bits - 1 - k))
                    spots.append(spot)
                done, end = start, start + count
                while done < end:
                    if done == group_end:
                        group += 1
                        wait_all(loads[group])
                        at_v[...] = a_v[group].T
                        group_end += plan[group][2]
                    upto = min(end, group_end)

                    @pl.loop(0, (upto - done) // tile)
                    def _(t):
                        cols = pl.ds(pl.multiple_of(done + t * tile, 128), tile)
                        part = mm(at_v[...], b_v[:, cols])
                        for b in range(ndp):
                            out_v[spots[b], :, cols] = part[b * block : (b + 1) * block, :].astype(BF16)

                    done = upto
                for half in range(2):
                    source = out_v.at[pl.ds(half * (ndp // 2), ndp // 2), :, pl.ds(start, count)]
                    stores += copy_all(sems, copies + 2 * number + half, (source, outs[2 * number + half]))
                start = end
            wait_all(stores)

    return job(
        kernel,
        flat,
        [],
        [shape((ndp // 2, block, count), BF16) for count, _ in chunks for _ in range(2)],
        [
            pltpu.VMEM((len(groups), pieces * length, width), BF16),
            pltpu.VMEM((width, pieces * length), BF16),
            pltpu.VMEM((pieces * length, columns), BF16),
            pltpu.VMEM((ndp, block, columns), BF16),
            pltpu.SemaphoreType.DMA((copies + 2 * len(chunks),)),
        ],
        result=lambda made: [(made[2 * number], made[2 * number + 1]) for number in range(len(chunks))],
    )


def along_dp(value, bit, sections, ndp):
    pairs = [(s * ndp + d, s * ndp + (d ^ bit)) for s in sections for d in range(ndp)]
    return lax.ppermute(value, ("section", "dp"), pairs)


def added(items):
    outs, kinds = [], []
    for keep, _, _ in items:
        kind = "sum" if keep.dtype == F32 else "last" if keep.shape[0] == 1 else "half"
        kinds.append(kind)
        if kind == "half":
            outs += [shape((keep.shape[0] // 2,) + keep.shape[1:], BF16)] * 2
        else:
            outs.append(shape(keep.shape if kind == "sum" else keep.shape[1:], F32))

    def kernel(*refs):
        count = len(items)
        sources, rest = refs[: 2 * count], refs[2 * count :]
        targets, rest = rest[: len(outs)], rest[len(outs) :]
        scratch, sems = rest[:-1], rest[-1]
        section = lax.axis_index("section")

        def takes_part(sections):
            active = section == sections[0]
            for one in sections[1:]:
                active = active | (section == one)
            return active

        for number, item in enumerate(items):
            @pl.when(takes_part(item[2]))
            def _():
                for k in range(2):
                    pltpu.make_async_copy(
                        sources[2 * number + k], scratch[3 * number + k], sems.at[4 * number + k]
                    ).start()

        place = 0
        for number, (item, kind) in enumerate(zip(items, kinds)):
            n = item[0].shape[0]
            keep_v, got_v, out_v = scratch[3 * number : 3 * number + 3]
            mine = targets[place : place + (2 if kind == "half" else 1)]
            place += len(mine)

            @pl.when(takes_part(item[2]))
            def _():
                for k, v in enumerate((keep_v, got_v)):
                    pltpu.make_async_copy(sources[2 * number + k], v, sems.at[4 * number + k]).wait()
                if kind == "half":
                    @pl.loop(0, n)
                    def _(i):
                        out_v[i] = (keep_v[i].astype(F32) + got_v[i].astype(F32)).astype(BF16)

                    wait_all(
                        copy_all(
                            sems, 4 * number + 2,
                            (out_v.at[pl.ds(0, n // 2)], mine[0]), (out_v.at[pl.ds(n // 2, n // 2)], mine[1]),
                        )
                    )
                else:
                    if kind == "last":
                        out_v[...] = keep_v[0].astype(F32) + got_v[0].astype(F32)
                    else:
                        out_v[...] = keep_v[...] + got_v[...]
                    wait_all(copy_all(sems, 4 * number + 2, (out_v, mine[0])))

    scratch = []
    for (keep, _, _), kind in zip(items, kinds):
        own = pltpu.VMEM(keep.shape, keep.dtype)
        scratch += [own, own, pltpu.VMEM(keep.shape[1:], F32) if kind == "last" else own]
    def result(made):
        results = []
        for kind in kinds:
            size = 2 if kind == "half" else 1
            results.append(tuple(made[:size]) if size == 2 else made[0])
            made = made[size:]
        return results

    return job(
        kernel,
        [array for keep, got, _ in items for array in (keep, got)],
        [],
        outs,
        scratch + [pltpu.SemaphoreType.DMA((4 * len(items),))],
        result=result,
    )


def joined(v, pieces):
    start = 0
    for piece in pieces:
        yield piece, v.at[:, pl.ds(start, piece.shape[1])]
        start += piece.shape[1]


def first_outputs(first, second, cross, rows_got, out_rows, after):
    length, width = rows_got.shape
    block = cross[0].shape[0]
    columns = 2 * cross[0].shape[1]

    def kernel(f0_h, f1_h, s0_h, s1_h, c0_h, c1_h, r_h, out_h, grad_h, f_v, s_v, c_v, r_v, sems):
        section = lax.axis_index("section")

        @pl.when(section != 3)
        def _():
            c_v[...] = jnp.zeros_like(c_v)
            stores = copy_all(sems, 0, (c_v, grad_h.at[2]))

            @pl.when(section != 1)
            def _():
                wait_all(copy_all(sems, 1, (c_v, grad_h.at[1])))

            @pl.when(section == 1)
            def _():
                wait_all(copy_all(sems, 1, *joined(f_v, (f0_h, f1_h)), *joined(s_v, (s0_h, s1_h))))
                wait_all(copy_all(sems, 5, (f_v, grad_h.at[0]), (s_v, grad_h.at[1])))

            wait_all(stores)

        @pl.when(section == 3)
        def _():
            parts = [*joined(f_v, (f0_h, f1_h)), *joined(s_v, (s0_h, s1_h)), *joined(c_v, (c0_h, c1_h))]
            wait_all(copy_all(sems, 0, *parts, (r_h, r_v)))
            wait_all(
                copy_all(
                    sems, 7,
                    (f_v, grad_h.at[1]), (s_v, grad_h.at[2]), (c_v, grad_h.at[0]), (r_v, out_h.at[pl.ds(0, length)]),
                )
            )

    return call(
        kernel,
        [*first, *second, *cross, rows_got],
        [],
        [shape((3, block, columns), F32)],
        [pltpu.VMEM((block, columns), F32)] * 3 + [pltpu.VMEM((length, width), F32), pltpu.SemaphoreType.DMA((11,))],
        flops_of(1, 1 << 20),
        [out_rows],
        after,
    )


def last_step(items, grad):
    block, columns = items[0][0].shape[1:]

    def kernel(k0_h, g0_h, k1_h, g1_h, grad_h, k_v, g_v, out_v, sems):
        @pl.when(lax.axis_index("section") % 2 == 0)
        def _():
            loads = copy_all(
                sems, 0, (k0_h.at[0], k_v.at[0]), (g0_h.at[0], g_v.at[0]), (k1_h.at[0], k_v.at[1]), (g1_h.at[0], g_v.at[1])
            )
            stores = []
            for n in range(2):
                wait_all(loads[2 * n : 2 * n + 2])
                out_v[n] = k_v[n].astype(F32) + g_v[n].astype(F32)
                stores += copy_all(sems, 4 + n, (out_v.at[n], grad_h.at[0, :, pl.ds(n * columns, columns)]))
            wait_all(stores)

    return job(
        kernel,
        [array for keep, got, _ in items for array in (keep, got)],
        [],
        [],
        [pltpu.VMEM((2, block, columns), BF16)] * 2 + [pltpu.VMEM((2, block, columns), F32), pltpu.SemaphoreType.DMA((6,))],
        [grad],
        lambda made: made[0],
    )


def per_device(section_ins, segments, buckets, section_mats, gains, tables):
    ndp = lax.axis_size("dp")
    ins = section_ins[0]
    mats = section_mats[0]
    length = segments.shape[1]
    width = ins.shape[1]
    segs = segments.astype(F32)
    flat_tables = jnp.pad(jnp.swapaxes(tables, 1, 2), ((0, 0), (0, 16 - H), (0, 0)))
    flipped = jnp.pad(buckets[:, ::-1], ((0, 0), (0, 1)), constant_values=-1)
    everywhere = (0, 1, 2, 3)
    move = lambda value, pairs: lax.ppermute(value, "section", pairs)

    fwd0 = self_forward(0, ins, mats, gains, segs, flat_tables, buckets)
    late_mats, _ = lax.optimization_barrier((section_mats, fwd0[0]))
    got_mats = move(late_mats, [(3, 2)])[0]
    first0 = move(fwd0[0], [(0, 1)])
    fwd1 = self_forward(1, ins, mats, gains, segs, flat_tables, buckets)
    first1 = move(fwd1[0], [(0, 1), (2, 3)])
    toe = transposed_bias(flat_tables, flipped, length, [fwd1[0]])
    out_rows, *enc0 = encoder_forward(0, first0, mats, gains, None)
    m_two = move(enc0[0], [(1, 2)])
    late_ins, _ = lax.optimization_barrier((ins, fwd1[0]))
    cot_got = move(late_ins[:length], [(3, 2)])
    out_rows, *enc1 = encoder_forward(1, first1, mats, gains, out_rows)
    m_three = move(enc1[0], [(1, 3)])
    here = marker([enc1[0], m_two])

    dec = decoder(fwd0[0], first1, m_two, m_three, ins, cot_got, mats, got_mats, gains, segs, [out_rows], [toe, here])
    out_rows, first_d, later_d, other, g_mem, g_self, dgain_d = dec
    extra = move(g_mem, [(2, 1), (3, 0)])
    even, odd = (0, 2), (1, 3)
    own0 = self_backward(0, (2,), ins, mats, gains, segs, toe, g_self, g_self, fwd0[1:], [out_rows], [extra])
    (first_sent, g_self_sent), _ = lax.optimization_barrier(((first_d, g_self), own0[1]))
    first_got = move(first_sent, [(2, 3)])
    g_self_got = move(g_self_sent, [(3, 2)])
    back0 = encoder_backward(0, ins, extra, first0, enc0[1], enc0[4], mats, gains, [first_got])
    g0 = move(back0[0], [(1, 0)])
    (later_sent, other, passed_on), _ = lax.optimization_barrier(((later_d, other, extra), back0[0]))
    extra1 = move(passed_on, [(0, 1)])
    later_got = move(later_sent, [(2, 3)])
    own0 = self_backward(0, (0,), ins, mats, gains, segs, toe, g0, g0, fwd0[1:], own0, [extra1, g_self_got])
    out_rows, acc = own0[:2]
    back1 = encoder_backward(1, ins, extra1, first1, enc1[1], enc1[4], mats, gains, [acc])
    g1 = move(back1[0], [(1, 0)])
    other, _ = lax.optimization_barrier((other, back1[0]))
    rows_got = move(other, [(2, 3)])

    plain = tuple(range(ndp.bit_length() - 1))
    turned = (1, 0) + plain[2:]
    orders = (plain, turned)
    steps = len(plain)
    halves = [(2 * width, order) for order in orders]

    def send_both(pairs, step, sections):
        return [
            (keep, along_dp(send, 1 << order[step], sections, ndp), sections)
            for (keep, send), order in zip(pairs, orders)
        ]

    def two_rows(a, b, columns=4 * width):
        return [(a, b, columns)]

    rows_of = lambda own, got, at: [(own, at * width), (got, at * width)]
    first_of, later_of = partial(rows_of, first_d, first_got), partial(rows_of, later_d, later_got)
    groups = two_rows([(enc0[2], 0), (enc1[2], 0)], [(back0[2], 0), (back1[2], 0)])
    made, = run([weight_grad(odd, groups, halves, ndp, two_rows(first_of(0), first_of(1)))], [back1[0]])
    one = send_both(made, 0, odd)
    groups = two_rows([(back0[1], 0), (back1[1], 0)], [(enc0[3], 0), (enc1[3], 0)])
    made, = run([weight_grad(odd, groups, halves, ndp, two_rows(later_of(0), later_of(1)))], [made[0][0]])
    two = send_both(made, 0, odd)
    groups = [(later_of(5 + k), later_of(at), count * width) for k, at, count in ((0, 8, 1), (1, 9, 2), (2, 11, 1))]
    made, = run([weight_grad((3,), groups, halves, ndp)], [made[0][0]])
    mem = send_both(made, 0, (3,))

    own1 = self_backward(
        1, even, ins, mats, gains, segs, toe, g1, g_self_got, fwd1[1:], [out_rows, acc], [made[0][0]]
    )
    out_rows, acc = own1[:2]
    dgains = ([own0[2], own1[2]], [back0[3], back1[3]], dgain_d)
    small, pairs = run([packed_small(acc, flipped, *dgains), added(one)], cost=LONG)
    one = send_both(pairs, 1, odd)
    small_steps = [lambda value: move(value, [(0, 1), (1, 0), (2, 3), (3, 2)])]
    small_steps += [lambda value: move(value, [(0, 2), (2, 0), (1, 3), (3, 1)])]
    small_steps += [partial(along_dp, bit=1 << k, sections=everywhere, ndp=ndp) for k in range(steps)]
    small_got = small_steps[0](small)
    groups = [
        ([(fwd0[1], 0), (fwd1[1], 0)], [(own0[3], 0), (own1[3], 0)], 3 * width),
        ([(fwd0[3], 0), (fwd1[3], 0)], [(own0[3], 3 * width), (own1[3], 3 * width)], width),
    ]
    made, = run([weight_grad(even, groups, halves, ndp)], [pairs[0][0]])
    slf = send_both(made, 0, even)
    (*pairs, small), = run([added([*two, *mem, (small, small_got, everywhere)])], [made[0][0]])
    two, mem = send_both(pairs[:2], 1, odd), send_both(pairs[2:], 1, (3,))
    small_got = small_steps[1](small)
    (*parts, small), = run([added([*one, (small, small_got, everywhere)])], [pairs[0][0]])
    one = send_both(parts, 2, odd)
    small_got = small_steps[2](small)
    tied = [parts[0][0]]
    one_step, two_step = 2, 1
    for k in range(steps):
        last = k + 1 == steps
        if two_step < steps:
            (*parts, s0, s1, small), = run([added([*two, *mem, *slf, (small, small_got, everywhere)])], tied)
            pairs = [s0, s1]
            two_step += 1
            if two_step < steps:
                two, mem = send_both(parts[:2], two_step, odd), send_both(parts[2:], two_step, (3,))
            else:
                two_shard, mem_shard = parts[:2], parts[2:]
            tied = [s0[0]]
        elif not last:
            (*pairs, small), = run([added([*slf, (small, small_got, everywhere)])], tied)
            tied = [pairs[0][0]]
        if last:
            out_rows, grad = first_outputs(one_shard, two_shard, mem_shard, rows_got, out_rows, tied)
            grad, (small,) = run([last_step(slf, grad), added([(small, small_got, everywhere)])])
        else:
            slf = send_both(pairs, k + 1, even)
            small_got = small_steps[k + 3](small)
            if one_step < steps:
                parts, = run([added(one)], tied)
                one_step += 1
                if one_step < steps:
                    one = send_both(parts, one_step, odd)
                    tied = [parts[0][0]]
                else:
                    one_shard = parts
                    tied = [parts[0]]

    gains_grad = small[: gains.shape[0]]
    heads = [
        jnp.concatenate([small[8:16, at : at + 32], small[8:12, at + 128 : at + 160]], axis=0)
        for at in range(0, 256 * tables.shape[0], 256)
    ]
    return out_rows[None], grad[None], gains_grad, jnp.swapaxes(jnp.stack(heads), 1, 2)


def solution(mesh):
    placed = (
        P("section", "dp", None),
        P("dp", None),
        P(),
        P("section", None, None, None),
        P(),
        P(),
    )
    return jax.shard_map(
        per_device,
        mesh=mesh,
        in_specs=placed,
        out_specs=(P("section", "dp", None), P("section", None, "dp", None), P(), P()),
        check_vma=False,
    )
```

```python
from functools import partial

import jax
import jax.numpy as jnp
from jax import lax
from jax.experimental import pallas as pl
from jax.experimental.pallas import tpu as pltpu
from jax.sharding import PartitionSpec as P

H = 12
HD = 64
PAIRS = H // 2
EPS = 1e-06
GELU = 0.7978845608028654
CUBIC = 0.044715
MASKED = -1e38
F32 = jnp.float32
BF16 = jnp.bfloat16
ROW_STEP = 128
VMEM_LIMIT = 60 * 1024 * 1024


def mm(a, b):
    return jnp.dot(a, b, preferred_element_type=F32)


def mm_nt(a, b):
    return lax.dot_general(a, b, (((1,), (1,)), ((), ())), preferred_element_type=F32)


def inverse_rms(x):
    return lax.rsqrt(jnp.mean(x * x, axis=-1, keepdims=True) + EPS)


def row_chunks(length):
    return [pl.ds(start, ROW_STEP) for start in range(0, length, ROW_STEP)]


def rms_back(x, gain, dy):
    r = inverse_rms(x)
    inner = jnp.mean(dy * gain * x, axis=-1, keepdims=True)
    dx = r * gain * dy - x * (r * r * r) * inner
    return dx, jnp.sum(dy * x * r, axis=0, keepdims=True)


def copy_all(sems, first, *pairs):
    started = []
    for offset, (source, target) in enumerate(pairs):
        one = pltpu.make_async_copy(source, target, sems.at[first + offset])
        one.start()
        started.append(one)
    return started


class Either:
    def __init__(self, sem, flag, yes, no):
        self.done = pltpu.make_async_copy(*yes, sem)

        @pl.when(flag)
        def _():
            pltpu.make_async_copy(*yes, sem).start()

        @pl.when(jnp.logical_not(flag))
        def _():
            pltpu.make_async_copy(*no, sem).start()

    def wait(self):
        self.done.wait()


def either_all(sems, first, flag, *choices):
    return [Either(sems.at[first + offset], flag, *choice) for offset, choice in enumerate(choices)]


def wait_all(started):
    for one in started:
        one.wait()


def head_lanes(second):
    lane = lax.broadcasted_iota(jnp.int32, (1, 2 * HD), 1)
    return (lane >= HD) if second else (lane < HD)


def fill_mask(mask_v, seg_row, transposed, slack):
    length = seg_row.shape[1]
    down = jnp.broadcast_to(seg_row, (128, length)).T
    for c in range(length // 128):
        along = seg_row[:, c * 128 : (c + 1) * 128]
        r = lax.broadcasted_iota(jnp.int32, (length, 128), 0)
        q = lax.broadcasted_iota(jnp.int32, (length, 128), 1) + c * 128
        key, query = (r, q) if transposed else (q, r)
        ok = (down == along) & (key <= query + slack)
        mask_v[:, c * 128 : (c + 1) * 128] = jnp.where(ok, 0.0, MASKED)


def fill_toeplitz(toe_v, vec_v, table, bucket_row):
    count = bucket_row.shape[1]
    ids = lax.broadcasted_iota(jnp.int32, (table.shape[0], count), 0)
    onehot = (ids == bucket_row).astype(F32)
    vec = lax.dot_general(
        table, onehot, (((0,), (0,)), ((), ())), precision=lax.Precision.HIGHEST, preferred_element_type=F32
    )
    vec_v[:H, :count] = vec

    @pl.loop(0, H)
    def _(h):
        wide = jnp.broadcast_to(vec_v[pl.ds(h, 1), :], (128, vec_v.shape[1]))
        rolled = pltpu.roll(wide, vec_v.shape[1] - 127, 1, stride=1, stride_axis=0)
        toe_v[h] = rolled[:, : toe_v.shape[2]]


def pair_cols(base, hp):
    return pl.ds(pl.multiple_of(base + hp * 128, 128), 128)


def over_pairs(scores, rest):
    scores(0, 0)

    @pl.loop(0, PAIRS // 2)
    def _(i):
        scores(2 * i + 1, 1)
        rest(2 * i, 0)
        scores(jnp.minimum(2 * i + 2, PAIRS - 1), 0)
        rest(2 * i + 1, 1)


def attend_ahead(q_v, k_v, v_v, q0, k0, v0, mask_v, toe_v, s_v, p_v, mix_v, lse_v, top_v, total_v):
    length = mix_v.shape[0]
    low, high = head_lanes(False), head_lanes(True)
    lane = lax.broadcasted_iota(jnp.int32, (1, 2 * HD), 1)
    top_v[...] = jnp.zeros_like(top_v)
    total_v[...] = jnp.ones_like(total_v)

    def scores(hp, slot):
        q2, k2 = q_v[:, pair_cols(q0, hp)], k_v[:, pair_cols(k0, hp)]
        for a, mine in enumerate((low, high)):
            s_v[2 * slot + a] = mm_nt(jnp.where(mine, q2, jnp.zeros_like(q2)), k2)

    def rest(hp, slot):
        v2 = v_v[:, pair_cols(v0, hp)]
        outs, tops = [], []
        for a, mine in enumerate((low, high)):
            top = []
            for c in range(length // 128):
                rows = pl.ds(c * 128, 128)
                s = s_v[2 * slot + a, rows, :] + mask_v[rows, :]
                if toe_v is not None:
                    left = toe_v.shape[2] - length - c * 128
                    s = s + toe_v[2 * hp + a, :, left : left + length]
                m = jnp.max(s, axis=-1, keepdims=True)
                p_v[2 * slot + a, rows, :] = jnp.exp(s - m).astype(BF16)
                top.append(m)
            tops.append(jnp.concatenate(top, axis=0))
            outs.append(mm(p_v[2 * slot + a], jnp.where(mine, v2, jnp.ones_like(v2))))
        total = pltpu.roll(jnp.where(low, outs[1], outs[0]), HD, 1)
        mix_v[:, pair_cols(0, hp)] = (jnp.where(low, outs[0], outs[1]) / total).astype(BF16)
        first, second = lane == 2 * hp, lane == 2 * hp + 1
        top_v[...] = jnp.where(first, tops[0], jnp.where(second, tops[1], top_v[...]))
        total_v[...] = jnp.where(first, total[:, :1], jnp.where(second, total[:, HD : HD + 1], total_v[...]))

    over_pairs(scores, rest)
    lse_v[...] = (top_v[...] + jnp.log(total_v[...])).T[: lse_v.shape[0], :]


def attend(q_v, k_v, v_v, q0, k0, v0, mask_v, toe_v, s_v, p_v, mix_v, lse_v):
    length = mix_v.shape[0]

    @pl.loop(0, PAIRS)
    def _(hp):
        at = lambda base: pl.ds(pl.multiple_of(base + hp * 128, 128), 128)
        q2, k2, v2 = q_v[:, at(q0)], k_v[:, at(k0)], v_v[:, at(v0)]
        low = head_lanes(False)
        outs, tops = [], []
        for a in range(2):
            mine = head_lanes(a == 1)
            s_v[a] = mm_nt(jnp.where(mine, q2, jnp.zeros_like(q2)), k2)
            top = []
            for c in range(length // 128):
                rows = pl.ds(c * 128, 128)
                s = s_v[a, rows, :] + mask_v[rows, :]
                if toe_v is not None:
                    left = toe_v.shape[2] - length - c * 128
                    s = s + toe_v[2 * hp + a, :, left : left + length]
                m = jnp.max(s, axis=-1, keepdims=True)
                p_v[a, rows, :] = jnp.exp(s - m).astype(BF16)
                top.append(m)
            tops.append(jnp.concatenate(top, axis=0))
            outs.append(mm(p_v[a], jnp.where(mine, v2, jnp.ones_like(v2))))
        total = pltpu.roll(jnp.where(low, outs[1], outs[0]), HD, 1)
        mix_v[:, at(0)] = (jnp.where(low, outs[0], outs[1]) / total).astype(BF16)
        stat = (jnp.where(low, tops[0], tops[1]) + jnp.log(total)).T
        lse_v[pl.ds(2 * hp, 1), :] = stat[0:1, :]
        lse_v[pl.ds(2 * hp + 1, 1), :] = stat[HD : HD + 1, :]


def attend_back(q_v, k_v, v_v, dm_v, mix_v, q0, k0, v0, mask_v, toe_v, lse_v, dp_v, s_v, p_v, ds_v, out_v, o0, acc_v):
    length = mix_v.shape[0]

    @pl.loop(0, PAIRS)
    def _(hp):
        at = lambda base: pl.ds(pl.multiple_of(base + hp * 128, 128), 128)
        q2, k2, v2, dm2 = q_v[:, at(q0)], k_v[:, at(k0)], v_v[:, at(v0)], dm_v[:, at(0)]
        low = head_lanes(False)
        prod = (dm2.astype(F32) * mix_v[:, at(0)].astype(F32)).T
        k2t = k2.T
        dvs, dks, dqs = [], [], []
        for a in range(2):
            mine = head_lanes(a == 1)
            s_v[a] = mm_nt(jnp.where(mine, k2, jnp.zeros_like(k2)), q2)
            dp_v[a] = mm_nt(jnp.where(mine, v2, jnp.zeros_like(v2)), dm2)
            delta = jnp.sum(prod[a * HD : (a + 1) * HD, :], axis=0, keepdims=True)
            lse = lse_v[pl.ds(2 * hp + a, 1), :]
            for c in range(length // 128):
                rows = pl.ds(c * 128, 128)
                s = s_v[a, rows, :] + mask_v[rows, :]
                if toe_v is not None:
                    left = toe_v.shape[2] - length - c * 128
                    s = s + toe_v[2 * hp + a, :, left : left + length]
                p = jnp.exp(s - lse)
                p_v[a, rows, :] = p.astype(BF16)
                ds = p * (dp_v[a, rows, :] - delta)
                ds_v[a, rows, :] = ds.astype(BF16)
                if acc_v is not None:
                    acc_v[2 * hp + a, :, left : left + length] += ds
            dvs.append(mm(p_v[a], dm2))
            dks.append(mm(ds_v[a], q2))
            dqs.append(mm(k2t[a * HD : (a + 1) * HD, :], ds_v[a]))
        out_v[:, at(o0)] = jnp.concatenate(dqs, axis=0).T.astype(BF16)
        out_v[:, at(o0 + PAIRS * 128)] = jnp.where(low, dks[0], dks[1]).astype(BF16)
        out_v[:, at(o0 + 2 * PAIRS * 128)] = jnp.where(low, dvs[0], dvs[1]).astype(BF16)


def fold_diagonals(acc_v, diag_v):

    @pl.loop(0, H, unroll=3)
    def _(h):
        value = jnp.concatenate([acc_v[h], jnp.zeros((128, 128), F32)], axis=1)
        half = 64
        while half >= 1:
            value = pltpu.roll(value[:half], half, 1) + value[half:]
            half //= 2
        diag_v[pl.ds(h, 1), :] = value


def gelu_parts(u):
    square = u * u
    bend = u * (GELU + (GELU * CUBIC) * square)
    half = 0.5 + 0.5 * jnp.tanh(bend)
    hidden = u * half
    slope = half + 2.0 * hidden * (1.0 - half) * (GELU + (3.0 * GELU * CUBIC) * square)
    return hidden, slope


COLUMN_PARTS = 3


def column_parts(sems, first, source, target, parts=COLUMN_PARTS):
    width = target.shape[1] // parts
    cuts = [pl.ds(c * width, width) for c in range(parts)]
    return copy_all(sems, first, *[(source.at[:, cut], target.at[:, cut]) for cut in cuts])


def ffn_up(n_v, win_v, h_v, slope_v, loads=()):
    tile = 512

    @pl.loop(0, win_v.shape[1] // tile)
    def _(t):
        for part, load in enumerate(loads):
            pl.when(t == part * (win_v.shape[1] // tile // len(loads)))(load.wait)

        cols = pl.ds(pl.multiple_of(t * tile, tile), tile)
        hidden, slope = gelu_parts(mm(n_v[...], win_v[:, cols]))
        h_v[:, cols] = hidden.astype(BF16)
        slope_v[:, cols] = slope.astype(BF16)


def rows_out(a_v, w_v, w0, out_v, add):
    tile = 256
    depth = a_v.shape[1]

    @pl.loop(0, w_v.shape[0] // tile)
    def _(t):
        cols = pl.ds(pl.multiple_of(t * tile, tile), tile)
        part = mm_nt(a_v[...], w_v[cols, w0 : w0 + depth])
        if add:
            out_v[:, cols] = out_v[:, cols] + part
        else:
            out_v[:, cols] = part.astype(out_v.dtype)


def ffn_down(d_v, wout_v, slope_v, du_v):
    tile = 512

    @pl.loop(0, wout_v.shape[1] // tile)
    def _(t):
        cols = pl.ds(pl.multiple_of(t * tile, tile), tile)
        grad = mm(d_v[...], wout_v[:, cols])
        du_v[:, cols] = (grad * slope_v[:, cols].astype(F32)).astype(BF16)


def project(a_v, w_v, w0, out_v, o0, width):
    tile = 384

    @pl.loop(0, width // tile)
    def _(t):
        source = pl.ds(pl.multiple_of(w0 + t * tile, 128), tile)
        target = pl.ds(pl.multiple_of(o0 + t * tile, 128), tile)
        out_v[:, target] = mm(a_v[...], w_v[:, source]).astype(out_v.dtype)


def flops_of(matmuls, size):
    return pl.CostEstimate(flops=matmuls * 1000, bytes_accessed=size // 1000, transcendentals=0)


LONG = pl.CostEstimate(flops=60_000_000_000, bytes_accessed=60 << 20, transcendentals=0)

SHORT = pl.CostEstimate(flops=20_000_000_000, bytes_accessed=20 << 20, transcendentals=0)


def shape(dims, kind):
    return jax.ShapeDtypeStruct(dims, kind)


def like(array):
    return shape(array.shape, array.dtype)


def job(kernel, ins, small, outs, scratch, passed=(), result=lambda made: made):
    return dict(kernel=kernel, ins=ins, small=small, outs=outs, scratch=scratch, passed=passed, result=result)


def run(jobs, after=(), cost=None):
    every = lambda key: [array for one in jobs for array in one[key]]
    ins, small, passed, outs, scratch = map(every, ("ins", "small", "passed", "outs", "scratch"))
    space = lambda count, where: [pl.BlockSpec(memory_space=where)] * count

    def body(*refs):
        refs = list(refs)
        take = lambda count: [refs.pop(0) for _ in range(count)]
        held = {"ins": take(len(ins)), "small": take(len(small))}
        take(len(passed) + len(after))
        held["passed"], held["outs"], held["scratch"] = take(len(passed)), take(len(outs)), refs
        for one in jobs:
            own = []
            for key in ("ins", "small", "passed", "outs", "scratch"):
                own += [held[key].pop(0) for _ in one[key]]
            one["kernel"](*own)

    lead = len(ins) + len(small)
    made = pl.pallas_call(
        body,
        out_shape=[like(array) for array in passed] + list(outs),
        in_specs=space(len(ins), pl.ANY) + space(len(small), pltpu.VMEM) + space(len(passed) + len(after), pl.ANY),
        out_specs=space(len(passed) + len(outs), pl.ANY),
        scratch_shapes=scratch,
        input_output_aliases={lead + index: index for index in range(len(passed))},
        compiler_params=pltpu.CompilerParams(vmem_limit_bytes=VMEM_LIMIT),
        cost_estimate=cost or flops_of(1, 1 << 20),
    )(*ins, *small, *passed, *after)
    changed, fresh, results = list(made[: len(passed)]), list(made[len(passed) :]), []
    for one in jobs:
        mine = [changed.pop(0) for _ in one["passed"]] + [fresh.pop(0) for _ in one["outs"]]
        results.append(one["result"](mine))
    return results


def call(kernel, ins, small, outs, scratch, cost, passed=(), after=()):
    return run([job(kernel, ins, small, outs, scratch, passed)], after, cost)[0]


def self_forward(row, x, w, gains, segs, tables, buckets, toe=None):
    length, width = segs.shape[1], x.shape[1]
    dist = 2 * length
    outs = [
        shape((length, width), BF16),
        shape((length, width), BF16),
        shape((length, 3 * width), BF16),
        shape((length, width), BF16),
        shape((16, length), F32),
    ]

    def kernel(x_h, w_h, *refs):
        if row:
            toe_h, *refs = refs
            body(x_h, w_h, *refs[:9], toe_h, *refs[9:])
        else:
            body(x_h, w_h, *refs)

    def body(x_h, w_h, gain_r, seg_r, table_r, bucket_r, e_h, n_h, qkv_h, mix_h, lse_h, toe_h,
               x_v, w_v, n_v, qkv_v, mix_v, lse_v, e_v, mask_v, toe_v, vec_v, s_v, p_v, top_v, total_v, sems):
        section = lax.axis_index("section")

        @pl.when(section % 2 == 0)
        def _():
            side = section // 2
            loads = copy_all(
                sems, 0,
                (x_h.at[pl.ds(row * length, length)], x_v),
                *[(w_h.at[0, :, pl.ds(c * width, width)], w_v.at[:, pl.ds(c * width, width)]) for c in range(4)],
            )
            if row:
                tiles = copy_all(sems, 10, (toe_h, toe_v))
            else:
                fill_toeplitz(toe_v, vec_v, table_r[side], bucket_r[pl.ds(side, 1), :])
                tiles = copy_all(sems, 10, (toe_v, toe_h))
            fill_mask(mask_v, seg_r[row : row + 1, :], False, jnp.where(side == 1, 0, 2 * length))
            gain = gain_r[pl.ds(3 * side, 1), :]
            loads[0].wait()
            for rows in row_chunks(length):
                x = x_v[rows, :].astype(F32)
                n_v[rows, :] = (x * inverse_rms(x) * gain).astype(BF16)
            stores = copy_all(sems, 5, (n_v, n_h))
            wait_all(loads[1:4])
            project(n_v, w_v, 0, qkv_v, 0, 3 * width)
            stores += copy_all(sems, 6, (qkv_v, qkv_h))
            if row:
                wait_all(tiles)
            attend_ahead(qkv_v, qkv_v, qkv_v, 0, width, 2 * width, mask_v, toe_v, s_v, p_v, mix_v, lse_v, top_v, total_v)
            stores += copy_all(sems, 7, (mix_v, mix_h), (lse_v, lse_h))
            loads[4].wait()

            @pl.loop(0, width // 256)
            def _(t):
                cols = pl.ds(pl.multiple_of(t * 256, 256), 256)
                part = mm(mix_v[...], w_v[:, pl.ds(pl.multiple_of(3 * width + t * 256, 256), 256)])
                e_v[:, cols] = (x_v[:, cols].astype(F32) + part).astype(BF16)

            stores += copy_all(sems, 9, (e_v, e_h))
            wait_all(stores if row else stores + tiles)

    return call(
        kernel,
        [x, w] + ([toe] if row else []),
        [gains, segs, tables, buckets],
        outs if row else outs + [shape((H, 128, dist - 128), F32)],
        [
            pltpu.VMEM((length, width), BF16),
            pltpu.VMEM((width, 4 * width), BF16),
            pltpu.VMEM((length, width), BF16),
            pltpu.VMEM((length, 3 * width), BF16),
            pltpu.VMEM((length, width), BF16),
            pltpu.VMEM((16, length), F32),
            pltpu.VMEM((length, width), BF16),
            pltpu.VMEM((length, length), F32),
            pltpu.VMEM((H, 128, dist - 128), F32),
            pltpu.VMEM((16, dist), F32),
            pltpu.VMEM((4, length, length), F32),
            pltpu.VMEM((4, length, length), BF16),
            pltpu.VMEM((length, 128), F32),
            pltpu.VMEM((length, 128), F32),
            pltpu.SemaphoreType.DMA((11,)),
        ],
        flops_of(3, 12 << 20),
    )


def transposed_bias(tables, flipped, length, after):
    dist = 2 * length

    def kernel(table_r, bucket_r, toe_h, toe_v, vec_v, sems):
        section = lax.axis_index("section")

        @pl.when(section % 2 == 0)
        def _():
            side = section // 2
            fill_toeplitz(toe_v, vec_v, table_r[side], bucket_r[pl.ds(side, 1), :])
            wait_all(copy_all(sems, 0, (toe_v, toe_h)))

    return call(
        kernel,
        [],
        [tables, flipped],
        [shape((H, 128, dist - 128), F32)],
        [pltpu.VMEM((H, 128, dist - 128), F32), pltpu.VMEM((16, dist), F32), pltpu.SemaphoreType.DMA((1,))],
        flops_of(1, 6 << 20),
        after=after,
    )[0]


def marker(after):
    def kernel(out_h):
        pass

    return call(kernel, [], [], [shape((8, 128), F32)], [], flops_of(1, 1 << 20), after=after)[0]


def packed_small(acc, flipped, dgains_s, dgains_e, dgain_d):
    dist, width = acc.shape[2] + 128, dgain_d.shape[1]

    def kernel(acc_h, bucket_r, ds0_r, ds1_r, de0_r, de1_r, dd_r, out_h, acc_v, diag_v, out_v, sems):
        section = lax.axis_index("section")
        side = section // 2
        out_v[...] = jnp.zeros_like(out_v)

        @pl.when(section % 2 == 0)
        def _():
            loads = copy_all(sems, 0, (acc_h, acc_v))
            diag_v[...] = jnp.zeros_like(diag_v)
            wait_all(loads)
            fold_diagonals(acc_v, diag_v)
            ids = lax.broadcasted_iota(jnp.int32, (32, dist), 0)
            onehot = (ids == bucket_r[pl.ds(side, 1), :]).astype(F32)
            part = lax.dot_general(
                diag_v[...], onehot, (((1,), (1,)), ((), ())),
                precision=lax.Precision.HIGHEST, preferred_element_type=F32,
            )
            for own in range(2):
                @pl.when(side == own)
                def _():
                    out_v[3 * own : 3 * own + 1, :] = ds0_r[...] + ds1_r[...]
                    out_v[8:16, 256 * own : 256 * own + 32] = part[:8]
                    out_v[8:16, 256 * own + 128 : 256 * own + 160] = part[8:]

        @pl.when(section == 1)
        def _():
            out_v[1:3, :] = de0_r[...] + de1_r[...]

        @pl.when(side == 1)
        def _():
            out_v[4:7, :] = dd_r[...]

        wait_all(copy_all(sems, 1, (out_v, out_h)))

    return job(
        kernel,
        [acc],
        [flipped, *dgains_s, *dgains_e, dgain_d],
        [shape((16, width), F32)],
        [
            pltpu.VMEM(acc.shape, F32),
            pltpu.VMEM((16, dist), F32),
            pltpu.VMEM((16, width), F32),
            pltpu.SemaphoreType.DMA((2,)),
        ],
        result=lambda made: made[0],
    )


def self_backward(row, sections, ins, mats, gains, segs, toe, g_enc, g_dec, kept, passed, after):
    length, width = segs.shape[1], ins.shape[1]
    dist = 2 * length

    def kernel(x_h, w_h, toe_h, ge_h, gd_h, qkv_h, mix_h, lse_h, gain_r, seg_r, out_h, acc_h, dgain_h, b_h,
               x_v, w_v, qkv_v, mix_v, lse_v, d_v, dm_v, dqkv_v, dn_v, gx_v, dgain_v,
               mask_v, toe_v, acc_v, s_v, dp_v, p_v, ds_v, sems):
        section = lax.axis_index("section")
        side = section // 2

        active = section == sections[0]
        for one in sections[1:]:
            active = active | (section == one)

        @pl.when(active)
        def _():
            loads = either_all(sems, 0, side == 0, ((ge_h, d_v), (gd_h, d_v)))
            loads += copy_all(
                sems, 1,
                (w_h.at[0, :, pl.ds(3 * width, width)], w_v.at[:, pl.ds(3 * width, width)]),
                (mix_h, mix_v),
                (lse_h, lse_v),
                (qkv_h, qkv_v),
                (toe_h, toe_v),
                (w_h.at[0, :, pl.ds(0, 3 * width)], w_v.at[:, pl.ds(0, 3 * width)]),
                (x_h.at[pl.ds(row * length, length)], x_v),
            )
            sums = copy_all(sems, 8, (acc_h, acc_v)) if row else []
            fill_mask(mask_v, seg_r[row : row + 1, :], True, jnp.where(side == 1, 0, 2 * length))
            if not row:
                acc_v[...] = jnp.zeros_like(acc_v)
            gain = gain_r[pl.ds(3 * side, 1), :]
            wait_all(loads[:2])
            stores = copy_all(sems, 9, (d_v, b_h.at[:, pl.ds(3 * width, width)]))
            rows_out(d_v, w_v, 3 * width, dm_v, False)
            wait_all(loads[2:6] + sums)
            attend_back(qkv_v, qkv_v, qkv_v, dm_v, mix_v, 0, width, 2 * width, mask_v, toe_v, lse_v,
                        dp_v, s_v, p_v, ds_v, dqkv_v, 0, acc_v)
            stores += copy_all(sems, 10, (dqkv_v, b_h.at[:, pl.ds(0, 3 * width)]), (acc_v, acc_h))
            wait_all(loads[6:])
            rows_out(dqkv_v, w_v, 0, dn_v, False)
            total = jnp.zeros((1, width), F32)
            for rows in row_chunks(length):
                dx, dgain = rms_back(x_v[rows, :].astype(F32), gain, dn_v[rows, :])
                gx_v[rows, :] = d_v[rows, :].astype(F32) + dx
                total = total + dgain
            dgain_v[...] = total
            stores += copy_all(sems, 12, (gx_v, out_h.at[pl.ds(row * length, length)]), (dgain_v, dgain_h))
            wait_all(stores)

    n, qkv, mix, lse = kept
    return call(
        kernel,
        [ins, mats, toe, g_enc, g_dec, qkv, mix, lse],
        [gains, segs],
        [like(toe), shape((1, width), F32), shape((length, 4 * width), BF16)][len(passed) - 1 :],
        [
            pltpu.VMEM((length, width), BF16),
            pltpu.VMEM((width, 4 * width), BF16),
            pltpu.VMEM((length, 3 * width), BF16),
            pltpu.VMEM((length, width), BF16),
            pltpu.VMEM((16, length), F32),
            pltpu.VMEM((length, width), BF16),
            pltpu.VMEM((length, width), BF16),
            pltpu.VMEM((length, 3 * width), BF16),
            pltpu.VMEM((length, width), F32),
            pltpu.VMEM((length, width), F32),
            pltpu.VMEM((1, width), F32),
            pltpu.VMEM((length, length), F32),
            pltpu.VMEM((H, 128, dist - 128), F32),
            pltpu.VMEM((H, 128, dist - 128), F32),
            pltpu.VMEM((2, length, length), F32),
            pltpu.VMEM((2, length, length), F32),
            pltpu.VMEM((2, length, length), BF16),
            pltpu.VMEM((2, length, length), BF16),
            pltpu.SemaphoreType.DMA((14,)),
        ],
        flops_of(6, 16 << 20),
        passed,
        after,
    )


def encoder_forward(row, e1, mats, gains, out_rows):
    length, width = e1.shape
    hidden = mats.shape[2]
    narrow, wide = shape((length, width), BF16), shape((length, hidden), BF16)
    rows_shape = shape((2 * length, width), F32)
    kept = [narrow, shape((length, width), F32), narrow, wide, wide]

    def kernel(e_h, w_h, gain_r, out_h, send_h, mid_h, n_h, h_h, slope_h,
               e_v, win_v, wout_v, n_v, h_v, slope_v, mid_v, out_v, send_v, sems):
        @pl.when(lax.axis_index("section") == 1)
        def _():
            loads = copy_all(sems, 0, (e_h, e_v))
            win_loads = column_parts(sems, 9, w_h.at[0], win_v)
            loads += copy_all(sems, 1, (w_h.at[1], wout_v))
            loads[0].wait()
            for rows in row_chunks(length):
                x = e_v[rows, :].astype(F32)
                mid_v[rows, :] = x
                n_v[rows, :] = (x * inverse_rms(x) * gain_r[1:2, :]).astype(BF16)
            stores = copy_all(sems, 3, (n_v, n_h))
            ffn_up(n_v, win_v, h_v, slope_v, win_loads)
            stores += copy_all(sems, 4, (h_v, h_h), (slope_v, slope_h))
            loads[1].wait()
            rows_out(h_v, wout_v, 0, mid_v, True)
            stores += copy_all(sems, 8, (mid_v, mid_h))
            for n, rows in enumerate(row_chunks(length)):
                x = mid_v[rows, :]
                y = x * inverse_rms(x) * gain_r[2:3, :]
                out_v[rows, :] = y
                send_v[rows, :] = y.astype(BF16)
                target = pl.ds(row * length + n * ROW_STEP, ROW_STEP)
                stores += copy_all(
                    sems, 12 + 2 * n, (send_v.at[rows], send_h.at[rows]), (out_v.at[rows], out_h.at[target])
                )
            wait_all(stores)

    return call(
        kernel,
        [e1, mats],
        [gains],
        kept if row else [rows_shape] + kept,
        [
            pltpu.VMEM((length, width), BF16),
            pltpu.VMEM((width, hidden), BF16),
            pltpu.VMEM((width, hidden), BF16),
            pltpu.VMEM((length, width), BF16),
            pltpu.VMEM((length, hidden), BF16),
            pltpu.VMEM((length, hidden), BF16),
            pltpu.VMEM((length, width), F32),
            pltpu.VMEM((length, width), F32),
            pltpu.VMEM((length, width), BF16),
            pltpu.SemaphoreType.DMA((20,)),
        ],
        flops_of(2, 20 << 20),
        [out_rows] if row else [],
    )


def encoder_backward(row, ins, extra, e1, mid, slope, mats, gains, after):
    length, width = extra.shape
    hidden = mats.shape[2]

    def kernel(cot_h, extra_h, e_h, mid_h, slope_h, w_h, gain_r, g_h, d_h, du_h, dgain_h,
               cot_v, extra_v, e_v, mid_v, slope_v, win_v, wout_v, d_v, du_v, dn_v, gm_v, g_v, dgain_v, sems):
        @pl.when(lax.axis_index("section") == 1)
        def _():
            loads = copy_all(
                sems, 0,
                (cot_h.at[pl.ds(row * length, length)], cot_v), (extra_h, extra_v), (mid_h, mid_v),
                (w_h.at[1], wout_v), (slope_h, slope_v), (w_h.at[0], win_v), (e_h, e_v),
            )
            wait_all(loads[:3])
            total = jnp.zeros((1, width), F32)
            for rows in row_chunks(length):
                dy = cot_v[rows, :].astype(F32) + extra_v[rows, :].astype(F32)
                dx, dgain = rms_back(mid_v[rows, :], gain_r[2:3, :], dy)
                gm_v[rows, :] = dx
                d_v[rows, :] = dx.astype(BF16)
                total = total + dgain
            dgain_v[1:2, :] = total
            stores = copy_all(sems, 7, (d_v, d_h))
            wait_all(loads[3:5])
            ffn_down(d_v, wout_v, slope_v, du_v)
            stores += copy_all(sems, 8, (du_v, du_h))
            wait_all(loads[5:])
            rows_out(du_v, win_v, 0, dn_v, False)
            total = jnp.zeros((1, width), F32)
            for rows in row_chunks(length):
                dx, dgain = rms_back(e_v[rows, :].astype(F32), gain_r[1:2, :], dn_v[rows, :])
                g_v[rows, :] = (gm_v[rows, :] + dx).astype(BF16)
                total = total + dgain
            dgain_v[0:1, :] = total
            stores += copy_all(sems, 9, (g_v, g_h), (dgain_v, dgain_h))
            wait_all(stores)

    return call(
        kernel,
        [ins, extra, e1, mid, slope, mats],
        [gains],
        [
            shape((length, width), BF16),
            shape((length, width), BF16),
            shape((length, hidden), BF16),
            shape((2, width), F32),
        ],
        [
            pltpu.VMEM((length, width), BF16),
            pltpu.VMEM((length, width), BF16),
            pltpu.VMEM((length, width), BF16),
            pltpu.VMEM((length, width), F32),
            pltpu.VMEM((length, hidden), BF16),
            pltpu.VMEM((width, hidden), BF16),
            pltpu.VMEM((width, hidden), BF16),
            pltpu.VMEM((length, width), BF16),
            pltpu.VMEM((length, hidden), BF16),
            pltpu.VMEM((length, width), F32),
            pltpu.VMEM((length, width), F32),
            pltpu.VMEM((length, width), BF16),
            pltpu.VMEM((2, width), F32),
            pltpu.SemaphoreType.DMA((11,)),
        ],
        flops_of(2, 20 << 20),
        after=after,
    )


def decoder(d_own, d_got, m_two, m_three, ins, cot_got, mats, got_mats, gains, segs, passed, after):
    length, width = d_own.shape
    hidden = mats.shape[2]

    def kernel(d2_h, d3_h, m2_h, m3_h, c1_h, c0_h, w1_h, w0_h, gain_r, seg_r,
               out_h, fa_h, fb_h, other_h, gm_h, gd_h, dgain_h,
               d_v, m_v, c_v, wca_v, win_v, wout_v, n_v, q_v, mix_v, lse_v, mask_v, s_v, p_v, h_v, slope_v,
               x_v, y_v, dn_v, n5_v, do_v, dgain_v, dp_v, ds_v, dq_v, dm_v, do4_v, gm_v, gd_v, out_v, sems):
        section = lax.axis_index("section")

        @pl.when(section >= 2)
        def _():
            own = section == 3
            second = pl.ds(length, length)

            def put(first, *choices):
                return either_all(sems, first, own, *choices)

            quarters = [pl.ds(c * width, width) for c in range(4)]
            loads = put(0, ((d3_h, d_v), (d2_h, d_v)))
            cross_loads = put(
                21, *[((w1_h.at[0, :, cut], wca_v.at[:, cut]), (w0_h.at[0, :, cut], wca_v.at[:, cut])) for cut in quarters]
            )
            loads += put(
                1,
                ((m3_h, m_v), (m2_h, m_v)),
                *[((w1_h.at[k], v), (w0_h.at[k], v)) for k, v in ((1, win_v), (2, wout_v))],
                ((c1_h.at[second], c_v), (c0_h, c_v)),
            )
            fill_mask(mask_v, seg_r[pl.ds(section - 2, 1), :], False, 2 * length)
            loads[0].wait()
            for rows in row_chunks(length):
                x = d_v[rows, :].astype(F32)
                x_v[rows, :] = x
                n_v[rows, :] = (x * inverse_rms(x) * gain_r[4:5, :]).astype(BF16)
            late = lambda n, count=1: fb_h.at[:, pl.ds(n * width, count * width)]
            stores = copy_all(sems, 6, (n_v, late(5)))
            cross_loads[0].wait()
            project(n_v, wca_v, 0, q_v, 0, width)
            loads[1].wait()
            stores += copy_all(sems, 7, (m_v, late(6)))
            wait_all(cross_loads[1:3])
            project(m_v, wca_v, width, q_v, width, 2 * width)
            attend(q_v, q_v, q_v, 0, width, 2 * width, mask_v, None, s_v, p_v, mix_v, lse_v)
            stores += copy_all(sems, 9, (mix_v, late(7)))

            cross_loads[3].wait()

            @pl.loop(0, width // 256)
            def _(t):
                cols = pl.ds(pl.multiple_of(t * 256, 256), 256)
                part = mm(mix_v[...], wca_v[:, pl.ds(pl.multiple_of(3 * width + t * 256, 256), 256)])
                x_v[:, cols] = x_v[:, cols] + part

            for rows in row_chunks(length):
                x = x_v[rows, :]
                y_v[rows, :] = x
                n5_v[rows, :] = (x * inverse_rms(x) * gain_r[5:6, :]).astype(BF16)
            stores += copy_all(sems, 10, (n5_v, fa_h.at[:, pl.ds(0, width)]))
            loads[2].wait()
            ffn_up(n5_v, win_v, h_v, slope_v)
            stores += copy_all(sems, 11, (h_v, late(1, 4)))
            loads[3].wait()
            rows_out(h_v, wout_v, 0, y_v, True)
            loads[4].wait()
            total = jnp.zeros((1, width), F32)
            for rows in row_chunks(length):
                y = y_v[rows, :]
                out_v[rows, :] = y * inverse_rms(y) * gain_r[6:7, :]
                dy, dgain = rms_back(y, gain_r[6:7, :], c_v[rows, :].astype(F32))
                total = total + dgain
                do_v[rows, :] = dy.astype(BF16)
                y_v[rows, :] = dy
            dgain_v[2:3, :] = total
            stores += put(12, ((out_v, out_h.at[second]), (out_v, other_h)))
            stores += copy_all(sems, 13, (do_v, late(0)))
            ffn_down(do_v, wout_v, slope_v, slope_v)
            stores += copy_all(sems, 14, (slope_v, fa_h.at[:, pl.ds(width, 4 * width)]))
            rows_out(slope_v, win_v, 0, dn_v, False)
            total = jnp.zeros((1, width), F32)
            for rows in row_chunks(length):
                dx, dgain = rms_back(x_v[rows, :], gain_r[5:6, :], dn_v[rows, :])
                dx = y_v[rows, :] + dx
                y_v[rows, :] = dx
                do4_v[rows, :] = dx.astype(BF16)
                total = total + dgain
            dgain_v[1:2, :] = total
            stores += copy_all(sems, 15, (do4_v, late(11)))
            rows_out(do4_v, wca_v, 3 * width, dm_v, False)
            attend_back(q_v, q_v, q_v, dm_v, mix_v, 0, width, 2 * width, mask_v, None, lse_v,
                        dp_v, s_v, p_v, ds_v, dq_v, 0, None)
            stores += copy_all(sems, 16, (dq_v, late(8, 3)))
            rows_out(dq_v.at[:, width:], wca_v, width, gm_v, False)
            stores += copy_all(sems, 18, (gm_v, gm_h))
            rows_out(dq_v.at[:, :width], wca_v, 0, dn_v, False)
            total = jnp.zeros((1, width), F32)
            for rows in row_chunks(length):
                dx, dgain = rms_back(d_v[rows, :].astype(F32), gain_r[4:5, :], dn_v[rows, :])
                gd_v[rows, :] = (y_v[rows, :] + dx).astype(BF16)
                total = total + dgain
            dgain_v[0:1, :] = total
            stores += copy_all(sems, 19, (gd_v, gd_h), (dgain_v, dgain_h))
            wait_all(stores)

    narrow = shape((length, width), BF16)
    return call(
        kernel,
        [d_own, d_got, m_two, m_three, ins, cot_got, mats, got_mats],
        [gains, segs],
        [
            shape((length, 5 * width), BF16),
            shape((length, 12 * width), BF16),
            shape((length, width), F32),
            *(narrow, narrow),
            shape((3, width), F32),
        ],
        [
            pltpu.VMEM((length, width), BF16),
            pltpu.VMEM((length, width), BF16),
            pltpu.VMEM((length, width), BF16),
            pltpu.VMEM((width, 4 * width), BF16),
            pltpu.VMEM((width, hidden), BF16),
            pltpu.VMEM((width, hidden), BF16),
            pltpu.VMEM((length, width), BF16),
            pltpu.VMEM((length, 3 * width), BF16),
            pltpu.VMEM((length, width), BF16),
            pltpu.VMEM((16, length), F32),
            pltpu.VMEM((length, length), F32),
            pltpu.VMEM((2, length, length), F32),
            pltpu.VMEM((2, length, length), BF16),
            pltpu.VMEM((length, hidden), BF16),
            pltpu.VMEM((length, hidden), BF16),
            pltpu.VMEM((length, width), F32),
            pltpu.VMEM((length, width), F32),
            pltpu.VMEM((length, width), F32),
            pltpu.VMEM((length, width), BF16),
            pltpu.VMEM((length, width), BF16),
            pltpu.VMEM((3, width), F32),
            pltpu.VMEM((2, length, length), F32),
            pltpu.VMEM((2, length, length), BF16),
            pltpu.VMEM((length, 3 * width), BF16),
            pltpu.VMEM((length, width), BF16),
            pltpu.VMEM((length, width), BF16),
            pltpu.VMEM((length, width), BF16),
            pltpu.VMEM((length, width), BF16),
            pltpu.VMEM((length, width), F32),
            pltpu.SemaphoreType.DMA((25,)),
        ],
        flops_of(12, 30 << 20),
        passed,
        after,
    )


def weight_grad(sections, groups, chunks, ndp, decoder=None, passed=()):
    length, width = groups[0][0][0][0].shape[0], 768
    columns = sum(group[2] for group in groups)
    pieces = len(groups[0][0])
    bits = ndp.bit_length() - 1
    block = width // ndp
    flat = []
    for a_list, b_list, _ in groups + (decoder or []):
        for array, _ in a_list + b_list:
            if not any(array is other for other in flat):
                flat.append(array)
    place = lambda array: [index for index, other in enumerate(flat) if other is array][0]
    plan_of = lambda groups: [
        ([(place(a), a0) for a, a0 in a_list], [(place(b), b0) for b, b0 in b_list], count)
        for a_list, b_list, count in groups
    ]
    plan, other_plan = plan_of(groups), plan_of(decoder or groups)
    tile = 768
    copies = 2 * pieces * len(groups)

    def kernel(*args):
        sources = args[: len(flat)]
        outs = args[len(flat) : len(flat) + 2 * len(chunks)]
        a_v, at_v, b_v, out_v, sems = args[len(flat) + 2 * len(chunks) :]
        me = lax.axis_index("dp")
        section = lax.axis_index("section")
        active = section == sections[0]
        for one in sections[1:]:
            active = active | (section == one)

        @pl.when(active)
        def _():
            loads, start = [], 0
            for g, (a_list, b_list, count) in enumerate(plan):
                group_loads = []
                for k in range(pieces):
                    rows = pl.ds(k * length, length)
                    choices = []
                    for a_of, b_of, _ in (other_plan[g], plan[g]):
                        (ai, a0), (bi, b0) = a_of[k], b_of[k]
                        choices.append((
                            (sources[ai].at[:, pl.ds(a0, width)], a_v.at[g, rows]),
                            (sources[bi].at[:, pl.ds(b0, count)], b_v.at[rows, pl.ds(start, count)]),
                        ))
                    first = 2 * (g * pieces + k)
                    if decoder:
                        group_loads += either_all(sems, first, section >= 2, *zip(*choices))
                    else:
                        group_loads += copy_all(sems, first, *choices[0])
                loads.append(group_loads)
                start += count
            stores, group, group_end, start = [], -1, 0, 0
            for number, (count, order) in enumerate(chunks):
                spots = []
                for b in range(ndp):
                    code = jnp.bitwise_xor(me, b)
                    spot = 0
                    for k in range(bits):
                        spot = spot + ((code >> order[k]) & 1) * (1 << (bits - 1 - k))
                    spots.append(spot)
                done, end = start, start + count
                while done < end:
                    if done == group_end:
                        group += 1
                        wait_all(loads[group])
                        at_v[...] = a_v[group].T
                        group_end += plan[group][2]
                    upto = min(end, group_end)

                    @pl.loop(0, (upto - done) // tile)
                    def _(t):
                        cols = pl.ds(pl.multiple_of(done + t * tile, 128), tile)
                        part = mm(at_v[...], b_v[:, cols])
                        for b in range(ndp):
                            out_v[spots[b], :, cols] = part[b * block : (b + 1) * block, :].astype(BF16)

                    done = upto
                for half in range(2):
                    source = out_v.at[pl.ds(half * (ndp // 2), ndp // 2), :, pl.ds(start, count)]
                    stores += copy_all(sems, copies + 2 * number + half, (source, outs[2 * number + half]))
                start = end
            wait_all(stores)

    return job(
        kernel,
        flat,
        [],
        [] if passed else [shape((ndp // 2, block, count), BF16) for count, _ in chunks for _ in range(2)],
        [
            pltpu.VMEM((len(groups), pieces * length, width), BF16),
            pltpu.VMEM((width, pieces * length), BF16),
            pltpu.VMEM((pieces * length, columns), BF16),
            pltpu.VMEM((ndp, block, columns), BF16),
            pltpu.SemaphoreType.DMA((copies + 2 * len(chunks),)),
        ],
        passed=passed,
        result=lambda made: [(made[2 * number], made[2 * number + 1]) for number in range(len(chunks))],
    )


def along_dp(value, bit, sections, ndp):
    pairs = [(s * ndp + d, s * ndp + (d ^ bit)) for s in sections for d in range(ndp)]
    return lax.ppermute(value, ("section", "dp"), pairs)


def added(items):
    outs, kinds = [], []
    for keep, _, _ in items:
        kind = "sum" if keep.dtype == F32 else "last" if keep.shape[0] == 1 else "half"
        kinds.append(kind)
        if kind == "half":
            outs += [shape((keep.shape[0] // 2,) + keep.shape[1:], BF16)] * 2
        else:
            outs.append(shape(keep.shape if kind == "sum" else keep.shape[1:], F32))

    def kernel(*refs):
        count = len(items)
        sources, rest = refs[: 2 * count], refs[2 * count :]
        targets, rest = rest[: len(outs)], rest[len(outs) :]
        scratch, sems = rest[:-1], rest[-1]
        section = lax.axis_index("section")

        def takes_part(sections):
            active = section == sections[0]
            for one in sections[1:]:
                active = active | (section == one)
            return active

        for number, item in enumerate(items):
            @pl.when(takes_part(item[2]))
            def _():
                for k in range(2):
                    pltpu.make_async_copy(
                        sources[2 * number + k], scratch[3 * number + k], sems.at[4 * number + k]
                    ).start()

        place = 0
        for number, (item, kind) in enumerate(zip(items, kinds)):
            n = item[0].shape[0]
            keep_v, got_v, out_v = scratch[3 * number : 3 * number + 3]
            mine = targets[place : place + (2 if kind == "half" else 1)]
            place += len(mine)

            @pl.when(takes_part(item[2]))
            def _():
                for k, v in enumerate((keep_v, got_v)):
                    pltpu.make_async_copy(sources[2 * number + k], v, sems.at[4 * number + k]).wait()
                if kind == "half":
                    @pl.loop(0, n)
                    def _(i):
                        out_v[i] = (keep_v[i].astype(F32) + got_v[i].astype(F32)).astype(BF16)

                    wait_all(
                        copy_all(
                            sems, 4 * number + 2,
                            (out_v.at[pl.ds(0, n // 2)], mine[0]), (out_v.at[pl.ds(n // 2, n // 2)], mine[1]),
                        )
                    )
                else:
                    if kind == "last":
                        out_v[...] = keep_v[0].astype(F32) + got_v[0].astype(F32)
                    else:
                        out_v[...] = keep_v[...] + got_v[...]
                    wait_all(copy_all(sems, 4 * number + 2, (out_v, mine[0])))

    scratch = []
    for (keep, _, _), kind in zip(items, kinds):
        own = pltpu.VMEM(keep.shape, keep.dtype)
        scratch += [own, own, pltpu.VMEM(keep.shape[1:], F32) if kind == "last" else own]
    def result(made):
        results = []
        for kind in kinds:
            size = 2 if kind == "half" else 1
            results.append(tuple(made[:size]) if size == 2 else made[0])
            made = made[size:]
        return results

    return job(
        kernel,
        [array for keep, got, _ in items for array in (keep, got)],
        [],
        outs,
        scratch + [pltpu.SemaphoreType.DMA((4 * len(items),))],
        result=result,
    )


def joined(v, pieces):
    start = 0
    for piece in pieces:
        yield piece, v.at[:, pl.ds(start, piece.shape[1])]
        start += piece.shape[1]


def outputs(one, two, three, rows_got, out_rows, after):
    length, width = rows_got.shape
    block, columns = two.shape

    def kernel(a_h, b_h, s_h, c_h, r_h, out_h, grad_h, f_v, s_v, c_v, r_v, sems):
        section = lax.axis_index("section")
        even = section % 2 == 0
        loads = copy_all(sems, 0, *joined(f_v, (a_h, b_h)))

        @pl.when(section == 3)
        def _():
            wait_all(copy_all(sems, 2, (s_h, s_v), (c_h, c_v), (r_h, r_v)))
            wait_all(loads)
            wait_all(
                copy_all(
                    sems, 5,
                    (f_v, grad_h.at[1]), (s_v, grad_h.at[2]), (c_v, grad_h.at[0]), (r_v, out_h.at[pl.ds(0, length)]),
                )
            )

        @pl.when(section != 3)
        def _():
            c_v[...] = jnp.zeros_like(c_v)
            stores = copy_all(sems, 5, (c_v, grad_h.at[2]))

            @pl.when(section == 1)
            def _():
                wait_all(copy_all(sems, 2, (s_h, s_v)))
                wait_all(copy_all(sems, 3, (s_v, grad_h.at[1])))

            @pl.when(even)
            def _():
                wait_all(copy_all(sems, 3, (c_v, grad_h.at[1])))

            wait_all(loads)
            wait_all(stores + copy_all(sems, 6, (f_v, grad_h.at[0])))

    return call(
        kernel,
        [*one, two, three, rows_got],
        [],
        [shape((3, block, columns), F32)],
        [pltpu.VMEM((block, columns), F32)] * 3 + [pltpu.VMEM((length, width), F32), pltpu.SemaphoreType.DMA((9,))],
        flops_of(1, 1 << 20),
        [out_rows],
        after,
    )


def per_device(section_ins, segments, buckets, section_mats, gains, tables):
    ndp = lax.axis_size("dp")
    ins = section_ins[0]
    mats = section_mats[0]
    length = segments.shape[1]
    width = ins.shape[1]
    segs = segments
    flipped = jnp.pad(buckets[:, ::-1], ((0, 0), (0, 1)), constant_values=-1)
    everywhere = (0, 1, 2, 3)
    move = lambda value, pairs: lax.ppermute(value, "section", pairs)

    *fwd0, tiles = self_forward(0, ins, mats, gains, segs, tables, buckets)
    late_mats, _ = lax.optimization_barrier((section_mats, fwd0[0]))
    got_mats = move(late_mats, [(3, 2)])[0]
    first0 = move(fwd0[0], [(0, 1)])
    fwd1 = self_forward(1, ins, mats, gains, segs, tables, buckets, tiles)
    first1 = move(fwd1[0], [(0, 1), (2, 3)])
    toe = transposed_bias(tables, flipped, length, [fwd1[0]])
    out_rows, *enc0 = encoder_forward(0, first0, mats, gains, None)
    m_two = move(enc0[0], [(1, 2)])
    late_ins, _ = lax.optimization_barrier((ins, fwd1[0]))
    cot_got = move(late_ins[:length], [(3, 2)])
    out_rows, *enc1 = encoder_forward(1, first1, mats, gains, out_rows)
    m_three = move(enc1[0], [(1, 3)])
    here = marker([enc1[0], m_two])

    dec = decoder(fwd0[0], first1, m_two, m_three, ins, cot_got, mats, got_mats, gains, segs, [out_rows], [toe, here])
    out_rows, first_d, later_d, other, g_mem, g_self, dgain_d = dec
    even, odd = (0, 2), (1, 3)
    extra0 = move(g_mem, [(2, 1)])
    extra1 = move(g_mem, [(3, 0)])
    (first_sent, later_sent, g_self_sent), _ = lax.optimization_barrier(((first_d, later_d, g_self), extra0))
    first_got = move(first_sent, [(2, 3)])
    g_self_got = move(g_self_sent, [(3, 2)])
    later_got = move(later_sent, [(2, 3)])
    back0 = encoder_backward(0, ins, extra0, first0, enc0[1], enc0[4], mats, gains, [extra1])
    g0 = move(back0[0], [(1, 0)])
    (other, extra1), _ = lax.optimization_barrier(((other, extra1), back0[0]))
    extra1 = move(extra1, [(0, 1)])
    own0 = self_backward(
        0, even, ins, mats, gains, segs, toe, g0, g_self, fwd0[1:], [out_rows], [extra1]
    )
    out_rows, acc = own0[:2]
    back1 = encoder_backward(1, ins, extra1, first1, enc1[1], enc1[4], mats, gains, [acc])
    g1 = move(back1[0], [(1, 0)])
    other, _ = lax.optimization_barrier((other, back1[0]))
    rows_got = move(other, [(2, 3)])

    plain = tuple(range(ndp.bit_length() - 1))
    turned = (1, 0) + plain[2:]
    orders = (plain, turned)
    steps = len(plain)
    whole = 4 * width
    rows_of = lambda own, got, at: [(own, at * width), (got, at * width)]
    first_of, later_of = partial(rows_of, first_d, first_got), partial(rows_of, later_d, later_got)
    halves = [(2 * width, order) for order in orders]
    groups = [([(enc0[2], 0), (enc1[2], 0)], [(back0[2], 0), (back1[2], 0)], whole)]
    groups_d = [(first_of(0), first_of(1), whole)]
    made, = run([weight_grad(odd, groups, halves, ndp, groups_d)], [back1[0]])
    own1 = self_backward(
        1, even, ins, mats, gains, segs, toe, g1, g_self_got, fwd1[1:], [out_rows, acc], [made[0][0]]
    )
    out_rows, acc = own1[:2]
    groups = [
        ([(fwd0[1], 0), (fwd1[1], 0)], [(own0[3], 0), (own1[3], 0)], 3 * width),
        ([(fwd0[3], 0), (fwd1[3], 0)], [(own0[3], 3 * width), (own1[3], 3 * width)], width),
    ]
    made, = run([weight_grad(even, groups, halves, ndp, passed=[*made[0], *made[1]])], [out_rows])

    def send(pair, order, step, sections):
        return (pair[0], along_dp(pair[1], 1 << order[step], sections, ndp), sections)

    def send_one(pairs, step):
        return [send(pair, order, step, everywhere) for pair, order in zip(pairs, orders)]

    def send_rest(pair, part, step):
        return send(pair, *((turned, step, odd) if part == 1 else (plain, step, (3,))))

    one = send_one(made, 0)
    groups = [([(back0[1], 0), (back1[1], 0)], [(enc0[3], 0), (enc1[3], 0)], whole)]
    groups_d = [(later_of(0), later_of(1), whole)]
    (two,), = run([weight_grad(odd, groups, [(whole, turned)], ndp, groups_d)], [made[0][0]])
    groups = [(later_of(5 + k), later_of(at), count * width) for k, at, count in ((0, 8, 1), (1, 9, 2), (2, 11, 1))]
    (three,), = run([weight_grad((3,), groups, [(whole, plain)], ndp)], [two[0]])
    rest = [send_rest(two, 1, 0), send_rest(three, 2, 0)]
    dgains = ([own0[2], own1[2]], [back0[3], back1[3]], dgain_d)
    small, = run([packed_small(acc, flipped, *dgains)], [three[0]])
    small_steps = [partial(along_dp, bit=1 << k, sections=everywhere, ndp=ndp) for k in range(steps)]
    small_steps += [lambda value: move(value, [(0, 1), (1, 0), (2, 3), (3, 2)])]
    small_steps += [lambda value: move(value, [(0, 2), (2, 0), (1, 3), (3, 1)])]
    small_got = small_steps.pop(0)(small)
    tied = [small]
    for k in range(steps):
        for part, items in enumerate((one, rest[:1], rest[1:])):
            cost = SHORT if part < 2 and k + 1 < steps else None if part == 2 else LONG
            if small_got is None or part == 2:
                sums, = run([added(items)], tied, cost)
            else:
                (*sums, small), = run([added([*items, (small, small_got, everywhere)])], tied, cost)
                small_got = small_steps.pop(0)(small) if small_steps else None
            if k + 1 == steps:
                tied = [sums[0]]
            else:
                tied = [sums[0][0]]
                sums = send_one(sums, k + 1) if not part else [send_rest(sums[0], part, k + 1)]
            if part:
                rest[part - 1] = sums[0]
            else:
                one = sums
    out_rows, grad = outputs(one, *rest, rows_got, out_rows, tied)

    gains_grad = small[: gains.shape[0]]
    heads = [
        jnp.concatenate([small[8:16, at : at + 32], small[8:12, at + 128 : at + 160]], axis=0)
        for at in range(0, 256 * tables.shape[0], 256)
    ]
    return out_rows[None], grad[None], gains_grad, jnp.swapaxes(jnp.stack(heads), 1, 2)


def solution(mesh):
    placed = (
        P("section", "dp", None),
        P("dp", None),
        P(),
        P("section", None, None, None),
        P(),
        P(),
    )
    return jax.shard_map(
        per_device,
        mesh=mesh,
        in_specs=placed,
        out_specs=(P("section", "dp", None), P("section", None, "dp", None), P(), P()),
        check_vma=False,
    )
```

```python
from functools import partial

import jax
import jax.numpy as jnp
from jax import lax
from jax.experimental import pallas as pl
from jax.experimental.pallas import tpu as pltpu
from jax.sharding import PartitionSpec as P

H = 12
HD = 64
PAIRS = H // 2
EPS = 1e-06
GELU = 0.7978845608028654
CUBIC = 0.044715
MASKED = -1e38
F32 = jnp.float32
BF16 = jnp.bfloat16
ROW_STEP = 128
VMEM_LIMIT = 60 * 1024 * 1024


def mm(a, b):
    return jnp.dot(a, b, preferred_element_type=F32)


def mm_nt(a, b):
    return lax.dot_general(a, b, (((1,), (1,)), ((), ())), preferred_element_type=F32)


def inverse_rms(x):
    return lax.rsqrt(jnp.mean(x * x, axis=-1, keepdims=True) + EPS)


def row_chunks(length):
    return [pl.ds(start, ROW_STEP) for start in range(0, length, ROW_STEP)]


def rms_back(x, gain, dy):
    r = inverse_rms(x)
    inner = jnp.mean(dy * gain * x, axis=-1, keepdims=True)
    dx = r * gain * dy - x * (r * r * r) * inner
    return dx, jnp.sum(dy * x * r, axis=0, keepdims=True)


def copy_all(sems, first, *pairs):
    started = []
    for offset, (source, target) in enumerate(pairs):
        one = pltpu.make_async_copy(source, target, sems.at[first + offset])
        one.start()
        started.append(one)
    return started


class Either:
    def __init__(self, sem, flag, yes, no):
        self.done = pltpu.make_async_copy(*yes, sem)

        @pl.when(flag)
        def _():
            pltpu.make_async_copy(*yes, sem).start()

        @pl.when(jnp.logical_not(flag))
        def _():
            pltpu.make_async_copy(*no, sem).start()

    def wait(self):
        self.done.wait()


def either_all(sems, first, flag, *choices):
    return [Either(sems.at[first + offset], flag, *choice) for offset, choice in enumerate(choices)]


def wait_all(started):
    for one in started:
        one.wait()


def head_lanes(second):
    lane = lax.broadcasted_iota(jnp.int32, (1, 2 * HD), 1)
    return (lane >= HD) if second else (lane < HD)


def fill_mask(mask_v, seg_row, transposed, slack):
    length = seg_row.shape[1]
    down = jnp.broadcast_to(seg_row, (128, length)).T
    for c in range(length // 128):
        along = seg_row[:, c * 128 : (c + 1) * 128]
        r = lax.broadcasted_iota(jnp.int32, (length, 128), 0)
        q = lax.broadcasted_iota(jnp.int32, (length, 128), 1) + c * 128
        key, query = (r, q) if transposed else (q, r)
        ok = (down == along) & (key <= query + slack)
        mask_v[:, c * 128 : (c + 1) * 128] = jnp.where(ok, 0.0, MASKED)


def fill_toeplitz(toe_v, vec_v, table, bucket_row):
    count = bucket_row.shape[1]
    ids = lax.broadcasted_iota(jnp.int32, (table.shape[0], count), 0)
    onehot = (ids == bucket_row).astype(F32)
    vec = lax.dot_general(
        table, onehot, (((0,), (0,)), ((), ())), precision=lax.Precision.HIGHEST, preferred_element_type=F32
    )
    vec_v[:H, :count] = vec

    @pl.loop(0, H)
    def _(h):
        wide = jnp.broadcast_to(vec_v[pl.ds(h, 1), :], (128, vec_v.shape[1]))
        rolled = pltpu.roll(wide, vec_v.shape[1] - 127, 1, stride=1, stride_axis=0)
        toe_v[h] = rolled[:, : toe_v.shape[2]]


def pair_cols(base, hp):
    return pl.ds(pl.multiple_of(base + hp * 128, 128), 128)


def over_pairs(scores, rest):
    scores(0, 0)

    @pl.loop(0, PAIRS // 2)
    def _(i):
        scores(2 * i + 1, 1)
        rest(2 * i, 0)
        scores(jnp.minimum(2 * i + 2, PAIRS - 1), 0)
        rest(2 * i + 1, 1)


def attend_ahead(q_v, k_v, v_v, q0, k0, v0, mask_v, toe_v, s_v, p_v, mix_v, lse_v, top_v, total_v):
    length = mix_v.shape[0]
    low, high = head_lanes(False), head_lanes(True)
    lane = lax.broadcasted_iota(jnp.int32, (1, 2 * HD), 1)
    top_v[...] = jnp.zeros_like(top_v)
    total_v[...] = jnp.ones_like(total_v)

    def scores(hp, slot):
        q2, k2 = q_v[:, pair_cols(q0, hp)], k_v[:, pair_cols(k0, hp)]
        for a, mine in enumerate((low, high)):
            s_v[2 * slot + a] = mm_nt(jnp.where(mine, q2, jnp.zeros_like(q2)), k2)

    def rest(hp, slot):
        v2 = v_v[:, pair_cols(v0, hp)]
        outs, tops = [], []
        for a, mine in enumerate((low, high)):
            top = []
            for c in range(length // 128):
                rows = pl.ds(c * 128, 128)
                s = s_v[2 * slot + a, rows, :] + mask_v[rows, :]
                if toe_v is not None:
                    left = toe_v.shape[2] - length - c * 128
                    s = s + toe_v[2 * hp + a, :, left : left + length]
                m = jnp.max(s, axis=-1, keepdims=True)
                p_v[2 * slot + a, rows, :] = jnp.exp(s - m).astype(BF16)
                top.append(m)
            tops.append(jnp.concatenate(top, axis=0))
            outs.append(mm(p_v[2 * slot + a], jnp.where(mine, v2, jnp.ones_like(v2))))
        total = pltpu.roll(jnp.where(low, outs[1], outs[0]), HD, 1)
        mix_v[:, pair_cols(0, hp)] = (jnp.where(low, outs[0], outs[1]) / total).astype(BF16)
        first, second = lane == 2 * hp, lane == 2 * hp + 1
        top_v[...] = jnp.where(first, tops[0], jnp.where(second, tops[1], top_v[...]))
        total_v[...] = jnp.where(first, total[:, :1], jnp.where(second, total[:, HD : HD + 1], total_v[...]))

    over_pairs(scores, rest)
    lse_v[...] = (top_v[...] + jnp.log(total_v[...])).T[: lse_v.shape[0], :]


def attend(q_v, k_v, v_v, q0, k0, v0, mask_v, toe_v, s_v, p_v, mix_v, lse_v):
    length = mix_v.shape[0]

    @pl.loop(0, PAIRS)
    def _(hp):
        at = lambda base: pl.ds(pl.multiple_of(base + hp * 128, 128), 128)
        q2, k2, v2 = q_v[:, at(q0)], k_v[:, at(k0)], v_v[:, at(v0)]
        low = head_lanes(False)
        outs, tops = [], []
        for a in range(2):
            mine = head_lanes(a == 1)
            s_v[a] = mm_nt(jnp.where(mine, q2, jnp.zeros_like(q2)), k2)
            top = []
            for c in range(length // 128):
                rows = pl.ds(c * 128, 128)
                s = s_v[a, rows, :] + mask_v[rows, :]
                if toe_v is not None:
                    left = toe_v.shape[2] - length - c * 128
                    s = s + toe_v[2 * hp + a, :, left : left + length]
                m = jnp.max(s, axis=-1, keepdims=True)
                p_v[a, rows, :] = jnp.exp(s - m).astype(BF16)
                top.append(m)
            tops.append(jnp.concatenate(top, axis=0))
            outs.append(mm(p_v[a], jnp.where(mine, v2, jnp.ones_like(v2))))
        total = pltpu.roll(jnp.where(low, outs[1], outs[0]), HD, 1)
        mix_v[:, at(0)] = (jnp.where(low, outs[0], outs[1]) / total).astype(BF16)
        stat = (jnp.where(low, tops[0], tops[1]) + jnp.log(total)).T
        lse_v[pl.ds(2 * hp, 1), :] = stat[0:1, :]
        lse_v[pl.ds(2 * hp + 1, 1), :] = stat[HD : HD + 1, :]


def attend_back(q_v, k_v, v_v, dm_v, mix_v, q0, k0, v0, mask_v, toe_v, lse_v, dp_v, s_v, p_v, ds_v, out_v, o0, acc_v):
    length = mix_v.shape[0]

    @pl.loop(0, PAIRS)
    def _(hp):
        at = lambda base: pl.ds(pl.multiple_of(base + hp * 128, 128), 128)
        q2, k2, v2, dm2 = q_v[:, at(q0)], k_v[:, at(k0)], v_v[:, at(v0)], dm_v[:, at(0)]
        low = head_lanes(False)
        prod = (dm2.astype(F32) * mix_v[:, at(0)].astype(F32)).T
        k2t = k2.T
        dvs, dks, dqs = [], [], []
        for a in range(2):
            mine = head_lanes(a == 1)
            s_v[a] = mm_nt(jnp.where(mine, k2, jnp.zeros_like(k2)), q2)
            dp_v[a] = mm_nt(jnp.where(mine, v2, jnp.zeros_like(v2)), dm2)
            delta = jnp.sum(prod[a * HD : (a + 1) * HD, :], axis=0, keepdims=True)
            lse = lse_v[pl.ds(2 * hp + a, 1), :]
            for c in range(length // 128):
                rows = pl.ds(c * 128, 128)
                s = s_v[a, rows, :] + mask_v[rows, :]
                if toe_v is not None:
                    left = toe_v.shape[2] - length - c * 128
                    s = s + toe_v[2 * hp + a, :, left : left + length]
                p = jnp.exp(s - lse)
                p_v[a, rows, :] = p.astype(BF16)
                ds = p * (dp_v[a, rows, :] - delta)
                ds_v[a, rows, :] = ds.astype(BF16)
                if acc_v is not None:
                    acc_v[2 * hp + a, :, left : left + length] += ds
            dvs.append(mm(p_v[a], dm2))
            dks.append(mm(ds_v[a], q2))
            dqs.append(mm(k2t[a * HD : (a + 1) * HD, :], ds_v[a]))
        out_v[:, at(o0)] = jnp.concatenate(dqs, axis=0).T.astype(BF16)
        out_v[:, at(o0 + PAIRS * 128)] = jnp.where(low, dks[0], dks[1]).astype(BF16)
        out_v[:, at(o0 + 2 * PAIRS * 128)] = jnp.where(low, dvs[0], dvs[1]).astype(BF16)


def fold_diagonals(acc_v, diag_v):

    @pl.loop(0, H, unroll=3)
    def _(h):
        value = jnp.concatenate([acc_v[h], jnp.zeros((128, 128), F32)], axis=1)
        half = 64
        while half >= 1:
            value = pltpu.roll(value[:half], half, 1) + value[half:]
            half //= 2
        diag_v[pl.ds(h, 1), :] = value


def gelu_parts(u):
    square = u * u
    bend = u * (GELU + (GELU * CUBIC) * square)
    half = 0.5 + 0.5 * jnp.tanh(bend)
    hidden = u * half
    slope = half + 2.0 * hidden * (1.0 - half) * (GELU + (3.0 * GELU * CUBIC) * square)
    return hidden, slope


COLUMN_PARTS = 3


def column_parts(sems, first, source, target, parts=COLUMN_PARTS):
    width = target.shape[1] // parts
    cuts = [pl.ds(c * width, width) for c in range(parts)]
    return copy_all(sems, first, *[(source.at[:, cut], target.at[:, cut]) for cut in cuts])


def ffn_up(n_v, win_v, h_v, slope_v, loads=()):
    tile = 512

    @pl.loop(0, win_v.shape[1] // tile)
    def _(t):
        for part, load in enumerate(loads):
            pl.when(t == part * (win_v.shape[1] // tile // len(loads)))(load.wait)

        cols = pl.ds(pl.multiple_of(t * tile, tile), tile)
        hidden, slope = gelu_parts(mm(n_v[...], win_v[:, cols]))
        h_v[:, cols] = hidden.astype(BF16)
        slope_v[:, cols] = slope.astype(BF16)


def rows_out(a_v, w_v, w0, out_v, add):
    tile = 256
    depth = a_v.shape[1]

    @pl.loop(0, w_v.shape[0] // tile)
    def _(t):
        cols = pl.ds(pl.multiple_of(t * tile, tile), tile)
        part = mm_nt(a_v[...], w_v[cols, w0 : w0 + depth])
        if add:
            out_v[:, cols] = out_v[:, cols] + part
        else:
            out_v[:, cols] = part.astype(out_v.dtype)


def ffn_down(d_v, wout_v, slope_v, du_v):
    tile = 512

    @pl.loop(0, wout_v.shape[1] // tile)
    def _(t):
        cols = pl.ds(pl.multiple_of(t * tile, tile), tile)
        grad = mm(d_v[...], wout_v[:, cols])
        du_v[:, cols] = (grad * slope_v[:, cols].astype(F32)).astype(BF16)


def project(a_v, w_v, w0, out_v, o0, width):
    tile = 384

    @pl.loop(0, width // tile)
    def _(t):
        source = pl.ds(pl.multiple_of(w0 + t * tile, 128), tile)
        target = pl.ds(pl.multiple_of(o0 + t * tile, 128), tile)
        out_v[:, target] = mm(a_v[...], w_v[:, source]).astype(out_v.dtype)


def flops_of(matmuls, size):
    return pl.CostEstimate(flops=matmuls * 1000, bytes_accessed=size // 1000, transcendentals=0)


LONG = pl.CostEstimate(flops=60_000_000_000, bytes_accessed=60 << 20, transcendentals=0)

SHORT = pl.CostEstimate(flops=20_000_000_000, bytes_accessed=20 << 20, transcendentals=0)


def shape(dims, kind):
    return jax.ShapeDtypeStruct(dims, kind)


def like(array):
    return shape(array.shape, array.dtype)


def job(kernel, ins, small, outs, scratch, passed=(), result=lambda made: made):
    return dict(kernel=kernel, ins=ins, small=small, outs=outs, scratch=scratch, passed=passed, result=result)


def run(jobs, after=(), cost=None):
    every = lambda key: [array for one in jobs for array in one[key]]
    ins, small, passed, outs, scratch = map(every, ("ins", "small", "passed", "outs", "scratch"))
    space = lambda count, where: [pl.BlockSpec(memory_space=where)] * count

    def body(*refs):
        refs = list(refs)
        take = lambda count: [refs.pop(0) for _ in range(count)]
        held = {"ins": take(len(ins)), "small": take(len(small))}
        take(len(passed) + len(after))
        held["passed"], held["outs"], held["scratch"] = take(len(passed)), take(len(outs)), refs
        for one in jobs:
            own = []
            for key in ("ins", "small", "passed", "outs", "scratch"):
                own += [held[key].pop(0) for _ in one[key]]
            one["kernel"](*own)

    lead = len(ins) + len(small)
    made = pl.pallas_call(
        body,
        out_shape=[like(array) for array in passed] + list(outs),
        in_specs=space(len(ins), pl.ANY) + space(len(small), pltpu.VMEM) + space(len(passed) + len(after), pl.ANY),
        out_specs=space(len(passed) + len(outs), pl.ANY),
        scratch_shapes=scratch,
        input_output_aliases={lead + index: index for index in range(len(passed))},
        compiler_params=pltpu.CompilerParams(vmem_limit_bytes=VMEM_LIMIT),
        cost_estimate=cost or flops_of(1, 1 << 20),
    )(*ins, *small, *passed, *after)
    changed, fresh, results = list(made[: len(passed)]), list(made[len(passed) :]), []
    for one in jobs:
        mine = [changed.pop(0) for _ in one["passed"]] + [fresh.pop(0) for _ in one["outs"]]
        results.append(one["result"](mine))
    return results


def call(kernel, ins, small, outs, scratch, cost, passed=(), after=()):
    return run([job(kernel, ins, small, outs, scratch, passed)], after, cost)[0]


def self_forward(row, x, w, gains, segs, tables, buckets, toe=None):
    length, width = segs.shape[1], x.shape[1]
    dist = 2 * length
    outs = [
        shape((length, width), BF16),
        shape((length, width), BF16),
        shape((length, 3 * width), BF16),
        shape((length, width), BF16),
        shape((16, length), F32),
    ]

    def kernel(x_h, w_h, *refs):
        if row:
            toe_h, *refs = refs
            body(x_h, w_h, *refs[:9], toe_h, *refs[9:])
        else:
            body(x_h, w_h, *refs)

    def body(x_h, w_h, gain_r, seg_r, table_r, bucket_r, e_h, n_h, qkv_h, mix_h, lse_h, toe_h,
               x_v, w_v, n_v, qkv_v, mix_v, lse_v, e_v, mask_v, toe_v, vec_v, s_v, p_v, top_v, total_v, sems):
        section = lax.axis_index("section")

        @pl.when(section % 2 == 0)
        def _():
            side = section // 2
            loads = copy_all(
                sems, 0,
                (x_h.at[pl.ds(row * length, length)], x_v),
                *[(w_h.at[0, :, pl.ds(c * width, width)], w_v.at[:, pl.ds(c * width, width)]) for c in range(4)],
            )
            if row:
                tiles = copy_all(sems, 10, (toe_h, toe_v))
            else:
                fill_toeplitz(toe_v, vec_v, table_r[side], bucket_r[pl.ds(side, 1), :])
                tiles = copy_all(sems, 10, (toe_v, toe_h))
            fill_mask(mask_v, seg_r[row : row + 1, :], False, jnp.where(side == 1, 0, 2 * length))
            gain = gain_r[pl.ds(3 * side, 1), :]
            loads[0].wait()
            for rows in row_chunks(length):
                x = x_v[rows, :].astype(F32)
                n_v[rows, :] = (x * inverse_rms(x) * gain).astype(BF16)
            stores = copy_all(sems, 5, (n_v, n_h))
            wait_all(loads[1:4])
            project(n_v, w_v, 0, qkv_v, 0, 3 * width)
            stores += copy_all(sems, 6, (qkv_v, qkv_h))
            if row:
                wait_all(tiles)
            attend_ahead(qkv_v, qkv_v, qkv_v, 0, width, 2 * width, mask_v, toe_v, s_v, p_v, mix_v, lse_v, top_v, total_v)
            stores += copy_all(sems, 7, (mix_v, mix_h), (lse_v, lse_h))
            loads[4].wait()

            @pl.loop(0, width // 256)
            def _(t):
                cols = pl.ds(pl.multiple_of(t * 256, 256), 256)
                part = mm(mix_v[...], w_v[:, pl.ds(pl.multiple_of(3 * width + t * 256, 256), 256)])
                e_v[:, cols] = (x_v[:, cols].astype(F32) + part).astype(BF16)

            stores += copy_all(sems, 9, (e_v, e_h))
            wait_all(stores if row else stores + tiles)

    return call(
        kernel,
        [x, w] + ([toe] if row else []),
        [gains, segs, tables, buckets],
        outs if row else outs + [shape((H, 128, dist - 128), F32)],
        [
            pltpu.VMEM((length, width), BF16),
            pltpu.VMEM((width, 4 * width), BF16),
            pltpu.VMEM((length, width), BF16),
            pltpu.VMEM((length, 3 * width), BF16),
            pltpu.VMEM((length, width), BF16),
            pltpu.VMEM((16, length), F32),
            pltpu.VMEM((length, width), BF16),
            pltpu.VMEM((length, length), F32),
            pltpu.VMEM((H, 128, dist - 128), F32),
            pltpu.VMEM((16, dist), F32),
            pltpu.VMEM((4, length, length), F32),
            pltpu.VMEM((4, length, length), BF16),
            pltpu.VMEM((length, 128), F32),
            pltpu.VMEM((length, 128), F32),
            pltpu.SemaphoreType.DMA((11,)),
        ],
        flops_of(3, 12 << 20),
    )


def transposed_bias(tables, flipped, length, after):
    dist = 2 * length

    def kernel(table_r, bucket_r, toe_h, toe_v, vec_v, sems):
        section = lax.axis_index("section")

        @pl.when(section % 2 == 0)
        def _():
            side = section // 2
            fill_toeplitz(toe_v, vec_v, table_r[side], bucket_r[pl.ds(side, 1), :])
            wait_all(copy_all(sems, 0, (toe_v, toe_h)))

    return call(
        kernel,
        [],
        [tables, flipped],
        [shape((H, 128, dist - 128), F32)],
        [pltpu.VMEM((H, 128, dist - 128), F32), pltpu.VMEM((16, dist), F32), pltpu.SemaphoreType.DMA((1,))],
        flops_of(1, 6 << 20),
        after=after,
    )[0]


def marker(after):
    def kernel(out_h):
        pass

    return call(kernel, [], [], [shape((8, 128), F32)], [], flops_of(1, 1 << 20), after=after)[0]


def packed_small(acc, flipped, dgains_s, dgains_e, dgain_d):
    dist, width = acc.shape[2] + 128, dgain_d.shape[1]

    def kernel(acc_h, bucket_r, ds0_r, ds1_r, de0_r, de1_r, dd_r, out_h, acc_v, diag_v, out_v, sems):
        section = lax.axis_index("section")
        side = section // 2
        out_v[...] = jnp.zeros_like(out_v)

        @pl.when(section % 2 == 0)
        def _():
            loads = copy_all(sems, 0, (acc_h, acc_v))
            diag_v[...] = jnp.zeros_like(diag_v)
            wait_all(loads)
            fold_diagonals(acc_v, diag_v)
            ids = lax.broadcasted_iota(jnp.int32, (32, dist), 0)
            onehot = (ids == bucket_r[pl.ds(side, 1), :]).astype(F32)
            part = lax.dot_general(
                diag_v[...], onehot, (((1,), (1,)), ((), ())),
                precision=lax.Precision.HIGHEST, preferred_element_type=F32,
            )
            for own in range(2):
                @pl.when(side == own)
                def _():
                    out_v[3 * own : 3 * own + 1, :] = ds0_r[...] + ds1_r[...]
                    out_v[8:16, 256 * own : 256 * own + 32] = part[:8]
                    out_v[8:16, 256 * own + 128 : 256 * own + 160] = part[8:]

        @pl.when(section == 1)
        def _():
            out_v[1:3, :] = de0_r[...] + de1_r[...]

        @pl.when(side == 1)
        def _():
            out_v[4:7, :] = dd_r[...]

        wait_all(copy_all(sems, 1, (out_v, out_h)))

    return job(
        kernel,
        [acc],
        [flipped, *dgains_s, *dgains_e, dgain_d],
        [shape((16, width), F32)],
        [
            pltpu.VMEM(acc.shape, F32),
            pltpu.VMEM((16, dist), F32),
            pltpu.VMEM((16, width), F32),
            pltpu.SemaphoreType.DMA((2,)),
        ],
        result=lambda made: made[0],
    )


def self_backward(row, sections, ins, mats, gains, segs, toe, g_enc, g_dec, kept, passed, after):
    length, width = segs.shape[1], ins.shape[1]
    dist = 2 * length

    def kernel(x_h, w_h, toe_h, ge_h, gd_h, qkv_h, mix_h, lse_h, gain_r, seg_r, out_h, acc_h, dgain_h, b_h,
               x_v, w_v, qkv_v, mix_v, lse_v, d_v, dm_v, dqkv_v, dn_v, gx_v, dgain_v,
               mask_v, toe_v, acc_v, s_v, dp_v, p_v, ds_v, sems):
        section = lax.axis_index("section")
        side = section // 2

        active = section == sections[0]
        for one in sections[1:]:
            active = active | (section == one)

        @pl.when(active)
        def _():
            loads = either_all(sems, 0, side == 0, ((ge_h, d_v), (gd_h, d_v)))
            loads += copy_all(
                sems, 1,
                (w_h.at[0, :, pl.ds(3 * width, width)], w_v.at[:, pl.ds(3 * width, width)]),
                (mix_h, mix_v),
                (lse_h, lse_v),
                (qkv_h, qkv_v),
                (toe_h, toe_v),
                (w_h.at[0, :, pl.ds(0, 3 * width)], w_v.at[:, pl.ds(0, 3 * width)]),
                (x_h.at[pl.ds(row * length, length)], x_v),
            )
            sums = copy_all(sems, 8, (acc_h, acc_v)) if row else []
            fill_mask(mask_v, seg_r[row : row + 1, :], True, jnp.where(side == 1, 0, 2 * length))
            if not row:
                acc_v[...] = jnp.zeros_like(acc_v)
            gain = gain_r[pl.ds(3 * side, 1), :]
            wait_all(loads[:2])
            stores = copy_all(sems, 9, (d_v, b_h.at[:, pl.ds(3 * width, width)]))
            rows_out(d_v, w_v, 3 * width, dm_v, False)
            wait_all(loads[2:6] + sums)
            attend_back(qkv_v, qkv_v, qkv_v, dm_v, mix_v, 0, width, 2 * width, mask_v, toe_v, lse_v,
                        dp_v, s_v, p_v, ds_v, dqkv_v, 0, acc_v)
            stores += copy_all(sems, 10, (dqkv_v, b_h.at[:, pl.ds(0, 3 * width)]), (acc_v, acc_h))
            wait_all(loads[6:])
            rows_out(dqkv_v, w_v, 0, dn_v, False)
            total = jnp.zeros((1, width), F32)
            for rows in row_chunks(length):
                dx, dgain = rms_back(x_v[rows, :].astype(F32), gain, dn_v[rows, :])
                gx_v[rows, :] = d_v[rows, :].astype(F32) + dx
                total = total + dgain
            dgain_v[...] = total
            stores += copy_all(sems, 12, (gx_v, out_h.at[pl.ds(row * length, length)]), (dgain_v, dgain_h))
            wait_all(stores)

    n, qkv, mix, lse = kept
    return call(
        kernel,
        [ins, mats, toe, g_enc, g_dec, qkv, mix, lse],
        [gains, segs],
        [like(toe), shape((1, width), F32), shape((length, 4 * width), BF16)][len(passed) - 1 :],
        [
            pltpu.VMEM((length, width), BF16),
            pltpu.VMEM((width, 4 * width), BF16),
            pltpu.VMEM((length, 3 * width), BF16),
            pltpu.VMEM((length, width), BF16),
            pltpu.VMEM((16, length), F32),
            pltpu.VMEM((length, width), BF16),
            pltpu.VMEM((length, width), BF16),
            pltpu.VMEM((length, 3 * width), BF16),
            pltpu.VMEM((length, width), F32),
            pltpu.VMEM((length, width), F32),
            pltpu.VMEM((1, width), F32),
            pltpu.VMEM((length, length), F32),
            pltpu.VMEM((H, 128, dist - 128), F32),
            pltpu.VMEM((H, 128, dist - 128), F32),
            pltpu.VMEM((2, length, length), F32),
            pltpu.VMEM((2, length, length), F32),
            pltpu.VMEM((2, length, length), BF16),
            pltpu.VMEM((2, length, length), BF16),
            pltpu.SemaphoreType.DMA((14,)),
        ],
        flops_of(6, 16 << 20),
        passed,
        after,
    )


def encoder_forward(row, e1, mats, gains, out_rows):
    length, width = e1.shape
    hidden = mats.shape[2]
    narrow, wide = shape((length, width), BF16), shape((length, hidden), BF16)
    rows_shape = shape((2 * length, width), F32)
    kept = [narrow, shape((length, width), F32), narrow, wide, wide]

    def kernel(e_h, w_h, gain_r, out_h, send_h, mid_h, n_h, h_h, slope_h,
               e_v, win_v, wout_v, n_v, h_v, slope_v, mid_v, out_v, send_v, sems):
        @pl.when(lax.axis_index("section") == 1)
        def _():
            loads = copy_all(sems, 0, (e_h, e_v))
            win_loads = column_parts(sems, 9, w_h.at[0], win_v)
            loads += copy_all(sems, 1, (w_h.at[1], wout_v))
            loads[0].wait()
            for rows in row_chunks(length):
                x = e_v[rows, :].astype(F32)
                mid_v[rows, :] = x
                n_v[rows, :] = (x * inverse_rms(x) * gain_r[1:2, :]).astype(BF16)
            stores = copy_all(sems, 3, (n_v, n_h))
            ffn_up(n_v, win_v, h_v, slope_v, win_loads)
            stores += copy_all(sems, 4, (h_v, h_h), (slope_v, slope_h))
            loads[1].wait()
            rows_out(h_v, wout_v, 0, mid_v, True)
            stores += copy_all(sems, 8, (mid_v, mid_h))
            for n, rows in enumerate(row_chunks(length)):
                x = mid_v[rows, :]
                y = x * inverse_rms(x) * gain_r[2:3, :]
                out_v[rows, :] = y
                send_v[rows, :] = y.astype(BF16)
                target = pl.ds(row * length + n * ROW_STEP, ROW_STEP)
                stores += copy_all(
                    sems, 12 + 2 * n, (send_v.at[rows], send_h.at[rows]), (out_v.at[rows], out_h.at[target])
                )
            wait_all(stores)

    return call(
        kernel,
        [e1, mats],
        [gains],
        kept if row else [rows_shape] + kept,
        [
            pltpu.VMEM((length, width), BF16),
            pltpu.VMEM((width, hidden), BF16),
            pltpu.VMEM((width, hidden), BF16),
            pltpu.VMEM((length, width), BF16),
            pltpu.VMEM((length, hidden), BF16),
            pltpu.VMEM((length, hidden), BF16),
            pltpu.VMEM((length, width), F32),
            pltpu.VMEM((length, width), F32),
            pltpu.VMEM((length, width), BF16),
            pltpu.SemaphoreType.DMA((20,)),
        ],
        flops_of(2, 20 << 20),
        [out_rows] if row else [],
    )


def encoder_backward(row, ins, extra, e1, mid, slope, mats, gains, after):
    length, width = extra.shape
    hidden = mats.shape[2]

    def kernel(cot_h, extra_h, e_h, mid_h, slope_h, w_h, gain_r, g_h, d_h, du_h, dgain_h,
               cot_v, extra_v, e_v, mid_v, slope_v, win_v, wout_v, d_v, du_v, dn_v, gm_v, g_v, dgain_v, sems):
        @pl.when(lax.axis_index("section") == 1)
        def _():
            loads = copy_all(
                sems, 0,
                (cot_h.at[pl.ds(row * length, length)], cot_v), (extra_h, extra_v), (mid_h, mid_v),
                (w_h.at[1], wout_v), (slope_h, slope_v), (w_h.at[0], win_v), (e_h, e_v),
            )
            wait_all(loads[:3])
            total = jnp.zeros((1, width), F32)
            for rows in row_chunks(length):
                dy = cot_v[rows, :].astype(F32) + extra_v[rows, :].astype(F32)
                dx, dgain = rms_back(mid_v[rows, :], gain_r[2:3, :], dy)
                gm_v[rows, :] = dx
                d_v[rows, :] = dx.astype(BF16)
                total = total + dgain
            dgain_v[1:2, :] = total
            stores = copy_all(sems, 7, (d_v, d_h))
            wait_all(loads[3:5])
            ffn_down(d_v, wout_v, slope_v, du_v)
            stores += copy_all(sems, 8, (du_v, du_h))
            wait_all(loads[5:])
            rows_out(du_v, win_v, 0, dn_v, False)
            total = jnp.zeros((1, width), F32)
            for rows in row_chunks(length):
                dx, dgain = rms_back(e_v[rows, :].astype(F32), gain_r[1:2, :], dn_v[rows, :])
                g_v[rows, :] = (gm_v[rows, :] + dx).astype(BF16)
                total = total + dgain
            dgain_v[0:1, :] = total
            stores += copy_all(sems, 9, (g_v, g_h), (dgain_v, dgain_h))
            wait_all(stores)

    return call(
        kernel,
        [ins, extra, e1, mid, slope, mats],
        [gains],
        [
            shape((length, width), BF16),
            shape((length, width), BF16),
            shape((length, hidden), BF16),
            shape((2, width), F32),
        ],
        [
            pltpu.VMEM((length, width), BF16),
            pltpu.VMEM((length, width), BF16),
            pltpu.VMEM((length, width), BF16),
            pltpu.VMEM((length, width), F32),
            pltpu.VMEM((length, hidden), BF16),
            pltpu.VMEM((width, hidden), BF16),
            pltpu.VMEM((width, hidden), BF16),
            pltpu.VMEM((length, width), BF16),
            pltpu.VMEM((length, hidden), BF16),
            pltpu.VMEM((length, width), F32),
            pltpu.VMEM((length, width), F32),
            pltpu.VMEM((length, width), BF16),
            pltpu.VMEM((2, width), F32),
            pltpu.SemaphoreType.DMA((11,)),
        ],
        flops_of(2, 20 << 20),
        after=after,
    )


def decoder(d_own, d_got, m_two, m_three, ins, cot_got, mats, got_mats, gains, segs, passed, after):
    length, width = d_own.shape
    hidden = mats.shape[2]

    def kernel(d2_h, d3_h, m2_h, m3_h, c1_h, c0_h, w1_h, w0_h, gain_r, seg_r,
               out_h, fa_h, fb_h, fc_h, other_h, gm_h, gd_h, dgain_h,
               d_v, m_v, c_v, wca_v, win_v, wout_v, n_v, q_v, mix_v, lse_v, mask_v, s_v, p_v, h_v, slope_v,
               x_v, y_v, dn_v, n5_v, do_v, dgain_v, dp_v, ds_v, dq_v, dm_v, do4_v, gm_v, gd_v, out_v, sems):
        section = lax.axis_index("section")

        @pl.when(section >= 2)
        def _():
            own = section == 3
            second = pl.ds(length, length)

            def put(first, *choices):
                return either_all(sems, first, own, *choices)

            quarters = [pl.ds(c * width, width) for c in range(4)]
            loads = put(0, ((d3_h, d_v), (d2_h, d_v)))
            cross_loads = put(
                21, *[((w1_h.at[0, :, cut], wca_v.at[:, cut]), (w0_h.at[0, :, cut], wca_v.at[:, cut])) for cut in quarters]
            )
            loads += put(
                1,
                ((m3_h, m_v), (m2_h, m_v)),
                *[((w1_h.at[k], v), (w0_h.at[k], v)) for k, v in ((1, win_v), (2, wout_v))],
                ((c1_h.at[second], c_v), (c0_h, c_v)),
            )
            fill_mask(mask_v, seg_r[pl.ds(section - 2, 1), :], False, 2 * length)
            loads[0].wait()
            for rows in row_chunks(length):
                x = d_v[rows, :].astype(F32)
                x_v[rows, :] = x
                n_v[rows, :] = (x * inverse_rms(x) * gain_r[4:5, :]).astype(BF16)
            part_of = lambda f_h, n, count=1: f_h.at[:, pl.ds(n * width, count * width)]
            stores = copy_all(sems, 6, (n_v, part_of(fc_h, 0)))
            cross_loads[0].wait()
            project(n_v, wca_v, 0, q_v, 0, width)
            loads[1].wait()
            stores += copy_all(sems, 7, (m_v, part_of(fc_h, 1)))
            wait_all(cross_loads[1:3])
            project(m_v, wca_v, width, q_v, width, 2 * width)
            attend(q_v, q_v, q_v, 0, width, 2 * width, mask_v, None, s_v, p_v, mix_v, lse_v)
            stores += copy_all(sems, 9, (mix_v, part_of(fc_h, 2)))

            cross_loads[3].wait()

            @pl.loop(0, width // 256)
            def _(t):
                cols = pl.ds(pl.multiple_of(t * 256, 256), 256)
                part = mm(mix_v[...], wca_v[:, pl.ds(pl.multiple_of(3 * width + t * 256, 256), 256)])
                x_v[:, cols] = x_v[:, cols] + part

            for rows in row_chunks(length):
                x = x_v[rows, :]
                y_v[rows, :] = x
                n5_v[rows, :] = (x * inverse_rms(x) * gain_r[5:6, :]).astype(BF16)
            stores += copy_all(sems, 10, (n5_v, part_of(fa_h, 0)))
            loads[2].wait()
            ffn_up(n5_v, win_v, h_v, slope_v)
            stores += copy_all(sems, 11, (h_v, part_of(fb_h, 1, 4)))
            loads[3].wait()
            rows_out(h_v, wout_v, 0, y_v, True)
            loads[4].wait()
            total = jnp.zeros((1, width), F32)
            for rows in row_chunks(length):
                y = y_v[rows, :]
                out_v[rows, :] = y * inverse_rms(y) * gain_r[6:7, :]
                dy, dgain = rms_back(y, gain_r[6:7, :], c_v[rows, :].astype(F32))
                total = total + dgain
                do_v[rows, :] = dy.astype(BF16)
                y_v[rows, :] = dy
            dgain_v[2:3, :] = total
            stores += put(12, ((out_v, out_h.at[second]), (out_v, other_h)))
            stores += copy_all(sems, 13, (do_v, part_of(fb_h, 0)))
            ffn_down(do_v, wout_v, slope_v, slope_v)
            stores += copy_all(sems, 14, (slope_v, part_of(fa_h, 1, 4)))
            rows_out(slope_v, win_v, 0, dn_v, False)
            total = jnp.zeros((1, width), F32)
            for rows in row_chunks(length):
                dx, dgain = rms_back(x_v[rows, :], gain_r[5:6, :], dn_v[rows, :])
                dx = y_v[rows, :] + dx
                y_v[rows, :] = dx
                do4_v[rows, :] = dx.astype(BF16)
                total = total + dgain
            dgain_v[1:2, :] = total
            stores += copy_all(sems, 15, (do4_v, part_of(fc_h, 6)))
            rows_out(do4_v, wca_v, 3 * width, dm_v, False)
            attend_back(q_v, q_v, q_v, dm_v, mix_v, 0, width, 2 * width, mask_v, None, lse_v,
                        dp_v, s_v, p_v, ds_v, dq_v, 0, None)
            stores += copy_all(sems, 16, (dq_v, part_of(fc_h, 3, 3)))
            rows_out(dq_v.at[:, width:], wca_v, width, gm_v, False)
            stores += copy_all(sems, 18, (gm_v, gm_h))
            rows_out(dq_v.at[:, :width], wca_v, 0, dn_v, False)
            total = jnp.zeros((1, width), F32)
            for rows in row_chunks(length):
                dx, dgain = rms_back(d_v[rows, :].astype(F32), gain_r[4:5, :], dn_v[rows, :])
                gd_v[rows, :] = (y_v[rows, :] + dx).astype(BF16)
                total = total + dgain
            dgain_v[0:1, :] = total
            stores += copy_all(sems, 19, (gd_v, gd_h), (dgain_v, dgain_h))
            wait_all(stores)

    narrow = shape((length, width), BF16)
    return call(
        kernel,
        [d_own, d_got, m_two, m_three, ins, cot_got, mats, got_mats],
        [gains, segs],
        [
            *[shape((length, count * width), BF16) for count in (5, 5, 7)],
            shape((length, width), F32),
            *(narrow, narrow),
            shape((3, width), F32),
        ],
        [
            pltpu.VMEM((length, width), BF16),
            pltpu.VMEM((length, width), BF16),
            pltpu.VMEM((length, width), BF16),
            pltpu.VMEM((width, 4 * width), BF16),
            pltpu.VMEM((width, hidden), BF16),
            pltpu.VMEM((width, hidden), BF16),
            pltpu.VMEM((length, width), BF16),
            pltpu.VMEM((length, 3 * width), BF16),
            pltpu.VMEM((length, width), BF16),
            pltpu.VMEM((16, length), F32),
            pltpu.VMEM((length, length), F32),
            pltpu.VMEM((2, length, length), F32),
            pltpu.VMEM((2, length, length), BF16),
            pltpu.VMEM((length, hidden), BF16),
            pltpu.VMEM((length, hidden), BF16),
            pltpu.VMEM((length, width), F32),
            pltpu.VMEM((length, width), F32),
            pltpu.VMEM((length, width), F32),
            pltpu.VMEM((length, width), BF16),
            pltpu.VMEM((length, width), BF16),
            pltpu.VMEM((3, width), F32),
            pltpu.VMEM((2, length, length), F32),
            pltpu.VMEM((2, length, length), BF16),
            pltpu.VMEM((length, 3 * width), BF16),
            pltpu.VMEM((length, width), BF16),
            pltpu.VMEM((length, width), BF16),
            pltpu.VMEM((length, width), BF16),
            pltpu.VMEM((length, width), BF16),
            pltpu.VMEM((length, width), F32),
            pltpu.SemaphoreType.DMA((25,)),
        ],
        flops_of(12, 30 << 20),
        passed,
        after,
    )


def weight_grad(sections, groups, chunks, ndp, decoder=None, passed=()):
    length, width = groups[0][0][0][0].shape[0], 768
    columns = sum(group[2] for group in groups)
    pieces = len(groups[0][0])
    bits = ndp.bit_length() - 1
    block = width // ndp
    flat = []
    for a_list, b_list, _ in groups + (decoder or []):
        for array, _ in a_list + b_list:
            if not any(array is other for other in flat):
                flat.append(array)
    place = lambda array: [index for index, other in enumerate(flat) if other is array][0]
    plan_of = lambda groups: [
        ([(place(a), a0) for a, a0 in a_list], [(place(b), b0) for b, b0 in b_list], count)
        for a_list, b_list, count in groups
    ]
    plan, other_plan = plan_of(groups), plan_of(decoder or groups)
    tile = 768
    copies = 2 * pieces * len(groups)

    def kernel(*args):
        sources = args[: len(flat)]
        outs = args[len(flat) : len(flat) + 2 * len(chunks)]
        a_v, at_v, b_v, out_v, sems = args[len(flat) + 2 * len(chunks) :]
        me = lax.axis_index("dp")
        section = lax.axis_index("section")
        active = section == sections[0]
        for one in sections[1:]:
            active = active | (section == one)

        @pl.when(active)
        def _():
            loads, start = [], 0
            for g, (a_list, b_list, count) in enumerate(plan):
                group_loads = []
                for k in range(pieces):
                    rows = pl.ds(k * length, length)
                    choices = []
                    for a_of, b_of, _ in (other_plan[g], plan[g]):
                        (ai, a0), (bi, b0) = a_of[k], b_of[k]
                        choices.append((
                            (sources[ai].at[:, pl.ds(a0, width)], a_v.at[g, rows]),
                            (sources[bi].at[:, pl.ds(b0, count)], b_v.at[rows, pl.ds(start, count)]),
                        ))
                    first = 2 * (g * pieces + k)
                    if decoder:
                        group_loads += either_all(sems, first, section >= 2, *zip(*choices))
                    else:
                        group_loads += copy_all(sems, first, *choices[0])
                loads.append(group_loads)
                start += count
            stores, group, group_end, start = [], -1, 0, 0
            for number, (count, order) in enumerate(chunks):
                spots = []
                for b in range(ndp):
                    code = jnp.bitwise_xor(me, b)
                    spot = 0
                    for k in range(bits):
                        spot = spot + ((code >> order[k]) & 1) * (1 << (bits - 1 - k))
                    spots.append(spot)
                done, end = start, start + count
                while done < end:
                    if done == group_end:
                        group += 1
                        wait_all(loads[group])
                        at_v[...] = a_v[group].T
                        group_end += plan[group][2]
                    upto = min(end, group_end)

                    @pl.loop(0, (upto - done) // tile)
                    def _(t):
                        cols = pl.ds(pl.multiple_of(done + t * tile, 128), tile)
                        part = mm(at_v[...], b_v[:, cols])
                        for b in range(ndp):
                            out_v[spots[b], :, cols] = part[b * block : (b + 1) * block, :].astype(BF16)

                    done = upto
                for half in range(2):
                    source = out_v.at[pl.ds(half * (ndp // 2), ndp // 2), :, pl.ds(start, count)]
                    stores += copy_all(sems, copies + 2 * number + half, (source, outs[2 * number + half]))
                start = end
            wait_all(stores)

    return job(
        kernel,
        flat,
        [],
        [] if passed else [shape((ndp // 2, block, count), BF16) for count, _ in chunks for _ in range(2)],
        [
            pltpu.VMEM((len(groups), pieces * length, width), BF16),
            pltpu.VMEM((width, pieces * length), BF16),
            pltpu.VMEM((pieces * length, columns), BF16),
            pltpu.VMEM((ndp, block, columns), BF16),
            pltpu.SemaphoreType.DMA((copies + 2 * len(chunks),)),
        ],
        passed=passed,
        result=lambda made: [(made[2 * number], made[2 * number + 1]) for number in range(len(chunks))],
    )


def along_dp(value, bit, sections, ndp):
    pairs = [(s * ndp + d, s * ndp + (d ^ bit)) for s in sections for d in range(ndp)]
    return lax.ppermute(value, ("section", "dp"), pairs)


def added(items):
    outs, kinds = [], []
    for keep, _, _ in items:
        kind = "sum" if keep.dtype == F32 else "last" if keep.shape[0] == 1 else "half"
        kinds.append(kind)
        if kind == "half":
            outs += [shape((keep.shape[0] // 2,) + keep.shape[1:], BF16)] * 2
        else:
            outs.append(shape(keep.shape if kind == "sum" else keep.shape[1:], F32))

    def kernel(*refs):
        count = len(items)
        sources, rest = refs[: 2 * count], refs[2 * count :]
        targets, rest = rest[: len(outs)], rest[len(outs) :]
        scratch, sems = rest[:-1], rest[-1]
        section = lax.axis_index("section")

        def takes_part(sections):
            active = section == sections[0]
            for one in sections[1:]:
                active = active | (section == one)
            return active

        for number, item in enumerate(items):
            @pl.when(takes_part(item[2]))
            def _():
                for k in range(2):
                    pltpu.make_async_copy(
                        sources[2 * number + k], scratch[3 * number + k], sems.at[4 * number + k]
                    ).start()

        place = 0
        for number, (item, kind) in enumerate(zip(items, kinds)):
            n = item[0].shape[0]
            keep_v, got_v, out_v = scratch[3 * number : 3 * number + 3]
            mine = targets[place : place + (2 if kind == "half" else 1)]
            place += len(mine)

            @pl.when(takes_part(item[2]))
            def _():
                for k, v in enumerate((keep_v, got_v)):
                    pltpu.make_async_copy(sources[2 * number + k], v, sems.at[4 * number + k]).wait()
                if kind == "half":
                    @pl.loop(0, n)
                    def _(i):
                        out_v[i] = (keep_v[i].astype(F32) + got_v[i].astype(F32)).astype(BF16)

                    wait_all(
                        copy_all(
                            sems, 4 * number + 2,
                            (out_v.at[pl.ds(0, n // 2)], mine[0]), (out_v.at[pl.ds(n // 2, n // 2)], mine[1]),
                        )
                    )
                else:
                    if kind == "last":
                        out_v[...] = keep_v[0].astype(F32) + got_v[0].astype(F32)
                    else:
                        out_v[...] = keep_v[...] + got_v[...]
                    wait_all(copy_all(sems, 4 * number + 2, (out_v, mine[0])))

    scratch = []
    for (keep, _, _), kind in zip(items, kinds):
        own = pltpu.VMEM(keep.shape, keep.dtype)
        scratch += [own, own, pltpu.VMEM(keep.shape[1:], F32) if kind == "last" else own]
    def result(made):
        results = []
        for kind in kinds:
            size = 2 if kind == "half" else 1
            results.append(tuple(made[:size]) if size == 2 else made[0])
            made = made[size:]
        return results

    return job(
        kernel,
        [array for keep, got, _ in items for array in (keep, got)],
        [],
        outs,
        scratch + [pltpu.SemaphoreType.DMA((4 * len(items),))],
        result=result,
    )


def joined(v, pieces):
    start = 0
    for piece in pieces:
        yield piece, v.at[:, pl.ds(start, piece.shape[1])]
        start += piece.shape[1]


def outputs(one, two, three, rows_got, out_rows, after):
    length, width = rows_got.shape
    block, columns = two.shape

    def kernel(a_h, b_h, s_h, c_h, r_h, out_h, grad_h, f_v, s_v, c_v, r_v, sems):
        section = lax.axis_index("section")
        even = section % 2 == 0
        loads = copy_all(sems, 0, *joined(f_v, (a_h, b_h)))

        @pl.when(section == 3)
        def _():
            wait_all(copy_all(sems, 2, (s_h, s_v), (c_h, c_v), (r_h, r_v)))
            wait_all(loads)
            wait_all(
                copy_all(
                    sems, 5,
                    (f_v, grad_h.at[1]), (s_v, grad_h.at[2]), (c_v, grad_h.at[0]), (r_v, out_h.at[pl.ds(0, length)]),
                )
            )

        @pl.when(section != 3)
        def _():
            c_v[...] = jnp.zeros_like(c_v)
            stores = copy_all(sems, 5, (c_v, grad_h.at[2]))

            @pl.when(section == 1)
            def _():
                wait_all(copy_all(sems, 2, (s_h, s_v)))
                wait_all(copy_all(sems, 3, (s_v, grad_h.at[1])))

            @pl.when(even)
            def _():
                wait_all(copy_all(sems, 3, (c_v, grad_h.at[1])))

            wait_all(loads)
            wait_all(stores + copy_all(sems, 6, (f_v, grad_h.at[0])))

    return call(
        kernel,
        [*one, two, three, rows_got],
        [],
        [shape((3, block, columns), F32)],
        [pltpu.VMEM((block, columns), F32)] * 3 + [pltpu.VMEM((length, width), F32), pltpu.SemaphoreType.DMA((9,))],
        flops_of(1, 1 << 20),
        [out_rows],
        after,
    )


def per_device(section_ins, segments, buckets, section_mats, gains, tables):
    ndp = lax.axis_size("dp")
    ins = section_ins[0]
    mats = section_mats[0]
    length = segments.shape[1]
    width = ins.shape[1]
    segs = segments
    flipped = jnp.pad(buckets[:, ::-1], ((0, 0), (0, 1)), constant_values=-1)
    everywhere = (0, 1, 2, 3)
    move = lambda value, pairs: lax.ppermute(value, "section", pairs)

    *fwd0, tiles = self_forward(0, ins, mats, gains, segs, tables, buckets)
    late_mats, _ = lax.optimization_barrier((section_mats, fwd0[0]))
    got_mats = move(late_mats, [(3, 2)])[0]
    first0 = move(fwd0[0], [(0, 1)])
    fwd1 = self_forward(1, ins, mats, gains, segs, tables, buckets, tiles)
    first1 = move(fwd1[0], [(0, 1), (2, 3)])
    toe = transposed_bias(tables, flipped, length, [fwd1[0]])
    out_rows, *enc0 = encoder_forward(0, first0, mats, gains, None)
    m_two = move(enc0[0], [(1, 2)])
    late_ins, _ = lax.optimization_barrier((ins, fwd1[0]))
    cot_got = move(late_ins[:length], [(3, 2)])
    out_rows, *enc1 = encoder_forward(1, first1, mats, gains, out_rows)
    m_three = move(enc1[0], [(1, 3)])
    here = marker([enc1[0], m_two])

    dec = decoder(fwd0[0], first1, m_two, m_three, ins, cot_got, mats, got_mats, gains, segs, [out_rows], [toe, here])
    out_rows, *factors, other, g_mem, g_self, dgain_d = dec
    even, odd = (0, 2), (1, 3)
    extra0 = move(g_mem, [(2, 1)])
    extra1 = move(g_mem, [(3, 0)])
    (sent, g_self_sent), _ = lax.optimization_barrier(((factors, g_self), extra0))
    got = [move(value, [(2, 3)]) for value in sent]
    g_self_got = move(g_self_sent, [(3, 2)])
    back0 = encoder_backward(0, ins, extra0, first0, enc0[1], enc0[4], mats, gains, [extra1])
    g0 = move(back0[0], [(1, 0)])
    (other, extra1), _ = lax.optimization_barrier(((other, extra1), back0[0]))
    extra1 = move(extra1, [(0, 1)])
    own0 = self_backward(
        0, even, ins, mats, gains, segs, toe, g0, g_self, fwd0[1:], [out_rows], [extra1]
    )
    out_rows, acc = own0[:2]
    back1 = encoder_backward(1, ins, extra1, first1, enc1[1], enc1[4], mats, gains, [acc])
    g1 = move(back1[0], [(1, 0)])
    other, _ = lax.optimization_barrier((other, back1[0]))
    rows_got = move(other, [(2, 3)])

    plain = tuple(range(ndp.bit_length() - 1))
    turned = (1, 0) + plain[2:]
    orders = (plain, turned)
    steps = len(plain)
    whole = 4 * width
    rows_of = lambda which, at: [(factors[which], at * width), (got[which], at * width)]
    halves = [(2 * width, order) for order in orders]
    groups = [([(enc0[2], 0), (enc1[2], 0)], [(back0[2], 0), (back1[2], 0)], whole)]
    groups_d = [(rows_of(0, 0), rows_of(0, 1), whole)]
    made, = run([weight_grad(odd, groups, halves, ndp, groups_d)], [back1[0]])
    own1 = self_backward(
        1, even, ins, mats, gains, segs, toe, g1, g_self_got, fwd1[1:], [out_rows, acc], [made[0][0]]
    )
    out_rows, acc = own1[:2]
    groups = [
        ([(fwd0[1], 0), (fwd1[1], 0)], [(own0[3], 0), (own1[3], 0)], 3 * width),
        ([(fwd0[3], 0), (fwd1[3], 0)], [(own0[3], 3 * width), (own1[3], 3 * width)], width),
    ]
    made, = run([weight_grad(even, groups, halves, ndp, passed=[*made[0], *made[1]])], [out_rows])

    def send(pair, order, step, sections):
        return (pair[0], along_dp(pair[1], 1 << order[step], sections, ndp), sections)

    def send_one(pairs, step):
        return [send(pair, order, step, everywhere) for pair, order in zip(pairs, orders)]

    def send_rest(pair, part, step):
        return send(pair, *((turned, step, odd) if part == 1 else (plain, step, (3,))))

    one = send_one(made, 0)
    groups = [([(back0[1], 0), (back1[1], 0)], [(enc0[3], 0), (enc1[3], 0)], whole)]
    groups_d = [(rows_of(1, 0), rows_of(1, 1), whole)]
    (two,), = run([weight_grad(odd, groups, [(whole, turned)], ndp, groups_d)], [made[0][0]])
    groups = [(rows_of(2, k), rows_of(2, at), count * width) for k, at, count in ((0, 3, 1), (1, 4, 2), (2, 6, 1))]
    (three,), = run([weight_grad((3,), groups, [(whole, plain)], ndp)], [two[0]])
    rest = [send_rest(two, 1, 0), send_rest(three, 2, 0)]
    dgains = ([own0[2], own1[2]], [back0[3], back1[3]], dgain_d)
    small, = run([packed_small(acc, flipped, *dgains)], [three[0]])
    small_got = along_dp(small, 1, everywhere, ndp)
    tied = [small]
    for k in range(steps):
        last = k + 1 == steps
        for part, items in enumerate((one, rest[:1], rest[1:])):
            cost = SHORT if part < 2 and not last else None if part == 2 else LONG
            number = 2 * k + part
            if part < 2 and (number < steps or last and not part):
                (*sums, small), = run([added([*items, (small, small_got, everywhere)])], tied, cost)
                if number + 1 < steps:
                    small_got = along_dp(small, 2 << number, everywhere, ndp)
            else:
                sums, = run([added(items)], tied, cost)
            tied = [sums[0] if last else sums[0][0]]
            if part == 1 and k + 2 == steps:
                held, _ = lax.optimization_barrier((small, tied[0]))
                small_got = move(held, [(0, 1), (1, 0), (2, 3), (3, 2)])
            if not last:
                sums = send_one(sums, k + 1) if not part else [send_rest(sums[0], part, k + 1)]
            if part:
                rest[part - 1] = sums[0]
            else:
                one = sums
    small, _ = lax.optimization_barrier((small, tied[0]))
    small = small + move(small, [(0, 2), (2, 0), (1, 3), (3, 1)])
    out_rows, grad = outputs(one, *rest, rows_got, out_rows, tied)

    gains_grad = small[: gains.shape[0]]
    heads = [
        jnp.concatenate([small[8:16, at : at + 32], small[8:12, at + 128 : at + 160]], axis=0)
        for at in range(0, 256 * tables.shape[0], 256)
    ]
    return out_rows[None], grad[None], gains_grad, jnp.swapaxes(jnp.stack(heads), 1, 2)


def solution(mesh):
    placed = (
        P("section", "dp", None),
        P("dp", None),
        P(),
        P("section", None, None, None),
        P(),
        P(),
    )
    return jax.shard_map(
        per_device,
        mesh=mesh,
        in_specs=placed,
        out_specs=(P("section", "dp", None), P("section", None, "dp", None), P(), P()),
        check_vma=False,
    )
```

```python
from functools import partial

import jax
import jax.numpy as jnp
from jax import lax
from jax.experimental import pallas as pl
from jax.experimental.pallas import tpu as pltpu
from jax.sharding import PartitionSpec as P

H = 12
HD = 64
PAIRS = H // 2
EPS = 1e-06
GELU = 0.7978845608028654
CUBIC = 0.044715
MASKED = -1e38
F32 = jnp.float32
BF16 = jnp.bfloat16
ROW_STEP = 128
VMEM_LIMIT = 60 * 1024 * 1024


def mm(a, b):
    return jnp.dot(a, b, preferred_element_type=F32)


def mm_nt(a, b):
    return lax.dot_general(a, b, (((1,), (1,)), ((), ())), preferred_element_type=F32)


def inverse_rms(x):
    return lax.rsqrt(jnp.mean(x * x, axis=-1, keepdims=True) + EPS)


def row_chunks(length):
    return [pl.ds(start, ROW_STEP) for start in range(0, length, ROW_STEP)]


def rms_back(x, gain, dy):
    r = inverse_rms(x)
    inner = jnp.mean(dy * gain * x, axis=-1, keepdims=True)
    dx = r * gain * dy - x * (r * r * r) * inner
    return dx, jnp.sum(dy * x * r, axis=0, keepdims=True)


def copy_all(sems, first, *pairs):
    started = []
    for offset, (source, target) in enumerate(pairs):
        one = pltpu.make_async_copy(source, target, sems.at[first + offset])
        one.start()
        started.append(one)
    return started


class Either:
    def __init__(self, sem, flag, yes, no):
        self.done = pltpu.make_async_copy(*yes, sem)

        @pl.when(flag)
        def _():
            pltpu.make_async_copy(*yes, sem).start()

        @pl.when(jnp.logical_not(flag))
        def _():
            pltpu.make_async_copy(*no, sem).start()

    def wait(self):
        self.done.wait()


def either_all(sems, first, flag, *choices):
    return [Either(sems.at[first + offset], flag, *choice) for offset, choice in enumerate(choices)]


def wait_all(started):
    for one in started:
        one.wait()


def head_lanes(second):
    lane = lax.broadcasted_iota(jnp.int32, (1, 2 * HD), 1)
    return (lane >= HD) if second else (lane < HD)


def fill_mask(mask_v, seg_row, transposed, slack):
    length = seg_row.shape[1]
    down = jnp.broadcast_to(seg_row, (128, length)).T
    for c in range(length // 128):
        along = seg_row[:, c * 128 : (c + 1) * 128]
        r = lax.broadcasted_iota(jnp.int32, (length, 128), 0)
        q = lax.broadcasted_iota(jnp.int32, (length, 128), 1) + c * 128
        key, query = (r, q) if transposed else (q, r)
        ok = (down == along) & (key <= query + slack)
        mask_v[:, c * 128 : (c + 1) * 128] = jnp.where(ok, 0.0, MASKED)


def fill_toeplitz(toe_v, vec_v, table, bucket_row):
    count = bucket_row.shape[1]
    ids = lax.broadcasted_iota(jnp.int32, (table.shape[1], count), 0)
    onehot = (ids == bucket_row).astype(F32)
    vec = jnp.dot(table, onehot, precision=lax.Precision.HIGHEST, preferred_element_type=F32)
    vec_v[:H, :count] = vec

    @pl.loop(0, H)
    def _(h):
        wide = jnp.broadcast_to(vec_v[pl.ds(h, 1), :], (128, vec_v.shape[1]))
        rolled = pltpu.roll(wide, vec_v.shape[1] - 127, 1, stride=1, stride_axis=0)
        toe_v[h] = rolled[:, : toe_v.shape[2]]


def pair_cols(base, hp):
    return pl.ds(pl.multiple_of(base + hp * 128, 128), 128)


def over_pairs(scores, rest):
    scores(0, 0)

    @pl.loop(0, PAIRS // 2)
    def _(i):
        scores(2 * i + 1, 1)
        rest(2 * i, 0)
        scores(jnp.minimum(2 * i + 2, PAIRS - 1), 0)
        rest(2 * i + 1, 1)


def attend_ahead(q_v, k_v, v_v, q0, k0, v0, mask_v, toe_v, s_v, p_v, mix_v, lse_v, top_v, total_v):
    length = mix_v.shape[0]
    low, high = head_lanes(False), head_lanes(True)
    lane = lax.broadcasted_iota(jnp.int32, (1, 2 * HD), 1)
    top_v[...] = jnp.zeros_like(top_v)
    total_v[...] = jnp.ones_like(total_v)

    def scores(hp, slot):
        q2, k2 = q_v[:, pair_cols(q0, hp)], k_v[:, pair_cols(k0, hp)]
        for a, mine in enumerate((low, high)):
            s_v[2 * slot + a] = mm_nt(jnp.where(mine, q2, jnp.zeros_like(q2)), k2)

    def rest(hp, slot):
        v2 = v_v[:, pair_cols(v0, hp)]
        outs, tops = [], []
        for a, mine in enumerate((low, high)):
            top = []
            for c in range(length // 128):
                rows = pl.ds(c * 128, 128)
                s = s_v[2 * slot + a, rows, :] + mask_v[rows, :]
                if toe_v is not None:
                    left = toe_v.shape[2] - length - c * 128
                    s = s + toe_v[2 * hp + a, :, left : left + length]
                m = jnp.max(s, axis=-1, keepdims=True)
                p_v[2 * slot + a, rows, :] = jnp.exp(s - m).astype(BF16)
                top.append(m)
            tops.append(jnp.concatenate(top, axis=0))
            outs.append(mm(p_v[2 * slot + a], jnp.where(mine, v2, jnp.ones_like(v2))))
        total = pltpu.roll(jnp.where(low, outs[1], outs[0]), HD, 1)
        mix_v[:, pair_cols(0, hp)] = (jnp.where(low, outs[0], outs[1]) / total).astype(BF16)
        first, second = lane == 2 * hp, lane == 2 * hp + 1
        top_v[...] = jnp.where(first, tops[0], jnp.where(second, tops[1], top_v[...]))
        total_v[...] = jnp.where(first, total[:, :1], jnp.where(second, total[:, HD : HD + 1], total_v[...]))

    over_pairs(scores, rest)
    lse_v[...] = (top_v[...] + jnp.log(total_v[...])).T[: lse_v.shape[0], :]


def attend(q_v, k_v, v_v, q0, k0, v0, mask_v, toe_v, s_v, p_v, mix_v, lse_v):
    length = mix_v.shape[0]

    @pl.loop(0, PAIRS)
    def _(hp):
        at = lambda base: pl.ds(pl.multiple_of(base + hp * 128, 128), 128)
        q2, k2, v2 = q_v[:, at(q0)], k_v[:, at(k0)], v_v[:, at(v0)]
        low = head_lanes(False)
        outs, tops = [], []
        for a in range(2):
            mine = head_lanes(a == 1)
            s_v[a] = mm_nt(jnp.where(mine, q2, jnp.zeros_like(q2)), k2)
            top = []
            for c in range(length // 128):
                rows = pl.ds(c * 128, 128)
                s = s_v[a, rows, :] + mask_v[rows, :]
                if toe_v is not None:
                    left = toe_v.shape[2] - length - c * 128
                    s = s + toe_v[2 * hp + a, :, left : left + length]
                m = jnp.max(s, axis=-1, keepdims=True)
                p_v[a, rows, :] = jnp.exp(s - m).astype(BF16)
                top.append(m)
            tops.append(jnp.concatenate(top, axis=0))
            outs.append(mm(p_v[a], jnp.where(mine, v2, jnp.ones_like(v2))))
        total = pltpu.roll(jnp.where(low, outs[1], outs[0]), HD, 1)
        mix_v[:, at(0)] = (jnp.where(low, outs[0], outs[1]) / total).astype(BF16)
        stat = (jnp.where(low, tops[0], tops[1]) + jnp.log(total)).T
        lse_v[pl.ds(2 * hp, 1), :] = stat[0:1, :]
        lse_v[pl.ds(2 * hp + 1, 1), :] = stat[HD : HD + 1, :]


def attend_back(q_v, k_v, v_v, dm_v, mix_v, q0, k0, v0, mask_v, toe_v, lse_v, dp_v, s_v, p_v, ds_v, out_v, o0, acc_v):
    length = mix_v.shape[0]

    @pl.loop(0, PAIRS)
    def _(hp):
        at = lambda base: pl.ds(pl.multiple_of(base + hp * 128, 128), 128)
        q2, k2, v2, dm2 = q_v[:, at(q0)], k_v[:, at(k0)], v_v[:, at(v0)], dm_v[:, at(0)]
        low = head_lanes(False)
        prod = (dm2.astype(F32) * mix_v[:, at(0)].astype(F32)).T
        k2t = k2.T
        dvs, dks, dqs = [], [], []
        for a in range(2):
            mine = head_lanes(a == 1)
            s_v[a] = mm_nt(jnp.where(mine, k2, jnp.zeros_like(k2)), q2)
            dp_v[a] = mm_nt(jnp.where(mine, v2, jnp.zeros_like(v2)), dm2)
            delta = jnp.sum(prod[a * HD : (a + 1) * HD, :], axis=0, keepdims=True)
            lse = lse_v[pl.ds(2 * hp + a, 1), :]
            for c in range(length // 128):
                rows = pl.ds(c * 128, 128)
                s = s_v[a, rows, :] + mask_v[rows, :]
                if toe_v is not None:
                    left = toe_v.shape[2] - length - c * 128
                    s = s + toe_v[2 * hp + a, :, left : left + length]
                p = jnp.exp(s - lse)
                p_v[a, rows, :] = p.astype(BF16)
                ds = p * (dp_v[a, rows, :] - delta)
                ds_v[a, rows, :] = ds.astype(BF16)
                if acc_v is not None:
                    acc_v[2 * hp + a, :, left : left + length] += ds
            dvs.append(mm(p_v[a], dm2))
            dks.append(mm(ds_v[a], q2))
            dqs.append(mm(k2t[a * HD : (a + 1) * HD, :], ds_v[a]))
        out_v[:, at(o0)] = jnp.concatenate(dqs, axis=0).T.astype(BF16)
        out_v[:, at(o0 + PAIRS * 128)] = jnp.where(low, dks[0], dks[1]).astype(BF16)
        out_v[:, at(o0 + 2 * PAIRS * 128)] = jnp.where(low, dvs[0], dvs[1]).astype(BF16)


def fold_diagonals(acc_v, diag_v):

    @pl.loop(0, H, unroll=3)
    def _(h):
        value = jnp.concatenate([acc_v[h], jnp.zeros((128, 128), F32)], axis=1)
        half = 64
        while half >= 1:
            value = pltpu.roll(value[:half], half, 1) + value[half:]
            half //= 2
        diag_v[pl.ds(h, 1), :] = value


def gelu_parts(u):
    square = u * u
    bend = u * (GELU + (GELU * CUBIC) * square)
    half = 0.5 + 0.5 * jnp.tanh(bend)
    hidden = u * half
    slope = half + 2.0 * hidden * (1.0 - half) * (GELU + (3.0 * GELU * CUBIC) * square)
    return hidden, slope


COLUMN_PARTS = 3


def column_parts(sems, first, source, target, parts=COLUMN_PARTS):
    width = target.shape[1] // parts
    cuts = [pl.ds(c * width, width) for c in range(parts)]
    return copy_all(sems, first, *[(source.at[:, cut], target.at[:, cut]) for cut in cuts])


def ffn_up(n_v, win_v, h_v, slope_v, loads=()):
    tile = 512

    @pl.loop(0, win_v.shape[1] // tile)
    def _(t):
        for part, load in enumerate(loads):
            pl.when(t == part * (win_v.shape[1] // tile // len(loads)))(load.wait)

        cols = pl.ds(pl.multiple_of(t * tile, tile), tile)
        hidden, slope = gelu_parts(mm(n_v[...], win_v[:, cols]))
        h_v[:, cols] = hidden.astype(BF16)
        slope_v[:, cols] = slope.astype(BF16)


def rows_out(a_v, w_v, w0, out_v, add):
    tile = 256
    depth = a_v.shape[1]

    @pl.loop(0, w_v.shape[0] // tile)
    def _(t):
        cols = pl.ds(pl.multiple_of(t * tile, tile), tile)
        part = mm_nt(a_v[...], w_v[cols, w0 : w0 + depth])
        if add:
            out_v[:, cols] = out_v[:, cols] + part
        else:
            out_v[:, cols] = part.astype(out_v.dtype)


def ffn_down(d_v, wout_v, slope_v, du_v):
    tile = 512

    @pl.loop(0, wout_v.shape[1] // tile)
    def _(t):
        cols = pl.ds(pl.multiple_of(t * tile, tile), tile)
        grad = mm(d_v[...], wout_v[:, cols])
        du_v[:, cols] = (grad * slope_v[:, cols].astype(F32)).astype(BF16)


def project(a_v, w_v, w0, out_v, o0, width):
    tile = 384

    @pl.loop(0, width // tile)
    def _(t):
        source = pl.ds(pl.multiple_of(w0 + t * tile, 128), tile)
        target = pl.ds(pl.multiple_of(o0 + t * tile, 128), tile)
        out_v[:, target] = mm(a_v[...], w_v[:, source]).astype(out_v.dtype)


def flops_of(matmuls, size):
    return pl.CostEstimate(flops=matmuls * 1000, bytes_accessed=size // 1000, transcendentals=0)


LONG = pl.CostEstimate(flops=60_000_000_000, bytes_accessed=60 << 20, transcendentals=0)

SHORT = pl.CostEstimate(flops=20_000_000_000, bytes_accessed=20 << 20, transcendentals=0)


def shape(dims, kind):
    return jax.ShapeDtypeStruct(dims, kind)


def like(array):
    return shape(array.shape, array.dtype)


def job(kernel, ins, small, outs, scratch, passed=(), result=lambda made: made):
    return dict(kernel=kernel, ins=ins, small=small, outs=outs, scratch=scratch, passed=passed, result=result)


def run(jobs, after=(), cost=None):
    every = lambda key: [array for one in jobs for array in one[key]]
    ins, small, passed, outs, scratch = map(every, ("ins", "small", "passed", "outs", "scratch"))
    space = lambda count, where: [pl.BlockSpec(memory_space=where)] * count

    def body(*refs):
        refs = list(refs)
        take = lambda count: [refs.pop(0) for _ in range(count)]
        held = {"ins": take(len(ins)), "small": take(len(small))}
        take(len(passed) + len(after))
        held["passed"], held["outs"], held["scratch"] = take(len(passed)), take(len(outs)), refs
        for one in jobs:
            own = []
            for key in ("ins", "small", "passed", "outs", "scratch"):
                own += [held[key].pop(0) for _ in one[key]]
            one["kernel"](*own)

    lead = len(ins) + len(small)
    made = pl.pallas_call(
        body,
        out_shape=[like(array) for array in passed] + list(outs),
        in_specs=space(len(ins), pl.ANY) + space(len(small), pltpu.VMEM) + space(len(passed) + len(after), pl.ANY),
        out_specs=space(len(passed) + len(outs), pl.ANY),
        scratch_shapes=scratch,
        input_output_aliases={lead + index: index for index in range(len(passed))},
        compiler_params=pltpu.CompilerParams(vmem_limit_bytes=VMEM_LIMIT),
        cost_estimate=cost or flops_of(1, 1 << 20),
    )(*ins, *small, *passed, *after)
    changed, fresh, results = list(made[: len(passed)]), list(made[len(passed) :]), []
    for one in jobs:
        mine = [changed.pop(0) for _ in one["passed"]] + [fresh.pop(0) for _ in one["outs"]]
        results.append(one["result"](mine))
    return results


def call(kernel, ins, small, outs, scratch, cost, passed=(), after=()):
    return run([job(kernel, ins, small, outs, scratch, passed)], after, cost)[0]


def self_forward(row, x, w, gains, segs, tables, buckets, toe=None):
    length, width = segs.shape[1], x.shape[1]
    dist = 2 * length
    outs = [
        shape((length, width), BF16),
        shape((length, width), BF16),
        shape((length, 3 * width), BF16),
        shape((length, width), BF16),
        shape((16, length), F32),
    ]

    def kernel(x_h, w_h, *refs):
        if row:
            toe_h, *refs = refs
            body(x_h, w_h, *refs[:9], toe_h, *refs[9:])
        else:
            body(x_h, w_h, *refs)

    def body(x_h, w_h, gain_r, seg_r, table_r, bucket_r, e_h, n_h, qkv_h, mix_h, lse_h, toe_h,
               x_v, w_v, n_v, qkv_v, mix_v, lse_v, e_v, mask_v, toe_v, vec_v, s_v, p_v, top_v, total_v, sems):
        section = lax.axis_index("section")

        @pl.when(section % 2 == 0)
        def _():
            side = section // 2
            loads = copy_all(
                sems, 0,
                (x_h.at[pl.ds(row * length, length)], x_v),
                *[(w_h.at[0, :, pl.ds(c * width, width)], w_v.at[:, pl.ds(c * width, width)]) for c in range(4)],
            )
            if row:
                tiles = copy_all(sems, 10, (toe_h, toe_v))
            else:
                fill_toeplitz(toe_v, vec_v, table_r[:, pl.ds(side, 1), :][:, 0, :], bucket_r[pl.ds(side, 1), :])
                tiles = copy_all(sems, 10, (toe_v, toe_h))
            fill_mask(mask_v, seg_r[row : row + 1, :], False, jnp.where(side == 1, 0, 2 * length))
            gain = gain_r[pl.ds(3 * side, 1), :]
            loads[0].wait()
            for rows in row_chunks(length):
                x = x_v[rows, :].astype(F32)
                n_v[rows, :] = (x * inverse_rms(x) * gain).astype(BF16)
            stores = copy_all(sems, 5, (n_v, n_h))
            wait_all(loads[1:4])
            project(n_v, w_v, 0, qkv_v, 0, 3 * width)
            stores += copy_all(sems, 6, (qkv_v, qkv_h))
            if row:
                wait_all(tiles)
            attend_ahead(qkv_v, qkv_v, qkv_v, 0, width, 2 * width, mask_v, toe_v, s_v, p_v, mix_v, lse_v, top_v, total_v)
            stores += copy_all(sems, 7, (mix_v, mix_h), (lse_v, lse_h))
            loads[4].wait()

            @pl.loop(0, width // 256)
            def _(t):
                cols = pl.ds(pl.multiple_of(t * 256, 256), 256)
                part = mm(mix_v[...], w_v[:, pl.ds(pl.multiple_of(3 * width + t * 256, 256), 256)])
                e_v[:, cols] = (x_v[:, cols].astype(F32) + part).astype(BF16)

            stores += copy_all(sems, 9, (e_v, e_h))
            wait_all(stores if row else stores + tiles)

    return call(
        kernel,
        [x, w] + ([toe] if row else []),
        [gains, segs, tables, buckets],
        outs if row else outs + [shape((H, 128, dist - 128), F32)],
        [
            pltpu.VMEM((length, width), BF16),
            pltpu.VMEM((width, 4 * width), BF16),
            pltpu.VMEM((length, width), BF16),
            pltpu.VMEM((length, 3 * width), BF16),
            pltpu.VMEM((length, width), BF16),
            pltpu.VMEM((16, length), F32),
            pltpu.VMEM((length, width), BF16),
            pltpu.VMEM((length, length), F32),
            pltpu.VMEM((H, 128, dist - 128), F32),
            pltpu.VMEM((16, dist), F32),
            pltpu.VMEM((4, length, length), F32),
            pltpu.VMEM((4, length, length), BF16),
            pltpu.VMEM((length, 128), F32),
            pltpu.VMEM((length, 128), F32),
            pltpu.SemaphoreType.DMA((11,)),
        ],
        flops_of(3, 12 << 20),
    )


def transposed_bias(tables, flipped, length, after):
    dist = 2 * length

    def kernel(table_r, bucket_r, toe_h, toe_v, vec_v, sems):
        section = lax.axis_index("section")

        @pl.when(section % 2 == 0)
        def _():
            side = section // 2
            fill_toeplitz(toe_v, vec_v, table_r[:, pl.ds(side, 1), :][:, 0, :], bucket_r[pl.ds(side, 1), :])
            wait_all(copy_all(sems, 0, (toe_v, toe_h)))

    return call(
        kernel,
        [],
        [tables, flipped],
        [shape((H, 128, dist - 128), F32)],
        [pltpu.VMEM((H, 128, dist - 128), F32), pltpu.VMEM((16, dist), F32), pltpu.SemaphoreType.DMA((1,))],
        flops_of(1, 6 << 20),
        after=after,
    )[0]


def marker(after):
    def kernel(out_h):
        pass

    return call(kernel, [], [], [shape((8, 128), F32)], [], flops_of(1, 1 << 20), after=after)[0]


def packed_small(acc, flipped, dgains_s, dgains_e, dgain_d):
    dist, width = acc.shape[2] + 128, dgain_d.shape[1]

    def kernel(acc_h, bucket_r, ds0_r, ds1_r, de0_r, de1_r, dd_r, out_h, acc_v, diag_v, out_v, sems):
        section = lax.axis_index("section")
        side = section // 2
        out_v[...] = jnp.zeros_like(out_v)

        @pl.when(section % 2 == 0)
        def _():
            loads = copy_all(sems, 0, (acc_h, acc_v))
            diag_v[...] = jnp.zeros_like(diag_v)
            wait_all(loads)
            fold_diagonals(acc_v, diag_v)
            ids = lax.broadcasted_iota(jnp.int32, (32, dist), 0)
            onehot = (ids == bucket_r[pl.ds(side, 1), :]).astype(F32)
            part = lax.dot_general(
                diag_v[...], onehot, (((1,), (1,)), ((), ())),
                precision=lax.Precision.HIGHEST, preferred_element_type=F32,
            )
            for own in range(2):
                @pl.when(side == own)
                def _():
                    out_v[3 * own : 3 * own + 1, :] = ds0_r[...] + ds1_r[...]
                    out_v[8:16, 256 * own : 256 * own + 32] = part[:8]
                    out_v[8:16, 256 * own + 128 : 256 * own + 160] = part[8:]

        @pl.when(section == 1)
        def _():
            out_v[1:3, :] = de0_r[...] + de1_r[...]

        @pl.when(side == 1)
        def _():
            out_v[4:7, :] = dd_r[...]

        wait_all(copy_all(sems, 1, (out_v, out_h)))

    return job(
        kernel,
        [acc],
        [flipped, *dgains_s, *dgains_e, dgain_d],
        [shape((16, width), F32)],
        [
            pltpu.VMEM(acc.shape, F32),
            pltpu.VMEM((16, dist), F32),
            pltpu.VMEM((16, width), F32),
            pltpu.SemaphoreType.DMA((2,)),
        ],
        result=lambda made: made[0],
    )


def self_backward(row, sections, ins, mats, gains, segs, toe, g_enc, g_dec, kept, passed, after):
    length, width = segs.shape[1], ins.shape[1]
    dist = 2 * length

    def kernel(x_h, w_h, toe_h, ge_h, gd_h, qkv_h, mix_h, lse_h, gain_r, seg_r, out_h, acc_h, dgain_h, b_h,
               x_v, w_v, qkv_v, mix_v, lse_v, d_v, dm_v, dqkv_v, dn_v, gx_v, dgain_v,
               mask_v, toe_v, acc_v, s_v, dp_v, p_v, ds_v, sems):
        section = lax.axis_index("section")
        side = section // 2

        active = section == sections[0]
        for one in sections[1:]:
            active = active | (section == one)

        @pl.when(active)
        def _():
            loads = either_all(sems, 0, side == 0, ((ge_h, d_v), (gd_h, d_v)))
            loads += copy_all(
                sems, 1,
                (w_h.at[0, :, pl.ds(3 * width, width)], w_v.at[:, pl.ds(3 * width, width)]),
                (mix_h, mix_v),
                (lse_h, lse_v),
                (qkv_h, qkv_v),
                (toe_h, toe_v),
                (w_h.at[0, :, pl.ds(0, 3 * width)], w_v.at[:, pl.ds(0, 3 * width)]),
                (x_h.at[pl.ds(row * length, length)], x_v),
            )
            sums = copy_all(sems, 8, (acc_h, acc_v)) if row else []
            fill_mask(mask_v, seg_r[row : row + 1, :], True, jnp.where(side == 1, 0, 2 * length))
            if not row:
                acc_v[...] = jnp.zeros_like(acc_v)
            gain = gain_r[pl.ds(3 * side, 1), :]
            wait_all(loads[:2])
            stores = copy_all(sems, 9, (d_v, b_h.at[:, pl.ds(3 * width, width)]))
            rows_out(d_v, w_v, 3 * width, dm_v, False)
            wait_all(loads[2:6] + sums)
            attend_back(qkv_v, qkv_v, qkv_v, dm_v, mix_v, 0, width, 2 * width, mask_v, toe_v, lse_v,
                        dp_v, s_v, p_v, ds_v, dqkv_v, 0, acc_v)
            stores += copy_all(sems, 10, (dqkv_v, b_h.at[:, pl.ds(0, 3 * width)]), (acc_v, acc_h))
            wait_all(loads[6:])
            rows_out(dqkv_v, w_v, 0, dn_v, False)
            total = jnp.zeros((1, width), F32)
            for rows in row_chunks(length):
                dx, dgain = rms_back(x_v[rows, :].astype(F32), gain, dn_v[rows, :])
                gx_v[rows, :] = d_v[rows, :].astype(F32) + dx
                total = total + dgain
            dgain_v[...] = total
            stores += copy_all(sems, 12, (gx_v, out_h.at[pl.ds(row * length, length)]), (dgain_v, dgain_h))
            wait_all(stores)

    n, qkv, mix, lse = kept
    return call(
        kernel,
        [ins, mats, toe, g_enc, g_dec, qkv, mix, lse],
        [gains, segs],
        [like(toe), shape((1, width), F32), shape((length, 4 * width), BF16)][len(passed) - 1 :],
        [
            pltpu.VMEM((length, width), BF16),
            pltpu.VMEM((width, 4 * width), BF16),
            pltpu.VMEM((length, 3 * width), BF16),
            pltpu.VMEM((length, width), BF16),
            pltpu.VMEM((16, length), F32),
            pltpu.VMEM((length, width), BF16),
            pltpu.VMEM((length, width), BF16),
            pltpu.VMEM((length, 3 * width), BF16),
            pltpu.VMEM((length, width), F32),
            pltpu.VMEM((length, width), F32),
            pltpu.VMEM((1, width), F32),
            pltpu.VMEM((length, length), F32),
            pltpu.VMEM((H, 128, dist - 128), F32),
            pltpu.VMEM((H, 128, dist - 128), F32),
            pltpu.VMEM((2, length, length), F32),
            pltpu.VMEM((2, length, length), F32),
            pltpu.VMEM((2, length, length), BF16),
            pltpu.VMEM((2, length, length), BF16),
            pltpu.SemaphoreType.DMA((14,)),
        ],
        flops_of(6, 16 << 20),
        passed,
        after,
    )


def encoder_forward(row, e1, mats, gains, out_rows):
    length, width = e1.shape
    hidden = mats.shape[2]
    narrow, wide = shape((length, width), BF16), shape((length, hidden), BF16)
    rows_shape = shape((2 * length, width), F32)
    kept = [narrow, shape((length, width), F32), narrow, wide, wide]

    def kernel(e_h, w_h, gain_r, out_h, send_h, mid_h, n_h, h_h, slope_h,
               e_v, win_v, wout_v, n_v, h_v, slope_v, mid_v, out_v, send_v, sems):
        @pl.when(lax.axis_index("section") == 1)
        def _():
            loads = copy_all(sems, 0, (e_h, e_v))
            win_loads = column_parts(sems, 9, w_h.at[0], win_v)
            loads += copy_all(sems, 1, (w_h.at[1], wout_v))
            loads[0].wait()
            for rows in row_chunks(length):
                x = e_v[rows, :].astype(F32)
                mid_v[rows, :] = x
                n_v[rows, :] = (x * inverse_rms(x) * gain_r[1:2, :]).astype(BF16)
            stores = copy_all(sems, 3, (n_v, n_h))
            ffn_up(n_v, win_v, h_v, slope_v, win_loads)
            stores += copy_all(sems, 4, (h_v, h_h), (slope_v, slope_h))
            loads[1].wait()
            rows_out(h_v, wout_v, 0, mid_v, True)
            stores += copy_all(sems, 8, (mid_v, mid_h))
            for n, rows in enumerate(row_chunks(length)):
                x = mid_v[rows, :]
                y = x * inverse_rms(x) * gain_r[2:3, :]
                out_v[rows, :] = y
                send_v[rows, :] = y.astype(BF16)
                target = pl.ds(row * length + n * ROW_STEP, ROW_STEP)
                stores += copy_all(
                    sems, 12 + 2 * n, (send_v.at[rows], send_h.at[rows]), (out_v.at[rows], out_h.at[target])
                )
            wait_all(stores)

    return call(
        kernel,
        [e1, mats],
        [gains],
        kept if row else [rows_shape] + kept,
        [
            pltpu.VMEM((length, width), BF16),
            pltpu.VMEM((width, hidden), BF16),
            pltpu.VMEM((width, hidden), BF16),
            pltpu.VMEM((length, width), BF16),
            pltpu.VMEM((length, hidden), BF16),
            pltpu.VMEM((length, hidden), BF16),
            pltpu.VMEM((length, width), F32),
            pltpu.VMEM((length, width), F32),
            pltpu.VMEM((length, width), BF16),
            pltpu.SemaphoreType.DMA((20,)),
        ],
        flops_of(2, 20 << 20),
        [out_rows] if row else [],
    )


def encoder_backward(row, ins, extra, e1, mid, slope, mats, gains, after):
    length, width = extra.shape
    hidden = mats.shape[2]

    def kernel(cot_h, extra_h, e_h, mid_h, slope_h, w_h, gain_r, g_h, d_h, du_h, dgain_h,
               cot_v, extra_v, e_v, mid_v, slope_v, win_v, wout_v, d_v, du_v, dn_v, gm_v, g_v, dgain_v, sems):
        @pl.when(lax.axis_index("section") == 1)
        def _():
            loads = copy_all(
                sems, 0,
                (cot_h.at[pl.ds(row * length, length)], cot_v), (extra_h, extra_v), (mid_h, mid_v),
                (w_h.at[1], wout_v), (slope_h, slope_v), (w_h.at[0], win_v), (e_h, e_v),
            )
            wait_all(loads[:3])
            total = jnp.zeros((1, width), F32)
            for rows in row_chunks(length):
                dy = cot_v[rows, :].astype(F32) + extra_v[rows, :].astype(F32)
                dx, dgain = rms_back(mid_v[rows, :], gain_r[2:3, :], dy)
                gm_v[rows, :] = dx
                d_v[rows, :] = dx.astype(BF16)
                total = total + dgain
            dgain_v[1:2, :] = total
            stores = copy_all(sems, 7, (d_v, d_h))
            wait_all(loads[3:5])
            ffn_down(d_v, wout_v, slope_v, du_v)
            stores += copy_all(sems, 8, (du_v, du_h))
            wait_all(loads[5:])
            rows_out(du_v, win_v, 0, dn_v, False)
            total = jnp.zeros((1, width), F32)
            for rows in row_chunks(length):
                dx, dgain = rms_back(e_v[rows, :].astype(F32), gain_r[1:2, :], dn_v[rows, :])
                g_v[rows, :] = (gm_v[rows, :] + dx).astype(BF16)
                total = total + dgain
            dgain_v[0:1, :] = total
            stores += copy_all(sems, 9, (g_v, g_h), (dgain_v, dgain_h))
            wait_all(stores)

    return call(
        kernel,
        [ins, extra, e1, mid, slope, mats],
        [gains],
        [
            shape((length, width), BF16),
            shape((length, width), BF16),
            shape((length, hidden), BF16),
            shape((2, width), F32),
        ],
        [
            pltpu.VMEM((length, width), BF16),
            pltpu.VMEM((length, width), BF16),
            pltpu.VMEM((length, width), BF16),
            pltpu.VMEM((length, width), F32),
            pltpu.VMEM((length, hidden), BF16),
            pltpu.VMEM((width, hidden), BF16),
            pltpu.VMEM((width, hidden), BF16),
            pltpu.VMEM((length, width), BF16),
            pltpu.VMEM((length, hidden), BF16),
            pltpu.VMEM((length, width), F32),
            pltpu.VMEM((length, width), F32),
            pltpu.VMEM((length, width), BF16),
            pltpu.VMEM((2, width), F32),
            pltpu.SemaphoreType.DMA((11,)),
        ],
        flops_of(2, 20 << 20),
        after=after,
    )


def decoder(d_own, d_got, m_two, m_three, ins, cot_got, mats, got_mats, gains, segs, passed, after):
    length, width = d_own.shape
    hidden = mats.shape[2]

    def kernel(d2_h, d3_h, m2_h, m3_h, c1_h, c0_h, w1_h, w0_h, gain_r, seg_r,
               out_h, fa_h, fb_h, fc_h, other_h, gm_h, gd_h, dgain_h,
               d_v, m_v, c_v, wca_v, win_v, wout_v, n_v, q_v, mix_v, lse_v, mask_v, s_v, p_v, h_v, slope_v,
               x_v, y_v, dn_v, n5_v, do_v, dgain_v, dp_v, ds_v, dq_v, dm_v, do4_v, gm_v, gd_v, out_v, sems):
        section = lax.axis_index("section")

        @pl.when(section >= 2)
        def _():
            own = section == 3
            first_row = pl.ds(0, length)

            def put(first, *choices):
                return either_all(sems, first, own, *choices)

            quarters = [pl.ds(c * width, width) for c in range(4)]
            loads = put(0, ((d3_h, d_v), (d2_h, d_v)))
            cross_loads = put(
                21, *[((w1_h.at[0, :, cut], wca_v.at[:, cut]), (w0_h.at[0, :, cut], wca_v.at[:, cut])) for cut in quarters]
            )
            loads += put(
                1,
                ((m3_h, m_v), (m2_h, m_v)),
                *[((w1_h.at[k], v), (w0_h.at[k], v)) for k, v in ((1, win_v), (2, wout_v))],
                ((c1_h.at[first_row], c_v), (c0_h, c_v)),
            )
            fill_mask(mask_v, seg_r[pl.ds(3 - section, 1), :], False, 2 * length)
            loads[0].wait()
            for rows in row_chunks(length):
                x = d_v[rows, :].astype(F32)
                x_v[rows, :] = x
                n_v[rows, :] = (x * inverse_rms(x) * gain_r[4:5, :]).astype(BF16)
            part_of = lambda f_h, n, count=1: f_h.at[:, pl.ds(n * width, count * width)]
            stores = copy_all(sems, 6, (n_v, part_of(fc_h, 0)))
            cross_loads[0].wait()
            project(n_v, wca_v, 0, q_v, 0, width)
            loads[1].wait()
            stores += copy_all(sems, 7, (m_v, part_of(fc_h, 1)))
            wait_all(cross_loads[1:3])
            project(m_v, wca_v, width, q_v, width, 2 * width)
            attend(q_v, q_v, q_v, 0, width, 2 * width, mask_v, None, s_v, p_v, mix_v, lse_v)
            stores += copy_all(sems, 9, (mix_v, part_of(fc_h, 2)))

            cross_loads[3].wait()

            @pl.loop(0, width // 256)
            def _(t):
                cols = pl.ds(pl.multiple_of(t * 256, 256), 256)
                part = mm(mix_v[...], wca_v[:, pl.ds(pl.multiple_of(3 * width + t * 256, 256), 256)])
                x_v[:, cols] = x_v[:, cols] + part

            for rows in row_chunks(length):
                x = x_v[rows, :]
                y_v[rows, :] = x
                n5_v[rows, :] = (x * inverse_rms(x) * gain_r[5:6, :]).astype(BF16)
            stores += copy_all(sems, 10, (n5_v, part_of(fa_h, 0)))
            loads[2].wait()
            ffn_up(n5_v, win_v, h_v, slope_v)
            stores += copy_all(sems, 11, (h_v, part_of(fb_h, 1, 4)))
            loads[3].wait()
            rows_out(h_v, wout_v, 0, y_v, True)
            loads[4].wait()
            total = jnp.zeros((1, width), F32)
            for rows in row_chunks(length):
                y = y_v[rows, :]
                out_v[rows, :] = y * inverse_rms(y) * gain_r[6:7, :]
                dy, dgain = rms_back(y, gain_r[6:7, :], c_v[rows, :].astype(F32))
                total = total + dgain
                do_v[rows, :] = dy.astype(BF16)
                y_v[rows, :] = dy
            dgain_v[2:3, :] = total
            stores += put(12, ((out_v, out_h.at[first_row]), (out_v, other_h)))
            stores += copy_all(sems, 13, (do_v, part_of(fb_h, 0)))
            ffn_down(do_v, wout_v, slope_v, slope_v)
            stores += copy_all(sems, 14, (slope_v, part_of(fa_h, 1, 4)))
            rows_out(slope_v, win_v, 0, dn_v, False)
            total = jnp.zeros((1, width), F32)
            for rows in row_chunks(length):
                dx, dgain = rms_back(x_v[rows, :], gain_r[5:6, :], dn_v[rows, :])
                dx = y_v[rows, :] + dx
                y_v[rows, :] = dx
                do4_v[rows, :] = dx.astype(BF16)
                total = total + dgain
            dgain_v[1:2, :] = total
            stores += copy_all(sems, 15, (do4_v, part_of(fc_h, 6)))
            rows_out(do4_v, wca_v, 3 * width, dm_v, False)
            attend_back(q_v, q_v, q_v, dm_v, mix_v, 0, width, 2 * width, mask_v, None, lse_v,
                        dp_v, s_v, p_v, ds_v, dq_v, 0, None)
            stores += copy_all(sems, 16, (dq_v, part_of(fc_h, 3, 3)))
            rows_out(dq_v.at[:, width:], wca_v, width, gm_v, False)
            stores += copy_all(sems, 18, (gm_v, gm_h))
            rows_out(dq_v.at[:, :width], wca_v, 0, dn_v, False)
            total = jnp.zeros((1, width), F32)
            for rows in row_chunks(length):
                dx, dgain = rms_back(d_v[rows, :].astype(F32), gain_r[4:5, :], dn_v[rows, :])
                gd_v[rows, :] = (y_v[rows, :] + dx).astype(BF16)
                total = total + dgain
            dgain_v[0:1, :] = total
            stores += copy_all(sems, 19, (gd_v, gd_h), (dgain_v, dgain_h))
            wait_all(stores)

    narrow = shape((length, width), BF16)
    return call(
        kernel,
        [d_own, d_got, m_two, m_three, ins, cot_got, mats, got_mats],
        [gains, segs],
        [
            *[shape((length, count * width), BF16) for count in (5, 5, 7)],
            shape((length, width), F32),
            *(narrow, narrow),
            shape((3, width), F32),
        ],
        [
            pltpu.VMEM((length, width), BF16),
            pltpu.VMEM((length, width), BF16),
            pltpu.VMEM((length, width), BF16),
            pltpu.VMEM((width, 4 * width), BF16),
            pltpu.VMEM((width, hidden), BF16),
            pltpu.VMEM((width, hidden), BF16),
            pltpu.VMEM((length, width), BF16),
            pltpu.VMEM((length, 3 * width), BF16),
            pltpu.VMEM((length, width), BF16),
            pltpu.VMEM((16, length), F32),
            pltpu.VMEM((length, length), F32),
            pltpu.VMEM((2, length, length), F32),
            pltpu.VMEM((2, length, length), BF16),
            pltpu.VMEM((length, hidden), BF16),
            pltpu.VMEM((length, hidden), BF16),
            pltpu.VMEM((length, width), F32),
            pltpu.VMEM((length, width), F32),
            pltpu.VMEM((length, width), F32),
            pltpu.VMEM((length, width), BF16),
            pltpu.VMEM((length, width), BF16),
            pltpu.VMEM((3, width), F32),
            pltpu.VMEM((2, length, length), F32),
            pltpu.VMEM((2, length, length), BF16),
            pltpu.VMEM((length, 3 * width), BF16),
            pltpu.VMEM((length, width), BF16),
            pltpu.VMEM((length, width), BF16),
            pltpu.VMEM((length, width), BF16),
            pltpu.VMEM((length, width), BF16),
            pltpu.VMEM((length, width), F32),
            pltpu.SemaphoreType.DMA((25,)),
        ],
        flops_of(12, 30 << 20),
        passed,
        after,
    )


def weight_grad(sections, groups, chunks, ndp, decoder=None, passed=()):
    length, width = groups[0][0][0][0].shape[0], 768
    columns = sum(group[2] for group in groups)
    pieces = len(groups[0][0])
    bits = ndp.bit_length() - 1
    block = width // ndp
    flat = []
    for a_list, b_list, _ in groups + (decoder or []):
        for array, _ in a_list + b_list:
            if not any(array is other for other in flat):
                flat.append(array)
    place = lambda array: [index for index, other in enumerate(flat) if other is array][0]
    plan_of = lambda groups: [
        ([(place(a), a0) for a, a0 in a_list], [(place(b), b0) for b, b0 in b_list], count)
        for a_list, b_list, count in groups
    ]
    plan, other_plan = plan_of(groups), plan_of(decoder or groups)
    tile = 768
    copies = 2 * pieces * len(groups)

    def kernel(*args):
        sources = args[: len(flat)]
        outs = args[len(flat) : len(flat) + 2 * len(chunks)]
        a_v, at_v, b_v, out_v, sems = args[len(flat) + 2 * len(chunks) :]
        me = lax.axis_index("dp")
        section = lax.axis_index("section")
        active = section == sections[0]
        for one in sections[1:]:
            active = active | (section == one)

        @pl.when(active)
        def _():
            loads, start = [], 0
            for g, (a_list, b_list, count) in enumerate(plan):
                group_loads = []
                for k in range(pieces):
                    rows = pl.ds(k * length, length)
                    choices = []
                    for a_of, b_of, _ in (other_plan[g], plan[g]):
                        (ai, a0), (bi, b0) = a_of[k], b_of[k]
                        choices.append((
                            (sources[ai].at[:, pl.ds(a0, width)], a_v.at[g, rows]),
                            (sources[bi].at[:, pl.ds(b0, count)], b_v.at[rows, pl.ds(start, count)]),
                        ))
                    first = 2 * (g * pieces + k)
                    if decoder:
                        group_loads += either_all(sems, first, section >= 2, *zip(*choices))
                    else:
                        group_loads += copy_all(sems, first, *choices[0])
                loads.append(group_loads)
                start += count
            stores, group, group_end, start = [], -1, 0, 0
            for number, (count, order) in enumerate(chunks):
                spots = []
                for b in range(ndp):
                    code = jnp.bitwise_xor(me, b)
                    spot = 0
                    for k in range(bits):
                        spot = spot + ((code >> order[k]) & 1) * (1 << (bits - 1 - k))
                    spots.append(spot)
                done, end = start, start + count
                while done < end:
                    if done == group_end:
                        group += 1
                        wait_all(loads[group])
                        at_v[...] = a_v[group].T
                        group_end += plan[group][2]
                    upto = min(end, group_end)

                    @pl.loop(0, (upto - done) // tile)
                    def _(t):
                        cols = pl.ds(pl.multiple_of(done + t * tile, 128), tile)
                        part = mm(at_v[...], b_v[:, cols])
                        for b in range(ndp):
                            out_v[spots[b], :, cols] = part[b * block : (b + 1) * block, :].astype(BF16)

                    done = upto
                for half in range(2):
                    source = out_v.at[pl.ds(half * (ndp // 2), ndp // 2), :, pl.ds(start, count)]
                    stores += copy_all(sems, copies + 2 * number + half, (source, outs[2 * number + half]))
                start = end
            wait_all(stores)

    return job(
        kernel,
        flat,
        [],
        [] if passed else [shape((ndp // 2, block, count), BF16) for count, _ in chunks for _ in range(2)],
        [
            pltpu.VMEM((len(groups), pieces * length, width), BF16),
            pltpu.VMEM((width, pieces * length), BF16),
            pltpu.VMEM((pieces * length, columns), BF16),
            pltpu.VMEM((ndp, block, columns), BF16),
            pltpu.SemaphoreType.DMA((copies + 2 * len(chunks),)),
        ],
        passed=passed,
        result=lambda made: [(made[2 * number], made[2 * number + 1]) for number in range(len(chunks))],
    )


def along_dp(value, bit, sections, ndp):
    pairs = [(s * ndp + d, s * ndp + (d ^ bit)) for s in sections for d in range(ndp)]
    return lax.ppermute(value, ("section", "dp"), pairs)


def added(items):
    outs, kinds = [], []
    for keep, _, _ in items:
        kind = "sum" if keep.dtype == F32 else "last" if keep.shape[0] == 1 else "half"
        kinds.append(kind)
        if kind == "half":
            outs += [shape((keep.shape[0] // 2,) + keep.shape[1:], BF16)] * 2
        else:
            outs.append(shape(keep.shape if kind == "sum" else keep.shape[1:], F32))

    def kernel(*refs):
        count = len(items)
        sources, rest = refs[: 2 * count], refs[2 * count :]
        targets, rest = rest[: len(outs)], rest[len(outs) :]
        scratch, sems = rest[:-1], rest[-1]
        section = lax.axis_index("section")

        def takes_part(sections):
            active = section == sections[0]
            for one in sections[1:]:
                active = active | (section == one)
            return active

        for number, item in enumerate(items):
            @pl.when(takes_part(item[2]))
            def _():
                for k in range(2):
                    pltpu.make_async_copy(
                        sources[2 * number + k], scratch[3 * number + k], sems.at[4 * number + k]
                    ).start()

        place = 0
        for number, (item, kind) in enumerate(zip(items, kinds)):
            n = item[0].shape[0]
            keep_v, got_v, out_v = scratch[3 * number : 3 * number + 3]
            mine = targets[place : place + (2 if kind == "half" else 1)]
            place += len(mine)

            @pl.when(takes_part(item[2]))
            def _():
                for k, v in enumerate((keep_v, got_v)):
                    pltpu.make_async_copy(sources[2 * number + k], v, sems.at[4 * number + k]).wait()
                if kind == "half":
                    @pl.loop(0, n)
                    def _(i):
                        out_v[i] = (keep_v[i].astype(F32) + got_v[i].astype(F32)).astype(BF16)

                    wait_all(
                        copy_all(
                            sems, 4 * number + 2,
                            (out_v.at[pl.ds(0, n // 2)], mine[0]), (out_v.at[pl.ds(n // 2, n // 2)], mine[1]),
                        )
                    )
                else:
                    if kind == "last":
                        out_v[...] = keep_v[0].astype(F32) + got_v[0].astype(F32)
                    else:
                        out_v[...] = keep_v[...] + got_v[...]
                    wait_all(copy_all(sems, 4 * number + 2, (out_v, mine[0])))

    scratch = []
    for (keep, _, _), kind in zip(items, kinds):
        own = pltpu.VMEM(keep.shape, keep.dtype)
        scratch += [own, own, pltpu.VMEM(keep.shape[1:], F32) if kind == "last" else own]
    def result(made):
        results = []
        for kind in kinds:
            size = 2 if kind == "half" else 1
            results.append(tuple(made[:size]) if size == 2 else made[0])
            made = made[size:]
        return results

    return job(
        kernel,
        [array for keep, got, _ in items for array in (keep, got)],
        [],
        outs,
        scratch + [pltpu.SemaphoreType.DMA((4 * len(items),))],
        result=result,
    )


def joined(v, pieces):
    start = 0
    for piece in pieces:
        yield piece, v.at[:, pl.ds(start, piece.shape[1])]
        start += piece.shape[1]


def outputs(one, two, three, rows_got, out_rows, after):
    length, width = rows_got.shape
    block, columns = two[0].shape[0], 2 * two[0].shape[1]

    def kernel(a_h, b_h, s0_h, s1_h, c0_h, c1_h, r_h, out_h, grad_h, f_v, s_v, c_v, r_v, sems):
        section = lax.axis_index("section")
        even = section % 2 == 0
        loads = copy_all(sems, 0, *joined(f_v, (a_h, b_h)))

        @pl.when(section == 3)
        def _():
            wait_all(copy_all(sems, 9, *joined(s_v, (s0_h, s1_h)), *joined(c_v, (c0_h, c1_h)), (r_h, r_v)))
            wait_all(loads)
            wait_all(
                copy_all(
                    sems, 5,
                    (f_v, grad_h.at[1]), (s_v, grad_h.at[2]), (c_v, grad_h.at[0]), (r_v, out_h.at[pl.ds(length, length)]),
                )
            )

        @pl.when(section != 3)
        def _():
            c_v[...] = jnp.zeros_like(c_v)
            stores = copy_all(sems, 5, (c_v, grad_h.at[2]))

            @pl.when(section == 1)
            def _():
                wait_all(copy_all(sems, 9, *joined(s_v, (s0_h, s1_h))))
                wait_all(copy_all(sems, 3, (s_v, grad_h.at[1])))

            @pl.when(even)
            def _():
                wait_all(copy_all(sems, 3, (c_v, grad_h.at[1])))

            wait_all(loads)
            wait_all(stores + copy_all(sems, 6, (f_v, grad_h.at[0])))

    return call(
        kernel,
        [*one, *two, *three, rows_got],
        [],
        [shape((3, block, columns), F32)],
        [pltpu.VMEM((block, columns), F32)] * 3 + [pltpu.VMEM((length, width), F32), pltpu.SemaphoreType.DMA((14,))],
        flops_of(1, 1 << 20),
        [out_rows],
        after,
    )


def per_device(section_ins, segments, buckets, section_mats, gains, tables):
    ndp = lax.axis_size("dp")
    ins = section_ins[0]
    mats = section_mats[0]
    length = segments.shape[1]
    width = ins.shape[1]
    segs = segments
    by_head = jnp.transpose(tables, (2, 0, 1))
    flipped = jnp.pad(buckets[:, ::-1], ((0, 0), (0, 1)), constant_values=-1)
    everywhere = (0, 1, 2, 3)
    move = lambda value, pairs: lax.ppermute(value, "section", pairs)

    got_mats = move(section_mats, [(3, 2), (1, 0)])[0]
    *fwd0, tiles = self_forward(0, ins, mats, gains, segs, by_head, buckets)
    first0 = move(fwd0[0], [(0, 1), (2, 3)])
    fwd1 = self_forward(1, ins, mats, gains, segs, by_head, buckets, tiles)
    first1 = move(fwd1[0], [(0, 1)])
    toe = transposed_bias(by_head, flipped, length, [fwd1[0]])
    out_rows, *enc0 = encoder_forward(0, first0, mats, gains, None)
    m_three = move(enc0[0], [(1, 3)])
    late_ins, _ = lax.optimization_barrier((ins, m_three))
    cot_got = move(late_ins[length:], [(3, 2)])
    out_rows, *enc1 = encoder_forward(1, first1, mats, gains, out_rows)
    m_two = move(enc1[0], [(1, 2)])
    here = marker([enc1[0], m_three])

    dec = decoder(fwd1[0], first0, m_two, m_three, ins, cot_got, mats, got_mats, gains, segs, [out_rows], [toe, here])
    out_rows, *factors, other, g_mem, g_self, dgain_d = dec
    even, odd = (0, 2), (1, 3)
    extra0 = move(g_mem, [(3, 1)])
    extra1 = move(g_mem, [(2, 0)])
    (sent, g_self_sent), _ = lax.optimization_barrier(((factors, g_self), extra0))
    got = [move(value, [(2, 3)]) for value in sent]
    g_self_got = move(g_self_sent, [(3, 2)])
    back0 = encoder_backward(0, ins, extra0, first0, enc0[1], enc0[4], mats, gains, [extra1])
    g0 = move(back0[0], [(1, 0)])
    (other, extra1), _ = lax.optimization_barrier(((other, extra1), back0[0]))
    extra1 = move(extra1, [(0, 1)])
    own0 = self_backward(
        0, even, ins, mats, gains, segs, toe, g0, g_self_got, fwd0[1:], [out_rows], [extra1]
    )
    out_rows, acc = own0[:2]
    back1 = encoder_backward(1, ins, extra1, first1, enc1[1], enc1[4], mats, gains, [acc])
    other, _ = lax.optimization_barrier((other, back1[0]))
    rows_got = move(other, [(2, 3)])

    plain = tuple(range(ndp.bit_length() - 1))
    turned = (1, 0) + plain[2:]
    orders = (plain, turned)
    steps = len(plain)
    whole = 4 * width
    rows_of = lambda which, at: [(factors[which], at * width), (got[which], at * width)]
    halves = [(2 * width, order) for order in orders]
    groups = [([(enc0[2], 0), (enc1[2], 0)], [(back0[2], 0), (back1[2], 0)], whole)]
    groups_d = [(rows_of(0, 0), rows_of(0, 1), whole)]
    made, = run([weight_grad(odd, groups, halves, ndp, groups_d)], [back1[0]])
    g1, _ = lax.optimization_barrier((back1[0], made[0][0]))
    g1 = move(g1, [(1, 0)])
    own1 = self_backward(
        1, even, ins, mats, gains, segs, toe, g1, g_self, fwd1[1:], [out_rows, acc], [made[0][0]]
    )
    out_rows, acc = own1[:2]
    groups = [
        ([(fwd0[1], 0), (fwd1[1], 0)], [(own0[3], 0), (own1[3], 0)], 3 * width),
        ([(fwd0[3], 0), (fwd1[3], 0)], [(own0[3], 3 * width), (own1[3], 3 * width)], width),
    ]
    made, = run([weight_grad(even, groups, halves, ndp, passed=[*made[0], *made[1]])], [out_rows])

    def send(pair, order, step, sections):
        return (pair[0], along_dp(pair[1], 1 << order[step], sections, ndp), sections)

    def send_one(pairs, step):
        return [send(pair, order, step, everywhere) for pair, order in zip(pairs, orders)]

    def send_rest(pairs, part, step):
        sections = odd if part == 1 else (3,)
        return [send(pair, order, step, sections) for pair, order in zip(pairs, orders)]

    one = send_one(made, 0)
    groups = [([(back0[1], 0), (back1[1], 0)], [(enc0[3], 0), (enc1[3], 0)], whole)]
    groups_d = [(rows_of(1, 0), rows_of(1, 1), whole)]
    two, = run([weight_grad(odd, groups, halves, ndp, groups_d)], [made[0][0]])
    groups = [(rows_of(2, k), rows_of(2, at), count * width) for k, at, count in ((0, 3, 1), (1, 4, 2), (2, 6, 1))]
    three, = run([weight_grad((3,), groups, halves, ndp)], [two[0][0]])
    rest = [send_rest(two, 1, 0), send_rest(three, 2, 0)]
    dgains = ([own0[2], own1[2]], [back0[3], back1[3]], dgain_d)
    small, = run([packed_small(acc, flipped, *dgains)], [three[0][0]])
    small_got = along_dp(small, 1, everywhere, ndp)
    tied = [small]
    sums_of = [one, *rest]
    turns = [(2 * k + (0, 1, 2.5)[part], k, part) for k in range(steps) for part in range(3)]
    for _, k, part in sorted(turns):
        last = k + 1 == steps
        items = sums_of[part]
        cost = SHORT if part < 2 and not last else None if part == 2 else LONG
        number = 2 * k + part
        if part < 2 and number < steps:
            (*sums, small), = run([added([*items, (small, small_got, everywhere)])], tied, cost)
            if number + 1 < steps:
                small_got = along_dp(small, 2 << number, everywhere, ndp)
        else:
            sums, = run([added(items)], tied, cost)
        tied = [sums[0] if last else sums[0][0]]
        if not last:
            sums = send_one(sums, k + 1) if not part else send_rest(sums, part, k + 1)
        sums_of[part] = sums
    one, *rest = sums_of
    small, _ = lax.optimization_barrier((small, tied[0]))
    small = small + move(small, [(0, 1), (1, 0), (2, 3), (3, 2)])
    small = small + move(small, [(0, 2), (2, 0), (1, 3), (3, 1)])
    out_rows, grad = outputs(one, *rest, rows_got, out_rows, tied)

    gains_grad = small[: gains.shape[0]]
    heads = [
        jnp.concatenate([small[8:16, at : at + 32], small[8:12, at + 128 : at + 160]], axis=0)
        for at in range(0, 256 * tables.shape[0], 256)
    ]
    return out_rows[None], grad[None], gains_grad, jnp.swapaxes(jnp.stack(heads), 1, 2)


def solution(mesh):
    placed = (
        P("section", "dp", None),
        P("dp", None),
        P(),
        P("section", None, None, None),
        P(),
        P(),
    )
    return jax.shard_map(
        per_device,
        mesh=mesh,
        in_specs=placed,
        out_specs=(P("section", "dp", None), P("section", None, "dp", None), P(), P()),
        check_vma=False,
    )
```

```python
from functools import partial

import jax
import jax.numpy as jnp
from jax import lax
from jax.experimental import pallas as pl
from jax.experimental.pallas import tpu as pltpu
from jax.sharding import PartitionSpec as P

H = 12
HD = 64
PAIRS = H // 2
EPS = 1e-06
GELU = 0.7978845608028654
CUBIC = 0.044715
MASKED = -1e38
F32 = jnp.float32
BF16 = jnp.bfloat16
ROW_STEP = 128
VMEM_LIMIT = 60 * 1024 * 1024


def mm(a, b):
    return jnp.dot(a, b, preferred_element_type=F32)


def mm_nt(a, b):
    return lax.dot_general(a, b, (((1,), (1,)), ((), ())), preferred_element_type=F32)


def inverse_rms(x):
    return lax.rsqrt(jnp.mean(x * x, axis=-1, keepdims=True) + EPS)


def row_chunks(length):
    return [pl.ds(start, ROW_STEP) for start in range(0, length, ROW_STEP)]


def rms_back(x, gain, dy):
    r = inverse_rms(x)
    inner = jnp.mean(dy * gain * x, axis=-1, keepdims=True)
    dx = r * gain * dy - x * (r * r * r) * inner
    return dx, jnp.sum(dy * x * r, axis=0, keepdims=True)


def copy_all(sems, first, *pairs):
    started = []
    for offset, (source, target) in enumerate(pairs):
        one = pltpu.make_async_copy(source, target, sems.at[first + offset])
        one.start()
        started.append(one)
    return started


class Either:
    def __init__(self, sem, flag, yes, no):
        self.done = pltpu.make_async_copy(*yes, sem)

        @pl.when(flag)
        def _():
            pltpu.make_async_copy(*yes, sem).start()

        @pl.when(jnp.logical_not(flag))
        def _():
            pltpu.make_async_copy(*no, sem).start()

    def wait(self):
        self.done.wait()


def either_all(sems, first, flag, *choices):
    return [Either(sems.at[first + offset], flag, *choice) for offset, choice in enumerate(choices)]


def wait_all(started):
    for one in started:
        one.wait()


def head_lanes(second):
    lane = lax.broadcasted_iota(jnp.int32, (1, 2 * HD), 1)
    return (lane >= HD) if second else (lane < HD)


def fill_mask(mask_v, seg_row, transposed, slack):
    length = seg_row.shape[1]
    down = jnp.broadcast_to(seg_row, (128, length)).T
    for c in range(length // 128):
        along = seg_row[:, c * 128 : (c + 1) * 128]
        r = lax.broadcasted_iota(jnp.int32, (length, 128), 0)
        q = lax.broadcasted_iota(jnp.int32, (length, 128), 1) + c * 128
        key, query = (r, q) if transposed else (q, r)
        ok = (down == along) & (key <= query + slack)
        mask_v[:, c * 128 : (c + 1) * 128] = jnp.where(ok, 0.0, MASKED)


def fill_toeplitz(toe_v, vec_v, table, bucket_row):
    count = bucket_row.shape[1]
    ids = lax.broadcasted_iota(jnp.int32, (table.shape[1], count), 0)
    onehot = (ids == bucket_row).astype(F32)
    vec = jnp.dot(table, onehot, precision=lax.Precision.HIGHEST, preferred_element_type=F32)
    vec_v[:H, :count] = vec

    @pl.loop(0, H)
    def _(h):
        wide = jnp.broadcast_to(vec_v[pl.ds(h, 1), :], (128, vec_v.shape[1]))
        rolled = pltpu.roll(wide, vec_v.shape[1] - 127, 1, stride=1, stride_axis=0)
        toe_v[h] = rolled[:, : toe_v.shape[2]]


def pair_cols(base, hp):
    return pl.ds(pl.multiple_of(base + hp * 128, 128), 128)


def over_pairs(scores, rest):
    scores(0, 0)

    @pl.loop(0, PAIRS // 2)
    def _(i):
        scores(2 * i + 1, 1)
        rest(2 * i, 0)
        scores(jnp.minimum(2 * i + 2, PAIRS - 1), 0)
        rest(2 * i + 1, 1)


def attend_ahead(q_v, k_v, v_v, q0, k0, v0, mask_v, toe_v, s_v, p_v, mix_v, lse_v, top_v, total_v):
    length = mix_v.shape[0]
    low, high = head_lanes(False), head_lanes(True)
    lane = lax.broadcasted_iota(jnp.int32, (1, 2 * HD), 1)
    top_v[...] = jnp.zeros_like(top_v)
    total_v[...] = jnp.ones_like(total_v)

    def scores(hp, slot):
        q2, k2 = q_v[:, pair_cols(q0, hp)], k_v[:, pair_cols(k0, hp)]
        for a, mine in enumerate((low, high)):
            s_v[2 * slot + a] = mm_nt(jnp.where(mine, q2, jnp.zeros_like(q2)), k2)

    def rest(hp, slot):
        v2 = v_v[:, pair_cols(v0, hp)]
        outs, tops = [], []
        for a, mine in enumerate((low, high)):
            top = []
            for c in range(length // 128):
                rows = pl.ds(c * 128, 128)
                s = s_v[2 * slot + a, rows, :] + mask_v[rows, :]
                if toe_v is not None:
                    left = toe_v.shape[2] - length - c * 128
                    s = s + toe_v[2 * hp + a, :, left : left + length]
                m = jnp.max(s, axis=-1, keepdims=True)
                p_v[2 * slot + a, rows, :] = jnp.exp(s - m).astype(BF16)
                top.append(m)
            tops.append(jnp.concatenate(top, axis=0))
            outs.append(mm(p_v[2 * slot + a], jnp.where(mine, v2, jnp.ones_like(v2))))
        total = pltpu.roll(jnp.where(low, outs[1], outs[0]), HD, 1)
        mix_v[:, pair_cols(0, hp)] = (jnp.where(low, outs[0], outs[1]) / total).astype(BF16)
        first, second = lane == 2 * hp, lane == 2 * hp + 1
        top_v[...] = jnp.where(first, tops[0], jnp.where(second, tops[1], top_v[...]))
        total_v[...] = jnp.where(first, total[:, :1], jnp.where(second, total[:, HD : HD + 1], total_v[...]))

    over_pairs(scores, rest)
    lse_v[...] = (top_v[...] + jnp.log(total_v[...])).T[: lse_v.shape[0], :]


def attend(q_v, k_v, v_v, q0, k0, v0, mask_v, toe_v, s_v, p_v, mix_v, lse_v):
    length = mix_v.shape[0]

    @pl.loop(0, PAIRS)
    def _(hp):
        at = lambda base: pl.ds(pl.multiple_of(base + hp * 128, 128), 128)
        q2, k2, v2 = q_v[:, at(q0)], k_v[:, at(k0)], v_v[:, at(v0)]
        low = head_lanes(False)
        outs, tops = [], []
        for a in range(2):
            mine = head_lanes(a == 1)
            s_v[a] = mm_nt(jnp.where(mine, q2, jnp.zeros_like(q2)), k2)
            top = []
            for c in range(length // 128):
                rows = pl.ds(c * 128, 128)
                s = s_v[a, rows, :] + mask_v[rows, :]
                if toe_v is not None:
                    left = toe_v.shape[2] - length - c * 128
                    s = s + toe_v[2 * hp + a, :, left : left + length]
                m = jnp.max(s, axis=-1, keepdims=True)
                p_v[a, rows, :] = jnp.exp(s - m).astype(BF16)
                top.append(m)
            tops.append(jnp.concatenate(top, axis=0))
            outs.append(mm(p_v[a], jnp.where(mine, v2, jnp.ones_like(v2))))
        total = pltpu.roll(jnp.where(low, outs[1], outs[0]), HD, 1)
        mix_v[:, at(0)] = (jnp.where(low, outs[0], outs[1]) / total).astype(BF16)
        stat = (jnp.where(low, tops[0], tops[1]) + jnp.log(total)).T
        lse_v[pl.ds(2 * hp, 1), :] = stat[0:1, :]
        lse_v[pl.ds(2 * hp + 1, 1), :] = stat[HD : HD + 1, :]


def attend_back(q_v, k_v, v_v, dm_v, mix_v, q0, k0, v0, mask_v, toe_v, lse_v, dp_v, s_v, p_v, ds_v, out_v, o0, acc_v):
    length = mix_v.shape[0]

    @pl.loop(0, PAIRS)
    def _(hp):
        at = lambda base: pl.ds(pl.multiple_of(base + hp * 128, 128), 128)
        q2, k2, v2, dm2 = q_v[:, at(q0)], k_v[:, at(k0)], v_v[:, at(v0)], dm_v[:, at(0)]
        low = head_lanes(False)
        prod = (dm2.astype(F32) * mix_v[:, at(0)].astype(F32)).T
        k2t = k2.T
        dvs, dks, dqs = [], [], []
        for a in range(2):
            mine = head_lanes(a == 1)
            s_v[a] = mm_nt(jnp.where(mine, k2, jnp.zeros_like(k2)), q2)
            dp_v[a] = mm_nt(jnp.where(mine, v2, jnp.zeros_like(v2)), dm2)
            delta = jnp.sum(prod[a * HD : (a + 1) * HD, :], axis=0, keepdims=True)
            lse = lse_v[pl.ds(2 * hp + a, 1), :]
            for c in range(length // 128):
                rows = pl.ds(c * 128, 128)
                s = s_v[a, rows, :] + mask_v[rows, :]
                if toe_v is not None:
                    left = toe_v.shape[2] - length - c * 128
                    s = s + toe_v[2 * hp + a, :, left : left + length]
                p = jnp.exp(s - lse)
                p_v[a, rows, :] = p.astype(BF16)
                ds = p * (dp_v[a, rows, :] - delta)
                ds_v[a, rows, :] = ds.astype(BF16)
                if acc_v is not None:
                    acc_v[2 * hp + a, :, left : left + length] += ds
            dvs.append(mm(p_v[a], dm2))
            dks.append(mm(ds_v[a], q2))
            dqs.append(mm(k2t[a * HD : (a + 1) * HD, :], ds_v[a]))
        out_v[:, at(o0)] = jnp.concatenate(dqs, axis=0).T.astype(BF16)
        out_v[:, at(o0 + PAIRS * 128)] = jnp.where(low, dks[0], dks[1]).astype(BF16)
        out_v[:, at(o0 + 2 * PAIRS * 128)] = jnp.where(low, dvs[0], dvs[1]).astype(BF16)


def fold_diagonals(acc_v, diag_v):

    @pl.loop(0, H, unroll=3)
    def _(h):
        value = jnp.concatenate([acc_v[h], jnp.zeros((128, 128), F32)], axis=1)
        half = 64
        while half >= 1:
            value = pltpu.roll(value[:half], half, 1) + value[half:]
            half //= 2
        diag_v[pl.ds(h, 1), :] = value


def gelu_parts(u):
    square = u * u
    bend = u * (GELU + (GELU * CUBIC) * square)
    half = 0.5 + 0.5 * jnp.tanh(bend)
    hidden = u * half
    slope = half + 2.0 * hidden * (1.0 - half) * (GELU + (3.0 * GELU * CUBIC) * square)
    return hidden, slope


COLUMN_PARTS = 3


def column_parts(sems, first, source, target, parts=COLUMN_PARTS):
    width = target.shape[1] // parts
    cuts = [pl.ds(c * width, width) for c in range(parts)]
    return copy_all(sems, first, *[(source.at[:, cut], target.at[:, cut]) for cut in cuts])


def ffn_up(n_v, win_v, h_v, slope_v, loads=()):
    tile = 1024

    @pl.loop(0, win_v.shape[1] // tile)
    def _(t):
        for part, load in enumerate(loads):
            pl.when(t == part * (win_v.shape[1] // tile // len(loads)))(load.wait)

        cols = pl.ds(pl.multiple_of(t * tile, tile), tile)
        hidden, slope = gelu_parts(mm(n_v[...], win_v[:, cols]))
        h_v[:, cols] = hidden.astype(BF16)
        slope_v[:, cols] = slope.astype(BF16)


def rows_out(a_v, w_v, w0, out_v, add):
    tile = 256
    depth = a_v.shape[1]

    @pl.loop(0, w_v.shape[0] // tile)
    def _(t):
        cols = pl.ds(pl.multiple_of(t * tile, tile), tile)
        part = mm_nt(a_v[...], w_v[cols, w0 : w0 + depth])
        if add:
            out_v[:, cols] = out_v[:, cols] + part
        else:
            out_v[:, cols] = part.astype(out_v.dtype)


def ffn_down(d_v, wout_v, slope_v, du_v):
    tile = 1024

    @pl.loop(0, wout_v.shape[1] // tile)
    def _(t):
        cols = pl.ds(pl.multiple_of(t * tile, tile), tile)
        grad = mm(d_v[...], wout_v[:, cols])
        du_v[:, cols] = (grad * slope_v[:, cols].astype(F32)).astype(BF16)


def project(a_v, w_v, w0, out_v, o0, width):
    tile = 768

    @pl.loop(0, width // tile)
    def _(t):
        source = pl.ds(pl.multiple_of(w0 + t * tile, 128), tile)
        target = pl.ds(pl.multiple_of(o0 + t * tile, 128), tile)
        out_v[:, target] = mm(a_v[...], w_v[:, source]).astype(out_v.dtype)


def flops_of(matmuls, size):
    return pl.CostEstimate(flops=matmuls * 1000, bytes_accessed=size // 1000, transcendentals=0)


LONG = pl.CostEstimate(flops=60_000_000_000, bytes_accessed=60 << 20, transcendentals=0)

SHORT = pl.CostEstimate(flops=20_000_000_000, bytes_accessed=20 << 20, transcendentals=0)


def shape(dims, kind):
    return jax.ShapeDtypeStruct(dims, kind)


def like(array):
    return shape(array.shape, array.dtype)


def job(kernel, ins, small, outs, scratch, passed=(), result=lambda made: made):
    return dict(kernel=kernel, ins=ins, small=small, outs=outs, scratch=scratch, passed=passed, result=result)


def run(jobs, after=(), cost=None):
    every = lambda key: [array for one in jobs for array in one[key]]
    ins, small, passed, outs, scratch = map(every, ("ins", "small", "passed", "outs", "scratch"))
    space = lambda count, where: [pl.BlockSpec(memory_space=where)] * count

    def body(*refs):
        refs = list(refs)
        take = lambda count: [refs.pop(0) for _ in range(count)]
        held = {"ins": take(len(ins)), "small": take(len(small))}
        take(len(passed) + len(after))
        held["passed"], held["outs"], held["scratch"] = take(len(passed)), take(len(outs)), refs
        for one in jobs:
            own = []
            for key in ("ins", "small", "passed", "outs", "scratch"):
                own += [held[key].pop(0) for _ in one[key]]
            one["kernel"](*own)

    lead = len(ins) + len(small)
    made = pl.pallas_call(
        body,
        out_shape=[like(array) for array in passed] + list(outs),
        in_specs=space(len(ins), pl.ANY) + space(len(small), pltpu.VMEM) + space(len(passed) + len(after), pl.ANY),
        out_specs=space(len(passed) + len(outs), pl.ANY),
        scratch_shapes=scratch,
        input_output_aliases={lead + index: index for index in range(len(passed))},
        compiler_params=pltpu.CompilerParams(vmem_limit_bytes=VMEM_LIMIT),
        cost_estimate=cost or flops_of(1, 1 << 20),
    )(*ins, *small, *passed, *after)
    changed, fresh, results = list(made[: len(passed)]), list(made[len(passed) :]), []
    for one in jobs:
        mine = [changed.pop(0) for _ in one["passed"]] + [fresh.pop(0) for _ in one["outs"]]
        results.append(one["result"](mine))
    return results


def call(kernel, ins, small, outs, scratch, cost, passed=(), after=()):
    return run([job(kernel, ins, small, outs, scratch, passed)], after, cost)[0]


def self_forward(row, x, w, gains, segs, tables, buckets, toe=None):
    length, width = segs.shape[1], x.shape[1]
    dist = 2 * length
    outs = [
        shape((length, width), BF16),
        shape((length, width), BF16),
        shape((length, 3 * width), BF16),
        shape((length, width), BF16),
        shape((16, length), F32),
    ]

    def kernel(x_h, w_h, *refs):
        if row:
            toe_h, *refs = refs
            body(x_h, w_h, *refs[:9], toe_h, *refs[9:])
        else:
            body(x_h, w_h, *refs)

    def body(x_h, w_h, gain_r, seg_r, table_r, bucket_r, e_h, n_h, qkv_h, mix_h, lse_h, toe_h,
               x_v, w_v, n_v, qkv_v, mix_v, lse_v, e_v, mask_v, toe_v, vec_v, s_v, p_v, top_v, total_v, sems):
        section = lax.axis_index("section")

        @pl.when(section % 2 == 0)
        def _():
            side = section // 2
            loads = copy_all(
                sems, 0,
                (x_h.at[pl.ds(row * length, length)], x_v),
                *[(w_h.at[0, :, pl.ds(c * width, width)], w_v.at[:, pl.ds(c * width, width)]) for c in range(4)],
            )
            if row:
                tiles = copy_all(sems, 10, (toe_h, toe_v))
            else:
                fill_toeplitz(toe_v, vec_v, table_r[:, pl.ds(side, 1), :][:, 0, :], bucket_r[pl.ds(side, 1), :])
                tiles = copy_all(sems, 10, (toe_v, toe_h))
            fill_mask(mask_v, seg_r[row : row + 1, :], False, jnp.where(side == 1, 0, 2 * length))
            gain = gain_r[pl.ds(3 * side, 1), :]
            loads[0].wait()
            for rows in row_chunks(length):
                x = x_v[rows, :].astype(F32)
                n_v[rows, :] = (x * inverse_rms(x) * gain).astype(BF16)
            stores = copy_all(sems, 5, (n_v, n_h))
            wait_all(loads[1:4])
            project(n_v, w_v, 0, qkv_v, 0, 3 * width)
            stores += copy_all(sems, 6, (qkv_v, qkv_h))
            if row:
                wait_all(tiles)
            attend_ahead(qkv_v, qkv_v, qkv_v, 0, width, 2 * width, mask_v, toe_v, s_v, p_v, mix_v, lse_v, top_v, total_v)
            stores += copy_all(sems, 7, (mix_v, mix_h), (lse_v, lse_h))
            loads[4].wait()

            @pl.loop(0, width // 256)
            def _(t):
                cols = pl.ds(pl.multiple_of(t * 256, 256), 256)
                part = mm(mix_v[...], w_v[:, pl.ds(pl.multiple_of(3 * width + t * 256, 256), 256)])
                e_v[:, cols] = (x_v[:, cols].astype(F32) + part).astype(BF16)

            stores += copy_all(sems, 9, (e_v, e_h))
            wait_all(stores if row else stores + tiles)

    return call(
        kernel,
        [x, w] + ([toe] if row else []),
        [gains, segs, tables, buckets],
        outs if row else outs + [shape((H, 128, dist - 128), F32)],
        [
            pltpu.VMEM((length, width), BF16),
            pltpu.VMEM((width, 4 * width), BF16),
            pltpu.VMEM((length, width), BF16),
            pltpu.VMEM((length, 3 * width), BF16),
            pltpu.VMEM((length, width), BF16),
            pltpu.VMEM((16, length), F32),
            pltpu.VMEM((length, width), BF16),
            pltpu.VMEM((length, length), F32),
            pltpu.VMEM((H, 128, dist - 128), F32),
            pltpu.VMEM((16, dist), F32),
            pltpu.VMEM((4, length, length), F32),
            pltpu.VMEM((4, length, length), BF16),
            pltpu.VMEM((length, 128), F32),
            pltpu.VMEM((length, 128), F32),
            pltpu.SemaphoreType.DMA((11,)),
        ],
        flops_of(3, 12 << 20),
    )


def transposed_bias(tables, flipped, length, after):
    dist = 2 * length

    def kernel(table_r, bucket_r, toe_h, toe_v, vec_v, sems):
        section = lax.axis_index("section")

        @pl.when(section % 2 == 0)
        def _():
            side = section // 2
            fill_toeplitz(toe_v, vec_v, table_r[:, pl.ds(side, 1), :][:, 0, :], bucket_r[pl.ds(side, 1), :])
            wait_all(copy_all(sems, 0, (toe_v, toe_h)))

    return call(
        kernel,
        [],
        [tables, flipped],
        [shape((H, 128, dist - 128), F32)],
        [pltpu.VMEM((H, 128, dist - 128), F32), pltpu.VMEM((16, dist), F32), pltpu.SemaphoreType.DMA((1,))],
        flops_of(1, 6 << 20),
        after=after,
    )[0]


def marker(after):
    def kernel(out_h):
        pass

    return call(kernel, [], [], [shape((8, 128), F32)], [], flops_of(1, 1 << 20), after=after)[0]


def packed_small(acc, flipped, dgains_s, dgains_e, dgain_d):
    dist, width = acc.shape[2] + 128, dgain_d.shape[1]

    def kernel(acc_h, bucket_r, ds0_r, ds1_r, de0_r, de1_r, dd_r, out_h, acc_v, diag_v, out_v, sems):
        section = lax.axis_index("section")
        side = section // 2
        out_v[...] = jnp.zeros_like(out_v)

        @pl.when(section % 2 == 0)
        def _():
            loads = copy_all(sems, 0, (acc_h, acc_v))
            diag_v[...] = jnp.zeros_like(diag_v)
            wait_all(loads)
            fold_diagonals(acc_v, diag_v)
            ids = lax.broadcasted_iota(jnp.int32, (32, dist), 0)
            onehot = (ids == bucket_r[pl.ds(side, 1), :]).astype(F32)
            part = lax.dot_general(
                diag_v[...], onehot, (((1,), (1,)), ((), ())),
                precision=lax.Precision.HIGHEST, preferred_element_type=F32,
            )
            for own in range(2):
                @pl.when(side == own)
                def _():
                    out_v[3 * own : 3 * own + 1, :] = ds0_r[...] + ds1_r[...]
                    out_v[8:16, 256 * own : 256 * own + 32] = part[:8]
                    out_v[8:16, 256 * own + 128 : 256 * own + 160] = part[8:]

        @pl.when(section == 1)
        def _():
            out_v[1:3, :] = de0_r[...] + de1_r[...]

        @pl.when(side == 1)
        def _():
            out_v[4:7, :] = dd_r[...]

        wait_all(copy_all(sems, 1, (out_v, out_h)))

    return job(
        kernel,
        [acc],
        [flipped, *dgains_s, *dgains_e, dgain_d],
        [shape((16, width), F32)],
        [
            pltpu.VMEM(acc.shape, F32),
            pltpu.VMEM((16, dist), F32),
            pltpu.VMEM((16, width), F32),
            pltpu.SemaphoreType.DMA((2,)),
        ],
        result=lambda made: made[0],
    )


def self_backward(row, sections, ins, mats, gains, segs, toe, g_enc, g_dec, kept, passed, after):
    length, width = segs.shape[1], ins.shape[1]
    dist = 2 * length

    def kernel(x_h, w_h, toe_h, ge_h, gd_h, qkv_h, mix_h, lse_h, gain_r, seg_r, out_h, acc_h, dgain_h, b_h,
               x_v, w_v, qkv_v, mix_v, lse_v, d_v, dm_v, dqkv_v, dn_v, gx_v, dgain_v,
               mask_v, toe_v, acc_v, s_v, dp_v, p_v, ds_v, sems):
        section = lax.axis_index("section")
        side = section // 2

        active = section == sections[0]
        for one in sections[1:]:
            active = active | (section == one)

        @pl.when(active)
        def _():
            loads = either_all(sems, 0, side == 0, ((ge_h, d_v), (gd_h, d_v)))
            loads += copy_all(
                sems, 1,
                (w_h.at[0, :, pl.ds(3 * width, width)], w_v.at[:, pl.ds(3 * width, width)]),
                (mix_h, mix_v),
                (lse_h, lse_v),
                (qkv_h, qkv_v),
                (toe_h, toe_v),
                (w_h.at[0, :, pl.ds(0, 3 * width)], w_v.at[:, pl.ds(0, 3 * width)]),
                (x_h.at[pl.ds(row * length, length)], x_v),
            )
            sums = copy_all(sems, 8, (acc_h, acc_v)) if row else []
            fill_mask(mask_v, seg_r[row : row + 1, :], True, jnp.where(side == 1, 0, 2 * length))
            if not row:
                acc_v[...] = jnp.zeros_like(acc_v)
            gain = gain_r[pl.ds(3 * side, 1), :]
            wait_all(loads[:2])
            stores = copy_all(sems, 9, (d_v, b_h.at[:, pl.ds(3 * width, width)]))
            rows_out(d_v, w_v, 3 * width, dm_v, False)
            wait_all(loads[2:6] + sums)
            attend_back(qkv_v, qkv_v, qkv_v, dm_v, mix_v, 0, width, 2 * width, mask_v, toe_v, lse_v,
                        dp_v, s_v, p_v, ds_v, dqkv_v, 0, acc_v)
            stores += copy_all(sems, 10, (dqkv_v, b_h.at[:, pl.ds(0, 3 * width)]), (acc_v, acc_h))
            wait_all(loads[6:])
            rows_out(dqkv_v, w_v, 0, dn_v, False)
            total = jnp.zeros((1, width), F32)
            for rows in row_chunks(length):
                dx, dgain = rms_back(x_v[rows, :].astype(F32), gain, dn_v[rows, :])
                gx_v[rows, :] = d_v[rows, :].astype(F32) + dx
                total = total + dgain
            dgain_v[...] = total
            stores += copy_all(sems, 12, (gx_v, out_h.at[pl.ds(row * length, length)]), (dgain_v, dgain_h))
            wait_all(stores)

    n, qkv, mix, lse = kept
    return call(
        kernel,
        [ins, mats, toe, g_enc, g_dec, qkv, mix, lse],
        [gains, segs],
        [like(toe), shape((1, width), F32), shape((length, 4 * width), BF16)][len(passed) - 1 :],
        [
            pltpu.VMEM((length, width), BF16),
            pltpu.VMEM((width, 4 * width), BF16),
            pltpu.VMEM((length, 3 * width), BF16),
            pltpu.VMEM((length, width), BF16),
            pltpu.VMEM((16, length), F32),
            pltpu.VMEM((length, width), BF16),
            pltpu.VMEM((length, width), BF16),
            pltpu.VMEM((length, 3 * width), BF16),
            pltpu.VMEM((length, width), F32),
            pltpu.VMEM((length, width), F32),
            pltpu.VMEM((1, width), F32),
            pltpu.VMEM((length, length), F32),
            pltpu.VMEM((H, 128, dist - 128), F32),
            pltpu.VMEM((H, 128, dist - 128), F32),
            pltpu.VMEM((2, length, length), F32),
            pltpu.VMEM((2, length, length), F32),
            pltpu.VMEM((2, length, length), BF16),
            pltpu.VMEM((2, length, length), BF16),
            pltpu.SemaphoreType.DMA((14,)),
        ],
        flops_of(6, 16 << 20),
        passed,
        after,
    )


def encoder_forward(row, e1, mats, gains, out_rows):
    length, width = e1.shape
    hidden = mats.shape[2]
    narrow, wide = shape((length, width), BF16), shape((length, hidden), BF16)
    rows_shape = shape((2 * length, width), F32)
    kept = [narrow, shape((length, width), F32), narrow, wide, wide]

    def kernel(e_h, w_h, gain_r, out_h, send_h, mid_h, n_h, h_h, slope_h,
               e_v, win_v, wout_v, n_v, h_v, slope_v, mid_v, out_v, send_v, sems):
        @pl.when(lax.axis_index("section") == 1)
        def _():
            loads = copy_all(sems, 0, (e_h, e_v))
            win_loads = column_parts(sems, 9, w_h.at[0], win_v)
            loads += copy_all(sems, 1, (w_h.at[1], wout_v))
            loads[0].wait()
            for rows in row_chunks(length):
                x = e_v[rows, :].astype(F32)
                mid_v[rows, :] = x
                n_v[rows, :] = (x * inverse_rms(x) * gain_r[1:2, :]).astype(BF16)
            stores = copy_all(sems, 3, (n_v, n_h))
            ffn_up(n_v, win_v, h_v, slope_v, win_loads)
            stores += copy_all(sems, 4, (h_v, h_h), (slope_v, slope_h))
            loads[1].wait()
            rows_out(h_v, wout_v, 0, mid_v, True)
            stores += copy_all(sems, 8, (mid_v, mid_h))
            for n, rows in enumerate(row_chunks(length)):
                x = mid_v[rows, :]
                y = x * inverse_rms(x) * gain_r[2:3, :]
                out_v[rows, :] = y
                send_v[rows, :] = y.astype(BF16)
                target = pl.ds(row * length + n * ROW_STEP, ROW_STEP)
                stores += copy_all(
                    sems, 12 + 2 * n, (send_v.at[rows], send_h.at[rows]), (out_v.at[rows], out_h.at[target])
                )
            wait_all(stores)

    return call(
        kernel,
        [e1, mats],
        [gains],
        kept if row else [rows_shape] + kept,
        [
            pltpu.VMEM((length, width), BF16),
            pltpu.VMEM((width, hidden), BF16),
            pltpu.VMEM((width, hidden), BF16),
            pltpu.VMEM((length, width), BF16),
            pltpu.VMEM((length, hidden), BF16),
            pltpu.VMEM((length, hidden), BF16),
            pltpu.VMEM((length, width), F32),
            pltpu.VMEM((length, width), F32),
            pltpu.VMEM((length, width), BF16),
            pltpu.SemaphoreType.DMA((20,)),
        ],
        flops_of(2, 20 << 20),
        [out_rows] if row else [],
    )


def encoder_backward(row, ins, extra, e1, mid, slope, mats, gains, after):
    length, width = extra.shape
    hidden = mats.shape[2]

    def kernel(cot_h, extra_h, e_h, mid_h, slope_h, w_h, gain_r, g_h, d_h, du_h, dgain_h,
               cot_v, extra_v, e_v, mid_v, slope_v, win_v, wout_v, d_v, du_v, dn_v, gm_v, g_v, dgain_v, sems):
        @pl.when(lax.axis_index("section") == 1)
        def _():
            loads = copy_all(
                sems, 0,
                (cot_h.at[pl.ds(row * length, length)], cot_v), (extra_h, extra_v), (mid_h, mid_v),
                (w_h.at[1], wout_v), (slope_h, slope_v), (w_h.at[0], win_v), (e_h, e_v),
            )
            wait_all(loads[:3])
            total = jnp.zeros((1, width), F32)
            for rows in row_chunks(length):
                dy = cot_v[rows, :].astype(F32) + extra_v[rows, :].astype(F32)
                dx, dgain = rms_back(mid_v[rows, :], gain_r[2:3, :], dy)
                gm_v[rows, :] = dx
                d_v[rows, :] = dx.astype(BF16)
                total = total + dgain
            dgain_v[1:2, :] = total
            stores = copy_all(sems, 7, (d_v, d_h))
            wait_all(loads[3:5])
            ffn_down(d_v, wout_v, slope_v, du_v)
            stores += copy_all(sems, 8, (du_v, du_h))
            wait_all(loads[5:])
            rows_out(du_v, win_v, 0, dn_v, False)
            total = jnp.zeros((1, width), F32)
            for rows in row_chunks(length):
                dx, dgain = rms_back(e_v[rows, :].astype(F32), gain_r[1:2, :], dn_v[rows, :])
                g_v[rows, :] = (gm_v[rows, :] + dx).astype(BF16)
                total = total + dgain
            dgain_v[0:1, :] = total
            stores += copy_all(sems, 9, (g_v, g_h), (dgain_v, dgain_h))
            wait_all(stores)

    return call(
        kernel,
        [ins, extra, e1, mid, slope, mats],
        [gains],
        [
            shape((length, width), BF16),
            shape((length, width), BF16),
            shape((length, hidden), BF16),
            shape((2, width), F32),
        ],
        [
            pltpu.VMEM((length, width), BF16),
            pltpu.VMEM((length, width), BF16),
            pltpu.VMEM((length, width), BF16),
            pltpu.VMEM((length, width), F32),
            pltpu.VMEM((length, hidden), BF16),
            pltpu.VMEM((width, hidden), BF16),
            pltpu.VMEM((width, hidden), BF16),
            pltpu.VMEM((length, width), BF16),
            pltpu.VMEM((length, hidden), BF16),
            pltpu.VMEM((length, width), F32),
            pltpu.VMEM((length, width), F32),
            pltpu.VMEM((length, width), BF16),
            pltpu.VMEM((2, width), F32),
            pltpu.SemaphoreType.DMA((11,)),
        ],
        flops_of(2, 20 << 20),
        after=after,
    )


def decoder(d_own, d_got, m_two, m_three, ins, cot_got, mats, got_mats, gains, segs, passed, after):
    length, width = d_own.shape
    hidden = mats.shape[2]

    def kernel(d2_h, d3_h, m2_h, m3_h, c1_h, c0_h, w1_h, w0_h, gain_r, seg_r,
               out_h, fa_h, fb_h, fc_h, other_h, gm_h, gd_h, dgain_h,
               d_v, m_v, c_v, wca_v, win_v, wout_v, n_v, q_v, mix_v, lse_v, mask_v, s_v, p_v, h_v, slope_v,
               x_v, y_v, dn_v, n5_v, do_v, dgain_v, dp_v, ds_v, dq_v, dm_v, do4_v, gm_v, gd_v, out_v, sems):
        section = lax.axis_index("section")

        @pl.when(section >= 2)
        def _():
            own = section == 3
            first_row = pl.ds(0, length)

            def put(first, *choices):
                return either_all(sems, first, own, *choices)

            quarters = [pl.ds(c * width, width) for c in range(4)]
            loads = put(0, ((d3_h, d_v), (d2_h, d_v)))
            cross_loads = put(
                21, *[((w1_h.at[0, :, cut], wca_v.at[:, cut]), (w0_h.at[0, :, cut], wca_v.at[:, cut])) for cut in quarters]
            )
            loads += put(
                1,
                ((m3_h, m_v), (m2_h, m_v)),
                *[((w1_h.at[k], v), (w0_h.at[k], v)) for k, v in ((1, win_v), (2, wout_v))],
                ((c1_h.at[first_row], c_v), (c0_h, c_v)),
            )
            fill_mask(mask_v, seg_r[pl.ds(3 - section, 1), :], False, 2 * length)
            loads[0].wait()
            for rows in row_chunks(length):
                x = d_v[rows, :].astype(F32)
                x_v[rows, :] = x
                n_v[rows, :] = (x * inverse_rms(x) * gain_r[4:5, :]).astype(BF16)
            part_of = lambda f_h, n, count=1: f_h.at[:, pl.ds(n * width, count * width)]
            stores = copy_all(sems, 6, (n_v, part_of(fc_h, 0)))
            cross_loads[0].wait()
            project(n_v, wca_v, 0, q_v, 0, width)
            loads[1].wait()
            stores += copy_all(sems, 7, (m_v, part_of(fc_h, 1)))
            wait_all(cross_loads[1:3])
            project(m_v, wca_v, width, q_v, width, 2 * width)
            attend(q_v, q_v, q_v, 0, width, 2 * width, mask_v, None, s_v, p_v, mix_v, lse_v)
            stores += copy_all(sems, 9, (mix_v, part_of(fc_h, 2)))

            cross_loads[3].wait()

            @pl.loop(0, width // 256)
            def _(t):
                cols = pl.ds(pl.multiple_of(t * 256, 256), 256)
                part = mm(mix_v[...], wca_v[:, pl.ds(pl.multiple_of(3 * width + t * 256, 256), 256)])
                x_v[:, cols] = x_v[:, cols] + part

            for rows in row_chunks(length):
                x = x_v[rows, :]
                y_v[rows, :] = x
                n5_v[rows, :] = (x * inverse_rms(x) * gain_r[5:6, :]).astype(BF16)
            stores += copy_all(sems, 10, (n5_v, part_of(fa_h, 0)))
            loads[2].wait()
            ffn_up(n5_v, win_v, h_v, slope_v)
            stores += copy_all(sems, 11, (h_v, part_of(fb_h, 1, 4)))
            loads[3].wait()
            rows_out(h_v, wout_v, 0, y_v, True)
            loads[4].wait()
            total = jnp.zeros((1, width), F32)
            for rows in row_chunks(length):
                y = y_v[rows, :]
                out_v[rows, :] = y * inverse_rms(y) * gain_r[6:7, :]
                dy, dgain = rms_back(y, gain_r[6:7, :], c_v[rows, :].astype(F32))
                total = total + dgain
                do_v[rows, :] = dy.astype(BF16)
                y_v[rows, :] = dy
            dgain_v[2:3, :] = total
            stores += put(12, ((out_v, out_h.at[first_row]), (out_v, other_h)))
            stores += copy_all(sems, 13, (do_v, part_of(fb_h, 0)))
            ffn_down(do_v, wout_v, slope_v, slope_v)
            stores += copy_all(sems, 14, (slope_v, part_of(fa_h, 1, 4)))
            rows_out(slope_v, win_v, 0, dn_v, False)
            total = jnp.zeros((1, width), F32)
            for rows in row_chunks(length):
                dx, dgain = rms_back(x_v[rows, :], gain_r[5:6, :], dn_v[rows, :])
                dx = y_v[rows, :] + dx
                y_v[rows, :] = dx
                do4_v[rows, :] = dx.astype(BF16)
                total = total + dgain
            dgain_v[1:2, :] = total
            stores += copy_all(sems, 15, (do4_v, part_of(fc_h, 6)))
            rows_out(do4_v, wca_v, 3 * width, dm_v, False)
            attend_back(q_v, q_v, q_v, dm_v, mix_v, 0, width, 2 * width, mask_v, None, lse_v,
                        dp_v, s_v, p_v, ds_v, dq_v, 0, None)
            stores += copy_all(sems, 16, (dq_v, part_of(fc_h, 3, 3)))
            rows_out(dq_v.at[:, width:], wca_v, width, gm_v, False)
            stores += copy_all(sems, 18, (gm_v, gm_h))
            rows_out(dq_v.at[:, :width], wca_v, 0, dn_v, False)
            total = jnp.zeros((1, width), F32)
            for rows in row_chunks(length):
                dx, dgain = rms_back(d_v[rows, :].astype(F32), gain_r[4:5, :], dn_v[rows, :])
                gd_v[rows, :] = (y_v[rows, :] + dx).astype(BF16)
                total = total + dgain
            dgain_v[0:1, :] = total
            stores += copy_all(sems, 19, (gd_v, gd_h), (dgain_v, dgain_h))
            wait_all(stores)

    narrow = shape((length, width), BF16)
    return call(
        kernel,
        [d_own, d_got, m_two, m_three, ins, cot_got, mats, got_mats],
        [gains, segs],
        [
            *[shape((length, count * width), BF16) for count in (5, 5, 7)],
            shape((length, width), F32),
            *(narrow, narrow),
            shape((3, width), F32),
        ],
        [
            pltpu.VMEM((length, width), BF16),
            pltpu.VMEM((length, width), BF16),
            pltpu.VMEM((length, width), BF16),
            pltpu.VMEM((width, 4 * width), BF16),
            pltpu.VMEM((width, hidden), BF16),
            pltpu.VMEM((width, hidden), BF16),
            pltpu.VMEM((length, width), BF16),
            pltpu.VMEM((length, 3 * width), BF16),
            pltpu.VMEM((length, width), BF16),
            pltpu.VMEM((16, length), F32),
            pltpu.VMEM((length, length), F32),
            pltpu.VMEM((2, length, length), F32),
            pltpu.VMEM((2, length, length), BF16),
            pltpu.VMEM((length, hidden), BF16),
            pltpu.VMEM((length, hidden), BF16),
            pltpu.VMEM((length, width), F32),
            pltpu.VMEM((length, width), F32),
            pltpu.VMEM((length, width), F32),
            pltpu.VMEM((length, width), BF16),
            pltpu.VMEM((length, width), BF16),
            pltpu.VMEM((3, width), F32),
            pltpu.VMEM((2, length, length), F32),
            pltpu.VMEM((2, length, length), BF16),
            pltpu.VMEM((length, 3 * width), BF16),
            pltpu.VMEM((length, width), BF16),
            pltpu.VMEM((length, width), BF16),
            pltpu.VMEM((length, width), BF16),
            pltpu.VMEM((length, width), BF16),
            pltpu.VMEM((length, width), F32),
            pltpu.SemaphoreType.DMA((25,)),
        ],
        flops_of(12, 30 << 20),
        passed,
        after,
    )


def weight_grad(sections, groups, chunks, ndp, decoder=None, passed=()):
    length, width = groups[0][0][0][0].shape[0], 768
    columns = sum(group[2] for group in groups)
    pieces = len(groups[0][0])
    bits = ndp.bit_length() - 1
    block = width // ndp
    flat = []
    for a_list, b_list, _ in groups + (decoder or []):
        for array, _ in a_list + b_list:
            if not any(array is other for other in flat):
                flat.append(array)
    place = lambda array: [index for index, other in enumerate(flat) if other is array][0]
    plan_of = lambda groups: [
        ([(place(a), a0) for a, a0 in a_list], [(place(b), b0) for b, b0 in b_list], count)
        for a_list, b_list, count in groups
    ]
    plan, other_plan = plan_of(groups), plan_of(decoder or groups)
    tile = 768
    copies = 2 * pieces * len(groups)

    def kernel(*args):
        sources = args[: len(flat)]
        outs = args[len(flat) : len(flat) + 2 * len(chunks)]
        a_v, at_v, b_v, out_v, sems = args[len(flat) + 2 * len(chunks) :]
        me = lax.axis_index("dp")
        section = lax.axis_index("section")
        active = section == sections[0]
        for one in sections[1:]:
            active = active | (section == one)

        @pl.when(active)
        def _():
            loads, start = [], 0
            for g, (a_list, b_list, count) in enumerate(plan):
                group_loads = []
                for k in range(pieces):
                    rows = pl.ds(k * length, length)
                    choices = []
                    for a_of, b_of, _ in (other_plan[g], plan[g]):
                        (ai, a0), (bi, b0) = a_of[k], b_of[k]
                        choices.append((
                            (sources[ai].at[:, pl.ds(a0, width)], a_v.at[g, rows]),
                            (sources[bi].at[:, pl.ds(b0, count)], b_v.at[rows, pl.ds(start, count)]),
                        ))
                    first = 2 * (g * pieces + k)
                    if decoder:
                        group_loads += either_all(sems, first, section >= 2, *zip(*choices))
                    else:
                        group_loads += copy_all(sems, first, *choices[0])
                loads.append(group_loads)
                start += count
            stores, group, group_end, start = [], -1, 0, 0
            for number, (count, order) in enumerate(chunks):
                spots = []
                for b in range(ndp):
                    code = jnp.bitwise_xor(me, b)
                    spot = 0
                    for k in range(bits):
                        spot = spot + ((code >> order[k]) & 1) * (1 << (bits - 1 - k))
                    spots.append(spot)
                done, end = start, start + count
                while done < end:
                    if done == group_end:
                        group += 1
                        wait_all(loads[group])
                        at_v[...] = a_v[group].T
                        group_end += plan[group][2]
                    upto = min(end, group_end)

                    @pl.loop(0, (upto - done) // tile)
                    def _(t):
                        cols = pl.ds(pl.multiple_of(done + t * tile, 128), tile)
                        part = mm(at_v[...], b_v[:, cols])
                        for b in range(ndp):
                            out_v[spots[b], :, cols] = part[b * block : (b + 1) * block, :].astype(BF16)

                    done = upto
                for half in range(2):
                    source = out_v.at[pl.ds(half * (ndp // 2), ndp // 2), :, pl.ds(start, count)]
                    stores += copy_all(sems, copies + 2 * number + half, (source, outs[2 * number + half]))
                start = end
            wait_all(stores)

    return job(
        kernel,
        flat,
        [],
        [] if passed else [shape((ndp // 2, block, count), BF16) for count, _ in chunks for _ in range(2)],
        [
            pltpu.VMEM((len(groups), pieces * length, width), BF16),
            pltpu.VMEM((width, pieces * length), BF16),
            pltpu.VMEM((pieces * length, columns), BF16),
            pltpu.VMEM((ndp, block, columns), BF16),
            pltpu.SemaphoreType.DMA((copies + 2 * len(chunks),)),
        ],
        passed=passed,
        result=lambda made: [(made[2 * number], made[2 * number + 1]) for number in range(len(chunks))],
    )


def along_dp(value, bit, sections, ndp):
    pairs = [(s * ndp + d, s * ndp + (d ^ bit)) for s in sections for d in range(ndp)]
    return lax.ppermute(value, ("section", "dp"), pairs)


def added(items):
    outs, kinds = [], []
    for keep, _, _ in items:
        kind = "sum" if keep.dtype == F32 else "last" if keep.shape[0] == 1 else "half"
        kinds.append(kind)
        if kind == "half":
            outs += [shape((keep.shape[0] // 2,) + keep.shape[1:], BF16)] * 2
        else:
            outs.append(shape(keep.shape if kind == "sum" else keep.shape[1:], F32))

    def kernel(*refs):
        count = len(items)
        sources, rest = refs[: 2 * count], refs[2 * count :]
        targets, rest = rest[: len(outs)], rest[len(outs) :]
        scratch, sems = rest[:-1], rest[-1]
        section = lax.axis_index("section")

        def takes_part(sections):
            active = section == sections[0]
            for one in sections[1:]:
                active = active | (section == one)
            return active

        for number, item in enumerate(items):
            @pl.when(takes_part(item[2]))
            def _():
                for k in range(2):
                    pltpu.make_async_copy(
                        sources[2 * number + k], scratch[3 * number + k], sems.at[4 * number + k]
                    ).start()

        place = 0
        for number, (item, kind) in enumerate(zip(items, kinds)):
            n = item[0].shape[0]
            keep_v, got_v, out_v = scratch[3 * number : 3 * number + 3]
            mine = targets[place : place + (2 if kind == "half" else 1)]
            place += len(mine)

            @pl.when(takes_part(item[2]))
            def _():
                for k, v in enumerate((keep_v, got_v)):
                    pltpu.make_async_copy(sources[2 * number + k], v, sems.at[4 * number + k]).wait()
                if kind == "half":
                    @pl.loop(0, n)
                    def _(i):
                        out_v[i] = (keep_v[i].astype(F32) + got_v[i].astype(F32)).astype(BF16)

                    wait_all(
                        copy_all(
                            sems, 4 * number + 2,
                            (out_v.at[pl.ds(0, n // 2)], mine[0]), (out_v.at[pl.ds(n // 2, n // 2)], mine[1]),
                        )
                    )
                else:
                    if kind == "last":
                        out_v[...] = keep_v[0].astype(F32) + got_v[0].astype(F32)
                    else:
                        out_v[...] = keep_v[...] + got_v[...]
                    wait_all(copy_all(sems, 4 * number + 2, (out_v, mine[0])))

    scratch = []
    for (keep, _, _), kind in zip(items, kinds):
        own = pltpu.VMEM(keep.shape, keep.dtype)
        scratch += [own, own, pltpu.VMEM(keep.shape[1:], F32) if kind == "last" else own]
    def result(made):
        results = []
        for kind in kinds:
            size = 2 if kind == "half" else 1
            results.append(tuple(made[:size]) if size == 2 else made[0])
            made = made[size:]
        return results

    return job(
        kernel,
        [array for keep, got, _ in items for array in (keep, got)],
        [],
        outs,
        scratch + [pltpu.SemaphoreType.DMA((4 * len(items),))],
        result=result,
    )


def joined(v, pieces):
    start = 0
    for piece in pieces:
        yield piece, v.at[:, pl.ds(start, piece.shape[1])]
        start += piece.shape[1]


def outputs(one, two, three, rows_got, out_rows, after):
    length, width = rows_got.shape
    block, columns = two[0].shape[0], 2 * two[0].shape[1]

    def kernel(a_h, b_h, s0_h, s1_h, c0_h, c1_h, r_h, out_h, grad_h, f_v, s_v, c_v, r_v, sems):
        section = lax.axis_index("section")
        even = section % 2 == 0
        loads = copy_all(sems, 0, *joined(f_v, (a_h, b_h)))

        @pl.when(section == 3)
        def _():
            wait_all(copy_all(sems, 9, *joined(s_v, (s0_h, s1_h)), *joined(c_v, (c0_h, c1_h)), (r_h, r_v)))
            wait_all(loads)
            wait_all(
                copy_all(
                    sems, 5,
                    (f_v, grad_h.at[1]), (s_v, grad_h.at[2]), (c_v, grad_h.at[0]), (r_v, out_h.at[pl.ds(length, length)]),
                )
            )

        @pl.when(section != 3)
        def _():
            c_v[...] = jnp.zeros_like(c_v)
            stores = copy_all(sems, 5, (c_v, grad_h.at[2]))

            @pl.when(section == 1)
            def _():
                wait_all(copy_all(sems, 9, *joined(s_v, (s0_h, s1_h))))
                wait_all(copy_all(sems, 3, (s_v, grad_h.at[1])))

            @pl.when(even)
            def _():
                wait_all(copy_all(sems, 3, (c_v, grad_h.at[1])))

            wait_all(loads)
            wait_all(stores + copy_all(sems, 6, (f_v, grad_h.at[0])))

    return call(
        kernel,
        [*one, *two, *three, rows_got],
        [],
        [shape((3, block, columns), F32)],
        [pltpu.VMEM((block, columns), F32)] * 3 + [pltpu.VMEM((length, width), F32), pltpu.SemaphoreType.DMA((14,))],
        flops_of(1, 1 << 20),
        [out_rows],
        after,
    )


def per_device(section_ins, segments, buckets, section_mats, gains, tables):
    ndp = lax.axis_size("dp")
    ins = section_ins[0]
    mats = section_mats[0]
    length = segments.shape[1]
    width = ins.shape[1]
    segs = segments
    by_head = jnp.transpose(tables, (2, 0, 1))
    flipped = jnp.pad(buckets[:, ::-1], ((0, 0), (0, 1)), constant_values=-1)
    everywhere = (0, 1, 2, 3)
    move = lambda value, pairs: lax.ppermute(value, "section", pairs)

    got_mats = move(section_mats, [(3, 2), (1, 0)])[0]
    *fwd0, tiles = self_forward(0, ins, mats, gains, segs, by_head, buckets)
    first0 = move(fwd0[0], [(0, 1), (2, 3)])
    fwd1 = self_forward(1, ins, mats, gains, segs, by_head, buckets, tiles)
    first1 = move(fwd1[0], [(0, 1)])
    toe = transposed_bias(by_head, flipped, length, [fwd1[0]])
    out_rows, *enc0 = encoder_forward(0, first0, mats, gains, None)
    m_three = move(enc0[0], [(1, 3)])
    late_ins, _ = lax.optimization_barrier((ins, m_three))
    cot_got = move(late_ins[length:], [(3, 2)])
    out_rows, *enc1 = encoder_forward(1, first1, mats, gains, out_rows)
    m_two = move(enc1[0], [(1, 2)])
    here = marker([enc1[0], m_three])

    dec = decoder(fwd1[0], first0, m_two, m_three, ins, cot_got, mats, got_mats, gains, segs, [out_rows], [toe, here])
    out_rows, *factors, other, g_mem, g_self, dgain_d = dec
    even, odd = (0, 2), (1, 3)
    extra0 = move(g_mem, [(3, 1)])
    extra1 = move(g_mem, [(2, 0)])
    (sent, g_self_sent), _ = lax.optimization_barrier(((factors, g_self), extra0))
    got = [move(value, [(2, 3)]) for value in sent]
    g_self_got = move(g_self_sent, [(3, 2)])
    back0 = encoder_backward(0, ins, extra0, first0, enc0[1], enc0[4], mats, gains, [extra1])
    g0 = move(back0[0], [(1, 0)])
    (other, extra1), _ = lax.optimization_barrier(((other, extra1), back0[0]))
    extra1 = move(extra1, [(0, 1)])
    own0 = self_backward(
        0, even, ins, mats, gains, segs, toe, g0, g_self_got, fwd0[1:], [out_rows], [extra1]
    )
    out_rows, acc = own0[:2]
    back1 = encoder_backward(1, ins, extra1, first1, enc1[1], enc1[4], mats, gains, [acc])
    other, _ = lax.optimization_barrier((other, back1[0]))
    rows_got = move(other, [(2, 3)])

    plain = tuple(range(ndp.bit_length() - 1))
    turned = (1, 0) + plain[2:]
    orders = (plain, turned)
    steps = len(plain)
    whole = 4 * width
    rows_of = lambda which, at: [(factors[which], at * width), (got[which], at * width)]
    halves = [(2 * width, order) for order in orders]
    groups = [([(enc0[2], 0), (enc1[2], 0)], [(back0[2], 0), (back1[2], 0)], whole)]
    groups_d = [(rows_of(0, 0), rows_of(0, 1), whole)]
    made, = run([weight_grad(odd, groups, halves, ndp, groups_d)], [back1[0]])
    g1, _ = lax.optimization_barrier((back1[0], made[0][0]))
    g1 = move(g1, [(1, 0)])
    own1 = self_backward(
        1, even, ins, mats, gains, segs, toe, g1, g_self, fwd1[1:], [out_rows, acc], [made[0][0]]
    )
    out_rows, acc = own1[:2]
    groups = [
        ([(fwd0[1], 0), (fwd1[1], 0)], [(own0[3], 0), (own1[3], 0)], 3 * width),
        ([(fwd0[3], 0), (fwd1[3], 0)], [(own0[3], 3 * width), (own1[3], 3 * width)], width),
    ]
    made, = run([weight_grad(even, groups, halves, ndp, passed=[*made[0], *made[1]])], [out_rows])

    def send(pair, order, step, sections):
        return (pair[0], along_dp(pair[1], 1 << order[step], sections, ndp), sections)

    def send_one(pairs, step):
        return [send(pair, order, step, everywhere) for pair, order in zip(pairs, orders)]

    def send_rest(pairs, part, step):
        sections = odd if part == 1 else (3,)
        return [send(pair, order, step, sections) for pair, order in zip(pairs, orders)]

    one = send_one(made, 0)
    groups = [([(back0[1], 0), (back1[1], 0)], [(enc0[3], 0), (enc1[3], 0)], whole)]
    groups_d = [(rows_of(1, 0), rows_of(1, 1), whole)]
    two, = run([weight_grad(odd, groups, halves, ndp, groups_d)], [made[0][0]])
    groups = [(rows_of(2, k), rows_of(2, at), count * width) for k, at, count in ((0, 3, 1), (1, 4, 2), (2, 6, 1))]
    three, = run([weight_grad((3,), groups, halves, ndp)], [two[0][0]])
    rest = [send_rest(two, 1, 0), send_rest(three, 2, 0)]
    dgains = ([own0[2], own1[2]], [back0[3], back1[3]], dgain_d)
    small, = run([packed_small(acc, flipped, *dgains)], [three[0][0]])
    small_got = along_dp(small, 1, everywhere, ndp)
    tied = [small]
    sums_of = [one, *rest]
    turns = [(2 * k + (0, 1, 2.5)[part], k, part) for k in range(steps) for part in range(3)]
    for _, k, part in sorted(turns):
        last = k + 1 == steps
        items = sums_of[part]
        cost = SHORT if part < 2 and not last else None if part == 2 else LONG
        number = 2 * k + part
        if part < 2 and number < steps:
            (*sums, small), = run([added([*items, (small, small_got, everywhere)])], tied, cost)
            if number + 1 < steps:
                small_got = along_dp(small, 2 << number, everywhere, ndp)
        else:
            sums, = run([added(items)], tied, cost)
        tied = [sums[0] if last else sums[0][0]]
        if not last:
            sums = send_one(sums, k + 1) if not part else send_rest(sums, part, k + 1)
        sums_of[part] = sums
    one, *rest = sums_of
    small, _ = lax.optimization_barrier((small, tied[0]))
    small = small + move(small, [(0, 1), (1, 0), (2, 3), (3, 2)])
    small = small + move(small, [(0, 2), (2, 0), (1, 3), (3, 1)])
    out_rows, grad = outputs(one, *rest, rows_got, out_rows, tied)

    gains_grad = small[: gains.shape[0]]
    heads = [
        jnp.concatenate([small[8:16, at : at + 32], small[8:12, at + 128 : at + 160]], axis=0)
        for at in range(0, 256 * tables.shape[0], 256)
    ]
    return out_rows[None], grad[None], gains_grad, jnp.swapaxes(jnp.stack(heads), 1, 2)


def solution(mesh):
    placed = (
        P("section", "dp", None),
        P("dp", None),
        P(),
        P("section", None, None, None),
        P(),
        P(),
    )
    return jax.shard_map(
        per_device,
        mesh=mesh,
        in_specs=placed,
        out_specs=(P("section", "dp", None), P("section", None, "dp", None), P(), P()),
        check_vma=False,
    )
```

```python
from functools import partial

import jax
import jax.numpy as jnp
from jax import lax
from jax.experimental import pallas as pl
from jax.experimental.pallas import tpu as pltpu
from jax.sharding import PartitionSpec as P

H = 12
HD = 64
PAIRS = H // 2
EPS = 1e-06
GELU = 0.7978845608028654
CUBIC = 0.044715
MASKED = -1e38
F32 = jnp.float32
BF16 = jnp.bfloat16
ROW_STEP = 128
VMEM_LIMIT = 60 * 1024 * 1024


def mm(a, b):
    return jnp.dot(a, b, preferred_element_type=F32)


def mm_nt(a, b):
    return lax.dot_general(a, b, (((1,), (1,)), ((), ())), preferred_element_type=F32)


def inverse_rms(x):
    return lax.rsqrt(jnp.mean(x * x, axis=-1, keepdims=True) + EPS)


def row_chunks(length):
    return [pl.ds(start, ROW_STEP) for start in range(0, length, ROW_STEP)]


def rms_back(x, gain, dy):
    r = inverse_rms(x)
    inner = jnp.mean(dy * gain * x, axis=-1, keepdims=True)
    dx = r * gain * dy - x * (r * r * r) * inner
    return dx, jnp.sum(dy * x * r, axis=0, keepdims=True)


def copy_all(sems, first, *pairs):
    started = []
    for offset, (source, target) in enumerate(pairs):
        one = pltpu.make_async_copy(source, target, sems.at[first + offset])
        one.start()
        started.append(one)
    return started


class Either:
    def __init__(self, sem, flag, yes, no):
        self.done = pltpu.make_async_copy(*yes, sem)

        @pl.when(flag)
        def _():
            pltpu.make_async_copy(*yes, sem).start()

        @pl.when(jnp.logical_not(flag))
        def _():
            pltpu.make_async_copy(*no, sem).start()

    def wait(self):
        self.done.wait()


def either_all(sems, first, flag, *choices):
    return [Either(sems.at[first + offset], flag, *choice) for offset, choice in enumerate(choices)]


def wait_all(started):
    for one in started:
        one.wait()


def head_lanes(second):
    lane = lax.broadcasted_iota(jnp.int32, (1, 2 * HD), 1)
    return (lane >= HD) if second else (lane < HD)


def fill_mask(mask_v, seg_row, transposed, slack):
    length = seg_row.shape[1]
    down = jnp.broadcast_to(seg_row, (128, length)).T
    for c in range(length // 128):
        along = seg_row[:, c * 128 : (c + 1) * 128]
        r = lax.broadcasted_iota(jnp.int32, (length, 128), 0)
        q = lax.broadcasted_iota(jnp.int32, (length, 128), 1) + c * 128
        key, query = (r, q) if transposed else (q, r)
        ok = (down == along) & (key <= query + slack)
        mask_v[:, c * 128 : (c + 1) * 128] = jnp.where(ok, 0.0, MASKED)


def fill_toeplitz(toe_v, vec_v, table, bucket_row):
    count = bucket_row.shape[1]
    ids = lax.broadcasted_iota(jnp.int32, (table.shape[1], count), 0)
    onehot = (ids == bucket_row).astype(F32)
    vec = jnp.dot(table, onehot, precision=lax.Precision.HIGHEST, preferred_element_type=F32)
    vec_v[:H, :count] = vec

    @pl.loop(0, H)
    def _(h):
        wide = jnp.broadcast_to(vec_v[pl.ds(h, 1), :], (128, vec_v.shape[1]))
        rolled = pltpu.roll(wide, vec_v.shape[1] - 127, 1, stride=1, stride_axis=0)
        toe_v[h] = rolled[:, : toe_v.shape[2]]


def pair_cols(base, hp):
    return pl.ds(pl.multiple_of(base + hp * 128, 128), 128)


def over_pairs(scores, rest):
    scores(0, 0)

    @pl.loop(0, PAIRS // 2)
    def _(i):
        scores(2 * i + 1, 1)
        rest(2 * i, 0)
        scores(jnp.minimum(2 * i + 2, PAIRS - 1), 0)
        rest(2 * i + 1, 1)


def attend_ahead(q_v, k_v, v_v, q0, k0, v0, mask_v, toe_v, s_v, p_v, mix_v, lse_v, top_v, total_v):
    length = mix_v.shape[0]
    low, high = head_lanes(False), head_lanes(True)
    lane = lax.broadcasted_iota(jnp.int32, (1, 2 * HD), 1)
    top_v[...] = jnp.zeros_like(top_v)
    total_v[...] = jnp.ones_like(total_v)

    def scores(hp, slot):
        q2, k2 = q_v[:, pair_cols(q0, hp)], k_v[:, pair_cols(k0, hp)]
        for a, mine in enumerate((low, high)):
            s_v[2 * slot + a] = mm_nt(jnp.where(mine, q2, jnp.zeros_like(q2)), k2)

    def rest(hp, slot):
        v2 = v_v[:, pair_cols(v0, hp)]
        outs, tops = [], []
        for a, mine in enumerate((low, high)):
            top = []
            for c in range(length // 128):
                rows = pl.ds(c * 128, 128)
                s = s_v[2 * slot + a, rows, :] + mask_v[rows, :]
                if toe_v is not None:
                    left = toe_v.shape[2] - length - c * 128
                    s = s + toe_v[2 * hp + a, :, left : left + length]
                m = jnp.max(s, axis=-1, keepdims=True)
                p_v[2 * slot + a, rows, :] = jnp.exp(s - m).astype(BF16)
                top.append(m)
            tops.append(jnp.concatenate(top, axis=0))
            outs.append(mm(p_v[2 * slot + a], jnp.where(mine, v2, jnp.ones_like(v2))))
        total = pltpu.roll(jnp.where(low, outs[1], outs[0]), HD, 1)
        mix_v[:, pair_cols(0, hp)] = (jnp.where(low, outs[0], outs[1]) / total).astype(BF16)
        first, second = lane == 2 * hp, lane == 2 * hp + 1
        top_v[...] = jnp.where(first, tops[0], jnp.where(second, tops[1], top_v[...]))
        total_v[...] = jnp.where(first, total[:, :1], jnp.where(second, total[:, HD : HD + 1], total_v[...]))

    over_pairs(scores, rest)
    lse_v[...] = (top_v[...] + jnp.log(total_v[...])).T[: lse_v.shape[0], :]


def attend(q_v, k_v, v_v, q0, k0, v0, mask_v, toe_v, s_v, p_v, mix_v, lse_v):
    length = mix_v.shape[0]

    @pl.loop(0, PAIRS)
    def _(hp):
        at = lambda base: pl.ds(pl.multiple_of(base + hp * 128, 128), 128)
        q2, k2, v2 = q_v[:, at(q0)], k_v[:, at(k0)], v_v[:, at(v0)]
        low = head_lanes(False)
        outs, tops = [], []
        for a in range(2):
            mine = head_lanes(a == 1)
            s_v[a] = mm_nt(jnp.where(mine, q2, jnp.zeros_like(q2)), k2)
            top = []
            for c in range(length // 128):
                rows = pl.ds(c * 128, 128)
                s = s_v[a, rows, :] + mask_v[rows, :]
                if toe_v is not None:
                    left = toe_v.shape[2] - length - c * 128
                    s = s + toe_v[2 * hp + a, :, left : left + length]
                m = jnp.max(s, axis=-1, keepdims=True)
                p_v[a, rows, :] = jnp.exp(s - m).astype(BF16)
                top.append(m)
            tops.append(jnp.concatenate(top, axis=0))
            outs.append(mm(p_v[a], jnp.where(mine, v2, jnp.ones_like(v2))))
        total = pltpu.roll(jnp.where(low, outs[1], outs[0]), HD, 1)
        mix_v[:, at(0)] = (jnp.where(low, outs[0], outs[1]) / total).astype(BF16)
        stat = (jnp.where(low, tops[0], tops[1]) + jnp.log(total)).T
        lse_v[pl.ds(2 * hp, 1), :] = stat[0:1, :]
        lse_v[pl.ds(2 * hp + 1, 1), :] = stat[HD : HD + 1, :]


def attend_back(q_v, k_v, v_v, dm_v, mix_v, q0, k0, v0, mask_v, toe_v, lse_v, dp_v, s_v, p_v, ds_v, out_v, o0, acc_v):
    length = mix_v.shape[0]

    @pl.loop(0, PAIRS)
    def _(hp):
        at = lambda base: pl.ds(pl.multiple_of(base + hp * 128, 128), 128)
        q2, k2, v2, dm2 = q_v[:, at(q0)], k_v[:, at(k0)], v_v[:, at(v0)], dm_v[:, at(0)]
        low = head_lanes(False)
        prod = (dm2.astype(F32) * mix_v[:, at(0)].astype(F32)).T
        k2t = k2.T
        dvs, dks, dqs = [], [], []
        for a in range(2):
            mine = head_lanes(a == 1)
            s_v[a] = mm_nt(jnp.where(mine, k2, jnp.zeros_like(k2)), q2)
            dp_v[a] = mm_nt(jnp.where(mine, v2, jnp.zeros_like(v2)), dm2)
            delta = jnp.sum(prod[a * HD : (a + 1) * HD, :], axis=0, keepdims=True)
            lse = lse_v[pl.ds(2 * hp + a, 1), :]
            for c in range(length // 128):
                rows = pl.ds(c * 128, 128)
                s = s_v[a, rows, :] + mask_v[rows, :]
                if toe_v is not None:
                    left = toe_v.shape[2] - length - c * 128
                    s = s + toe_v[2 * hp + a, :, left : left + length]
                p = jnp.exp(s - lse)
                p_v[a, rows, :] = p.astype(BF16)
                ds = p * (dp_v[a, rows, :] - delta)
                ds_v[a, rows, :] = ds.astype(BF16)
                if acc_v is not None:
                    acc_v[2 * hp + a, :, left : left + length] += ds
            dvs.append(mm(p_v[a], dm2))
            dks.append(mm(ds_v[a], q2))
            dqs.append(mm(k2t[a * HD : (a + 1) * HD, :], ds_v[a]))
        out_v[:, at(o0)] = jnp.concatenate(dqs, axis=0).T.astype(BF16)
        out_v[:, at(o0 + PAIRS * 128)] = jnp.where(low, dks[0], dks[1]).astype(BF16)
        out_v[:, at(o0 + 2 * PAIRS * 128)] = jnp.where(low, dvs[0], dvs[1]).astype(BF16)


def fold_diagonals(acc_v, diag_v):

    @pl.loop(0, H, unroll=3)
    def _(h):
        value = jnp.concatenate([acc_v[h], jnp.zeros((128, 128), F32)], axis=1)
        half = 64
        while half >= 1:
            value = pltpu.roll(value[:half], half, 1) + value[half:]
            half //= 2
        diag_v[pl.ds(h, 1), :] = value


def gelu_parts(u):
    square = u * u
    bend = u * (GELU + (GELU * CUBIC) * square)
    half = 0.5 + 0.5 * jnp.tanh(bend)
    hidden = u * half
    slope = half + 2.0 * hidden * (1.0 - half) * (GELU + (3.0 * GELU * CUBIC) * square)
    return hidden, slope


COLUMN_PARTS = 3


def column_parts(sems, first, source, target, parts=COLUMN_PARTS):
    width = target.shape[1] // parts
    cuts = [pl.ds(c * width, width) for c in range(parts)]
    return copy_all(sems, first, *[(source.at[:, cut], target.at[:, cut]) for cut in cuts])


def ffn_up(n_v, win_v, h_v, slope_v, loads=()):
    tile = 1024

    @pl.loop(0, win_v.shape[1] // tile)
    def _(t):
        for part, load in enumerate(loads):
            pl.when(t == part * (win_v.shape[1] // tile // len(loads)))(load.wait)

        cols = pl.ds(pl.multiple_of(t * tile, tile), tile)
        hidden, slope = gelu_parts(mm(n_v[...], win_v[:, cols]))
        h_v[:, cols] = hidden.astype(BF16)
        slope_v[:, cols] = slope.astype(BF16)


def rows_out(a_v, w_v, w0, out_v, add):
    tile = 768
    depth = a_v.shape[1]

    @pl.loop(0, w_v.shape[0] // tile)
    def _(t):
        cols = pl.ds(pl.multiple_of(t * tile, tile), tile)
        part = mm_nt(a_v[...], w_v[cols, w0 : w0 + depth])
        if add:
            out_v[:, cols] = out_v[:, cols] + part
        else:
            out_v[:, cols] = part.astype(out_v.dtype)


def ffn_down(d_v, wout_v, slope_v, du_v):
    tile = 1024

    @pl.loop(0, wout_v.shape[1] // tile)
    def _(t):
        cols = pl.ds(pl.multiple_of(t * tile, tile), tile)
        grad = mm(d_v[...], wout_v[:, cols])
        du_v[:, cols] = (grad * slope_v[:, cols].astype(F32)).astype(BF16)


def project(a_v, w_v, w0, out_v, o0, width):
    tile = 768

    @pl.loop(0, width // tile)
    def _(t):
        source = pl.ds(pl.multiple_of(w0 + t * tile, 128), tile)
        target = pl.ds(pl.multiple_of(o0 + t * tile, 128), tile)
        out_v[:, target] = mm(a_v[...], w_v[:, source]).astype(out_v.dtype)


def flops_of(matmuls, size):
    return pl.CostEstimate(flops=matmuls * 1000, bytes_accessed=size // 1000, transcendentals=0)


LONG = pl.CostEstimate(flops=60_000_000_000, bytes_accessed=60 << 20, transcendentals=0)

SHORT = pl.CostEstimate(flops=20_000_000_000, bytes_accessed=20 << 20, transcendentals=0)


def shape(dims, kind):
    return jax.ShapeDtypeStruct(dims, kind)


def like(array):
    return shape(array.shape, array.dtype)


def job(kernel, ins, small, outs, scratch, passed=(), result=lambda made: made):
    return dict(kernel=kernel, ins=ins, small=small, outs=outs, scratch=scratch, passed=passed, result=result)


def run(jobs, after=(), cost=None):
    every = lambda key: [array for one in jobs for array in one[key]]
    ins, small, passed, outs, scratch = map(every, ("ins", "small", "passed", "outs", "scratch"))
    space = lambda count, where: [pl.BlockSpec(memory_space=where)] * count

    def body(*refs):
        refs = list(refs)
        take = lambda count: [refs.pop(0) for _ in range(count)]
        held = {"ins": take(len(ins)), "small": take(len(small))}
        take(len(passed) + len(after))
        held["passed"], held["outs"], held["scratch"] = take(len(passed)), take(len(outs)), refs
        for one in jobs:
            own = []
            for key in ("ins", "small", "passed", "outs", "scratch"):
                own += [held[key].pop(0) for _ in one[key]]
            one["kernel"](*own)

    lead = len(ins) + len(small)
    made = pl.pallas_call(
        body,
        out_shape=[like(array) for array in passed] + list(outs),
        in_specs=space(len(ins), pl.ANY) + space(len(small), pltpu.VMEM) + space(len(passed) + len(after), pl.ANY),
        out_specs=space(len(passed) + len(outs), pl.ANY),
        scratch_shapes=scratch,
        input_output_aliases={lead + index: index for index in range(len(passed))},
        compiler_params=pltpu.CompilerParams(vmem_limit_bytes=VMEM_LIMIT),
        cost_estimate=cost or flops_of(1, 1 << 20),
    )(*ins, *small, *passed, *after)
    changed, fresh, results = list(made[: len(passed)]), list(made[len(passed) :]), []
    for one in jobs:
        mine = [changed.pop(0) for _ in one["passed"]] + [fresh.pop(0) for _ in one["outs"]]
        results.append(one["result"](mine))
    return results


def call(kernel, ins, small, outs, scratch, cost, passed=(), after=()):
    return run([job(kernel, ins, small, outs, scratch, passed)], after, cost)[0]


def self_forward(row, x, w, gains, segs, tables, buckets, toe=None):
    length, width = segs.shape[1], x.shape[1]
    dist = 2 * length
    outs = [
        shape((length, width), BF16),
        shape((length, width), BF16),
        shape((length, 3 * width), BF16),
        shape((length, width), BF16),
        shape((16, length), F32),
    ]

    def kernel(x_h, w_h, *refs):
        if row:
            toe_h, *refs = refs
            body(x_h, w_h, *refs[:9], toe_h, *refs[9:])
        else:
            body(x_h, w_h, *refs)

    def body(x_h, w_h, gain_r, seg_r, table_r, bucket_r, e_h, n_h, qkv_h, mix_h, lse_h, toe_h,
               x_v, w_v, n_v, qkv_v, mix_v, lse_v, e_v, mask_v, toe_v, vec_v, s_v, p_v, top_v, total_v, sems):
        section = lax.axis_index("section")

        @pl.when(section % 2 == 0)
        def _():
            side = section // 2
            loads = copy_all(
                sems, 0,
                (x_h.at[pl.ds(row * length, length)], x_v),
                *[(w_h.at[0, :, pl.ds(c * width, width)], w_v.at[:, pl.ds(c * width, width)]) for c in range(4)],
            )
            if row:
                tiles = copy_all(sems, 10, (toe_h, toe_v))
            else:
                fill_toeplitz(toe_v, vec_v, table_r[:, pl.ds(side, 1), :][:, 0, :], bucket_r[pl.ds(side, 1), :])
                tiles = copy_all(sems, 10, (toe_v, toe_h))
            fill_mask(mask_v, seg_r[row : row + 1, :], False, jnp.where(side == 1, 0, 2 * length))
            gain = gain_r[pl.ds(3 * side, 1), :]
            loads[0].wait()
            for rows in row_chunks(length):
                x = x_v[rows, :].astype(F32)
                n_v[rows, :] = (x * inverse_rms(x) * gain).astype(BF16)
            stores = copy_all(sems, 5, (n_v, n_h))
            wait_all(loads[1:4])
            project(n_v, w_v, 0, qkv_v, 0, 3 * width)
            stores += copy_all(sems, 6, (qkv_v, qkv_h))
            if row:
                wait_all(tiles)
            attend_ahead(qkv_v, qkv_v, qkv_v, 0, width, 2 * width, mask_v, toe_v, s_v, p_v, mix_v, lse_v, top_v, total_v)
            stores += copy_all(sems, 7, (mix_v, mix_h), (lse_v, lse_h))
            loads[4].wait()

            @pl.loop(0, width // 256)
            def _(t):
                cols = pl.ds(pl.multiple_of(t * 256, 256), 256)
                part = mm(mix_v[...], w_v[:, pl.ds(pl.multiple_of(3 * width + t * 256, 256), 256)])
                e_v[:, cols] = (x_v[:, cols].astype(F32) + part).astype(BF16)

            stores += copy_all(sems, 9, (e_v, e_h))
            wait_all(stores if row else stores + tiles)

    return call(
        kernel,
        [x, w] + ([toe] if row else []),
        [gains, segs, tables, buckets],
        outs if row else outs + [shape((H, 128, dist - 128), F32)],
        [
            pltpu.VMEM((length, width), BF16),
            pltpu.VMEM((width, 4 * width), BF16),
            pltpu.VMEM((length, width), BF16),
            pltpu.VMEM((length, 3 * width), BF16),
            pltpu.VMEM((length, width), BF16),
            pltpu.VMEM((16, length), F32),
            pltpu.VMEM((length, width), BF16),
            pltpu.VMEM((length, length), F32),
            pltpu.VMEM((H, 128, dist - 128), F32),
            pltpu.VMEM((16, dist), F32),
            pltpu.VMEM((4, length, length), F32),
            pltpu.VMEM((4, length, length), BF16),
            pltpu.VMEM((length, 128), F32),
            pltpu.VMEM((length, 128), F32),
            pltpu.SemaphoreType.DMA((11,)),
        ],
        flops_of(3, 12 << 20),
    )


def transposed_bias(tables, flipped, length, after):
    dist = 2 * length

    def kernel(table_r, bucket_r, toe_h, toe_v, vec_v, sems):
        section = lax.axis_index("section")

        @pl.when(section % 2 == 0)
        def _():
            side = section // 2
            fill_toeplitz(toe_v, vec_v, table_r[:, pl.ds(side, 1), :][:, 0, :], bucket_r[pl.ds(side, 1), :])
            wait_all(copy_all(sems, 0, (toe_v, toe_h)))

    return call(
        kernel,
        [],
        [tables, flipped],
        [shape((H, 128, dist - 128), F32)],
        [pltpu.VMEM((H, 128, dist - 128), F32), pltpu.VMEM((16, dist), F32), pltpu.SemaphoreType.DMA((1,))],
        flops_of(1, 6 << 20),
        after=after,
    )[0]


def marker(after):
    def kernel(out_h):
        pass

    return call(kernel, [], [], [shape((8, 128), F32)], [], flops_of(1, 1 << 20), after=after)[0]


def packed_small(acc, flipped, dgains_s, dgains_e, dgain_d):
    dist, width = acc.shape[2] + 128, dgain_d.shape[1]

    def kernel(acc_h, bucket_r, ds0_r, ds1_r, de0_r, de1_r, dd_r, out_h, acc_v, diag_v, out_v, sems):
        section = lax.axis_index("section")
        side = section // 2
        out_v[...] = jnp.zeros_like(out_v)

        @pl.when(section % 2 == 0)
        def _():
            loads = copy_all(sems, 0, (acc_h, acc_v))
            diag_v[...] = jnp.zeros_like(diag_v)
            wait_all(loads)
            fold_diagonals(acc_v, diag_v)
            ids = lax.broadcasted_iota(jnp.int32, (32, dist), 0)
            onehot = (ids == bucket_r[pl.ds(side, 1), :]).astype(F32)
            part = lax.dot_general(
                diag_v[...], onehot, (((1,), (1,)), ((), ())),
                precision=lax.Precision.HIGHEST, preferred_element_type=F32,
            )
            for own in range(2):
                @pl.when(side == own)
                def _():
                    out_v[3 * own : 3 * own + 1, :] = ds0_r[...] + ds1_r[...]
                    out_v[8:16, 256 * own : 256 * own + 32] = part[:8]
                    out_v[8:16, 256 * own + 128 : 256 * own + 160] = part[8:]

        @pl.when(section == 1)
        def _():
            out_v[1:3, :] = de0_r[...] + de1_r[...]

        @pl.when(side == 1)
        def _():
            out_v[4:7, :] = dd_r[...]

        wait_all(copy_all(sems, 1, (out_v, out_h)))

    return job(
        kernel,
        [acc],
        [flipped, *dgains_s, *dgains_e, dgain_d],
        [shape((16, width), F32)],
        [
            pltpu.VMEM(acc.shape, F32),
            pltpu.VMEM((16, dist), F32),
            pltpu.VMEM((16, width), F32),
            pltpu.SemaphoreType.DMA((2,)),
        ],
        result=lambda made: made[0],
    )


def self_backward(row, sections, ins, mats, gains, segs, toe, g_enc, g_dec, kept, passed, after):
    length, width = segs.shape[1], ins.shape[1]
    dist = 2 * length

    def kernel(x_h, w_h, toe_h, ge_h, gd_h, qkv_h, mix_h, lse_h, gain_r, seg_r, out_h, acc_h, dgain_h, b_h,
               x_v, w_v, qkv_v, mix_v, lse_v, d_v, dm_v, dqkv_v, dn_v, gx_v, dgain_v,
               mask_v, toe_v, acc_v, s_v, dp_v, p_v, ds_v, sems):
        section = lax.axis_index("section")
        side = section // 2

        active = section == sections[0]
        for one in sections[1:]:
            active = active | (section == one)

        @pl.when(active)
        def _():
            loads = either_all(sems, 0, side == 0, ((ge_h, d_v), (gd_h, d_v)))
            loads += copy_all(
                sems, 1,
                (w_h.at[0, :, pl.ds(3 * width, width)], w_v.at[:, pl.ds(3 * width, width)]),
                (mix_h, mix_v),
                (lse_h, lse_v),
                (qkv_h, qkv_v),
                (toe_h, toe_v),
                (w_h.at[0, :, pl.ds(0, 3 * width)], w_v.at[:, pl.ds(0, 3 * width)]),
                (x_h.at[pl.ds(row * length, length)], x_v),
            )
            sums = copy_all(sems, 8, (acc_h, acc_v)) if row else []
            fill_mask(mask_v, seg_r[row : row + 1, :], True, jnp.where(side == 1, 0, 2 * length))
            if not row:
                acc_v[...] = jnp.zeros_like(acc_v)
            gain = gain_r[pl.ds(3 * side, 1), :]
            wait_all(loads[:2])
            stores = copy_all(sems, 9, (d_v, b_h.at[:, pl.ds(3 * width, width)]))
            rows_out(d_v, w_v, 3 * width, dm_v, False)
            wait_all(loads[2:6] + sums)
            attend_back(qkv_v, qkv_v, qkv_v, dm_v, mix_v, 0, width, 2 * width, mask_v, toe_v, lse_v,
                        dp_v, s_v, p_v, ds_v, dqkv_v, 0, acc_v)
            stores += copy_all(sems, 10, (dqkv_v, b_h.at[:, pl.ds(0, 3 * width)]), (acc_v, acc_h))
            wait_all(loads[6:])
            rows_out(dqkv_v, w_v, 0, dn_v, False)
            total = jnp.zeros((1, width), F32)
            for rows in row_chunks(length):
                dx, dgain = rms_back(x_v[rows, :].astype(F32), gain, dn_v[rows, :])
                gx_v[rows, :] = d_v[rows, :].astype(F32) + dx
                total = total + dgain
            dgain_v[...] = total
            stores += copy_all(sems, 12, (gx_v, out_h.at[pl.ds(row * length, length)]), (dgain_v, dgain_h))
            wait_all(stores)

    n, qkv, mix, lse = kept
    return call(
        kernel,
        [ins, mats, toe, g_enc, g_dec, qkv, mix, lse],
        [gains, segs],
        [like(toe), shape((1, width), F32), shape((length, 4 * width), BF16)][len(passed) - 1 :],
        [
            pltpu.VMEM((length, width), BF16),
            pltpu.VMEM((width, 4 * width), BF16),
            pltpu.VMEM((length, 3 * width), BF16),
            pltpu.VMEM((length, width), BF16),
            pltpu.VMEM((16, length), F32),
            pltpu.VMEM((length, width), BF16),
            pltpu.VMEM((length, width), BF16),
            pltpu.VMEM((length, 3 * width), BF16),
            pltpu.VMEM((length, width), F32),
            pltpu.VMEM((length, width), F32),
            pltpu.VMEM((1, width), F32),
            pltpu.VMEM((length, length), F32),
            pltpu.VMEM((H, 128, dist - 128), F32),
            pltpu.VMEM((H, 128, dist - 128), F32),
            pltpu.VMEM((2, length, length), F32),
            pltpu.VMEM((2, length, length), F32),
            pltpu.VMEM((2, length, length), BF16),
            pltpu.VMEM((2, length, length), BF16),
            pltpu.SemaphoreType.DMA((14,)),
        ],
        flops_of(6, 16 << 20),
        passed,
        after,
    )


def encoder_forward(row, e1, mats, gains, out_rows):
    length, width = e1.shape
    hidden = mats.shape[2]
    narrow, wide = shape((length, width), BF16), shape((length, hidden), BF16)
    rows_shape = shape((2 * length, width), F32)
    kept = [narrow, shape((length, width), F32), narrow, wide, wide]

    def kernel(e_h, w_h, gain_r, out_h, send_h, mid_h, n_h, h_h, slope_h,
               e_v, win_v, wout_v, n_v, h_v, slope_v, mid_v, out_v, send_v, sems):
        @pl.when(lax.axis_index("section") == 1)
        def _():
            loads = copy_all(sems, 0, (e_h, e_v))
            win_loads = column_parts(sems, 9, w_h.at[0], win_v)
            loads += copy_all(sems, 1, (w_h.at[1], wout_v))
            loads[0].wait()
            for rows in row_chunks(length):
                x = e_v[rows, :].astype(F32)
                mid_v[rows, :] = x
                n_v[rows, :] = (x * inverse_rms(x) * gain_r[1:2, :]).astype(BF16)
            stores = copy_all(sems, 3, (n_v, n_h))
            ffn_up(n_v, win_v, h_v, slope_v, win_loads)
            stores += copy_all(sems, 4, (h_v, h_h), (slope_v, slope_h))
            loads[1].wait()
            rows_out(h_v, wout_v, 0, mid_v, True)
            stores += copy_all(sems, 8, (mid_v, mid_h))
            for n, rows in enumerate(row_chunks(length)):
                x = mid_v[rows, :]
                y = x * inverse_rms(x) * gain_r[2:3, :]
                out_v[rows, :] = y
                send_v[rows, :] = y.astype(BF16)
                target = pl.ds(row * length + n * ROW_STEP, ROW_STEP)
                stores += copy_all(
                    sems, 12 + 2 * n, (send_v.at[rows], send_h.at[rows]), (out_v.at[rows], out_h.at[target])
                )
            wait_all(stores)

    return call(
        kernel,
        [e1, mats],
        [gains],
        kept if row else [rows_shape] + kept,
        [
            pltpu.VMEM((length, width), BF16),
            pltpu.VMEM((width, hidden), BF16),
            pltpu.VMEM((width, hidden), BF16),
            pltpu.VMEM((length, width), BF16),
            pltpu.VMEM((length, hidden), BF16),
            pltpu.VMEM((length, hidden), BF16),
            pltpu.VMEM((length, width), F32),
            pltpu.VMEM((length, width), F32),
            pltpu.VMEM((length, width), BF16),
            pltpu.SemaphoreType.DMA((20,)),
        ],
        flops_of(2, 20 << 20),
        [out_rows] if row else [],
    )


def encoder_backward(row, ins, extra, e1, mid, slope, mats, gains, after):
    length, width = extra.shape
    hidden = mats.shape[2]

    def kernel(cot_h, extra_h, e_h, mid_h, slope_h, w_h, gain_r, g_h, d_h, du_h, dgain_h,
               cot_v, extra_v, e_v, mid_v, slope_v, win_v, wout_v, d_v, du_v, dn_v, gm_v, g_v, dgain_v, sems):
        @pl.when(lax.axis_index("section") == 1)
        def _():
            loads = copy_all(
                sems, 0,
                (cot_h.at[pl.ds(row * length, length)], cot_v), (extra_h, extra_v), (mid_h, mid_v),
                (w_h.at[1], wout_v), (slope_h, slope_v), (w_h.at[0], win_v), (e_h, e_v),
            )
            wait_all(loads[:3])
            total = jnp.zeros((1, width), F32)
            for rows in row_chunks(length):
                dy = cot_v[rows, :].astype(F32) + extra_v[rows, :].astype(F32)
                dx, dgain = rms_back(mid_v[rows, :], gain_r[2:3, :], dy)
                gm_v[rows, :] = dx
                d_v[rows, :] = dx.astype(BF16)
                total = total + dgain
            dgain_v[1:2, :] = total
            stores = copy_all(sems, 7, (d_v, d_h))
            wait_all(loads[3:5])
            ffn_down(d_v, wout_v, slope_v, du_v)
            stores += copy_all(sems, 8, (du_v, du_h))
            wait_all(loads[5:])
            rows_out(du_v, win_v, 0, dn_v, False)
            total = jnp.zeros((1, width), F32)
            for rows in row_chunks(length):
                dx, dgain = rms_back(e_v[rows, :].astype(F32), gain_r[1:2, :], dn_v[rows, :])
                g_v[rows, :] = (gm_v[rows, :] + dx).astype(BF16)
                total = total + dgain
            dgain_v[0:1, :] = total
            stores += copy_all(sems, 9, (g_v, g_h), (dgain_v, dgain_h))
            wait_all(stores)

    return call(
        kernel,
        [ins, extra, e1, mid, slope, mats],
        [gains],
        [
            shape((length, width), BF16),
            shape((length, width), BF16),
            shape((length, hidden), BF16),
            shape((2, width), F32),
        ],
        [
            pltpu.VMEM((length, width), BF16),
            pltpu.VMEM((length, width), BF16),
            pltpu.VMEM((length, width), BF16),
            pltpu.VMEM((length, width), F32),
            pltpu.VMEM((length, hidden), BF16),
            pltpu.VMEM((width, hidden), BF16),
            pltpu.VMEM((width, hidden), BF16),
            pltpu.VMEM((length, width), BF16),
            pltpu.VMEM((length, hidden), BF16),
            pltpu.VMEM((length, width), F32),
            pltpu.VMEM((length, width), F32),
            pltpu.VMEM((length, width), BF16),
            pltpu.VMEM((2, width), F32),
            pltpu.SemaphoreType.DMA((11,)),
        ],
        flops_of(2, 20 << 20),
        after=after,
    )


def decoder(d_own, d_got, m_two, m_three, ins, cot_got, mats, got_mats, gains, segs, passed, after):
    length, width = d_own.shape
    hidden = mats.shape[2]

    def kernel(d2_h, d3_h, m2_h, m3_h, c1_h, c0_h, w1_h, w0_h, gain_r, seg_r,
               out_h, fa_h, fb_h, fc_h, other_h, gm_h, gd_h, dgain_h,
               d_v, m_v, c_v, wca_v, win_v, wout_v, n_v, q_v, mix_v, lse_v, mask_v, s_v, p_v, h_v, slope_v,
               x_v, y_v, dn_v, n5_v, do_v, dgain_v, dp_v, ds_v, dq_v, dm_v, do4_v, gm_v, gd_v, out_v, sems):
        section = lax.axis_index("section")

        @pl.when(section >= 2)
        def _():
            own = section == 3
            first_row = pl.ds(0, length)

            def put(first, *choices):
                return either_all(sems, first, own, *choices)

            quarters = [pl.ds(c * width, width) for c in range(4)]
            loads = put(0, ((d3_h, d_v), (d2_h, d_v)))
            cross_loads = put(
                21, *[((w1_h.at[0, :, cut], wca_v.at[:, cut]), (w0_h.at[0, :, cut], wca_v.at[:, cut])) for cut in quarters]
            )
            loads += put(
                1,
                ((m3_h, m_v), (m2_h, m_v)),
                *[((w1_h.at[k], v), (w0_h.at[k], v)) for k, v in ((1, win_v), (2, wout_v))],
                ((c1_h.at[first_row], c_v), (c0_h, c_v)),
            )
            fill_mask(mask_v, seg_r[pl.ds(3 - section, 1), :], False, 2 * length)
            loads[0].wait()
            for rows in row_chunks(length):
                x = d_v[rows, :].astype(F32)
                x_v[rows, :] = x
                n_v[rows, :] = (x * inverse_rms(x) * gain_r[4:5, :]).astype(BF16)
            part_of = lambda f_h, n, count=1: f_h.at[:, pl.ds(n * width, count * width)]
            stores = copy_all(sems, 6, (n_v, part_of(fc_h, 0)))
            cross_loads[0].wait()
            project(n_v, wca_v, 0, q_v, 0, width)
            loads[1].wait()
            stores += copy_all(sems, 7, (m_v, part_of(fc_h, 1)))
            wait_all(cross_loads[1:3])
            project(m_v, wca_v, width, q_v, width, 2 * width)
            attend(q_v, q_v, q_v, 0, width, 2 * width, mask_v, None, s_v, p_v, mix_v, lse_v)
            stores += copy_all(sems, 9, (mix_v, part_of(fc_h, 2)))

            cross_loads[3].wait()

            @pl.loop(0, width // 256)
            def _(t):
                cols = pl.ds(pl.multiple_of(t * 256, 256), 256)
                part = mm(mix_v[...], wca_v[:, pl.ds(pl.multiple_of(3 * width + t * 256, 256), 256)])
                x_v[:, cols] = x_v[:, cols] + part

            for rows in row_chunks(length):
                x = x_v[rows, :]
                y_v[rows, :] = x
                n5_v[rows, :] = (x * inverse_rms(x) * gain_r[5:6, :]).astype(BF16)
            stores += copy_all(sems, 10, (n5_v, part_of(fa_h, 0)))
            loads[2].wait()
            ffn_up(n5_v, win_v, h_v, slope_v)
            stores += copy_all(sems, 11, (h_v, part_of(fb_h, 1, 4)))
            loads[3].wait()
            rows_out(h_v, wout_v, 0, y_v, True)
            loads[4].wait()
            total = jnp.zeros((1, width), F32)
            for rows in row_chunks(length):
                y = y_v[rows, :]
                out_v[rows, :] = y * inverse_rms(y) * gain_r[6:7, :]
                dy, dgain = rms_back(y, gain_r[6:7, :], c_v[rows, :].astype(F32))
                total = total + dgain
                do_v[rows, :] = dy.astype(BF16)
                y_v[rows, :] = dy
            dgain_v[2:3, :] = total
            stores += put(12, ((out_v, out_h.at[first_row]), (out_v, other_h)))
            stores += copy_all(sems, 13, (do_v, part_of(fb_h, 0)))
            ffn_down(do_v, wout_v, slope_v, slope_v)
            stores += copy_all(sems, 14, (slope_v, part_of(fa_h, 1, 4)))
            rows_out(slope_v, win_v, 0, dn_v, False)
            total = jnp.zeros((1, width), F32)
            for rows in row_chunks(length):
                dx, dgain = rms_back(x_v[rows, :], gain_r[5:6, :], dn_v[rows, :])
                dx = y_v[rows, :] + dx
                y_v[rows, :] = dx
                do4_v[rows, :] = dx.astype(BF16)
                total = total + dgain
            dgain_v[1:2, :] = total
            stores += copy_all(sems, 15, (do4_v, part_of(fc_h, 6)))
            rows_out(do4_v, wca_v, 3 * width, dm_v, False)
            attend_back(q_v, q_v, q_v, dm_v, mix_v, 0, width, 2 * width, mask_v, None, lse_v,
                        dp_v, s_v, p_v, ds_v, dq_v, 0, None)
            stores += copy_all(sems, 16, (dq_v, part_of(fc_h, 3, 3)))
            rows_out(dq_v.at[:, width:], wca_v, width, gm_v, False)
            stores += copy_all(sems, 18, (gm_v, gm_h))
            rows_out(dq_v.at[:, :width], wca_v, 0, dn_v, False)
            total = jnp.zeros((1, width), F32)
            for rows in row_chunks(length):
                dx, dgain = rms_back(d_v[rows, :].astype(F32), gain_r[4:5, :], dn_v[rows, :])
                gd_v[rows, :] = (y_v[rows, :] + dx).astype(BF16)
                total = total + dgain
            dgain_v[0:1, :] = total
            stores += copy_all(sems, 19, (gd_v, gd_h), (dgain_v, dgain_h))
            wait_all(stores)

    narrow = shape((length, width), BF16)
    return call(
        kernel,
        [d_own, d_got, m_two, m_three, ins, cot_got, mats, got_mats],
        [gains, segs],
        [
            *[shape((length, count * width), BF16) for count in (5, 5, 7)],
            shape((length, width), F32),
            *(narrow, narrow),
            shape((3, width), F32),
        ],
        [
            pltpu.VMEM((length, width), BF16),
            pltpu.VMEM((length, width), BF16),
            pltpu.VMEM((length, width), BF16),
            pltpu.VMEM((width, 4 * width), BF16),
            pltpu.VMEM((width, hidden), BF16),
            pltpu.VMEM((width, hidden), BF16),
            pltpu.VMEM((length, width), BF16),
            pltpu.VMEM((length, 3 * width), BF16),
            pltpu.VMEM((length, width), BF16),
            pltpu.VMEM((16, length), F32),
            pltpu.VMEM((length, length), F32),
            pltpu.VMEM((2, length, length), F32),
            pltpu.VMEM((2, length, length), BF16),
            pltpu.VMEM((length, hidden), BF16),
            pltpu.VMEM((length, hidden), BF16),
            pltpu.VMEM((length, width), F32),
            pltpu.VMEM((length, width), F32),
            pltpu.VMEM((length, width), F32),
            pltpu.VMEM((length, width), BF16),
            pltpu.VMEM((length, width), BF16),
            pltpu.VMEM((3, width), F32),
            pltpu.VMEM((2, length, length), F32),
            pltpu.VMEM((2, length, length), BF16),
            pltpu.VMEM((length, 3 * width), BF16),
            pltpu.VMEM((length, width), BF16),
            pltpu.VMEM((length, width), BF16),
            pltpu.VMEM((length, width), BF16),
            pltpu.VMEM((length, width), BF16),
            pltpu.VMEM((length, width), F32),
            pltpu.SemaphoreType.DMA((25,)),
        ],
        flops_of(12, 30 << 20),
        passed,
        after,
    )


def weight_grad(sections, groups, chunks, ndp, decoder=None, passed=()):
    length, width = groups[0][0][0][0].shape[0], 768
    columns = sum(group[2] for group in groups)
    pieces = len(groups[0][0])
    bits = ndp.bit_length() - 1
    block = width // ndp
    flat = []
    for a_list, b_list, _ in groups + (decoder or []):
        for array, _ in a_list + b_list:
            if not any(array is other for other in flat):
                flat.append(array)
    place = lambda array: [index for index, other in enumerate(flat) if other is array][0]
    plan_of = lambda groups: [
        ([(place(a), a0) for a, a0 in a_list], [(place(b), b0) for b, b0 in b_list], count)
        for a_list, b_list, count in groups
    ]
    plan, other_plan = plan_of(groups), plan_of(decoder or groups)
    tile = 768
    copies = 2 * pieces * len(groups)

    def kernel(*args):
        sources = args[: len(flat)]
        outs = args[len(flat) : len(flat) + 2 * len(chunks)]
        a_v, at_v, b_v, out_v, sems = args[len(flat) + 2 * len(chunks) :]
        me = lax.axis_index("dp")
        section = lax.axis_index("section")
        active = section == sections[0]
        for one in sections[1:]:
            active = active | (section == one)

        @pl.when(active)
        def _():
            loads, start = [], 0
            for g, (a_list, b_list, count) in enumerate(plan):
                group_loads = []
                for k in range(pieces):
                    rows = pl.ds(k * length, length)
                    choices = []
                    for a_of, b_of, _ in (other_plan[g], plan[g]):
                        (ai, a0), (bi, b0) = a_of[k], b_of[k]
                        choices.append((
                            (sources[ai].at[:, pl.ds(a0, width)], a_v.at[g, rows]),
                            (sources[bi].at[:, pl.ds(b0, count)], b_v.at[rows, pl.ds(start, count)]),
                        ))
                    first = 2 * (g * pieces + k)
                    if decoder:
                        group_loads += either_all(sems, first, section >= 2, *zip(*choices))
                    else:
                        group_loads += copy_all(sems, first, *choices[0])
                loads.append(group_loads)
                start += count
            stores, group, group_end, start = [], -1, 0, 0
            for number, (count, order) in enumerate(chunks):
                spots = []
                for b in range(ndp):
                    code = jnp.bitwise_xor(me, b)
                    spot = 0
                    for k in range(bits):
                        spot = spot + ((code >> order[k]) & 1) * (1 << (bits - 1 - k))
                    spots.append(spot)
                done, end = start, start + count
                while done < end:
                    if done == group_end:
                        group += 1
                        wait_all(loads[group])
                        at_v[...] = a_v[group].T
                        group_end += plan[group][2]
                    upto = min(end, group_end)

                    @pl.loop(0, (upto - done) // tile)
                    def _(t):
                        cols = pl.ds(pl.multiple_of(done + t * tile, 128), tile)
                        part = mm(at_v[...], b_v[:, cols])
                        for b in range(ndp):
                            out_v[spots[b], :, cols] = part[b * block : (b + 1) * block, :].astype(BF16)

                    done = upto
                for half in range(2):
                    source = out_v.at[pl.ds(half * (ndp // 2), ndp // 2), :, pl.ds(start, count)]
                    stores += copy_all(sems, copies + 2 * number + half, (source, outs[2 * number + half]))
                start = end
            wait_all(stores)

    return job(
        kernel,
        flat,
        [],
        [] if passed else [shape((ndp // 2, block, count), BF16) for count, _ in chunks for _ in range(2)],
        [
            pltpu.VMEM((len(groups), pieces * length, width), BF16),
            pltpu.VMEM((width, pieces * length), BF16),
            pltpu.VMEM((pieces * length, columns), BF16),
            pltpu.VMEM((ndp, block, columns), BF16),
            pltpu.SemaphoreType.DMA((copies + 2 * len(chunks),)),
        ],
        passed=passed,
        result=lambda made: [(made[2 * number], made[2 * number + 1]) for number in range(len(chunks))],
    )


def along_dp(value, bit, sections, ndp):
    pairs = [(s * ndp + d, s * ndp + (d ^ bit)) for s in sections for d in range(ndp)]
    return lax.ppermute(value, ("section", "dp"), pairs)


def added(items):
    outs, kinds = [], []
    for keep, _, _ in items:
        kind = "sum" if keep.dtype == F32 else "last" if keep.shape[0] == 1 else "half"
        kinds.append(kind)
        if kind == "half":
            outs += [shape((keep.shape[0] // 2,) + keep.shape[1:], BF16)] * 2
        else:
            outs.append(shape(keep.shape if kind == "sum" else keep.shape[1:], F32))

    def kernel(*refs):
        count = len(items)
        sources, rest = refs[: 2 * count], refs[2 * count :]
        targets, rest = rest[: len(outs)], rest[len(outs) :]
        scratch, sems = rest[:-1], rest[-1]
        section = lax.axis_index("section")

        def takes_part(sections):
            active = section == sections[0]
            for one in sections[1:]:
                active = active | (section == one)
            return active

        for number, item in enumerate(items):
            @pl.when(takes_part(item[2]))
            def _():
                for k in range(2):
                    pltpu.make_async_copy(
                        sources[2 * number + k], scratch[3 * number + k], sems.at[4 * number + k]
                    ).start()

        place = 0
        for number, (item, kind) in enumerate(zip(items, kinds)):
            n = item[0].shape[0]
            keep_v, got_v, out_v = scratch[3 * number : 3 * number + 3]
            mine = targets[place : place + (2 if kind == "half" else 1)]
            place += len(mine)

            @pl.when(takes_part(item[2]))
            def _():
                for k, v in enumerate((keep_v, got_v)):
                    pltpu.make_async_copy(sources[2 * number + k], v, sems.at[4 * number + k]).wait()
                if kind == "half":
                    @pl.loop(0, n)
                    def _(i):
                        out_v[i] = (keep_v[i].astype(F32) + got_v[i].astype(F32)).astype(BF16)

                    wait_all(
                        copy_all(
                            sems, 4 * number + 2,
                            (out_v.at[pl.ds(0, n // 2)], mine[0]), (out_v.at[pl.ds(n // 2, n // 2)], mine[1]),
                        )
                    )
                else:
                    if kind == "last":
                        out_v[...] = keep_v[0].astype(F32) + got_v[0].astype(F32)
                    else:
                        out_v[...] = keep_v[...] + got_v[...]
                    wait_all(copy_all(sems, 4 * number + 2, (out_v, mine[0])))

    scratch = []
    for (keep, _, _), kind in zip(items, kinds):
        own = pltpu.VMEM(keep.shape, keep.dtype)
        scratch += [own, own, pltpu.VMEM(keep.shape[1:], F32) if kind == "last" else own]
    def result(made):
        results = []
        for kind in kinds:
            size = 2 if kind == "half" else 1
            results.append(tuple(made[:size]) if size == 2 else made[0])
            made = made[size:]
        return results

    return job(
        kernel,
        [array for keep, got, _ in items for array in (keep, got)],
        [],
        outs,
        scratch + [pltpu.SemaphoreType.DMA((4 * len(items),))],
        result=result,
    )


def joined(v, pieces):
    start = 0
    for piece in pieces:
        yield piece, v.at[:, pl.ds(start, piece.shape[1])]
        start += piece.shape[1]


def outputs(one, two, three, rows_got, out_rows, after):
    length, width = rows_got.shape
    block, columns = two[0].shape[0], 2 * two[0].shape[1]

    def kernel(a_h, b_h, s0_h, s1_h, c0_h, c1_h, r_h, out_h, grad_h, f_v, s_v, c_v, r_v, sems):
        section = lax.axis_index("section")
        even = section % 2 == 0
        loads = copy_all(sems, 0, *joined(f_v, (a_h, b_h)))

        @pl.when(section == 3)
        def _():
            wait_all(copy_all(sems, 9, *joined(s_v, (s0_h, s1_h)), *joined(c_v, (c0_h, c1_h)), (r_h, r_v)))
            wait_all(loads)
            wait_all(
                copy_all(
                    sems, 5,
                    (f_v, grad_h.at[1]), (s_v, grad_h.at[2]), (c_v, grad_h.at[0]), (r_v, out_h.at[pl.ds(length, length)]),
                )
            )

        @pl.when(section != 3)
        def _():
            c_v[...] = jnp.zeros_like(c_v)
            stores = copy_all(sems, 5, (c_v, grad_h.at[2]))

            @pl.when(section == 1)
            def _():
                wait_all(copy_all(sems, 9, *joined(s_v, (s0_h, s1_h))))
                wait_all(copy_all(sems, 3, (s_v, grad_h.at[1])))

            @pl.when(even)
            def _():
                wait_all(copy_all(sems, 3, (c_v, grad_h.at[1])))

            wait_all(loads)
            wait_all(stores + copy_all(sems, 6, (f_v, grad_h.at[0])))

    return call(
        kernel,
        [*one, *two, *three, rows_got],
        [],
        [shape((3, block, columns), F32)],
        [pltpu.VMEM((block, columns), F32)] * 3 + [pltpu.VMEM((length, width), F32), pltpu.SemaphoreType.DMA((14,))],
        flops_of(1, 1 << 20),
        [out_rows],
        after,
    )


def per_device(section_ins, segments, buckets, section_mats, gains, tables):
    ndp = lax.axis_size("dp")
    ins = section_ins[0]
    mats = section_mats[0]
    length = segments.shape[1]
    width = ins.shape[1]
    segs = segments
    by_head = jnp.transpose(tables, (2, 0, 1))
    flipped = jnp.pad(buckets[:, ::-1], ((0, 0), (0, 1)), constant_values=-1)
    everywhere = (0, 1, 2, 3)
    move = lambda value, pairs: lax.ppermute(value, "section", pairs)

    got_mats = move(section_mats, [(3, 2), (1, 0)])[0]
    *fwd0, tiles = self_forward(0, ins, mats, gains, segs, by_head, buckets)
    first0 = move(fwd0[0], [(0, 1), (2, 3)])
    fwd1 = self_forward(1, ins, mats, gains, segs, by_head, buckets, tiles)
    first1 = move(fwd1[0], [(0, 1)])
    toe = transposed_bias(by_head, flipped, length, [fwd1[0]])
    out_rows, *enc0 = encoder_forward(0, first0, mats, gains, None)
    m_three = move(enc0[0], [(1, 3)])
    late_ins, _ = lax.optimization_barrier((ins, m_three))
    cot_got = move(late_ins[length:], [(3, 2)])
    out_rows, *enc1 = encoder_forward(1, first1, mats, gains, out_rows)
    m_two = move(enc1[0], [(1, 2)])
    here = marker([enc1[0], m_three])

    dec = decoder(fwd1[0], first0, m_two, m_three, ins, cot_got, mats, got_mats, gains, segs, [out_rows], [toe, here])
    out_rows, *factors, other, g_mem, g_self, dgain_d = dec
    even, odd = (0, 2), (1, 3)
    extra0 = move(g_mem, [(3, 1)])
    extra1 = move(g_mem, [(2, 0)])
    (sent, g_self_sent), _ = lax.optimization_barrier(((factors, g_self), extra0))
    got = [move(value, [(2, 3)]) for value in sent]
    g_self_got = move(g_self_sent, [(3, 2)])
    back0 = encoder_backward(0, ins, extra0, first0, enc0[1], enc0[4], mats, gains, [extra1])
    g0 = move(back0[0], [(1, 0)])
    (other, extra1), _ = lax.optimization_barrier(((other, extra1), back0[0]))
    extra1 = move(extra1, [(0, 1)])
    own0 = self_backward(
        0, even, ins, mats, gains, segs, toe, g0, g_self_got, fwd0[1:], [out_rows], [extra1]
    )
    out_rows, acc = own0[:2]
    back1 = encoder_backward(1, ins, extra1, first1, enc1[1], enc1[4], mats, gains, [acc])
    other, _ = lax.optimization_barrier((other, back1[0]))
    rows_got = move(other, [(2, 3)])

    plain = tuple(range(ndp.bit_length() - 1))
    turned = (1, 0) + plain[2:]
    orders = (plain, turned)
    steps = len(plain)
    whole = 4 * width
    rows_of = lambda which, at: [(factors[which], at * width), (got[which], at * width)]
    halves = [(2 * width, order) for order in orders]
    groups = [([(enc0[2], 0), (enc1[2], 0)], [(back0[2], 0), (back1[2], 0)], whole)]
    groups_d = [(rows_of(0, 0), rows_of(0, 1), whole)]
    made, = run([weight_grad(odd, groups, halves, ndp, groups_d)], [back1[0]])
    g1, _ = lax.optimization_barrier((back1[0], made[0][0]))
    g1 = move(g1, [(1, 0)])
    own1 = self_backward(
        1, even, ins, mats, gains, segs, toe, g1, g_self, fwd1[1:], [out_rows, acc], [made[0][0]]
    )
    out_rows, acc = own1[:2]
    groups = [
        ([(fwd0[1], 0), (fwd1[1], 0)], [(own0[3], 0), (own1[3], 0)], 3 * width),
        ([(fwd0[3], 0), (fwd1[3], 0)], [(own0[3], 3 * width), (own1[3], 3 * width)], width),
    ]
    made, = run([weight_grad(even, groups, halves, ndp, passed=[*made[0], *made[1]])], [out_rows])

    def send(pair, order, step, sections):
        return (pair[0], along_dp(pair[1], 1 << order[step], sections, ndp), sections)

    def send_one(pairs, step):
        return [send(pair, order, step, everywhere) for pair, order in zip(pairs, orders)]

    def send_rest(pairs, part, step):
        sections = odd if part == 1 else (3,)
        return [send(pair, order, step, sections) for pair, order in zip(pairs, orders)]

    one = send_one(made, 0)
    groups = [([(back0[1], 0), (back1[1], 0)], [(enc0[3], 0), (enc1[3], 0)], whole)]
    groups_d = [(rows_of(1, 0), rows_of(1, 1), whole)]
    two, = run([weight_grad(odd, groups, halves, ndp, groups_d)], [made[0][0]])
    groups = [(rows_of(2, k), rows_of(2, at), count * width) for k, at, count in ((0, 3, 1), (1, 4, 2), (2, 6, 1))]
    three, = run([weight_grad((3,), groups, halves, ndp)], [two[0][0]])
    rest = [send_rest(two, 1, 0), send_rest(three, 2, 0)]
    dgains = ([own0[2], own1[2]], [back0[3], back1[3]], dgain_d)
    small, = run([packed_small(acc, flipped, *dgains)], [three[0][0]])
    small_got = along_dp(small, 1, everywhere, ndp)
    tied = [small]
    sums_of = [one, *rest]
    turns = [(2 * k + (0, 1, 2.5)[part], k, part) for k in range(steps) for part in range(3)]
    for _, k, part in sorted(turns):
        last = k + 1 == steps
        items = sums_of[part]
        cost = SHORT if part < 2 and not last else None if part == 2 else LONG
        number = 2 * k + part
        if part < 2 and number < steps:
            (*sums, small), = run([added([*items, (small, small_got, everywhere)])], tied, cost)
            if number + 1 < steps:
                small_got = along_dp(small, 2 << number, everywhere, ndp)
        else:
            sums, = run([added(items)], tied, cost)
        tied = [sums[0] if last else sums[0][0]]
        if not last:
            sums = send_one(sums, k + 1) if not part else send_rest(sums, part, k + 1)
        sums_of[part] = sums
    one, *rest = sums_of
    small, _ = lax.optimization_barrier((small, tied[0]))
    small = small + move(small, [(0, 1), (1, 0), (2, 3), (3, 2)])
    small = small + move(small, [(0, 2), (2, 0), (1, 3), (3, 1)])
    out_rows, grad = outputs(one, *rest, rows_got, out_rows, tied)

    gains_grad = small[: gains.shape[0]]
    heads = [
        jnp.concatenate([small[8:16, at : at + 32], small[8:12, at + 128 : at + 160]], axis=0)
        for at in range(0, 256 * tables.shape[0], 256)
    ]
    return out_rows[None], grad[None], gains_grad, jnp.swapaxes(jnp.stack(heads), 1, 2)


def solution(mesh):
    placed = (
        P("section", "dp", None),
        P("dp", None),
        P(),
        P("section", None, None, None),
        P(),
        P(),
    )
    return jax.shard_map(
        per_device,
        mesh=mesh,
        in_specs=placed,
        out_specs=(P("section", "dp", None), P("section", None, "dp", None), P(), P()),
        check_vma=False,
    )
```
